32 devices in a mesh: dp: 4 (over y, core), expert: 8 (over z, x).
Axes of the slice: x: 2, y: 2, z: 4, core: 2. Of those that a mesh axis runs over, the one named last changes fastest.
Arguments:
- tokens: bfloat16 [2, 8192, 1536], P(None, ('dp', 'expert')), may hold values from -6 to 6
- segments: int32 [2, 8192], P(None, ('dp', 'expert')), may hold values from 0 to 3, as said below
- routes: int32 [2, 8192, 4], P(None, ('dp', 'expert')), may hold values from 0 to 31, all different within a row; in each aligned block of 256 rows (0 to 255, 256 to 511, ..., all dimensions but the last counted through in order) at most 64 rows name the same one
- norm_one: bfloat16 [1536], P('dp'), may hold values from 0.099609375 to 1.8984375
- norm_two: bfloat16 [1536], P('dp'), may hold values from 0.099609375 to 1.8984375
- w_query: bfloat16 [1536, 1536], P('dp'), may hold values from -0.15625 to 0.15625
- key_value_weight: bfloat16 [1536, 512], P('dp'), may hold values from -0.15625 to 0.15625
- w_out_attn: bfloat16 [1536, 1536], P('dp'), may hold values from -0.875 to 0.875
- w_router: bfloat16 [1536, 32], P('dp'), may hold values from -0.076171875 to 0.076171875
- w_in: bfloat16 [32, 1536, 1536], P('expert'), may hold values from -0.15625 to 0.15625
- w_out: bfloat16 [32, 768, 1536], P('expert'), may hold values from -0.4375 to 0.4375
- cotangent: bfloat16 [2, 8192, 1536], P(None, ('dp', 'expert')), may hold values from -6 to 6
Outputs:
- output_act: bfloat16 [2, 8192, 1536], P(None, ('dp', 'expert'))
- grad_input: bfloat16 [2, 8192, 1536], P(None, ('dp', 'expert'))
- grad_norm_one: float32 [1536], P('dp')
- grad_norm_two: float32 [1536], P('dp')
- grad_query: float32 [1536, 1536], P('dp')
- grad_keyval: float32 [1536, 512], P('dp')
- grad_out_attn: float32 [1536, 1536], P('dp')
- grad_router: float32 [1536, 32], P('dp')
- grad_w_in: float32 [32, 1536, 1536], P('expert', 'dp')
- grad_w_out: float32 [32, 768, 1536], P('expert', 'dp')
The draws below stay inside these ranges and needn't reach their ends.
Inputs may be any that keep to these rules, and one draw needn't show every extreme that they name: `routes`: in each aligned block of 256 rows (the tokens of one device in one micro-batch) no expert is named by more than 64 rows, a bound that some block reaches. `segments`: within each sequence of 256 tokens the numbers start at 0, never fall and rise by one at three places; equal numbers mark one document.
All inputs are finite; a program needn't handle non-finite values.
Results may differ from the reference program's by a relative error of at most 0.02.
Values may be sent and summed in bfloat16 or wider, within the bound.
No kernel may reach another device: no remote copies, remote signals or barrier semaphores. Data moves between devices by JAX's collectives and lax.ppermute only.
A program may use at most 320 MiB of HBM per device.

```python
import math
import jax
import jax.numpy as jnp
import numpy as np
from jax import lax

MODEL_DIMENSION = 1536
QUERY_HEADS = 12
KEY_VALUE_HEADS = 2
HEAD_SIZE = 128
FF = 768
EXPERTS = 32
TOPK = 4
TOK_MB = 256
MB = 2
CAP = 64
TOKENS = 8192


def draw_segments(key, part):
    key = jax.random.fold_in(key, 11)
    seq_count = MB * (TOKENS // TOK_MB)
    seq_keys = jax.random.split(key, seq_count)

    def one_sequence(seq_key):
        cuts = jax.random.permutation(seq_key, TOK_MB - 1)[:3] + 1
        position = jnp.arange(TOK_MB, dtype=jnp.int32)
        return jnp.sum((position[:, None] >= cuts[None, :]).astype(jnp.int32), axis=1).astype(jnp.int32)
    return jax.vmap(one_sequence)(seq_keys).reshape(MB, TOKENS).astype(jnp.int32)


def block_levels(rng, shape, shards, smallest, top_value):
    def one(dim, parts):
        steps = jax.random.uniform(jax.random.fold_in(jax.random.fold_in(rng, 6), dim), (parts,), jnp.float32, smallest / len(shards), top_value / len(shards))
        return jnp.repeat(jnp.exp(steps), shape[dim] // parts).reshape((-1,) + (1,) * (len(shape) - dim - 1))

    level = one(*shards[0])
    for cut in shards[1:]:
        level = level * one(*cut)
    return level


def deal_out(own_key, own, number, rows, count, top, limit, skew):
    ranking = jax.random.permutation(own_key, count)
    heavy_load, ordinary = load_shares(count, rows * top, limit, skew, True), load_shares(count, rows * top, limit, skew, False)
    places = jnp.arange(count)

    def named(tallies, offset_by):
        used = int((tallies > 0).sum())
        fixed = max(1, used // 4)
        passed = fixed + (places - fixed + offset_by * (used - fixed)) % max(1, count - fixed)
        return jnp.zeros((count,), jnp.int32).at[ranking[jnp.where(places < fixed, places, passed)]].set(jnp.asarray(tallies, jnp.int32))

    tallies = jnp.where(number % 4 == 0, named(heavy_load, number // 4), named(ordinary, number - number // 4 - 1))
    mixed = jax.random.permutation(jax.random.fold_in(own, 3), count)
    source_of, taker = mixed[0:count // 2 * 2:2], mixed[1:count // 2 * 2:2]
    room = jnp.minimum(tallies[source_of] - 1, limit - tallies[taker]) // 2
    room = jnp.where((source_of == ranking[0]) | (taker == ranking[0]) | (tallies[taker] == 0), 0, jnp.maximum(room, 0))
    passed = jax.random.randint(jax.random.fold_in(own, 4), (count // 2,), 0, 1 << 20) % (room + 1)
    tallies = tallies.at[source_of].add(-passed).at[taker].add(passed)
    labels = jnp.searchsorted(jnp.cumsum(tallies), jnp.arange(rows * top), side="right").astype(jnp.int32)
    grid = labels.reshape(top, rows).T
    grid = grid[jax.random.permutation(jax.random.fold_in(own, 1), rows)]
    offset_by = jax.random.randint(jax.random.fold_in(own, 2), (rows, 1), 0, top)
    return jnp.take_along_axis(grid, (jnp.arange(top)[None, :] + offset_by) % top, axis=1)


def load_shares(amount, total, limit, lean, full):
    loads = [(1 << 20) // math.isqrt(standing ** lean) + 1 for standing in range(1, amount + 1)]
    largest = limit if full else min(limit, max(-(-total // amount), total * loads[0] // sum(loads)))
    least = 1 if total - largest >= amount - 1 else 0
    counts, surplus = [largest] + [least] * (amount - 1), total - largest - least * (amount - 1)
    while surplus > 0:
        candidates = [i for i in range(1, amount) if counts[i] < largest] or [i for i in range(1, amount) if counts[i] < limit]
        whole, remaining = sum([loads[i] for i in candidates]), surplus
        for i in candidates:
            more = min(limit - counts[i], max(1, remaining * loads[i] // whole), surplus)
            counts[i] = counts[i] + more
            surplus = surplus - more
    return np.array(counts)


def centred(rng, extent, spread, limit, shards=(), kind=jnp.bfloat16):
    values = spread * jax.random.normal(rng, extent, jnp.float32)
    if shards:
        values = values * block_levels(rng, extent, shards, -0.22, 0.18)
    return jnp.clip(values, -limit, limit).astype(kind)


def setup_inputs(seed: int = 0) -> dict:
    seeds = jax.random.split(jax.random.key(seed), 13)
    tokens = centred(seeds[0], (MB, TOKENS, MODEL_DIMENSION), 1.0, 6.0, ((1, 32),))
    segments = draw_segments(jax.random.fold_in(seeds[12], 71), 0)
    routes_keys = jax.random.split(jax.random.fold_in(seeds[2], 1), MB * TOKENS // TOK_MB)
    routes_turns = jax.random.permutation(jax.random.fold_in(seeds[2], 3), MB * TOKENS // TOK_MB)
    routes = jax.vmap(lambda own, number: deal_out(jax.random.fold_in(seeds[2], 2), own, number, TOK_MB, EXPERTS, TOPK, CAP, 2))(routes_keys, routes_turns).reshape((MB, TOKENS, TOPK))
    norm_one = jnp.clip(1.0 + 0.18 * jax.random.normal(seeds[3], (MODEL_DIMENSION,), jnp.float32), 0.099609375, 1.8984375).astype(jnp.bfloat16)
    norm_two = jnp.clip(1.0 + 0.18 * jax.random.normal(seeds[4], (MODEL_DIMENSION,), jnp.float32), 0.099609375, 1.8984375).astype(jnp.bfloat16)
    w_query = centred(seeds[5], (MODEL_DIMENSION, QUERY_HEADS * HEAD_SIZE), MODEL_DIMENSION ** -0.5, 0.15625, ((0, 4),))
    key_value_weight = centred(seeds[6], (MODEL_DIMENSION, 2 * KEY_VALUE_HEADS * HEAD_SIZE), MODEL_DIMENSION ** -0.5, 0.15625, ((0, 4),))
    w_out_attn = centred(seeds[7], (QUERY_HEADS * HEAD_SIZE, MODEL_DIMENSION), (max(QUERY_HEADS * HEAD_SIZE // 32, 8)) ** -0.5, 0.875, ((0, 4),))
    w_router = centred(seeds[8], (MODEL_DIMENSION, EXPERTS), (0.5 / MODEL_DIMENSION ** 0.5), 0.076171875, ((0, 4),))
    w_in = centred(seeds[9], (EXPERTS, MODEL_DIMENSION, 2 * FF), MODEL_DIMENSION ** -0.5, 0.15625, ((0, 8),))
    w_out = centred(seeds[10], (EXPERTS, FF, MODEL_DIMENSION), (FF // 4) ** -0.5, 0.4375, ((0, 8),))
    cotangent = centred(seeds[11], (MB, TOKENS, MODEL_DIMENSION), 1.0, 6.0, ((1, 32),))
    return dict(tokens=tokens, segments=segments, routes=routes, norm_one=norm_one, norm_two=norm_two, w_query=w_query, key_value_weight=key_value_weight, w_out_attn=w_out_attn, w_router=w_router, w_in=w_in, w_out=w_out, cotangent=cotangent)


@jax.custom_vjp
def lower_half(v):
    return lax.optimization_barrier(v.astype(jnp.bfloat16)).astype(jnp.float32)

@jax.custom_vjp
def low_back(v):
    return v

def low_keep(v):
    return (lower_half(v), None)

def low_pass(kept, grad):
    return (grad,)

def back_keep(v):
    return (v, None)

def back_low(kept, grad):
    return (lower_half(grad),)
lower_half.defvjp(low_keep, low_pass)
low_back.defvjp(back_keep, back_low)
eps_norm = 1e-06
rope_base = 1000000.0
mask_fill = -1e+30
highest = lax.Precision.HIGHEST

def round_both(tensor):
    return low_back(lower_half(tensor))

def product(left_side, right_side):
    return jnp.dot(left_side, right_side, precision=highest)

def rms_scale(tensor):
    return lax.rsqrt(lax.optimization_barrier(jnp.mean(tensor * tensor, axis=-1, keepdims=True)) + eps_norm)

def rope_tables(sequence_length, head_width):
    positions = jnp.arange(sequence_length).astype(jnp.float32)
    frequency = rope_base ** (-(jnp.arange(head_width // 2).astype(jnp.float32) * 2.0) / head_width)
    angles = positions[:, None] * frequency[None, :]
    return (jnp.cos(angles), jnp.sin(angles))

def apply_rotation(tensor, cosine_table, sine_values):
    midway = tensor.shape[-1] // 2
    front_half = tensor[..., :midway]
    back_half = tensor[..., midway:]
    cos_rows = cosine_table[:, None, :]
    sin_rows = sine_values[:, None, :]
    return jnp.concatenate([front_half * cos_rows - back_half * sin_rows, back_half * cos_rows + front_half * sin_rows], axis=-1)

def layer_block(group_items, params):
    tokens, segments, routes = group_items
    norm_one, norm_two, w_query, key_value_weight, w_out_attn, w_router, w_in, w_out = params
    group_count, sequence_length, model_width = tokens.shape
    heads_per_group = QUERY_HEADS // KEY_VALUE_HEADS
    score_scale = 1.0 / math.sqrt(HEAD_SIZE)
    cosine_table, sine_values = rope_tables(sequence_length, HEAD_SIZE)
    scale_one = rms_scale(tokens)
    normed = lower_half(tokens * scale_one * norm_one)
    query_lin = low_back(product(normed, w_query))
    key_value_linear = low_back(product(normed, key_value_weight))
    query_rows = lower_half(apply_rotation(query_lin.reshape(group_count, sequence_length, QUERY_HEADS, HEAD_SIZE), cosine_table, sine_values))
    key_matrix = lower_half(apply_rotation(key_value_linear[..., :KEY_VALUE_HEADS * HEAD_SIZE].reshape(group_count, sequence_length, KEY_VALUE_HEADS, HEAD_SIZE), cosine_table, sine_values))
    value_rows = lower_half(key_value_linear[..., KEY_VALUE_HEADS * HEAD_SIZE:].reshape(group_count, sequence_length, KEY_VALUE_HEADS, HEAD_SIZE))
    grouped_rows = query_rows.reshape(group_count, sequence_length, KEY_VALUE_HEADS, heads_per_group, HEAD_SIZE)
    scores = low_back(jnp.einsum('bskgd,btkd->bkgst', grouped_rows, key_matrix, precision=highest) * score_scale)
    position = jnp.arange(sequence_length)
    allowed = (segments[:, :, None] == segments[:, None, :]) & (position[:, None] >= position[None, :])
    scores = jnp.where(allowed[:, None, None], scores, mask_fill)
    row_max = lax.optimization_barrier(jnp.max(scores, axis=-1, keepdims=True))
    exp_scores = jnp.exp(scores - row_max)
    prob_rows = lower_half(exp_scores / lax.optimization_barrier(jnp.sum(exp_scores, axis=-1, keepdims=True)))
    mixed_out = jnp.einsum('bkgst,btkd->bskgd', prob_rows, value_rows, precision=highest)
    mixed_out = round_both(mixed_out.reshape(group_count, sequence_length, QUERY_HEADS * HEAD_SIZE))
    hidden = tokens + low_back(product(mixed_out, w_out_attn))
    scale_two = rms_scale(hidden)
    normed_two = lower_half(hidden * scale_two * norm_two)
    logits = product(normed, w_router)
    onehot = (routes[..., None] == jnp.arange(EXPERTS)).astype(jnp.float32)
    chosen = lax.optimization_barrier(jnp.sum(onehot * logits[:, :, None, :], axis=-1))
    chosen_max = lax.optimization_barrier(jnp.max(chosen, axis=-1, keepdims=True))
    gate_exp = jnp.exp(chosen - chosen_max)
    gate_probs = gate_exp / lax.optimization_barrier(jnp.sum(gate_exp, axis=-1, keepdims=True))
    combine = lax.optimization_barrier(jnp.sum(gate_probs[..., None] * onehot, axis=2)).reshape(-1, EXPERTS)
    flat_rows = normed_two.reshape(-1, model_width)

    def expert_step(running, inputs):
        weight_in, weight_out, column = inputs
        rows_in = low_back(flat_rows)
        pre_act = low_back(product(rows_in, weight_in))
        activated = lower_half(jax.nn.gelu(pre_act[:, :FF], approximate=True) * pre_act[:, FF:])
        result_rows = round_both(product(activated, weight_out))
        return (running + column[:, None] * result_rows, None)
    expert_sum, unused_out = lax.scan(jax.checkpoint(expert_step), jnp.zeros_like(flat_rows), (w_in, w_out, combine.T))
    return hidden + expert_sum.reshape(hidden.shape)

def reference(tokens, segments, routes, norm_one, norm_two, w_query, key_value_weight, w_out_attn, w_router, w_in, w_out, cotangent):
    params = (norm_one.astype(jnp.float32), norm_two.astype(jnp.float32), w_query.astype(jnp.float32), key_value_weight.astype(jnp.float32), w_out_attn.astype(jnp.float32), w_router.astype(jnp.float32), w_in.astype(jnp.float32), w_out.astype(jnp.float32))
    seq_total = MB * TOKENS // TOK_MB
    per_group = math.gcd(seq_total, max(1, 4096 // TOK_MB))
    shape_groups = (seq_total // per_group, per_group, TOK_MB)
    tok_groups = tokens.astype(jnp.float32).reshape(shape_groups + (MODEL_DIMENSION,))
    seg_groups = segments.reshape(shape_groups)
    route_groups = routes.reshape(shape_groups + (TOPK,))

    def whole_layer(inputs_x, weights):
        block_fn = jax.checkpoint(lambda group_items: layer_block(group_items, weights))
        return lax.map(block_fn, (inputs_x, seg_groups, route_groups))
    result, pullback = jax.vjp(whole_layer, tok_groups, params)
    grad_tok, grad_params = pullback(cotangent.astype(jnp.float32).reshape(tok_groups.shape))
    gain_one, gain_two, query_grad, keyval_grad, attn_grad, router_grad, in_grad, out_grad = grad_params
    return (result.reshape(MB, TOKENS, MODEL_DIMENSION).astype(jnp.bfloat16), grad_tok.reshape(MB, TOKENS, MODEL_DIMENSION).astype(jnp.bfloat16), gain_one, gain_two, query_grad, keyval_grad, attn_grad, router_grad, in_grad, out_grad)
```

```python
import math

import jax
import jax.numpy as jnp
from jax import lax
from jax.sharding import PartitionSpec as P

QUERY_HEADS = 12
KEY_VALUE_HEADS = 2
HEAD_SIZE = 128
FF = 768
TOPK = 4


eps_norm = 1e-06
rope_base = 1000000.0
mask_fill = -1e30
highest = lax.Precision.HIGHEST


def rms_scale(tensor):
    return lax.rsqrt(jnp.mean(tensor * tensor, axis=-1, keepdims=True) + eps_norm)


def rope_tables(sequence_length, head_width):
    positions = jnp.arange(sequence_length).astype(jnp.float32)
    frequency = rope_base ** (-(jnp.arange(head_width // 2).astype(jnp.float32) * 2.0) / head_width)
    angles = positions[:, None] * frequency[None, :]
    return (jnp.cos(angles), jnp.sin(angles))


def apply_rotation(tensor, cosine_table, sine_values):
    midway = tensor.shape[-1] // 2
    front_half = tensor[..., :midway]
    back_half = tensor[..., midway:]
    cos_rows = cosine_table[:, None, :]
    sin_rows = sine_values[:, None, :]
    return jnp.concatenate(
        [
            front_half * cos_rows - back_half * sin_rows,
            back_half * cos_rows + front_half * sin_rows,
        ],
        axis=-1,
    )


def inverse_rotation(grad_in, cosine_table, sine_values):
    midway = grad_in.shape[-1] // 2
    front_half = grad_in[..., :midway]
    back_half = grad_in[..., midway:]
    cos_rows = cosine_table[:, None, :]
    sin_rows = sine_values[:, None, :]
    return jnp.concatenate(
        [
            front_half * cos_rows + back_half * sin_rows,
            back_half * cos_rows - front_half * sin_rows,
        ],
        axis=-1,
    )


def gelu_tanh(tensor):
    return jax.nn.gelu(tensor, approximate=True)


def dot32(left, right):
    return jnp.dot(left, right, preferred_element_type=jnp.float32)


def slot_tables(routes_all, gates_all, first_expert, local_experts, capacity):
    sources, _, rows = routes_all.shape
    local = first_expert + jnp.arange(local_experts, dtype=jnp.int32)
    named = routes_all[:, None, :, :] == local[None, :, None, None]
    member = jnp.any(named, axis=2)
    gate_rows = jnp.sum(jnp.where(named, gates_all[:, None, :, :], 0.0), axis=2)
    lower = (jnp.arange(rows)[:, None] < jnp.arange(rows)[None, :]).astype(jnp.bfloat16)
    rank = dot32(member.astype(jnp.bfloat16).reshape(-1, rows), lower).reshape(member.shape)
    slots = jnp.arange(capacity, dtype=jnp.float32)
    hit = member[:, :, None, :] & (rank[:, :, None, :] == slots[None, None, :, None])
    gate_slots = jnp.sum(jnp.where(hit, gate_rows[:, :, None, :], 0.0), axis=-1)
    place = hit.astype(jnp.bfloat16).reshape(sources, local_experts * capacity, rows)
    return place, member, gate_slots


def expert_pass(rows_all, grads_all, place, gate_slots, w_in, w_out):
    sources, rows, width = rows_all.shape
    local_experts = w_in.shape[0]
    capacity = place.shape[1] // local_experts
    shape4 = (sources, local_experts, capacity, width)
    picked = jnp.einsum("skt,std->skd", place, rows_all, preferred_element_type=jnp.float32)
    picked = picked.astype(jnp.bfloat16).reshape(shape4)
    grad_picked = jnp.einsum("skt,std->skd", place, grads_all, preferred_element_type=jnp.float32)
    grad_picked = grad_picked.reshape(shape4)
    gates = gate_slots[..., None]
    grad_result = (gates * grad_picked).astype(jnp.bfloat16)
    pre_act = jnp.einsum("pecd,edf->pecf", picked, w_in, preferred_element_type=jnp.float32)
    gate_part = pre_act[..., :FF]
    up_part = pre_act[..., FF:]
    gelu_val, gelu_pull = jax.vjp(gelu_tanh, gate_part)
    activated = (gelu_val * up_part).astype(jnp.bfloat16)
    result = jnp.einsum("pecf,efd->pecd", activated, w_out, preferred_element_type=jnp.float32)
    grad_gate_slots = jnp.sum(result * grad_picked, axis=-1)
    weighted = (result * gates).astype(jnp.bfloat16).reshape(sources, -1, width)
    back_rows = jnp.einsum("skt,skd->std", place, weighted, preferred_element_type=jnp.float32)
    grad_act = jnp.einsum("pecd,efd->pecf", grad_result, w_out, preferred_element_type=jnp.float32)
    grad_up = grad_act * gelu_val
    grad_gate = gelu_pull(grad_act * up_part)[0]
    grad_pre = jnp.concatenate([grad_gate, grad_up], axis=-1).astype(jnp.bfloat16)
    grad_picked_in = jnp.einsum(
        "pecf,edf->pecd", grad_pre, w_in, preferred_element_type=jnp.float32
    ).astype(jnp.bfloat16)
    back_grads = jnp.einsum(
        "skt,skd->std",
        place,
        grad_picked_in.reshape(sources, -1, width),
        preferred_element_type=jnp.float32,
    )
    kept = (picked, grad_result, activated, grad_pre)
    return (
        back_rows.astype(jnp.bfloat16),
        back_grads.astype(jnp.bfloat16),
        grad_gate_slots,
        kept,
    )


def attention_forward(xn1, segments, proj, cosine_table, sine_values):
    sequence_length = xn1.shape[0]
    heads_per_group = QUERY_HEADS // KEY_VALUE_HEADS
    score_scale = 1.0 / math.sqrt(HEAD_SIZE)
    q_width = QUERY_HEADS * HEAD_SIZE
    k_width = KEY_VALUE_HEADS * HEAD_SIZE
    query_rows = apply_rotation(
        proj[:, :q_width].reshape(sequence_length, QUERY_HEADS, HEAD_SIZE),
        cosine_table,
        sine_values,
    ).astype(jnp.bfloat16)
    query_rows = query_rows.reshape(sequence_length, KEY_VALUE_HEADS, heads_per_group, HEAD_SIZE)
    key_matrix = apply_rotation(
        proj[:, q_width : q_width + k_width].reshape(sequence_length, KEY_VALUE_HEADS, HEAD_SIZE),
        cosine_table,
        sine_values,
    ).astype(jnp.bfloat16)
    value_rows = (
        proj[:, q_width + k_width : q_width + 2 * k_width]
        .reshape(sequence_length, KEY_VALUE_HEADS, HEAD_SIZE)
        .astype(jnp.bfloat16)
    )
    position = jnp.arange(sequence_length)
    allowed = (segments[:, None] == segments[None, :]) & (position[:, None] >= position[None, :])
    scores = (
        jnp.einsum("skgd,tkd->kgst", query_rows, key_matrix, preferred_element_type=jnp.float32)
        * score_scale
    )
    scores = jnp.where(allowed, scores, mask_fill)
    row_max = jnp.max(scores, axis=-1, keepdims=True)
    exp_scores = jnp.exp(scores - row_max)
    row_total = jnp.sum(exp_scores, axis=-1, keepdims=True)
    prob_rows = (exp_scores / row_total).astype(jnp.bfloat16)
    log_total = row_max + jnp.log(row_total)
    mixed_out = jnp.einsum(
        "kgst,tkd->skgd", prob_rows, value_rows, preferred_element_type=jnp.float32
    )
    mixed_out = mixed_out.reshape(sequence_length, q_width).astype(jnp.bfloat16)
    return mixed_out, (query_rows, key_matrix, value_rows, log_total, allowed)


def attention_backward(mixed_gradient, kept, cosine_table, sine_values):
    query_rows, key_matrix, value_rows, log_total, allowed = kept
    sequence_length = mixed_gradient.shape[0]
    heads_per_group = QUERY_HEADS // KEY_VALUE_HEADS
    score_scale = 1.0 / math.sqrt(HEAD_SIZE)
    mixed_gradient = mixed_gradient.reshape(
        sequence_length, KEY_VALUE_HEADS, heads_per_group, HEAD_SIZE
    )
    scores = (
        jnp.einsum("skgd,tkd->kgst", query_rows, key_matrix, preferred_element_type=jnp.float32)
        * score_scale
    )
    prob_rows = jnp.where(allowed, jnp.exp(scores - log_total), 0.0)
    value_gradient = jnp.einsum(
        "kgst,skgd->tkd",
        prob_rows.astype(jnp.bfloat16),
        mixed_gradient,
        preferred_element_type=jnp.float32,
    )
    grad_probs = jnp.einsum(
        "skgd,tkd->kgst", mixed_gradient, value_rows, preferred_element_type=jnp.float32
    )
    grad_scores = prob_rows * (grad_probs - jnp.sum(prob_rows * grad_probs, axis=-1, keepdims=True))
    grad_scores = grad_scores.astype(jnp.bfloat16)
    grad_queries = (
        jnp.einsum("kgst,tkd->skgd", grad_scores, key_matrix, preferred_element_type=jnp.float32)
        * score_scale
    )
    key_gradient = (
        jnp.einsum("kgst,skgd->tkd", grad_scores, query_rows, preferred_element_type=jnp.float32)
        * score_scale
    )
    grad_query_lin = inverse_rotation(
        grad_queries.reshape(sequence_length, QUERY_HEADS, HEAD_SIZE), cosine_table, sine_values
    ).reshape(sequence_length, -1)
    grad_key_linear = inverse_rotation(key_gradient, cosine_table, sine_values).reshape(
        sequence_length, -1
    )
    return jnp.concatenate(
        [grad_query_lin, grad_key_linear, value_gradient.reshape(sequence_length, -1)], axis=-1
    ).astype(jnp.bfloat16)


def per_device(
    tokens,
    segments,
    routes,
    norm_one,
    norm_two,
    w_query,
    key_value_weight,
    w_out_attn,
    w_router,
    w_in,
    w_out,
    cotangent,
):
    micro_count, rows, width = tokens.shape
    peers = lax.axis_size("expert")
    local_experts = w_in.shape[0]
    experts = local_experts * peers
    capacity = rows // 4
    q_width = w_query.shape[1]
    kv_width = key_value_weight.shape[1]
    proj_width = q_width + kv_width
    first_expert = lax.axis_index("expert") * local_experts
    cosine_table, sine_values = rope_tables(rows, HEAD_SIZE)

    def gather_dp(part, axis=0):
        return lax.all_gather(part, "dp", axis=axis, tiled=True)

    def gather_peers(part):
        return lax.all_gather(part, "expert", axis=0, tiled=False)

    router_pad = jnp.zeros((w_router.shape[0], 128 - 2 * experts), jnp.bfloat16)
    first_weight = jnp.concatenate(
        [w_query, key_value_weight, w_router, w_router, router_pad], axis=1
    )
    gains = gather_dp(jnp.stack([norm_one, norm_two]), axis=1).astype(jnp.float32)
    first_weight = gather_dp(first_weight)
    out_weight = gather_dp(w_out_attn)
    gain_one, gain_two = gains[0], gains[1]
    routes_t = jnp.swapaxes(routes, 1, 2)
    routes_all = gather_peers(routes_t)
    grads_all = [gather_peers(cotangent[m]) for m in range(micro_count)]

    tok_float = tokens.astype(jnp.float32)
    scale_one = rms_scale(tok_float)
    xn1 = (tok_float * scale_one * gain_one).astype(jnp.bfloat16)
    proj = dot32(xn1.reshape(-1, width), first_weight).reshape(micro_count, rows, -1)
    logits = proj[..., proj_width : proj_width + experts]
    onehot = (routes[..., None] == jnp.arange(experts, dtype=jnp.int32)).astype(jnp.float32)
    chosen = jnp.sum(onehot * logits[:, :, None, :], axis=-1)
    gate_exp = jnp.exp(chosen - jnp.max(chosen, axis=-1, keepdims=True))
    gate_probs = gate_exp / jnp.sum(gate_exp, axis=-1, keepdims=True)
    gate_dense = jnp.sum(gate_probs[..., None] * onehot, axis=2)
    gates_all = gather_peers(jnp.swapaxes(gate_probs, 1, 2))

    forward = []
    for m in range(micro_count):
        mixed_out, attn_kept = attention_forward(
            xn1[m], segments[m], proj[m], cosine_table, sine_values
        )
        hidden = tok_float[m] + dot32(mixed_out, out_weight)
        scale_two = rms_scale(hidden)
        xn2 = (hidden * scale_two * gain_two).astype(jnp.bfloat16)
        forward.append((mixed_out, attn_kept, hidden, scale_two, gather_peers(xn2)))

    expert_kept = []
    back_rows_list = []
    back_grads_list = []
    grad_gate_list = []
    for m in range(micro_count):
        place, member, gate_slots = slot_tables(
            routes_all[:, m], gates_all[:, m], first_expert, local_experts, capacity
        )
        back_rows, back_grads, grad_gate_slots, kept = expert_pass(
            forward[m][4], grads_all[m], place, gate_slots, w_in, w_out
        )
        grad_gate_rows = jnp.einsum(
            "sect,sec->set",
            place.reshape(peers, local_experts, capacity, rows).astype(jnp.float32),
            grad_gate_slots,
            precision=highest,
        )
        grad_gate_list.append(
            lax.all_to_all(grad_gate_rows, "expert", split_axis=0, concat_axis=0, tiled=True)
        )
        back_grads_list.append(
            lax.psum_scatter(back_grads.reshape(-1, width), "expert", scatter_dimension=0, tiled=True)
        )
        back_rows_list.append(back_rows)
        expert_kept.append(kept)
    back_rows_list = [
        lax.psum_scatter(b.reshape(-1, width), "expert", scatter_dimension=0, tiled=True)
        for b in back_rows_list
    ]

    picked, grad_result, activated, grad_pre = [
        jnp.concatenate(parts, axis=0) for parts in zip(*expert_kept)
    ]
    w_in_sum = jnp.einsum(
        "pecd,pecf->edf", picked, grad_pre, preferred_element_type=jnp.float32
    ).astype(jnp.bfloat16)
    w_out_sum = jnp.einsum(
        "pecf,pecd->efd", activated, grad_result, preferred_element_type=jnp.float32
    ).astype(jnp.bfloat16)
    grad_w_in = lax.psum_scatter(w_in_sum, "dp", scatter_dimension=1, tiled=True)
    grad_w_out = lax.psum_scatter(w_out_sum, "dp", scatter_dimension=1, tiled=True)

    outputs = []
    grad_tokens_list = []
    grad_proj_list = []
    grad_attn_list = []
    gain_sums = []
    for m in range(micro_count):
        mixed_out, attn_kept, hidden, scale_two, _ = forward[m]
        outputs.append((hidden + back_rows_list[m].astype(jnp.float32)).astype(jnp.bfloat16))
        grad_out = cotangent[m].astype(jnp.float32)
        grad_normed_two = back_grads_list[m].astype(jnp.float32)
        unit_two = hidden * scale_two
        grad_unit_two = grad_normed_two * gain_two
        gain_two_sum = jnp.sum(grad_normed_two * unit_two, axis=0)
        grad_hidden = grad_out + scale_two * (
            grad_unit_two - unit_two * jnp.mean(grad_unit_two * unit_two, axis=-1, keepdims=True)
        )
        grad_attn = grad_hidden.astype(jnp.bfloat16)
        mixed_gradient = jnp.einsum(
            "sd,fd->sf", grad_attn, out_weight, preferred_element_type=jnp.float32
        ).astype(jnp.bfloat16)
        grad_qkv = attention_backward(mixed_gradient, attn_kept, cosine_table, sine_values)
        grad_gates = grad_gate_list[m].reshape(experts, rows).T
        gates = gate_dense[m]
        grad_logits = gates * (grad_gates - jnp.sum(gates * grad_gates, axis=-1, keepdims=True))
        high_part = grad_logits.astype(jnp.bfloat16)
        low_part = (grad_logits - high_part.astype(jnp.float32)).astype(jnp.bfloat16)
        grad_proj = jnp.concatenate(
            [
                grad_qkv,
                high_part,
                low_part,
                jnp.zeros((rows, 128 - 2 * experts), jnp.bfloat16),
            ],
            axis=1,
        )
        grad_normed = jnp.einsum(
            "sf,df->sd", grad_proj, first_weight, preferred_element_type=jnp.float32
        )
        unit_one = tok_float[m] * scale_one[m]
        grad_unit_one = grad_normed * gain_one
        gain_one_sum = jnp.sum(grad_normed * unit_one, axis=0)
        grad_tokens = grad_hidden + scale_one[m] * (
            grad_unit_one - unit_one * jnp.mean(grad_unit_one * unit_one, axis=-1, keepdims=True)
        )
        grad_tokens_list.append(grad_tokens.astype(jnp.bfloat16))
        grad_proj_list.append(grad_proj)
        grad_attn_list.append(grad_attn)
        gain_sums.append((gain_one_sum, gain_two_sum))

    grad_first = jnp.einsum(
        "sd,sf->df",
        xn1.reshape(-1, width),
        jnp.concatenate(grad_proj_list, axis=0),
        preferred_element_type=jnp.float32,
    )
    grad_attn_out = jnp.einsum(
        "sf,sd->fd",
        jnp.concatenate([forward[m][0] for m in range(micro_count)], axis=0),
        jnp.concatenate(grad_attn_list, axis=0),
        preferred_element_type=jnp.float32,
    )
    gain_one_sum = sum(pair[0] for pair in gain_sums)
    gain_two_sum = sum(pair[1] for pair in gain_sums)
    router_sum = (
        grad_first[:, proj_width : proj_width + experts]
        + grad_first[:, proj_width + experts : proj_width + 2 * experts]
    )
    small = jnp.concatenate(
        [
            router_sum,
            gain_one_sum[:, None],
            gain_two_sum[:, None],
            jnp.zeros((width, 126 - experts), jnp.float32),
        ],
        axis=1,
    )
    packed = jnp.concatenate(
        [
            grad_first[:, :proj_width].astype(jnp.bfloat16),
            small.astype(jnp.bfloat16),
            grad_attn_out.astype(jnp.bfloat16),
        ],
        axis=1,
    )
    share = lax.psum_scatter(packed, "dp", scatter_dimension=0, tiled=True)
    share = lax.psum(share, "expert").astype(jnp.float32)
    edge = proj_width
    return (
        jnp.stack(outputs),
        jnp.stack(grad_tokens_list),
        share[:, edge + experts],
        share[:, edge + experts + 1],
        share[:, :q_width],
        share[:, q_width:proj_width],
        share[:, edge + 128 :],
        share[:, edge : edge + experts],
        grad_w_in.astype(jnp.float32),
        grad_w_out.astype(jnp.float32),
    )


def solution(mesh):
    return jax.shard_map(
        per_device,
        mesh=mesh,
        in_specs=(
            P(None, ("dp", "expert"), None),
            P(None, ("dp", "expert")),
            P(None, ("dp", "expert"), None),
            P("dp"),
            P("dp"),
            P("dp", None),
            P("dp", None),
            P("dp", None),
            P("dp", None),
            P("expert", None, None),
            P("expert", None, None),
            P(None, ("dp", "expert"), None),
        ),
        out_specs=(
            P(None, ("dp", "expert"), None),
            P(None, ("dp", "expert"), None),
            P("dp"),
            P("dp"),
            P("dp", None),
            P("dp", None),
            P("dp", None),
            P("dp", None),
            P("expert", "dp", None),
            P("expert", "dp", None),
        ),
        check_vma=False,
    )
```

```python
import functools
import math

import jax
import jax.numpy as jnp
from jax import lax
from jax.experimental import pallas as pl
from jax.experimental.pallas import tpu as pltpu
from jax.sharding import PartitionSpec as P

QUERY_HEADS = 12
KEY_VALUE_HEADS = 2
HEAD_SIZE = 128
FF = 768
TOPK = 4


eps_norm = 1e-06
rope_base = 1000000.0
mask_fill = -1e30
highest = lax.Precision.HIGHEST


def rms_scale(tensor):
    return lax.rsqrt(jnp.mean(tensor * tensor, axis=-1, keepdims=True) + eps_norm)


def rope_tables(sequence_length, head_width):
    positions = jnp.arange(sequence_length).astype(jnp.float32)
    frequency = rope_base ** (-(jnp.arange(head_width // 2).astype(jnp.float32) * 2.0) / head_width)
    angles = positions[:, None] * frequency[None, :]
    return (jnp.cos(angles), jnp.sin(angles))


def apply_rotation(tensor, cosine_table, sine_values):
    midway = tensor.shape[-1] // 2
    front_half = tensor[..., :midway]
    back_half = tensor[..., midway:]
    cos_rows = cosine_table[:, None, :]
    sin_rows = sine_values[:, None, :]
    return jnp.concatenate(
        [
            front_half * cos_rows - back_half * sin_rows,
            back_half * cos_rows + front_half * sin_rows,
        ],
        axis=-1,
    )


def inverse_rotation(grad_in, cosine_table, sine_values):
    midway = grad_in.shape[-1] // 2
    front_half = grad_in[..., :midway]
    back_half = grad_in[..., midway:]
    cos_rows = cosine_table[:, None, :]
    sin_rows = sine_values[:, None, :]
    return jnp.concatenate(
        [
            front_half * cos_rows + back_half * sin_rows,
            back_half * cos_rows - front_half * sin_rows,
        ],
        axis=-1,
    )


def dot32(left, right):
    return jnp.dot(left, right, preferred_element_type=jnp.float32)


def slot_tables(routes_all, gates_all, first_expert, local_experts, capacity):
    sources, _, rows = routes_all.shape
    local = first_expert + jnp.arange(local_experts, dtype=jnp.int32)
    named = routes_all[:, None, :, :] == local[None, :, None, None]
    member = jnp.any(named, axis=2)
    gate_rows = jnp.sum(jnp.where(named, gates_all[:, None, :, :], 0.0), axis=2)
    lower = (jnp.arange(rows)[:, None] < jnp.arange(rows)[None, :]).astype(jnp.bfloat16)
    rank = dot32(member.astype(jnp.bfloat16).reshape(-1, rows), lower).reshape(member.shape)
    slots = jnp.arange(capacity, dtype=jnp.float32)
    hit = member[:, :, None, :] & (rank[:, :, None, :] == slots[None, None, :, None])
    gate_slots = jnp.sum(jnp.where(hit, gate_rows[:, :, None, :], 0.0), axis=-1)
    place = hit.astype(jnp.bfloat16).reshape(sources, local_experts * capacity, rows)
    return place, jnp.swapaxes(gate_slots, 0, 1)


def ring_order(peers):
    minor = peers // 4
    walk = []
    for col in range(minor):
        line = range(4) if col % 2 == 0 else range(3, -1, -1)
        walk += [row * minor + col for row in line]
    return walk


def ring_step(part, shift, peers):
    order = ring_order(peers)
    pairs = [(order[i], order[(i + shift) % peers]) for i in range(peers)]
    return lax.ppermute(part, "expert", pairs)


def ring_gather(part, peers):
    half = part.shape[0] // 2
    from_left, from_right = [part], [part]
    for _ in range(1, peers // 2):
        from_left.append(ring_step(from_left[-1], 1, peers))
        from_right.append(ring_step(from_right[-1], -1, peers))
    far = jnp.concatenate(
        [
            ring_step(from_left[-1][:half], 1, peers),
            ring_step(from_right[-1][half:], -1, peers),
        ],
        axis=0,
    )
    return from_left + [far] + from_right[:0:-1]


def ring_scatter(parts, peers):
    middle = peers // 2
    half = parts[0].shape[0] // 2

    def narrow(part):
        return part.astype(jnp.bfloat16)

    left_in = ring_step(narrow(parts[middle][:half]), -1, peers)
    right_in = ring_step(narrow(parts[middle][half:]), 1, peers)
    for k in range(middle - 1, 0, -1):
        left_part, right_part = parts[k], parts[peers - k]
        if k == middle - 1:
            left_sum = jnp.concatenate([left_part[:half] + left_in, left_part[half:]], axis=0)
            right_sum = jnp.concatenate([right_part[:half], right_part[half:] + right_in], axis=0)
        else:
            left_sum = left_part + left_in
            right_sum = right_part + right_in
        left_in = ring_step(narrow(left_sum), -1, peers)
        right_in = ring_step(narrow(right_sum), 1, peers)
    return parts[0] + left_in + right_in


def direct_gather(part, peers):
    return jnp.stack([part] + [ring_step(part, k, peers) for k in range(1, peers)])


GELU_SCALE = math.sqrt(2.0 / math.pi)
GELU_CUBE = 0.044715
GROUP = 8


def expert_kernel(sources, *refs):
    rows_refs = refs[:sources]
    grad_refs = refs[sources : 2 * sources]
    gate_ref, w_in_ref, w_out_ref = refs[2 * sources : 2 * sources + 3]
    (
        back_rows_ref,
        back_grads_ref,
        grad_gate_ref,
        picked_ref,
        grad_result_ref,
        activated_ref,
        grad_pre_ref,
    ) = refs[-7:]
    capacity, width = rows_refs[0].shape
    for k in range(sources):
        picked_ref[pl.ds(k * capacity, capacity), :] = rows_refs[k][...]
    pre_act = dot32(picked_ref[...], w_in_ref[...])
    gate_part = pre_act[:, :FF]
    up_part = pre_act[:, FF:]
    square = gate_part * gate_part
    bend = jnp.tanh(GELU_SCALE * gate_part * (1.0 + GELU_CUBE * square))
    lift = 0.5 * (1.0 + bend)
    gelu_val = gate_part * lift
    slope = lift + 0.5 * gate_part * (1.0 - bend * bend) * (
        GELU_SCALE * (1.0 + 3.0 * GELU_CUBE * square)
    )
    activated_ref[...] = (gelu_val * up_part).astype(jnp.bfloat16)
    result = dot32(activated_ref[...], w_out_ref[...])
    gates = gate_ref[...]
    for k in range(sources):
        span = slice(k * capacity, (k + 1) * capacity)
        grad_rows = grad_refs[k][...].astype(jnp.float32)
        grad_gate_ref[span, :] = jnp.sum(result[span] * grad_rows, axis=-1, keepdims=True)
        back_rows_ref[k] = (result[span] * gates[span]).astype(jnp.bfloat16)
        grad_result_ref[span, :] = (grad_rows * gates[span]).astype(jnp.bfloat16)
    grad_act = lax.dot_general(
        grad_result_ref[...],
        w_out_ref[...],
        (((1,), (1,)), ((), ())),
        preferred_element_type=jnp.float32,
    )
    grad_pre_ref[:, :FF] = (grad_act * up_part * slope).astype(jnp.bfloat16)
    grad_pre_ref[:, FF:] = (grad_act * gelu_val).astype(jnp.bfloat16)
    grad_in = lax.dot_general(
        grad_pre_ref[...],
        w_in_ref[...],
        (((1,), (1,)), ((), ())),
        preferred_element_type=jnp.float32,
    ).astype(jnp.bfloat16)
    for k in range(sources):
        back_grads_ref[k] = grad_in[k * capacity : (k + 1) * capacity]


def expert_pass(rows_list, grads_list, gate_slots, w_in, w_out, kept, group, group_count):
    sources = len(rows_list)
    local_experts, width, _ = w_in.shape
    slots = rows_list[0].shape[0]
    capacity = slots // local_experts
    held = sources * capacity
    block_spec = pl.BlockSpec((capacity, width), lambda e: (e, 0))
    back_spec = pl.BlockSpec((sources, capacity, width), lambda e: (0, e, 0))
    column_spec = pl.BlockSpec((None, held, 1), lambda e: (e, 0, 0))

    def kept_spec(columns):
        return pl.BlockSpec((None, held, columns), lambda e: (e, group, 0))

    def kept_shape(columns):
        return jax.ShapeDtypeStruct((local_experts, group_count * held, columns), jnp.bfloat16)

    kept_widths = (width, width, FF, 2 * FF)
    first_kept = 2 * sources + 3
    kept_args = () if kept is None else tuple(kept)
    flops = 12 * local_experts * held * width * FF * 2
    outs = pl.pallas_call(
        functools.partial(expert_kernel, sources),
        grid=(local_experts,),
        in_specs=[block_spec] * (2 * sources)
        + [
            column_spec,
            pl.BlockSpec((None, width, 2 * FF), lambda e: (e, 0, 0)),
            pl.BlockSpec((None, FF, width), lambda e: (e, 0, 0)),
        ]
        + [pl.BlockSpec(memory_space=pl.ANY)] * len(kept_args),
        out_specs=[back_spec, back_spec, column_spec] + [kept_spec(c) for c in kept_widths],
        out_shape=[
            jax.ShapeDtypeStruct((sources, slots, width), jnp.bfloat16),
            jax.ShapeDtypeStruct((sources, slots, width), jnp.bfloat16),
            jax.ShapeDtypeStruct((local_experts, held, 1), jnp.float32),
        ]
        + [kept_shape(c) for c in kept_widths],
        input_output_aliases={first_kept + i: 3 + i for i in range(len(kept_args))},
        compiler_params=pltpu.CompilerParams(vmem_limit_bytes=60 * 1024 * 1024),
        cost_estimate=pl.CostEstimate(
            flops=flops,
            bytes_accessed=2 * (3 * local_experts * width * FF + 8 * local_experts * held * width),
            transcendentals=local_experts * held * FF,
        ),
        name="expert_pass",
    )(*rows_list, *grads_list, gate_slots, w_in, w_out, *kept_args)
    return outs[0], outs[1], outs[2], outs[3:]


def attention_forward(xn1, segments, proj, cosine_table, sine_values):
    sequence_length = xn1.shape[0]
    heads_per_group = QUERY_HEADS // KEY_VALUE_HEADS
    score_scale = 1.0 / math.sqrt(HEAD_SIZE)
    q_width = QUERY_HEADS * HEAD_SIZE
    k_width = KEY_VALUE_HEADS * HEAD_SIZE
    query_rows = apply_rotation(
        proj[:, :q_width].reshape(sequence_length, QUERY_HEADS, HEAD_SIZE),
        cosine_table,
        sine_values,
    ).astype(jnp.bfloat16)
    query_rows = query_rows.reshape(sequence_length, KEY_VALUE_HEADS, heads_per_group, HEAD_SIZE)
    key_matrix = apply_rotation(
        proj[:, q_width : q_width + k_width].reshape(sequence_length, KEY_VALUE_HEADS, HEAD_SIZE),
        cosine_table,
        sine_values,
    ).astype(jnp.bfloat16)
    value_rows = (
        proj[:, q_width + k_width : q_width + 2 * k_width]
        .reshape(sequence_length, KEY_VALUE_HEADS, HEAD_SIZE)
        .astype(jnp.bfloat16)
    )
    position = jnp.arange(sequence_length)
    allowed = (segments[:, None] == segments[None, :]) & (position[:, None] >= position[None, :])
    scores = (
        jnp.einsum("skgd,tkd->kgst", query_rows, key_matrix, preferred_element_type=jnp.float32)
        * score_scale
    )
    scores = jnp.where(allowed, scores, mask_fill)
    row_max = jnp.max(scores, axis=-1, keepdims=True)
    exp_scores = jnp.exp(scores - row_max)
    row_total = jnp.sum(exp_scores, axis=-1, keepdims=True)
    prob_rows = (exp_scores / row_total).astype(jnp.bfloat16)
    log_total = row_max + jnp.log(row_total)
    mixed_out = jnp.einsum(
        "kgst,tkd->skgd", prob_rows, value_rows, preferred_element_type=jnp.float32
    )
    mixed_out = mixed_out.reshape(sequence_length, q_width).astype(jnp.bfloat16)
    return mixed_out, (query_rows, key_matrix, value_rows, log_total, allowed)


def attention_backward(mixed_gradient, kept, cosine_table, sine_values):
    query_rows, key_matrix, value_rows, log_total, allowed = kept
    sequence_length = mixed_gradient.shape[0]
    heads_per_group = QUERY_HEADS // KEY_VALUE_HEADS
    score_scale = 1.0 / math.sqrt(HEAD_SIZE)
    mixed_gradient = mixed_gradient.reshape(
        sequence_length, KEY_VALUE_HEADS, heads_per_group, HEAD_SIZE
    )
    scores = (
        jnp.einsum("skgd,tkd->kgst", query_rows, key_matrix, preferred_element_type=jnp.float32)
        * score_scale
    )
    prob_rows = jnp.where(allowed, jnp.exp(scores - log_total), 0.0)
    value_gradient = jnp.einsum(
        "kgst,skgd->tkd",
        prob_rows.astype(jnp.bfloat16),
        mixed_gradient,
        preferred_element_type=jnp.float32,
    )
    grad_probs = jnp.einsum(
        "skgd,tkd->kgst", mixed_gradient, value_rows, preferred_element_type=jnp.float32
    )
    grad_scores = prob_rows * (grad_probs - jnp.sum(prob_rows * grad_probs, axis=-1, keepdims=True))
    grad_scores = grad_scores.astype(jnp.bfloat16)
    grad_queries = (
        jnp.einsum("kgst,tkd->skgd", grad_scores, key_matrix, preferred_element_type=jnp.float32)
        * score_scale
    )
    key_gradient = (
        jnp.einsum("kgst,skgd->tkd", grad_scores, query_rows, preferred_element_type=jnp.float32)
        * score_scale
    )
    grad_query_lin = inverse_rotation(
        grad_queries.reshape(sequence_length, QUERY_HEADS, HEAD_SIZE), cosine_table, sine_values
    ).reshape(sequence_length, -1)
    grad_key_linear = inverse_rotation(key_gradient, cosine_table, sine_values).reshape(
        sequence_length, -1
    )
    return jnp.concatenate(
        [grad_query_lin, grad_key_linear, value_gradient.reshape(sequence_length, -1)], axis=-1
    ).astype(jnp.bfloat16)


def per_device(
    tokens,
    segments,
    routes,
    norm_one,
    norm_two,
    w_query,
    key_value_weight,
    w_out_attn,
    w_router,
    w_in,
    w_out,
    cotangent,
):
    micro_count, rows, width = tokens.shape
    peers = lax.axis_size("expert")
    local_experts = w_in.shape[0]
    experts = local_experts * peers
    capacity = rows // 4
    q_width = w_query.shape[1]
    kv_width = key_value_weight.shape[1]
    proj_width = q_width + kv_width
    first_expert = lax.axis_index("expert") * local_experts
    cosine_table, sine_values = rope_tables(rows, HEAD_SIZE)
    order = ring_order(peers)
    spot = [order.index(dev) for dev in range(peers)]
    distances = [[(spot[dev] - spot[me]) % peers for dev in range(peers)] for me in range(peers)]
    right_distance = jnp.array(distances, jnp.int32)[lax.axis_index("expert")]

    def gather_dp(part, axis=0):
        return lax.all_gather(part, "dp", axis=axis, tiled=True)

    router_pad = jnp.zeros((w_router.shape[0], 128 - 2 * experts), jnp.bfloat16)
    first_weight = jnp.concatenate(
        [w_query, key_value_weight, w_router, w_router, router_pad], axis=1
    )
    gains = gather_dp(jnp.stack([norm_one, norm_two]), axis=1).astype(jnp.float32)
    first_weight = gather_dp(first_weight)
    out_weight = gather_dp(w_out_attn)
    gain_one, gain_two = gains[0], gains[1]
    routes_t = jnp.swapaxes(routes, 1, 2)
    grads_all = [ring_gather(cotangent[m], peers) for m in range(micro_count)]

    tok_float = tokens.astype(jnp.float32)
    scale_one = rms_scale(tok_float)
    xn1 = (tok_float * scale_one * gain_one).astype(jnp.bfloat16)
    proj = dot32(xn1.reshape(-1, width), first_weight).reshape(micro_count, rows, -1)
    logits = proj[..., proj_width : proj_width + experts]
    onehot = (routes[..., None] == jnp.arange(experts, dtype=jnp.int32)).astype(jnp.float32)
    chosen = jnp.sum(onehot * logits[:, :, None, :], axis=-1)
    gate_exp = jnp.exp(chosen - jnp.max(chosen, axis=-1, keepdims=True))
    gate_probs = gate_exp / jnp.sum(gate_exp, axis=-1, keepdims=True)
    gate_dense = jnp.sum(gate_probs[..., None] * onehot, axis=2)
    choices = jnp.concatenate(
        [jnp.swapaxes(gate_probs, 1, 2), routes_t.astype(jnp.float32)], axis=1
    )
    choices = direct_gather(choices, peers)
    gates_all = choices[:, :, :TOPK]
    routes_all = choices[:, :, TOPK:].astype(jnp.int32)

    forward = []
    for m in range(micro_count):
        mixed_out, attn_kept = attention_forward(
            xn1[m], segments[m], proj[m], cosine_table, sine_values
        )
        hidden = tok_float[m] + dot32(mixed_out, out_weight)
        scale_two = rms_scale(hidden)
        xn2 = (hidden * scale_two * gain_two).astype(jnp.bfloat16)
        forward.append((mixed_out, attn_kept, hidden, scale_two, ring_gather(xn2, peers)))

    kept = None
    groups = peers // GROUP
    back_rows_list = []
    back_grads_list = []
    grad_gate_list = []
    for m in range(micro_count):
        place, gate_slots = slot_tables(
            routes_all[:, m], gates_all[:, m], first_expert, local_experts, capacity
        )
        rows_list = [
            dot32(place[k], forward[m][4][k]).astype(jnp.bfloat16) for k in range(peers)
        ]
        grads_list = [
            dot32(place[k], grads_all[m][k]).astype(jnp.bfloat16) for k in range(peers)
        ]
        back_rows, back_grads, grad_gate_slots = [], [], []
        for g in range(groups):
            span = slice(g * GROUP, (g + 1) * GROUP)
            rows_out, grads_out, gate_out, kept = expert_pass(
                rows_list[span],
                grads_list[span],
                gate_slots[:, span].reshape(local_experts, -1, 1),
                w_in,
                w_out,
                kept,
                m * groups + g,
                micro_count * groups,
            )
            back_rows += [rows_out[k] for k in range(GROUP)]
            back_grads += [grads_out[k] for k in range(GROUP)]
            grad_gate_slots.append(gate_out.reshape(local_experts, GROUP, capacity, 1))
        grad_gate_slots = jnp.concatenate(grad_gate_slots, axis=1)
        grad_gate_rows = jnp.sum(
            place.reshape(peers, local_experts, capacity, rows).astype(jnp.float32)
            * jnp.swapaxes(grad_gate_slots, 0, 1),
            axis=2,
        )
        returned = [grad_gate_rows[0]] + [
            ring_step(grad_gate_rows[k], -k, peers) for k in range(1, peers)
        ]
        grad_gate_list.append(jnp.take(jnp.stack(returned), right_distance, axis=0))
        back_grads_list.append(
            ring_scatter(
                [dot32(place[k].T, back_grads[k]) for k in range(peers)], peers
            )
        )
        back_rows_list.append((place, back_rows))
    back_rows_list = [
        ring_scatter([dot32(place[k].T, back_rows[k]) for k in range(peers)], peers)
        for place, back_rows in back_rows_list
    ]

    picked, grad_result, activated, grad_pre = kept
    w_in_sum = jnp.einsum(
        "erd,erf->edf", picked, grad_pre, preferred_element_type=jnp.float32
    ).astype(jnp.bfloat16)
    w_out_sum = jnp.einsum(
        "erf,erd->efd", activated, grad_result, preferred_element_type=jnp.float32
    ).astype(jnp.bfloat16)
    grad_w_in = lax.psum_scatter(w_in_sum, "dp", scatter_dimension=1, tiled=True)
    grad_w_out = lax.psum_scatter(w_out_sum, "dp", scatter_dimension=1, tiled=True)

    outputs = []
    grad_tokens_list = []
    grad_proj_list = []
    grad_attn_list = []
    gain_sums = []
    for m in range(micro_count):
        mixed_out, attn_kept, hidden, scale_two, _ = forward[m]
        outputs.append((hidden + back_rows_list[m]).astype(jnp.bfloat16))
        grad_out = cotangent[m].astype(jnp.float32)
        grad_normed_two = back_grads_list[m]
        unit_two = hidden * scale_two
        grad_unit_two = grad_normed_two * gain_two
        gain_two_sum = jnp.sum(grad_normed_two * unit_two, axis=0)
        grad_hidden = grad_out + scale_two * (
            grad_unit_two - unit_two * jnp.mean(grad_unit_two * unit_two, axis=-1, keepdims=True)
        )
        grad_attn = grad_hidden.astype(jnp.bfloat16)
        mixed_gradient = jnp.einsum(
            "sd,fd->sf", grad_attn, out_weight, preferred_element_type=jnp.float32
        ).astype(jnp.bfloat16)
        grad_qkv = attention_backward(mixed_gradient, attn_kept, cosine_table, sine_values)
        grad_gates = grad_gate_list[m].reshape(experts, rows).T
        gates = gate_dense[m]
        grad_logits = gates * (grad_gates - jnp.sum(gates * grad_gates, axis=-1, keepdims=True))
        high_part = grad_logits.astype(jnp.bfloat16)
        low_part = (grad_logits - high_part.astype(jnp.float32)).astype(jnp.bfloat16)
        grad_proj = jnp.concatenate(
            [
                grad_qkv,
                high_part,
                low_part,
                jnp.zeros((rows, 128 - 2 * experts), jnp.bfloat16),
            ],
            axis=1,
        )
        grad_normed = jnp.einsum(
            "sf,df->sd", grad_proj, first_weight, preferred_element_type=jnp.float32
        )
        unit_one = tok_float[m] * scale_one[m]
        grad_unit_one = grad_normed * gain_one
        gain_one_sum = jnp.sum(grad_normed * unit_one, axis=0)
        grad_tokens = grad_hidden + scale_one[m] * (
            grad_unit_one - unit_one * jnp.mean(grad_unit_one * unit_one, axis=-1, keepdims=True)
        )
        grad_tokens_list.append(grad_tokens.astype(jnp.bfloat16))
        grad_proj_list.append(grad_proj)
        grad_attn_list.append(grad_attn)
        gain_sums.append((gain_one_sum, gain_two_sum))

    grad_first = jnp.einsum(
        "sd,sf->df",
        xn1.reshape(-1, width),
        jnp.concatenate(grad_proj_list, axis=0),
        preferred_element_type=jnp.float32,
    )
    grad_attn_out = jnp.einsum(
        "sf,sd->fd",
        jnp.concatenate([forward[m][0] for m in range(micro_count)], axis=0),
        jnp.concatenate(grad_attn_list, axis=0),
        preferred_element_type=jnp.float32,
    )
    gain_one_sum = sum(pair[0] for pair in gain_sums)
    gain_two_sum = sum(pair[1] for pair in gain_sums)
    router_sum = (
        grad_first[:, proj_width : proj_width + experts]
        + grad_first[:, proj_width + experts : proj_width + 2 * experts]
    )
    small = jnp.concatenate(
        [
            router_sum,
            gain_one_sum[:, None],
            gain_two_sum[:, None],
            jnp.zeros((width, 126 - experts), jnp.float32),
        ],
        axis=1,
    )
    packed = jnp.concatenate(
        [
            grad_first[:, :proj_width].astype(jnp.bfloat16),
            small.astype(jnp.bfloat16),
            grad_attn_out.astype(jnp.bfloat16),
        ],
        axis=1,
    )
    share = lax.psum_scatter(packed, "dp", scatter_dimension=0, tiled=True)
    share = lax.psum(share, "expert").astype(jnp.float32)
    edge = proj_width
    return (
        jnp.stack(outputs),
        jnp.stack(grad_tokens_list),
        share[:, edge + experts],
        share[:, edge + experts + 1],
        share[:, :q_width],
        share[:, q_width:proj_width],
        share[:, edge + 128 :],
        share[:, edge : edge + experts],
        grad_w_in.astype(jnp.float32),
        grad_w_out.astype(jnp.float32),
    )


def solution(mesh):
    return jax.shard_map(
        per_device,
        mesh=mesh,
        in_specs=(
            P(None, ("dp", "expert"), None),
            P(None, ("dp", "expert")),
            P(None, ("dp", "expert"), None),
            P("dp"),
            P("dp"),
            P("dp", None),
            P("dp", None),
            P("dp", None),
            P("dp", None),
            P("expert", None, None),
            P("expert", None, None),
            P(None, ("dp", "expert"), None),
        ),
        out_specs=(
            P(None, ("dp", "expert"), None),
            P(None, ("dp", "expert"), None),
            P("dp"),
            P("dp"),
            P("dp", None),
            P("dp", None),
            P("dp", None),
            P("dp", None),
            P("expert", "dp", None),
            P("expert", "dp", None),
        ),
        check_vma=False,
    )
```

```python
import functools
import math

import jax
import jax.numpy as jnp
from jax import lax
from jax.experimental import pallas as pl
from jax.experimental.pallas import tpu as pltpu
from jax.sharding import PartitionSpec as P

QUERY_HEADS = 12
KEY_VALUE_HEADS = 2
HEAD_SIZE = 128
FF = 768
TOPK = 4
EXPERTS = 32
GROUP = 8

eps_norm = 1e-06
rope_base = 1000000.0
mask_fill = -1e30
highest = lax.Precision.HIGHEST


def rms_scale(tensor):
    return lax.rsqrt(jnp.mean(tensor * tensor, axis=-1, keepdims=True) + eps_norm)


def rope_tables(sequence_length, head_width):
    positions = jnp.arange(sequence_length).astype(jnp.float32)
    frequency = rope_base ** (-(jnp.arange(head_width // 2).astype(jnp.float32) * 2.0) / head_width)
    angles = positions[:, None] * frequency[None, :]
    return (jnp.cos(angles), jnp.sin(angles))

SCORE_SCALE = 1.0 / math.sqrt(HEAD_SIZE)
GELU_SCALE = math.sqrt(2.0 / math.pi)
GELU_CUBE = 0.044715


def after(value, *earlier):
    return lax.optimization_barrier((value,) + earlier)[0]


def slot_tables(gates_all, capacity):
    sources, local_experts, rows = gates_all.shape
    member = gates_all >= 0.0
    lower = (jnp.arange(rows)[:, None] < jnp.arange(rows)[None, :]).astype(jnp.bfloat16)
    rank = dot32(member.astype(jnp.bfloat16).reshape(-1, rows), lower).reshape(member.shape)
    slots = jnp.arange(capacity, dtype=jnp.float32)
    hit = member[:, :, None, :] & (rank[:, :, None, :] == slots[None, None, :, None])
    gate_slots = jnp.sum(jnp.where(hit, gates_all[:, :, None, :], 0.0), axis=-1)
    place = hit.astype(jnp.bfloat16).reshape(sources, local_experts * capacity, rows)
    return place, jnp.swapaxes(gate_slots, 0, 1)


def dot32(left, right):
    return jnp.dot(left, right, preferred_element_type=jnp.float32)


def dot_nt(left, right):
    return lax.dot_general(
        left, right, (((1,), (1,)), ((), ())), preferred_element_type=jnp.float32
    )


def dot_tn(left, right):
    return lax.dot_general(
        left, right, (((0,), (0,)), ((), ())), preferred_element_type=jnp.float32
    )


def mask_of(seg_col, seg_row):
    rows = seg_col.shape[0]
    query_at = lax.broadcasted_iota(jnp.int32, (rows, rows), 0)
    key_at = lax.broadcasted_iota(jnp.int32, (rows, rows), 1)
    return (seg_col == seg_row) & (query_at >= key_at)


def softmax_rows(query, key, allowed):
    scores = jnp.where(allowed, dot_nt(query, key) * SCORE_SCALE, mask_fill)
    weight = jnp.exp(scores - jnp.max(scores, axis=-1, keepdims=True))
    return weight / jnp.sum(weight, axis=-1, keepdims=True)


def attention_kernel(
    tok_ref,
    seg_col_ref,
    seg_row_ref,
    routes_ref,
    gains_ref,
    weight_ref,
    cos_ref,
    sin_ref,
    xn1_ref,
    query_ref,
    keyval_ref,
    mixed_ref,
    gates_ref,
):
    tok = tok_ref[...].astype(jnp.float32)
    xn1_ref[...] = (tok * rms_scale(tok) * gains_ref[0:1, :]).astype(jnp.bfloat16)
    proj = dot32(xn1_ref[...], weight_ref[...])
    cos, sin = cos_ref[...], sin_ref[...]

    def rotate(part):
        return (part * cos + pltpu.roll(part, HEAD_SIZE // 2, 1) * sin).astype(jnp.bfloat16)

    q_width = QUERY_HEADS * HEAD_SIZE
    k_width = KEY_VALUE_HEADS * HEAD_SIZE
    for head in range(QUERY_HEADS):
        span = slice(head * HEAD_SIZE, (head + 1) * HEAD_SIZE)
        query_ref[:, span] = rotate(proj[:, span])
    for head in range(KEY_VALUE_HEADS):
        span = slice(head * HEAD_SIZE, (head + 1) * HEAD_SIZE)
        keyval_ref[:, span] = rotate(proj[:, q_width:][:, span])
    keyval_ref[:, k_width:] = proj[:, q_width + k_width : q_width + 2 * k_width].astype(
        jnp.bfloat16
    )
    logits = proj[:, q_width + 2 * k_width :]
    columns = lax.broadcasted_iota(jnp.int32, logits.shape, 1)
    named = [columns == routes_ref[:, j : j + 1] for j in range(TOPK)]
    chosen = [jnp.sum(jnp.where(hit, logits, 0.0), axis=-1, keepdims=True) for hit in named]
    top = functools.reduce(jnp.maximum, chosen)
    weight = [jnp.exp(part - top) for part in chosen]
    total = functools.reduce(jnp.add, weight)
    gates = jnp.full(logits.shape, -1.0, jnp.float32)
    for hit, part in zip(named, weight):
        gates = jnp.where(hit, part / total, gates)
    gates_ref[...] = gates
    allowed = mask_of(seg_col_ref[...], seg_row_ref[...])
    for head in range(QUERY_HEADS):
        span = slice(head * HEAD_SIZE, (head + 1) * HEAD_SIZE)
        group = head // (QUERY_HEADS // KEY_VALUE_HEADS)
        key = keyval_ref[:, group * HEAD_SIZE : (group + 1) * HEAD_SIZE]
        value = keyval_ref[:, k_width + group * HEAD_SIZE : k_width + (group + 1) * HEAD_SIZE]
        probs = softmax_rows(query_ref[:, span], key, allowed)
        mixed_ref[:, span] = dot32(probs.astype(jnp.bfloat16), value).astype(jnp.bfloat16)


def hidden_kernel(mixed_ref, tok_ref, gains_ref, weight_ref, hidden_ref, xn2_ref):
    hidden = tok_ref[...].astype(jnp.float32) + dot32(mixed_ref[...], weight_ref[...])
    hidden_ref[...] = hidden
    xn2_ref[...] = (hidden * rms_scale(hidden) * gains_ref[1:2, :]).astype(jnp.bfloat16)


def backward_kernel(
    own_ref,
    left_ref,
    right_ref,
    cot_ref,
    hidden_ref,
    tok_ref,
    query_ref,
    keyval_ref,
    seg_col_ref,
    seg_row_ref,
    gates_ref,
    grad_gates_ref,
    gains_ref,
    weight_ref,
    out_weight_ref,
    cos_ref,
    sin_ref,
    grad_tok_ref,
    grad_proj_ref,
    grad_attn_ref,
    gain_sum_ref,
    mixed_grad_ref,
):
    width = tok_ref.shape[1]
    q_width = QUERY_HEADS * HEAD_SIZE
    k_width = KEY_VALUE_HEADS * HEAD_SIZE
    proj_width = q_width + 2 * k_width
    grad_xn2 = (
        own_ref[...].astype(jnp.float32)
        + left_ref[...].astype(jnp.float32)
        + right_ref[...].astype(jnp.float32)
    )
    hidden = hidden_ref[...]
    scale = rms_scale(hidden)
    unit = hidden * scale
    gain_sum_ref[...] = jnp.zeros(gain_sum_ref.shape, jnp.float32)
    gain_sum_ref[1:2, :] = jnp.sum(grad_xn2 * unit, axis=0, keepdims=True)
    grad_unit = grad_xn2 * gains_ref[1:2, :]
    grad_hidden = cot_ref[...].astype(jnp.float32) + scale * (
        grad_unit - unit * jnp.mean(grad_unit * unit, axis=-1, keepdims=True)
    )
    grad_attn_ref[...] = grad_hidden.astype(jnp.bfloat16)
    mixed_grad_ref[...] = dot_nt(grad_attn_ref[...], out_weight_ref[...]).astype(jnp.bfloat16)
    cos, sin = cos_ref[...], sin_ref[...]

    def unrotate(part):
        return (part * cos - pltpu.roll(part, HEAD_SIZE // 2, 1) * sin).astype(jnp.bfloat16)

    allowed = mask_of(seg_col_ref[...], seg_row_ref[...])
    per_group = QUERY_HEADS // KEY_VALUE_HEADS
    for group in range(KEY_VALUE_HEADS):
        key_span = slice(group * HEAD_SIZE, (group + 1) * HEAD_SIZE)
        value_span = slice(k_width + group * HEAD_SIZE, k_width + (group + 1) * HEAD_SIZE)
        key, value = keyval_ref[:, key_span], keyval_ref[:, value_span]
        grad_key = jnp.zeros(key.shape, jnp.float32)
        grad_value = jnp.zeros(key.shape, jnp.float32)
        for head in range(group * per_group, (group + 1) * per_group):
            span = slice(head * HEAD_SIZE, (head + 1) * HEAD_SIZE)
            query, grad_mixed = query_ref[:, span], mixed_grad_ref[:, span]
            probs = softmax_rows(query, key, allowed)
            grad_value += dot_tn(probs.astype(jnp.bfloat16), grad_mixed)
            grad_probs = dot_nt(grad_mixed, value)
            mean = jnp.sum(probs * grad_probs, axis=-1, keepdims=True)
            grad_scores = (probs * (grad_probs - mean)).astype(jnp.bfloat16)
            grad_proj_ref[:, span] = unrotate(dot32(grad_scores, key) * SCORE_SCALE)
            grad_key += dot_tn(grad_scores, query)
        grad_proj_ref[:, q_width + group * HEAD_SIZE : q_width + (group + 1) * HEAD_SIZE] = (
            unrotate(grad_key * SCORE_SCALE)
        )
        first = q_width + k_width + group * HEAD_SIZE
        grad_proj_ref[:, first : first + HEAD_SIZE] = grad_value.astype(jnp.bfloat16)
    gates = jnp.maximum(gates_ref[...], 0.0)
    grad_gates = grad_gates_ref[...]
    grad_logits = gates * (grad_gates - jnp.sum(gates * grad_gates, axis=-1, keepdims=True))
    high = grad_logits.astype(jnp.bfloat16).astype(jnp.float32)
    low = pltpu.roll(grad_logits - high, EXPERTS, 1)
    grad_proj_ref[:, proj_width:] = (high + low).astype(jnp.bfloat16)
    grad_xn1 = dot_nt(grad_proj_ref[...], weight_ref[...])
    tok = tok_ref[...].astype(jnp.float32)
    scale = rms_scale(tok)
    unit = tok * scale
    gain_sum_ref[0:1, :] = jnp.sum(grad_xn1 * unit, axis=0, keepdims=True)
    grad_unit = grad_xn1 * gains_ref[0:1, :]
    grad_tok_ref[...] = (
        grad_hidden
        + scale * (grad_unit - unit * jnp.mean(grad_unit * unit, axis=-1, keepdims=True))
    ).astype(jnp.bfloat16)


def ring_order(peers):
    minor = peers // 4
    walk = []
    for col in range(minor):
        line = range(4) if col % 2 == 0 else range(3, -1, -1)
        walk += [row * minor + col for row in line]
    return walk


def ring_step(part, shift, peers):
    order = ring_order(peers)
    pairs = [(order[i], order[(i + shift) % peers]) for i in range(peers)]
    return lax.ppermute(part, "expert", pairs)


class RingGather:
    def __init__(self, part, peers):
        self.peers = peers
        self.half = part.shape[0] // 2
        self.from_left, self.from_right = [part], [part]
        self.far = None

    def step(self, *earlier):
        left, right = self.from_left[-1], self.from_right[-1]
        last = len(self.from_left) == self.peers // 2
        if last:
            left, right = left[: self.half], right[self.half :]
        if earlier:
            left, right = lax.optimization_barrier((left, right) + earlier)[:2]
        left, right = ring_step(left, 1, self.peers), ring_step(right, -1, self.peers)
        if last:
            self.far = jnp.concatenate([left, right], axis=0)
        else:
            self.from_left.append(left)
            self.from_right.append(right)
        return self

    def newest(self):
        return (self.from_left[-1], self.from_right[-1])

    def blocks(self):
        return self.from_left + [self.far] + self.from_right[:0:-1]


class RingScatter:
    def __init__(self, part, peers):
        self.part, self.peers = part, peers
        self.at = peers // 2
        self.sent = None

    def step(self, *earlier):
        peers, k = self.peers, self.at
        if k == peers // 2:
            block = self.part(k)
            self.half = block.shape[0] // 2
            left, right = block[: self.half], block[self.half :]
        else:
            left, right = self.part(k), self.part(peers - k)
            half = self.half
            if k == peers // 2 - 1:
                left = jnp.concatenate([left[:half] + self.left, left[half:]], axis=0)
                right = jnp.concatenate([right[:half], right[half:] + self.right], axis=0)
            else:
                left, right = left + self.left, right + self.right
        left, right = left.astype(jnp.bfloat16), right.astype(jnp.bfloat16)
        if earlier:
            left, right = lax.optimization_barrier((left, right) + earlier)[:2]
        self.sent = (left, right)
        self.left = ring_step(left, -1, peers)
        self.right = ring_step(right, 1, peers)
        self.at = k - 1
        return self

    def pieces(self):
        return self.part(0), self.left, self.right


def expert_kernel(sources, *refs):
    rows_refs = refs[:sources]
    grad_refs = refs[sources : 2 * sources]
    gate_ref, w_in_ref, w_out_ref = refs[2 * sources : 2 * sources + 3]
    (
        back_rows_ref,
        back_grads_ref,
        grad_gate_ref,
        picked_ref,
        grad_result_ref,
        activated_ref,
        grad_pre_ref,
    ) = refs[-7:]
    capacity, width = rows_refs[0].shape
    for k in range(sources):
        picked_ref[pl.ds(k * capacity, capacity), :] = rows_refs[k][...]
    pre_act = dot32(picked_ref[...], w_in_ref[...])
    gate_part = pre_act[:, :FF]
    up_part = pre_act[:, FF:]
    square = gate_part * gate_part
    bend = jnp.tanh(GELU_SCALE * gate_part * (1.0 + GELU_CUBE * square))
    lift = 0.5 * (1.0 + bend)
    gelu_val = gate_part * lift
    slope = lift + 0.5 * gate_part * (1.0 - bend * bend) * (
        GELU_SCALE * (1.0 + 3.0 * GELU_CUBE * square)
    )
    activated_ref[...] = (gelu_val * up_part).astype(jnp.bfloat16)
    result = dot32(activated_ref[...], w_out_ref[...])
    gates = gate_ref[...]
    for k in range(sources):
        span = slice(k * capacity, (k + 1) * capacity)
        grad_rows = grad_refs[k][...].astype(jnp.float32)
        grad_gate_ref[span, :] = jnp.sum(result[span] * grad_rows, axis=-1, keepdims=True)
        back_rows_ref[k] = (result[span] * gates[span]).astype(jnp.bfloat16)
        grad_result_ref[span, :] = (grad_rows * gates[span]).astype(jnp.bfloat16)
    grad_act = lax.dot_general(
        grad_result_ref[...],
        w_out_ref[...],
        (((1,), (1,)), ((), ())),
        preferred_element_type=jnp.float32,
    )
    grad_pre_ref[:, :FF] = (grad_act * up_part * slope).astype(jnp.bfloat16)
    grad_pre_ref[:, FF:] = (grad_act * gelu_val).astype(jnp.bfloat16)
    grad_in = lax.dot_general(
        grad_pre_ref[...],
        w_in_ref[...],
        (((1,), (1,)), ((), ())),
        preferred_element_type=jnp.float32,
    ).astype(jnp.bfloat16)
    for k in range(sources):
        back_grads_ref[k] = grad_in[k * capacity : (k + 1) * capacity]


def expert_pass(rows_list, grads_list, gate_slots, w_in, w_out, held_outs, position, first, count):
    sources = len(rows_list)
    local_experts, width, _ = w_in.shape
    slots = rows_list[0].shape[0]
    capacity = slots // local_experts
    held = sources * capacity
    block_spec = pl.BlockSpec((capacity, width), lambda e: (e + first, 0))
    back_spec = pl.BlockSpec((sources, capacity, width), lambda e: (0, e + first, 0))
    column_spec = pl.BlockSpec((None, held, 1), lambda e: (e + first, 0, 0))

    def kept_spec(columns):
        return pl.BlockSpec((None, held, columns), lambda e: (e + first, position[0], 0))

    def kept_shape(columns):
        return jax.ShapeDtypeStruct((local_experts, position[1] * held, columns), jnp.bfloat16)

    kept_widths = (width, width, FF, 2 * FF)
    first_held = 2 * sources + 3
    given = [(i, part) for i, part in enumerate(held_outs) if part is not None]
    return pl.pallas_call(
        functools.partial(expert_kernel, sources),
        grid=(count,),
        in_specs=[block_spec] * (2 * sources)
        + [
            column_spec,
            pl.BlockSpec((None, width, 2 * FF), lambda e: (e + first, 0, 0)),
            pl.BlockSpec((None, FF, width), lambda e: (e + first, 0, 0)),
        ]
        + [pl.BlockSpec(memory_space=pl.ANY)] * len(given),
        out_specs=[back_spec, back_spec, column_spec] + [kept_spec(c) for c in kept_widths],
        out_shape=[
            jax.ShapeDtypeStruct((sources, slots, width), jnp.bfloat16),
            jax.ShapeDtypeStruct((sources, slots, width), jnp.bfloat16),
            jax.ShapeDtypeStruct((local_experts, held, 1), jnp.float32),
        ]
        + [kept_shape(c) for c in kept_widths],
        input_output_aliases={first_held + at: i for at, (i, _) in enumerate(given)},
        compiler_params=pltpu.CompilerParams(vmem_limit_bytes=60 * 1024 * 1024),
        cost_estimate=pl.CostEstimate(
            flops=12 * count * held * width * FF * 2,
            bytes_accessed=2 * (3 * count * width * FF + 8 * count * held * width),
            transcendentals=count * held * FF,
        ),
        name="expert_pass",
    )(*rows_list, *grads_list, gate_slots, w_in, w_out, *[part for _, part in given])


def whole_call(kernel, out_shape, flops, name, scratch=()):
    return pl.pallas_call(
        kernel,
        out_shape=out_shape,
        scratch_shapes=list(scratch),
        compiler_params=pltpu.CompilerParams(vmem_limit_bytes=60 * 1024 * 1024),
        cost_estimate=pl.CostEstimate(flops=flops, bytes_accessed=20_000_000, transcendentals=0),
        name=name,
    )


def attention_forward(tokens, seg_col, seg_row, routes, gains, weight, cos, sin):
    count, rows, width = tokens.shape

    def by_micro(*shape):
        return pl.BlockSpec((None,) + shape, lambda m: (m,) + (0,) * len(shape))

    def shared(part):
        return pl.BlockSpec(part.shape, lambda m: (0, 0))

    kv_width = 2 * KEY_VALUE_HEADS * HEAD_SIZE
    shapes = [
        ((rows, width), jnp.bfloat16),
        ((rows, QUERY_HEADS * HEAD_SIZE), jnp.bfloat16),
        ((rows, kv_width), jnp.bfloat16),
        ((rows, QUERY_HEADS * HEAD_SIZE), jnp.bfloat16),
        ((rows, 128), jnp.float32),
    ]
    return pl.pallas_call(
        attention_kernel,
        grid=(count,),
        in_specs=[
            by_micro(rows, width),
            by_micro(rows, 1),
            by_micro(1, rows),
            by_micro(rows, TOPK),
            shared(gains),
            shared(weight),
            shared(cos),
            shared(sin),
        ],
        out_specs=[by_micro(*shape) for shape, _ in shapes],
        out_shape=[jax.ShapeDtypeStruct((count,) + shape, kind) for shape, kind in shapes],
        compiler_params=pltpu.CompilerParams(vmem_limit_bytes=60 * 1024 * 1024),
        cost_estimate=pl.CostEstimate(
            flops=2 * count * rows * width * 2600, bytes_accessed=20_000_000, transcendentals=0
        ),
        name="attention_forward",
    )(tokens, seg_col, seg_row, routes, gains, weight, cos, sin)


def attention_grad_kernel(core_ref, *refs):
    count = (len(refs) - 2) // 4
    xn1, proj, mixed, attn = [refs[i * count : (i + 1) * count] for i in range(4)]
    gain_ref, out_ref = refs[-2:]
    split = proj[0].shape[1]
    span = out_ref.shape[1]
    grad = sum(dot_tn(x[...], g[...]) for x, g in zip(xn1, proj))
    router = grad[:, split - 128 :]
    lane = lax.broadcasted_iota(jnp.int32, router.shape, 1)
    router = router + pltpu.roll(router, 128 - EXPERTS, 1)
    router = jnp.where(lane < EXPERTS, router, gain_ref[...])
    grad_out = sum(dot_tn(o[...], a[...]) for o, a in zip(mixed, attn))
    for half in range(2):
        at = lax.rem(half + core_ref[0], 2)
        rows = slice(half * span, (half + 1) * span)
        out_ref[at, :, : split - 128] = grad[rows, : split - 128].astype(jnp.bfloat16)
        out_ref[at, :, split - 128 : split] = router[rows].astype(jnp.bfloat16)
        out_ref[at, :, split:] = grad_out[rows].astype(jnp.bfloat16)


def attention_grads(core, xn1, proj, mixed, attn, gain_columns, parts):
    rows, width = xn1[0].shape
    span = width // parts
    lines = parts // 2
    columns = proj[0].shape[1] + attn[0].shape[1]
    by_line = pl.BlockSpec((rows, 2 * span), lambda i, c: (0, i))

    def shared(part):
        return pl.BlockSpec(part.shape, lambda i, c: (0, 0))

    return pl.pallas_call(
        attention_grad_kernel,
        grid_spec=pltpu.PrefetchScalarGridSpec(
            num_scalar_prefetch=1,
            grid=(lines,),
            in_specs=[by_line for _ in xn1]
            + [shared(p) for p in proj]
            + [by_line for _ in mixed]
            + [shared(p) for p in attn]
            + [pl.BlockSpec((2 * span, 128), lambda i, c: (i, 0))],
            out_specs=pl.BlockSpec((2, None, span, columns), lambda i, c: (0, i, 0, 0)),
        ),
        out_shape=jax.ShapeDtypeStruct((2, lines, span, columns), jnp.bfloat16),
        compiler_params=pltpu.CompilerParams(vmem_limit_bytes=60 * 1024 * 1024),
        cost_estimate=pl.CostEstimate(
            flops=2 * len(xn1) * rows * width * columns, bytes_accessed=20_000_000, transcendentals=0
        ),
        name="attention_grads",
    )(core, *xn1, *proj, *mixed, *attn, gain_columns)


def per_device(
    tokens,
    segments,
    routes,
    norm_one,
    norm_two,
    w_query,
    key_value_weight,
    w_out_attn,
    w_router,
    w_in,
    w_out,
    cotangent,
):
    micro_count, rows, width = tokens.shape
    micros = range(micro_count)
    peers = lax.axis_size("expert")
    dp_count = lax.axis_size("dp")
    local_experts = w_in.shape[0]
    experts = local_experts * peers
    capacity = rows // 4
    q_width = w_query.shape[1]
    kv_width = key_value_weight.shape[1]
    proj_width = q_width + kv_width
    cosine_table, sine_values = rope_tables(rows, HEAD_SIZE)
    cos = jnp.concatenate([cosine_table, cosine_table], axis=1)
    sin = jnp.concatenate([-sine_values, sine_values], axis=1)
    order = ring_order(peers)
    spot = [order.index(dev) for dev in range(peers)]
    left_devices = [[order[(spot[me] - k) % peers] for k in range(peers)] for me in range(peers)]
    left_device = jnp.array(left_devices, jnp.int32)[lax.axis_index("expert")]
    left_distances = [[(spot[me] - spot[dev]) % peers for dev in range(peers)] for me in range(peers)]
    left_distance = jnp.array(left_distances, jnp.int32)[lax.axis_index("expert")]
    my_spot = jnp.array(spot, jnp.int32)[lax.axis_index("expert")]

    def gather_dp(part, axis=0):
        return lax.all_gather(part, "dp", axis=axis, tiled=True)

    router_pad = jnp.zeros((w_router.shape[0], 128 - 2 * experts), jnp.bfloat16)
    first_weight = jnp.concatenate(
        [w_query, key_value_weight, w_router, w_router, router_pad], axis=1
    )
    gains = gather_dp(jnp.stack([norm_one, norm_two]), axis=1).astype(jnp.float32)
    first_weight = gather_dp(first_weight)
    out_weight = gather_dp(w_out_attn)

    cot_rings = [RingGather(cotangent[m], peers) for m in micros]
    for _ in range(peers // 2 - 2):
        for ring in cot_rings:
            ring.step()

    seg_col, seg_row = segments[:, :, None], segments[:, None, :]
    xn1, query, keyval, mixed, gates = attention_forward(
        tokens, seg_col, seg_row, routes, gains, first_weight, cos, sin
    )
    for ring in cot_rings:
        ring.step(gates)
    gates_out = jnp.transpose(
        gates[:, :, :experts].reshape(micro_count, rows, peers, local_experts), (2, 0, 3, 1)
    )
    gates_in = lax.all_to_all(gates_out, "expert", split_axis=0, concat_axis=0, tiled=True)
    gates_in = jnp.take(gates_in, left_device, axis=0)

    hidden, xn2 = [], []
    for m in micros:
        out = whole_call(
            hidden_kernel,
            [
                jax.ShapeDtypeStruct((rows, width), jnp.float32),
                jax.ShapeDtypeStruct((rows, width), jnp.bfloat16),
            ],
            2 * rows * width * width,
            "hidden_rows",
        )(mixed[m], tokens[m], gains, out_weight)
        hidden.append(out[0])
        xn2.append(out[1])
    for ring in cot_rings:
        ring.step(xn2[-1])
    tables = [slot_tables(gates_in[:, m], capacity) for m in micros]

    def pick(place, blocks, k):
        return dot32(place[k], blocks[k]).astype(jnp.bfloat16)

    grads_lists = [
        [pick(tables[m][0], cot_rings[m].blocks(), k) for k in range(peers)] for m in micros
    ]
    row_rings = [RingGather(xn2[m], peers) for m in micros]
    steps = peers // 2
    for at in range(steps + 2):
        for m, ring in enumerate(row_rings):
            if m == 0 and at < steps:
                ring.step()
            if m > 0 and 2 <= at and at - 2 < steps - 2:
                ring.step(*row_rings[0].newest())

    groups = peers // GROUP
    splits = 2
    per_call = local_experts // splits
    kept = [None] * 4
    grad_rings, back_rings, grad_gate_list = [], [], []
    for m in micros:
        place, gate_slots = tables[m]
        blocks = row_rings[m].blocks()
        rows_list = [pick(place, blocks, k) for k in range(peers)]
        grads_list = grads_lists[m]
        outs = [[None] * 3 for _ in range(groups)]
        for call in range(splits):
            for g in range(groups):
                span = slice(g * GROUP, (g + 1) * GROUP)
                wait_for = []
                if m == 0:
                    for ring in row_rings[1:]:
                        wait_for += ring.newest()
                else:
                    wait_for += grad_rings[0].sent + back_rings[0].sent
                here = rows_list[span]
                here[0] = after(here[0], *wait_for)
                done = expert_pass(
                    here,
                    grads_list[span],
                    gate_slots[:, span].reshape(local_experts, -1, 1),
                    w_in,
                    w_out,
                    outs[g] + kept,
                    (m * groups + g, micro_count * groups),
                    call * per_call,
                    per_call,
                )
                outs[g], kept = list(done[:3]), list(done[3:])
            if m == 0:
                for ring in row_rings[1:]:
                    ring.step(kept[3])
            elif call < splits - 1:
                grad_rings[0].step(kept[3])
                back_rings[0].step(kept[3])
        rows_back = [outs[k // GROUP][0][k % GROUP] for k in range(peers)]
        grads_back = [outs[k // GROUP][1][k % GROUP] for k in range(peers)]
        grad_gate_slots = jnp.concatenate(
            [out[2].reshape(local_experts, GROUP, capacity, 1) for out in outs], axis=1
        )
        grad_rings.append(
            RingScatter(lambda k, p=place, b=grads_back: dot_tn(p[k], b[k]), peers).step()
        )
        back_rings.append(RingScatter(lambda k, p=place, b=rows_back: dot_tn(p[k], b[k]), peers))
        if m == 0:
            back_rings[0].step()
        grad_gate_rows = jnp.sum(
            place.reshape(peers, local_experts, capacity, rows).astype(jnp.float32)
            * jnp.swapaxes(grad_gate_slots, 0, 1),
            axis=2,
        )
        grad_gate_list.append(grad_gate_rows)

    picked, grad_result, activated, grad_pre = kept
    for ring in grad_rings[:-1]:
        ring.step(kept[3])
    activated = after(activated, *grad_rings[-1].sent, *grad_rings[0].sent)
    w_out_sum = jnp.einsum(
        "erf,erd->efd", activated, grad_result, preferred_element_type=jnp.float32
    ).astype(jnp.bfloat16)
    grad_w_out = lax.psum_scatter(w_out_sum, "dp", scatter_dimension=1, tiled=True)
    for ring in grad_rings:
        ring.step(w_out_sum)
    picked = after(picked, *grad_rings[-1].sent)
    w_in_sum = jnp.einsum(
        "erd,erf->edf", picked, grad_pre, preferred_element_type=jnp.float32
    ).astype(jnp.bfloat16)
    grad_w_in = lax.psum_scatter(w_in_sum, "dp", scatter_dimension=1, tiled=True)
    for ring in grad_rings:
        while ring.at > 0:
            ring.step(w_in_sum)

    grad_gates_out = jnp.take(jnp.stack(grad_gate_list, axis=1), left_distance, axis=0)
    grad_gates = lax.all_to_all(
        grad_gates_out, "expert", split_axis=0, concat_axis=0, tiled=True
    )
    grad_gates = jnp.transpose(grad_gates, (1, 3, 0, 2)).reshape(micro_count, rows, experts)
    grad_gates = jnp.pad(grad_gates, ((0, 0), (0, 0), (0, 128 - experts)))

    grad_tokens, grad_proj, grad_attn, gain_sums = [], [], [], []
    for m in micros:
        out = whole_call(
            backward_kernel,
            [
                jax.ShapeDtypeStruct((rows, width), jnp.bfloat16),
                jax.ShapeDtypeStruct((rows, proj_width + 128), jnp.bfloat16),
                jax.ShapeDtypeStruct((rows, width), jnp.bfloat16),
                jax.ShapeDtypeStruct((8, width), jnp.float32),
            ],
            2 * rows * width * 6000,
            "attention_backward",
            [pltpu.VMEM((rows, q_width), jnp.bfloat16)],
        )(
            *grad_rings[m].pieces(),
            cotangent[m],
            hidden[m],
            tokens[m],
            query[m],
            keyval[m],
            seg_col[m],
            seg_row[m],
            gates[m],
            grad_gates[m],
            gains,
            first_weight,
            out_weight,
            cos,
            sin,
        )
        grad_tokens.append(out[0])
        grad_proj.append(out[1])
        grad_attn.append(out[2])
        gain_sums.append(out[3])
    gain_columns = jnp.pad(sum(gain_sums)[:2].T, ((0, 0), (experts, 126 - experts)))
    core = lax.rem(lax.axis_index("dp"), 2).astype(jnp.int32).reshape(1)
    packed = attention_grads(
        core,
        [xn1[m] for m in micros],
        grad_proj,
        [mixed[m] for m in micros],
        grad_attn,
        gain_columns,
        dp_count,
    )
    share = reduce_packed(packed, my_spot, peers, dp_count)

    outputs = []
    for m in micros:
        while back_rings[m].at > 0:
            back_rings[m].step()
        own, left, right = back_rings[m].pieces()
        outputs.append((hidden[m] + own + left + right).astype(jnp.bfloat16))
    edge = proj_width
    return (
        jnp.stack(outputs),
        jnp.stack(grad_tokens),
        share[:, edge + experts],
        share[:, edge + experts + 1],
        share[:, :q_width],
        share[:, q_width:proj_width],
        share[:, edge + 128 :],
        share[:, edge : edge + experts],
        grad_w_in.astype(jnp.float32),
        grad_w_out.astype(jnp.float32),
    )


def reduce_packed(packed, my_spot, peers, dp_count):
    _, lines, span, columns = packed.shape
    swap = [(d, d ^ 1) for d in range(dp_count)]
    total = packed[0] + lax.ppermute(packed[1], "dp", swap)
    piece = span // peers
    total = total.reshape(lines, peers, piece, columns)

    def part(k):
        at = lax.rem(my_spot - k + peers, peers)
        chunk = lax.dynamic_slice_in_dim(total, at, 1, axis=1)
        return chunk.astype(jnp.float32).reshape(lines * piece, columns)

    ring = RingScatter(part, peers)
    while ring.at > 0:
        ring.step()
    own, left, right = ring.pieces()
    mine = (own + left + right).astype(jnp.bfloat16).reshape(lines, piece, columns)
    line = lax.axis_index("dp") // 2

    def for_line(at):
        return lax.dynamic_index_in_dim(mine, lax.rem(at, lines), 0, keepdims=False)

    share = for_line(line).astype(jnp.float32)
    for k in range(1, lines):
        pairs = [(d, (d + 2 * k) % dp_count) for d in range(dp_count)]
        share = share + lax.ppermute(for_line(line + k), "dp", pairs)
    gather = RingGather(share.astype(jnp.bfloat16), peers)
    for _ in range(peers // 2):
        gather.step()
    by_distance = jnp.stack(gather.blocks())
    distance = lax.rem(my_spot - jnp.arange(peers, dtype=jnp.int32) + peers, peers)
    by_spot = jnp.take(by_distance, distance, axis=0)
    return by_spot.reshape(span, columns).astype(jnp.float32)


def solution(mesh):
    return jax.shard_map(
        per_device,
        mesh=mesh,
        in_specs=(
            P(None, ("dp", "expert"), None),
            P(None, ("dp", "expert")),
            P(None, ("dp", "expert"), None),
            P("dp"),
            P("dp"),
            P("dp", None),
            P("dp", None),
            P("dp", None),
            P("dp", None),
            P("expert", None, None),
            P("expert", None, None),
            P(None, ("dp", "expert"), None),
        ),
        out_specs=(
            P(None, ("dp", "expert"), None),
            P(None, ("dp", "expert"), None),
            P("dp"),
            P("dp"),
            P("dp", None),
            P("dp", None),
            P("dp", None),
            P("dp", None),
            P("expert", "dp", None),
            P("expert", "dp", None),
        ),
        check_vma=False,
    )
```

```python
import functools
import math

import jax
import jax.numpy as jnp
from jax import lax
from jax.experimental import pallas as pl
from jax.experimental.pallas import tpu as pltpu
from jax.sharding import PartitionSpec as P

QUERY_HEADS = 12
KEY_VALUE_HEADS = 2
HEAD_SIZE = 128
FF = 768
TOPK = 4
EXPERTS = 32
GROUP = 8

eps_norm = 1e-06
rope_base = 1000000.0
mask_fill = -1e30
highest = lax.Precision.HIGHEST


def rms_scale(tensor):
    return lax.rsqrt(jnp.mean(tensor * tensor, axis=-1, keepdims=True) + eps_norm)


def rope_tables(sequence_length, head_width):
    positions = jnp.arange(sequence_length).astype(jnp.float32)
    frequency = rope_base ** (-(jnp.arange(head_width // 2).astype(jnp.float32) * 2.0) / head_width)
    angles = positions[:, None] * frequency[None, :]
    return (jnp.cos(angles), jnp.sin(angles))

SCORE_SCALE = 1.0 / math.sqrt(HEAD_SIZE)
GELU_SCALE = math.sqrt(2.0 / math.pi)
GELU_CUBE = 0.044715


def after(value, *earlier):
    return lax.optimization_barrier((value,) + earlier)[0]


def slot_tables(gates_all, capacity):
    sources, local_experts, rows = gates_all.shape
    member = gates_all >= 0.0
    lower = (jnp.arange(rows)[:, None] < jnp.arange(rows)[None, :]).astype(jnp.bfloat16)
    rank = dot32(member.astype(jnp.bfloat16).reshape(-1, rows), lower).reshape(member.shape)
    slots = jnp.arange(capacity, dtype=jnp.float32)
    hit = member[:, :, None, :] & (rank[:, :, None, :] == slots[None, None, :, None])
    gate_slots = jnp.sum(jnp.where(hit, gates_all[:, :, None, :], 0.0), axis=-1)
    place = hit.astype(jnp.bfloat16).reshape(sources, local_experts * capacity, rows)
    return place, jnp.swapaxes(gate_slots, 0, 1)


def dot32(left, right):
    return jnp.dot(left, right, preferred_element_type=jnp.float32)


def dot_nt(left, right):
    return lax.dot_general(
        left, right, (((1,), (1,)), ((), ())), preferred_element_type=jnp.float32
    )


def dot_tn(left, right):
    return lax.dot_general(
        left, right, (((0,), (0,)), ((), ())), preferred_element_type=jnp.float32
    )


def mask_of(seg_col, seg_row):
    rows = seg_col.shape[0]
    query_at = lax.broadcasted_iota(jnp.int32, (rows, rows), 0)
    key_at = lax.broadcasted_iota(jnp.int32, (rows, rows), 1)
    return (seg_col == seg_row) & (query_at >= key_at)


def softmax_rows(query, key, allowed):
    scores = jnp.where(allowed, dot_nt(query, key) * SCORE_SCALE, mask_fill)
    weight = jnp.exp(scores - jnp.max(scores, axis=-1, keepdims=True))
    return weight / jnp.sum(weight, axis=-1, keepdims=True)


def attention_kernel(
    tok_ref,
    seg_col_ref,
    seg_row_ref,
    routes_ref,
    gains_ref,
    weight_ref,
    cos_ref,
    sin_ref,
    xn1_ref,
    query_ref,
    keyval_ref,
    mixed_ref,
    gates_ref,
):
    tok = tok_ref[...].astype(jnp.float32)
    xn1_ref[...] = (tok * rms_scale(tok) * gains_ref[0:1, :]).astype(jnp.bfloat16)
    proj = dot32(xn1_ref[...], weight_ref[...])
    cos, sin = cos_ref[...], sin_ref[...]

    def rotate(part):
        return (part * cos + pltpu.roll(part, HEAD_SIZE // 2, 1) * sin).astype(jnp.bfloat16)

    q_width = QUERY_HEADS * HEAD_SIZE
    k_width = KEY_VALUE_HEADS * HEAD_SIZE
    for head in range(QUERY_HEADS):
        span = slice(head * HEAD_SIZE, (head + 1) * HEAD_SIZE)
        query_ref[:, span] = rotate(proj[:, span])
    for head in range(KEY_VALUE_HEADS):
        span = slice(head * HEAD_SIZE, (head + 1) * HEAD_SIZE)
        keyval_ref[:, span] = rotate(proj[:, q_width:][:, span])
    keyval_ref[:, k_width:] = proj[:, q_width + k_width : q_width + 2 * k_width].astype(
        jnp.bfloat16
    )
    logits = proj[:, q_width + 2 * k_width :]
    columns = lax.broadcasted_iota(jnp.int32, logits.shape, 1)
    named = [columns == routes_ref[:, j : j + 1] for j in range(TOPK)]
    chosen = [jnp.sum(jnp.where(hit, logits, 0.0), axis=-1, keepdims=True) for hit in named]
    top = functools.reduce(jnp.maximum, chosen)
    weight = [jnp.exp(part - top) for part in chosen]
    total = functools.reduce(jnp.add, weight)
    gates = jnp.full(logits.shape, -1.0, jnp.float32)
    for hit, part in zip(named, weight):
        gates = jnp.where(hit, part / total, gates)
    gates_ref[...] = gates
    allowed = mask_of(seg_col_ref[...], seg_row_ref[...])
    for head in range(QUERY_HEADS):
        span = slice(head * HEAD_SIZE, (head + 1) * HEAD_SIZE)
        group = head // (QUERY_HEADS // KEY_VALUE_HEADS)
        key = keyval_ref[:, group * HEAD_SIZE : (group + 1) * HEAD_SIZE]
        value = keyval_ref[:, k_width + group * HEAD_SIZE : k_width + (group + 1) * HEAD_SIZE]
        probs = softmax_rows(query_ref[:, span], key, allowed)
        mixed_ref[:, span] = dot32(probs.astype(jnp.bfloat16), value).astype(jnp.bfloat16)


def hidden_kernel(mixed_ref, tok_ref, gains_ref, weight_ref, hidden_ref, xn2_ref):
    hidden = tok_ref[...].astype(jnp.float32) + dot32(mixed_ref[...], weight_ref[...])
    hidden_ref[...] = hidden
    xn2_ref[...] = (hidden * rms_scale(hidden) * gains_ref[1:2, :]).astype(jnp.bfloat16)


def backward_kernel(
    own_ref,
    left_ref,
    right_ref,
    cot_ref,
    hidden_ref,
    tok_ref,
    query_ref,
    keyval_ref,
    seg_col_ref,
    seg_row_ref,
    gates_ref,
    grad_gates_ref,
    gains_ref,
    weight_ref,
    out_weight_ref,
    cos_ref,
    sin_ref,
    grad_tok_ref,
    grad_proj_ref,
    grad_attn_ref,
    gain_sum_ref,
    mixed_grad_ref,
):
    width = tok_ref.shape[1]
    q_width = QUERY_HEADS * HEAD_SIZE
    k_width = KEY_VALUE_HEADS * HEAD_SIZE
    proj_width = q_width + 2 * k_width
    grad_xn2 = (
        own_ref[...].astype(jnp.float32)
        + left_ref[...].astype(jnp.float32)
        + right_ref[...].astype(jnp.float32)
    )
    hidden = hidden_ref[...]
    scale = rms_scale(hidden)
    unit = hidden * scale
    gain_sum_ref[...] = jnp.zeros(gain_sum_ref.shape, jnp.float32)
    gain_sum_ref[1:2, :] = jnp.sum(grad_xn2 * unit, axis=0, keepdims=True)
    grad_unit = grad_xn2 * gains_ref[1:2, :]
    grad_hidden = cot_ref[...].astype(jnp.float32) + scale * (
        grad_unit - unit * jnp.mean(grad_unit * unit, axis=-1, keepdims=True)
    )
    grad_attn_ref[...] = grad_hidden.astype(jnp.bfloat16)
    mixed_grad_ref[...] = dot_nt(grad_attn_ref[...], out_weight_ref[...]).astype(jnp.bfloat16)
    cos, sin = cos_ref[...], sin_ref[...]

    def unrotate(part):
        return (part * cos - pltpu.roll(part, HEAD_SIZE // 2, 1) * sin).astype(jnp.bfloat16)

    allowed = mask_of(seg_col_ref[...], seg_row_ref[...])
    per_group = QUERY_HEADS // KEY_VALUE_HEADS
    for group in range(KEY_VALUE_HEADS):
        key_span = slice(group * HEAD_SIZE, (group + 1) * HEAD_SIZE)
        value_span = slice(k_width + group * HEAD_SIZE, k_width + (group + 1) * HEAD_SIZE)
        key, value = keyval_ref[:, key_span], keyval_ref[:, value_span]
        grad_key = jnp.zeros(key.shape, jnp.float32)
        grad_value = jnp.zeros(key.shape, jnp.float32)
        for head in range(group * per_group, (group + 1) * per_group):
            span = slice(head * HEAD_SIZE, (head + 1) * HEAD_SIZE)
            query, grad_mixed = query_ref[:, span], mixed_grad_ref[:, span]
            probs = softmax_rows(query, key, allowed)
            grad_value += dot_tn(probs.astype(jnp.bfloat16), grad_mixed)
            grad_probs = dot_nt(grad_mixed, value)
            mean = jnp.sum(probs * grad_probs, axis=-1, keepdims=True)
            grad_scores = (probs * (grad_probs - mean)).astype(jnp.bfloat16)
            grad_proj_ref[:, span] = unrotate(dot32(grad_scores, key) * SCORE_SCALE)
            grad_key += dot_tn(grad_scores, query)
        grad_proj_ref[:, q_width + group * HEAD_SIZE : q_width + (group + 1) * HEAD_SIZE] = (
            unrotate(grad_key * SCORE_SCALE)
        )
        first = q_width + k_width + group * HEAD_SIZE
        grad_proj_ref[:, first : first + HEAD_SIZE] = grad_value.astype(jnp.bfloat16)
    gates = jnp.maximum(gates_ref[...], 0.0)
    grad_gates = grad_gates_ref[...]
    grad_logits = gates * (grad_gates - jnp.sum(gates * grad_gates, axis=-1, keepdims=True))
    high = grad_logits.astype(jnp.bfloat16).astype(jnp.float32)
    low = pltpu.roll(grad_logits - high, EXPERTS, 1)
    grad_proj_ref[:, proj_width:] = (high + low).astype(jnp.bfloat16)
    grad_xn1 = dot_nt(grad_proj_ref[...], weight_ref[...])
    tok = tok_ref[...].astype(jnp.float32)
    scale = rms_scale(tok)
    unit = tok * scale
    gain_sum_ref[0:1, :] = jnp.sum(grad_xn1 * unit, axis=0, keepdims=True)
    grad_unit = grad_xn1 * gains_ref[0:1, :]
    grad_tok_ref[...] = (
        grad_hidden
        + scale * (grad_unit - unit * jnp.mean(grad_unit * unit, axis=-1, keepdims=True))
    ).astype(jnp.bfloat16)


def ring_order(peers):
    minor = peers // 4
    walk = []
    for col in range(minor):
        line = range(4) if col % 2 == 0 else range(3, -1, -1)
        walk += [row * minor + col for row in line]
    return walk


def ring_step(part, shift, peers):
    order = ring_order(peers)
    pairs = [(order[i], order[(i + shift) % peers]) for i in range(peers)]
    return lax.ppermute(part, "expert", pairs)


class RingGather:
    def __init__(self, part, peers):
        self.peers = peers
        self.half = part.shape[0] // 2
        self.from_left, self.from_right = [part], [part]
        self.far = None
        self.sent = None

    def step(self, *earlier):
        left, right = self.from_left[-1], self.from_right[-1]
        last = len(self.from_left) == self.peers // 2
        if last:
            left, right = left[: self.half], right[self.half :]
        if earlier:
            left, right = lax.optimization_barrier((left, right) + earlier)[:2]
        self.sent = (left, right)
        left, right = ring_step(left, 1, self.peers), ring_step(right, -1, self.peers)
        if last:
            self.far = jnp.concatenate([left, right], axis=0)
        else:
            self.from_left.append(left)
            self.from_right.append(right)
        return self

    def blocks(self):
        return self.from_left + [self.far] + self.from_right[:0:-1]

    def block(self, k):
        if k < len(self.from_left):
            return self.from_left[k]
        return self.far if k == self.peers // 2 else self.from_right[self.peers - k]


class RingScatter:
    def __init__(self, part, peers):
        self.part, self.peers = part, peers
        self.at = peers // 2
        self.sent = None

    def step(self, *earlier):
        peers, k = self.peers, self.at
        if k == peers // 2:
            block = self.part(k)
            self.half = block.shape[0] // 2
            left, right = block[: self.half], block[self.half :]
        else:
            left, right = self.part(k), self.part(peers - k)
            half = self.half
            if k == peers // 2 - 1:
                left = jnp.concatenate([add_rows(left[:half], self.left), left[half:]], axis=0)
                right = jnp.concatenate([right[:half], add_rows(right[half:], self.right)], axis=0)
            else:
                left, right = add_rows(left, self.left), add_rows(right, self.right)
        if earlier:
            left, right = lax.optimization_barrier((left, right) + earlier)[:2]
        self.sent = (left, right)
        self.left = ring_step(left, -1, peers)
        self.right = ring_step(right, 1, peers)
        self.at = k - 1
        return self

    def pieces(self):
        return self.part(0), self.left, self.right


def add_rows(left, right):
    return (left.astype(jnp.float32) + right.astype(jnp.float32)).astype(jnp.bfloat16)


def expert_kernel(sources, *refs):
    rows_refs = refs[:sources]
    grad_refs = refs[sources : 2 * sources]
    gate_ref, w_in_ref, w_out_ref = refs[2 * sources : 2 * sources + 3]
    (
        back_rows_ref,
        back_grads_ref,
        grad_gate_ref,
        picked_ref,
        grad_result_ref,
        activated_ref,
        grad_pre_ref,
    ) = refs[-7:]
    capacity, width = rows_refs[0].shape
    for k in range(sources):
        picked_ref[pl.ds(k * capacity, capacity), :] = rows_refs[k][...]
    pre_act = dot32(picked_ref[...], w_in_ref[...])
    gate_part = pre_act[:, :FF]
    up_part = pre_act[:, FF:]
    square = gate_part * gate_part
    bend = jnp.tanh(GELU_SCALE * gate_part * (1.0 + GELU_CUBE * square))
    lift = 0.5 * (1.0 + bend)
    gelu_val = gate_part * lift
    slope = lift + 0.5 * gate_part * (1.0 - bend * bend) * (
        GELU_SCALE * (1.0 + 3.0 * GELU_CUBE * square)
    )
    activated_ref[...] = (gelu_val * up_part).astype(jnp.bfloat16)
    result = dot32(activated_ref[...], w_out_ref[...])
    gates = gate_ref[...]
    for k in range(sources):
        span = slice(k * capacity, (k + 1) * capacity)
        grad_rows = grad_refs[k][...].astype(jnp.float32)
        grad_gate_ref[span, :] = jnp.sum(result[span] * grad_rows, axis=-1, keepdims=True)
        back_rows_ref[k] = (result[span] * gates[span]).astype(jnp.bfloat16)
        grad_result_ref[span, :] = (grad_rows * gates[span]).astype(jnp.bfloat16)
    grad_act = lax.dot_general(
        grad_result_ref[...],
        w_out_ref[...],
        (((1,), (1,)), ((), ())),
        preferred_element_type=jnp.float32,
    )
    grad_pre_ref[:, :FF] = (grad_act * up_part * slope).astype(jnp.bfloat16)
    grad_pre_ref[:, FF:] = (grad_act * gelu_val).astype(jnp.bfloat16)
    grad_in = lax.dot_general(
        grad_pre_ref[...],
        w_in_ref[...],
        (((1,), (1,)), ((), ())),
        preferred_element_type=jnp.float32,
    ).astype(jnp.bfloat16)
    for k in range(sources):
        back_grads_ref[k] = grad_in[k * capacity : (k + 1) * capacity]


def expert_pass(rows_list, grads_list, gate_slots, w_in, w_out, held_outs, position, first, count):
    sources = len(rows_list)
    local_experts, width, _ = w_in.shape
    slots = rows_list[0].shape[0]
    capacity = slots // local_experts
    held = sources * capacity
    block_spec = pl.BlockSpec((capacity, width), lambda e: (e + first, 0))
    back_spec = pl.BlockSpec((sources, capacity, width), lambda e: (0, e + first, 0))
    column_spec = pl.BlockSpec((None, held, 1), lambda e: (e + first, 0, 0))

    def kept_spec(columns):
        return pl.BlockSpec((None, held, columns), lambda e: (e + first, position[0], 0))

    def kept_shape(columns):
        return jax.ShapeDtypeStruct((local_experts, position[1] * held, columns), jnp.bfloat16)

    kept_widths = (width, width, FF, 2 * FF)
    first_held = 2 * sources + 3
    given = [(i, part) for i, part in enumerate(held_outs) if part is not None]
    return pl.pallas_call(
        functools.partial(expert_kernel, sources),
        grid=(count,),
        in_specs=[block_spec] * (2 * sources)
        + [
            column_spec,
            pl.BlockSpec((None, width, 2 * FF), lambda e: (e + first, 0, 0)),
            pl.BlockSpec((None, FF, width), lambda e: (e + first, 0, 0)),
        ]
        + [pl.BlockSpec(memory_space=pl.ANY)] * len(given),
        out_specs=[back_spec, back_spec, column_spec] + [kept_spec(c) for c in kept_widths],
        out_shape=[
            jax.ShapeDtypeStruct((sources, slots, width), jnp.bfloat16),
            jax.ShapeDtypeStruct((sources, slots, width), jnp.bfloat16),
            jax.ShapeDtypeStruct((local_experts, held, 1), jnp.float32),
        ]
        + [kept_shape(c) for c in kept_widths],
        input_output_aliases={first_held + at: i for at, (i, _) in enumerate(given)},
        compiler_params=pltpu.CompilerParams(vmem_limit_bytes=60 * 1024 * 1024),
        cost_estimate=pl.CostEstimate(
            flops=12 * count * held * width * FF * 2,
            bytes_accessed=2 * (3 * count * width * FF + 8 * count * held * width),
            transcendentals=count * held * FF,
        ),
        name="expert_pass",
    )(*rows_list, *grads_list, gate_slots, w_in, w_out, *[part for _, part in given])


def pick_kernel(distances, micro_idx, *refs):
    count = len(distances)
    place_ref = refs[0]
    for at, k in enumerate(distances):
        block_ref = refs[1 + at]
        block = block_ref[...] if micro_idx is None else block_ref[micro_idx]
        refs[1 + count + at][...] = dot32(place_ref[k], block).astype(jnp.bfloat16)


def pick_rows(place, blocks, distances, micro_idx=None):
    _, slots, rows = place.shape
    width = blocks[0].shape[-1]
    block_spec = pl.BlockSpec(blocks[0].shape, lambda: (0,) * blocks[0].ndim)
    return pl.pallas_call(
        functools.partial(pick_kernel, distances, micro_idx),
        out_shape=[jax.ShapeDtypeStruct((slots, width), jnp.bfloat16) for _ in distances],
        in_specs=[pl.BlockSpec(place.shape, lambda: (0, 0, 0))] + [block_spec for _ in distances],
        out_specs=[pl.BlockSpec((slots, width), lambda: (0, 0)) for _ in distances],
        compiler_params=pltpu.CompilerParams(vmem_limit_bytes=60 * 1024 * 1024),
        cost_estimate=pl.CostEstimate(
            flops=2 * len(distances) * slots * rows * width,
            bytes_accessed=4 * len(distances) * slots * width,
            transcendentals=0,
        ),
        name="pick_rows",
    )(place, *blocks)


def spread_kernel(place_ref, rows_ref, grads_ref, rows_out_ref, grads_out_ref):
    place = place_ref[...]
    rows_out_ref[...] = dot_tn(place, rows_ref[...]).astype(jnp.bfloat16)
    grads_out_ref[...] = dot_tn(place, grads_ref[...]).astype(jnp.bfloat16)


def spread_rows(place, rows_back, grads_back):
    sources, slots, rows = place.shape
    width = rows_back.shape[-1]
    by_source = pl.BlockSpec((None, slots, width), lambda k: (k, 0, 0))
    out_spec = pl.BlockSpec((None, rows, width), lambda k: (k, 0, 0))
    out_shape = jax.ShapeDtypeStruct((sources, rows, width), jnp.bfloat16)
    return pl.pallas_call(
        spread_kernel,
        grid=(sources,),
        in_specs=[pl.BlockSpec((None, slots, rows), lambda k: (k, 0, 0)), by_source, by_source],
        out_specs=[out_spec, out_spec],
        out_shape=[out_shape, out_shape],
        compiler_params=pltpu.CompilerParams(vmem_limit_bytes=60 * 1024 * 1024),
        cost_estimate=pl.CostEstimate(
            flops=4 * sources * slots * rows * width,
            bytes_accessed=8 * sources * slots * width,
            transcendentals=0,
        ),
        name="spread_rows",
    )(place, rows_back, grads_back)


def whole_call(kernel, out_shape, flops, name, scratch=()):
    return pl.pallas_call(
        kernel,
        out_shape=out_shape,
        scratch_shapes=list(scratch),
        compiler_params=pltpu.CompilerParams(vmem_limit_bytes=60 * 1024 * 1024),
        cost_estimate=pl.CostEstimate(flops=flops, bytes_accessed=20_000_000, transcendentals=0),
        name=name,
    )


def attention_forward(tokens, seg_col, seg_row, routes, gains, weight, cos, sin):
    count, rows, width = tokens.shape

    def by_micro(*shape):
        return pl.BlockSpec((None,) + shape, lambda m: (m,) + (0,) * len(shape))

    def shared(part):
        return pl.BlockSpec(part.shape, lambda m: (0, 0))

    kv_width = 2 * KEY_VALUE_HEADS * HEAD_SIZE
    shapes = [
        ((rows, width), jnp.bfloat16),
        ((rows, QUERY_HEADS * HEAD_SIZE), jnp.bfloat16),
        ((rows, kv_width), jnp.bfloat16),
        ((rows, QUERY_HEADS * HEAD_SIZE), jnp.bfloat16),
        ((rows, 128), jnp.float32),
    ]
    return pl.pallas_call(
        attention_kernel,
        grid=(count,),
        in_specs=[
            by_micro(rows, width),
            by_micro(rows, 1),
            by_micro(1, rows),
            by_micro(rows, TOPK),
            shared(gains),
            shared(weight),
            shared(cos),
            shared(sin),
        ],
        out_specs=[by_micro(*shape) for shape, _ in shapes],
        out_shape=[jax.ShapeDtypeStruct((count,) + shape, kind) for shape, kind in shapes],
        compiler_params=pltpu.CompilerParams(vmem_limit_bytes=60 * 1024 * 1024),
        cost_estimate=pl.CostEstimate(
            flops=2 * count * rows * width * 2600, bytes_accessed=20_000_000, transcendentals=0
        ),
        name="attention_forward",
    )(tokens, seg_col, seg_row, routes, gains, weight, cos, sin)


def attention_grad_kernel(core_ref, *refs):
    count = (len(refs) - 2) // 4
    xn1, proj, mixed, attn = [refs[i * count : (i + 1) * count] for i in range(4)]
    gain_ref, out_ref = refs[-2:]
    split = proj[0].shape[1]
    span = out_ref.shape[1]
    grad = sum(dot_tn(x[...], g[...]) for x, g in zip(xn1, proj))
    router = grad[:, split - 128 :]
    lane = lax.broadcasted_iota(jnp.int32, router.shape, 1)
    router = router + pltpu.roll(router, 128 - EXPERTS, 1)
    router = jnp.where(lane < EXPERTS, router, gain_ref[...])
    grad_out = sum(dot_tn(o[...], a[...]) for o, a in zip(mixed, attn))
    for half in range(2):
        at = lax.rem(half + core_ref[0], 2)
        rows = slice(half * span, (half + 1) * span)
        out_ref[at, :, : split - 128] = grad[rows, : split - 128].astype(jnp.bfloat16)
        out_ref[at, :, split - 128 : split] = router[rows].astype(jnp.bfloat16)
        out_ref[at, :, split:] = grad_out[rows].astype(jnp.bfloat16)


def attention_grads(core, xn1, proj, mixed, attn, gain_columns, parts):
    rows, width = xn1[0].shape
    span = width // parts
    lines = parts // 2
    columns = proj[0].shape[1] + attn[0].shape[1]
    by_line = pl.BlockSpec((rows, 2 * span), lambda i, c: (0, i))

    def shared(part):
        return pl.BlockSpec(part.shape, lambda i, c: (0, 0))

    return pl.pallas_call(
        attention_grad_kernel,
        grid_spec=pltpu.PrefetchScalarGridSpec(
            num_scalar_prefetch=1,
            grid=(lines,),
            in_specs=[by_line for _ in xn1]
            + [shared(p) for p in proj]
            + [by_line for _ in mixed]
            + [shared(p) for p in attn]
            + [pl.BlockSpec((2 * span, 128), lambda i, c: (i, 0))],
            out_specs=pl.BlockSpec((2, None, span, columns), lambda i, c: (0, i, 0, 0)),
        ),
        out_shape=jax.ShapeDtypeStruct((2, lines, span, columns), jnp.bfloat16),
        compiler_params=pltpu.CompilerParams(vmem_limit_bytes=60 * 1024 * 1024),
        cost_estimate=pl.CostEstimate(
            flops=2 * len(xn1) * rows * width * columns, bytes_accessed=20_000_000, transcendentals=0
        ),
        name="attention_grads",
    )(core, *xn1, *proj, *mixed, *attn, gain_columns)


def per_device(
    tokens,
    segments,
    routes,
    norm_one,
    norm_two,
    w_query,
    key_value_weight,
    w_out_attn,
    w_router,
    w_in,
    w_out,
    cotangent,
):
    micro_count, rows, width = tokens.shape
    micros = range(micro_count)
    peers = lax.axis_size("expert")
    dp_count = lax.axis_size("dp")
    local_experts = w_in.shape[0]
    experts = local_experts * peers
    capacity = rows // 4
    q_width = w_query.shape[1]
    kv_width = key_value_weight.shape[1]
    proj_width = q_width + kv_width
    cosine_table, sine_values = rope_tables(rows, HEAD_SIZE)
    cos = jnp.concatenate([cosine_table, cosine_table], axis=1)
    sin = jnp.concatenate([-sine_values, sine_values], axis=1)
    order = ring_order(peers)
    spot = [order.index(dev) for dev in range(peers)]
    left_devices = [[order[(spot[me] - k) % peers] for k in range(peers)] for me in range(peers)]
    left_device = jnp.array(left_devices, jnp.int32)[lax.axis_index("expert")]
    left_distances = [[(spot[me] - spot[dev]) % peers for dev in range(peers)] for me in range(peers)]
    left_distance = jnp.array(left_distances, jnp.int32)[lax.axis_index("expert")]
    my_spot = jnp.array(spot, jnp.int32)[lax.axis_index("expert")]

    def gather_dp(part, axis=0):
        return lax.all_gather(part, "dp", axis=axis, tiled=True)

    router_pad = jnp.zeros((w_router.shape[0], 128 - 2 * experts), jnp.bfloat16)
    first_weight = jnp.concatenate(
        [w_query, key_value_weight, w_router, w_router, router_pad], axis=1
    )
    gains = gather_dp(jnp.stack([norm_one, norm_two]), axis=1).astype(jnp.float32)
    first_weight = gather_dp(first_weight)
    out_weight = gather_dp(w_out_attn)

    cot_ring = RingGather(cotangent, peers)
    steps = peers // 2
    for _ in range(steps - 2):
        cot_ring.step()

    seg_col, seg_row = segments[:, :, None], segments[:, None, :]
    xn1, query, keyval, mixed, gates = attention_forward(
        tokens, seg_col, seg_row, routes, gains, first_weight, cos, sin
    )
    cot_ring.step(gates)
    mixed = after(mixed, *cot_ring.sent)
    gates_out = jnp.transpose(
        gates[:, :, :experts].reshape(micro_count, rows, peers, local_experts), (2, 0, 3, 1)
    )
    gates_in = lax.all_to_all(gates_out, "expert", split_axis=0, concat_axis=0, tiled=True)
    gates_in = jnp.take(gates_in, left_device, axis=0)

    hidden, xn2 = [], []
    for m in micros:
        out = whole_call(
            hidden_kernel,
            [
                jax.ShapeDtypeStruct((rows, width), jnp.float32),
                jax.ShapeDtypeStruct((rows, width), jnp.bfloat16),
            ],
            2 * rows * width * width,
            "hidden_rows",
        )(mixed[m], tokens[m], gains, out_weight)
        hidden.append(out[0])
        xn2.append(out[1])
    cot_ring.step()
    tables = [slot_tables(gates_in[:, m], capacity) for m in micros]
    every = list(range(peers))
    late = [steps - 1, steps, steps + 1]
    early = [k for k in every if k not in late]
    row_rings = [RingGather(xn2[m], peers) for m in micros]
    for at in range(steps):
        row_rings[0].step()
        if 2 <= at:
            row_rings[1].step(*row_rings[0].sent)
    groups = peers // GROUP
    splits = 2
    per_call = local_experts // splits

    def picked_rows(m):
        place, ring = tables[m][0], row_rings[m]
        rows_of = dict(zip(early, pick_rows(place, [ring.block(k) for k in early], early)))
        rows_of.update(zip(late, pick_rows(place, [ring.block(k) for k in late], late)))
        return [rows_of[k] for k in every]

    class Experts:
        kept = [None] * 4

        def __init__(self, m):
            place, gate_slots = tables[m]
            self.m = m
            self.gate_slots = gate_slots
            self.rows = None
            self.grads = pick_rows(place, cot_ring.blocks(), every, m)
            self.outs = [[None] * 3 for _ in range(groups)]

        def call(self, number, *earlier):
            for g in range(groups):
                span = slice(g * GROUP, (g + 1) * GROUP)
                here = self.rows[span]
                here[0] = after(here[0], *earlier)
                done = expert_pass(
                    here,
                    self.grads[span],
                    self.gate_slots[:, span].reshape(local_experts, -1, 1),
                    w_in,
                    w_out,
                    self.outs[g] + Experts.kept,
                    (self.m * groups + g, micro_count * groups),
                    number * per_call,
                    per_call,
                )
                self.outs[g], Experts.kept = list(done[:3]), list(done[3:])
            return done[2]

        def finish(self, *earlier):
            place = tables[self.m][0]
            place = after(place, *earlier) if earlier else place
            spread = [
                spread_rows(place[g * GROUP : (g + 1) * GROUP], self.outs[g][0], self.outs[g][1])
                for g in range(groups)
            ]
            out_ring, grad_ring = [
                RingScatter(lambda k, w=w: spread[k // GROUP][w][k % GROUP], peers)
                for w in range(2)
            ]
            slots = jnp.concatenate(
                [out[2].reshape(local_experts, GROUP, capacity, 1) for out in self.outs], axis=1
            )
            gate_rows = jnp.sum(
                place.reshape(peers, local_experts, capacity, rows).astype(jnp.float32)
                * jnp.swapaxes(slots, 0, 1),
                axis=2,
            )
            return out_ring, grad_ring, gate_rows

    first, second = Experts(0), Experts(1)
    first.rows = picked_rows(0)
    row_rings[1].step()
    token = first.call(0, *row_rings[1].sent)
    row_rings[1].step(token)
    token = first.call(1, *row_rings[1].sent)
    out_first, grad_first, gates_first = first.finish()
    grad_first.step()
    out_first.step()
    second.rows = picked_rows(1)
    token = second.call(0, *grad_first.sent, *out_first.sent)
    grad_first.step(token)
    out_first.step(token)
    token = second.call(1, *grad_first.sent, *out_first.sent)
    grad_first.step(token)
    out_first.step(token)
    out_second, grad_second, gates_second = second.finish(*grad_first.sent, *out_first.sent)
    picked, grad_result, activated, grad_pre = Experts.kept
    grad_second.step()
    grad_first.step(*grad_second.sent)
    picked = after(picked, *grad_second.sent, *grad_first.sent)
    w_in_sum = jnp.einsum(
        "erd,erf->edf", picked, grad_pre, preferred_element_type=jnp.float32
    ).astype(jnp.bfloat16)
    grad_w_in = lax.psum_scatter(w_in_sum, "dp", scatter_dimension=1, tiled=True)
    grad_second.step(w_in_sum)
    while out_first.at > 0:
        out_first.step(w_in_sum)
    activated = after(activated, *grad_second.sent, *out_first.sent)
    w_out_sum = jnp.einsum(
        "erf,erd->efd", activated, grad_result, preferred_element_type=jnp.float32
    ).astype(jnp.bfloat16)
    grad_w_out = lax.psum_scatter(w_out_sum, "dp", scatter_dimension=1, tiled=True)
    while grad_first.at > 0:
        grad_first.step(w_out_sum)
    grad_second.step(w_out_sum)

    grad_gates_out = jnp.take(jnp.stack([gates_first, gates_second], axis=1), left_distance, axis=0)
    grad_gates = lax.all_to_all(
        grad_gates_out, "expert", split_axis=0, concat_axis=0, tiled=True
    )
    grad_gates = jnp.transpose(grad_gates, (1, 3, 0, 2)).reshape(micro_count, rows, experts)
    grad_gates = jnp.pad(grad_gates, ((0, 0), (0, 0), (0, 128 - experts)))

    def backward(m, ring, *earlier):
        own, left, right = ring.pieces()
        return whole_call(
            backward_kernel,
            [
                jax.ShapeDtypeStruct((rows, width), jnp.bfloat16),
                jax.ShapeDtypeStruct((rows, proj_width + 128), jnp.bfloat16),
                jax.ShapeDtypeStruct((rows, width), jnp.bfloat16),
                jax.ShapeDtypeStruct((8, width), jnp.float32),
            ],
            2 * rows * width * 6000,
            "attention_backward",
            [pltpu.VMEM((rows, q_width), jnp.bfloat16)],
        )(
            after(own, *earlier),
            left,
            right,
            cotangent[m],
            hidden[m],
            tokens[m],
            query[m],
            keyval[m],
            seg_col[m],
            seg_row[m],
            gates[m],
            grad_gates[m],
            gains,
            first_weight,
            out_weight,
            cos,
            sin,
        )

    back_first = backward(0, grad_first, *grad_second.sent)
    while grad_second.at > 0:
        grad_second.step(back_first[3])
    out_second.step(grad_second.left, grad_second.right)
    back_second = backward(1, grad_second, *out_second.sent)
    out_second.step(back_second[3])
    grad_tokens, grad_proj, grad_attn, gain_sums = zip(back_first, back_second)
    gain_columns = jnp.pad(sum(gain_sums)[:2].T, ((0, 0), (experts, 126 - experts)))
    core = lax.rem(lax.axis_index("dp"), 2).astype(jnp.int32).reshape(1)
    packed = attention_grads(
        core,
        [after(xn1[0], *out_second.sent)] + [xn1[m] for m in micros[1:]],
        grad_proj,
        [mixed[m] for m in micros],
        grad_attn,
        gain_columns,
        dp_count,
    )
    out_second.step(packed)
    share, grad_w_in, grad_w_out = reduce_packed(
        packed, my_spot, peers, dp_count, out_second, (grad_w_in, grad_w_out)
    )

    outputs = []
    for m, ring in enumerate((out_first, out_second)):
        own, left, right = [part.astype(jnp.float32) for part in ring.pieces()]
        outputs.append((hidden[m] + own + left + right).astype(jnp.bfloat16))
    edge = proj_width
    return (
        jnp.stack(outputs),
        jnp.stack(grad_tokens),
        share[:, edge + experts],
        share[:, edge + experts + 1],
        share[:, :q_width],
        share[:, q_width:proj_width],
        share[:, edge + 128 :],
        share[:, edge : edge + experts],
        grad_w_in,
        grad_w_out,
    )


def reduce_packed(packed, my_spot, peers, dp_count, out_ring, expert_grads):
    _, lines, span, columns = packed.shape
    swap = [(d, d ^ 1) for d in range(dp_count)]
    total = packed[0] + lax.ppermute(packed[1], "dp", swap)
    piece = span // peers
    while out_ring.at > 0:
        out_ring.step(total)
    total = total.reshape(lines, peers, piece, columns)

    def part(k):
        at = lax.rem(my_spot - k + peers, peers)
        return lax.dynamic_slice_in_dim(total, at, 1, axis=1).reshape(lines * piece, columns)

    ring = RingScatter(part, peers)
    while ring.at > 0:
        ring.step()
    own, left, right = [part.astype(jnp.float32) for part in ring.pieces()]
    mine = (own + left + right).astype(jnp.bfloat16).reshape(lines, piece, columns)
    line = lax.axis_index("dp") // 2

    def for_line(at):
        return lax.dynamic_index_in_dim(mine, lax.rem(at, lines), 0, keepdims=False)

    share = for_line(line).astype(jnp.float32)
    for k in range(1, lines):
        pairs = [(d, (d + 2 * k) % dp_count) for d in range(dp_count)]
        share = share + lax.ppermute(for_line(line + k), "dp", pairs)
    gather = RingGather(share.astype(jnp.bfloat16), peers)
    gather.step()
    expert_grads = [part.astype(jnp.float32) for part in expert_grads]
    gather.step(*expert_grads)
    while gather.far is None:
        gather.step()
    by_distance = jnp.stack(gather.blocks())
    distance = lax.rem(my_spot - jnp.arange(peers, dtype=jnp.int32) + peers, peers)
    by_spot = jnp.take(by_distance, distance, axis=0)
    return by_spot.reshape(span, columns).astype(jnp.float32), *expert_grads


def solution(mesh):
    return jax.shard_map(
        per_device,
        mesh=mesh,
        in_specs=(
            P(None, ("dp", "expert"), None),
            P(None, ("dp", "expert")),
            P(None, ("dp", "expert"), None),
            P("dp"),
            P("dp"),
            P("dp", None),
            P("dp", None),
            P("dp", None),
            P("dp", None),
            P("expert", None, None),
            P("expert", None, None),
            P(None, ("dp", "expert"), None),
        ),
        out_specs=(
            P(None, ("dp", "expert"), None),
            P(None, ("dp", "expert"), None),
            P("dp"),
            P("dp"),
            P("dp", None),
            P("dp", None),
            P("dp", None),
            P("dp", None),
            P("expert", "dp", None),
            P("expert", "dp", None),
        ),
        check_vma=False,
    )
```

```python
import functools
import math

import jax
import jax.numpy as jnp
from jax import lax
from jax.experimental import pallas as pl
from jax.experimental.pallas import tpu as pltpu
from jax.sharding import PartitionSpec as P

QUERY_HEADS = 12
KEY_VALUE_HEADS = 2
HEAD_SIZE = 128
FF = 768
TOPK = 4
EXPERTS = 32
GROUP = 8

eps_norm = 1e-06
rope_base = 1000000.0
mask_fill = -1e30
highest = lax.Precision.HIGHEST


def rms_scale(tensor):
    return lax.rsqrt(jnp.mean(tensor * tensor, axis=-1, keepdims=True) + eps_norm)


def rope_tables(sequence_length, head_width):
    positions = jnp.arange(sequence_length).astype(jnp.float32)
    frequency = rope_base ** (-(jnp.arange(head_width // 2).astype(jnp.float32) * 2.0) / head_width)
    angles = positions[:, None] * frequency[None, :]
    return (jnp.cos(angles), jnp.sin(angles))

SCORE_SCALE = 1.0 / math.sqrt(HEAD_SIZE)
GELU_SCALE = math.sqrt(2.0 / math.pi)
GELU_CUBE = 0.044715
SMALL_COST = pl.CostEstimate(flops=1_000_000, bytes_accessed=1_000_000, transcendentals=0)


def after(value, *earlier):
    return lax.optimization_barrier((value,) + earlier)[0]


def slot_codes(routes, experts):
    rows = routes.shape[1]
    names = jnp.arange(experts, dtype=jnp.int32)[None, None, :, None]
    member = jnp.any(jnp.swapaxes(routes, 1, 2)[:, :, None, :] == names, axis=1)
    lower = (jnp.arange(rows)[:, None] < jnp.arange(rows)[None, :]).astype(jnp.bfloat16)
    rank = dot32(member.astype(jnp.bfloat16).reshape(-1, rows), lower).reshape(member.shape)
    return jnp.where(member, rank, -1.0).astype(jnp.bfloat16)


def slot_hits(codes, capacity):
    slots = jnp.arange(capacity, dtype=jnp.float32).astype(jnp.bfloat16)
    return codes[:, :, None, :] == slots[None, None, :, None]


def dot32(left, right):
    return jnp.dot(left, right, preferred_element_type=jnp.float32)


def dot_nt(left, right):
    return lax.dot_general(
        left, right, (((1,), (1,)), ((), ())), preferred_element_type=jnp.float32
    )


def dot_tn(left, right):
    return lax.dot_general(
        left, right, (((0,), (0,)), ((), ())), preferred_element_type=jnp.float32
    )


def mask_of(seg_col, seg_row):
    rows = seg_col.shape[0]
    query_at = lax.broadcasted_iota(jnp.int32, (rows, rows), 0)
    key_at = lax.broadcasted_iota(jnp.int32, (rows, rows), 1)
    return (seg_col == seg_row) & (query_at >= key_at)


def softmax_rows(query, key, allowed):
    scores = jnp.where(allowed, dot_nt(query, key) * SCORE_SCALE, mask_fill)
    weight = jnp.exp(scores - jnp.max(scores, axis=-1, keepdims=True))
    return weight / jnp.sum(weight, axis=-1, keepdims=True)


def attention_kernel(
    tok_ref,
    seg_col_ref,
    seg_row_ref,
    routes_ref,
    gains_ref,
    weight_ref,
    cos_ref,
    sin_ref,
    xn1_ref,
    query_ref,
    keyval_ref,
    mixed_ref,
    gates_ref,
):
    tok = tok_ref[...].astype(jnp.float32)
    xn1_ref[...] = (tok * rms_scale(tok) * gains_ref[0:1, :]).astype(jnp.bfloat16)
    proj = dot32(xn1_ref[...], weight_ref[...])
    cos, sin = cos_ref[...], sin_ref[...]

    def rotate(part):
        return (part * cos + pltpu.roll(part, HEAD_SIZE // 2, 1) * sin).astype(jnp.bfloat16)

    q_width = QUERY_HEADS * HEAD_SIZE
    k_width = KEY_VALUE_HEADS * HEAD_SIZE
    for head in range(QUERY_HEADS):
        span = slice(head * HEAD_SIZE, (head + 1) * HEAD_SIZE)
        query_ref[:, span] = rotate(proj[:, span])
    for head in range(KEY_VALUE_HEADS):
        span = slice(head * HEAD_SIZE, (head + 1) * HEAD_SIZE)
        keyval_ref[:, span] = rotate(proj[:, q_width:][:, span])
    keyval_ref[:, k_width:] = proj[:, q_width + k_width : q_width + 2 * k_width].astype(
        jnp.bfloat16
    )
    logits = proj[:, q_width + 2 * k_width :]
    columns = lax.broadcasted_iota(jnp.int32, logits.shape, 1)
    named = [columns == routes_ref[:, j : j + 1] for j in range(TOPK)]
    chosen = [jnp.sum(jnp.where(hit, logits, 0.0), axis=-1, keepdims=True) for hit in named]
    top = functools.reduce(jnp.maximum, chosen)
    weight = [jnp.exp(part - top) for part in chosen]
    total = functools.reduce(jnp.add, weight)
    gates = jnp.full(logits.shape, -1.0, jnp.float32)
    for hit, part in zip(named, weight):
        gates = jnp.where(hit, part / total, gates)
    gates_ref[...] = gates
    allowed = mask_of(seg_col_ref[...], seg_row_ref[...])
    for head in range(QUERY_HEADS):
        span = slice(head * HEAD_SIZE, (head + 1) * HEAD_SIZE)
        group = head // (QUERY_HEADS // KEY_VALUE_HEADS)
        key = keyval_ref[:, group * HEAD_SIZE : (group + 1) * HEAD_SIZE]
        value = keyval_ref[:, k_width + group * HEAD_SIZE : k_width + (group + 1) * HEAD_SIZE]
        probs = softmax_rows(query_ref[:, span], key, allowed)
        mixed_ref[:, span] = dot32(probs.astype(jnp.bfloat16), value).astype(jnp.bfloat16)


def hidden_kernel(mixed_ref, tok_ref, gains_ref, weight_ref, hidden_ref, xn2_ref):
    hidden = tok_ref[...].astype(jnp.float32) + dot32(mixed_ref[...], weight_ref[...])
    hidden_ref[...] = hidden
    xn2_ref[...] = (hidden * rms_scale(hidden) * gains_ref[1:2, :]).astype(jnp.bfloat16)


def backward_kernel(
    own_ref,
    left_ref,
    right_ref,
    cot_ref,
    hidden_ref,
    tok_ref,
    query_ref,
    keyval_ref,
    seg_col_ref,
    seg_row_ref,
    gates_ref,
    grad_gates_ref,
    gains_ref,
    weight_ref,
    out_weight_ref,
    cos_ref,
    sin_ref,
    grad_tok_ref,
    grad_proj_ref,
    grad_attn_ref,
    gain_sum_ref,
    mixed_grad_ref,
):
    width = tok_ref.shape[1]
    q_width = QUERY_HEADS * HEAD_SIZE
    k_width = KEY_VALUE_HEADS * HEAD_SIZE
    proj_width = q_width + 2 * k_width
    grad_xn2 = (
        own_ref[...].astype(jnp.float32)
        + left_ref[...].astype(jnp.float32)
        + right_ref[...].astype(jnp.float32)
    )
    hidden = hidden_ref[...]
    scale = rms_scale(hidden)
    unit = hidden * scale
    gain_sum_ref[...] = jnp.zeros(gain_sum_ref.shape, jnp.float32)
    gain_sum_ref[1:2, :] = jnp.sum(grad_xn2 * unit, axis=0, keepdims=True)
    grad_unit = grad_xn2 * gains_ref[1:2, :]
    grad_hidden = cot_ref[...].astype(jnp.float32) + scale * (
        grad_unit - unit * jnp.mean(grad_unit * unit, axis=-1, keepdims=True)
    )
    grad_attn_ref[...] = grad_hidden.astype(jnp.bfloat16)
    mixed_grad_ref[...] = dot_nt(grad_attn_ref[...], out_weight_ref[...]).astype(jnp.bfloat16)
    cos, sin = cos_ref[...], sin_ref[...]

    def unrotate(part):
        return (part * cos - pltpu.roll(part, HEAD_SIZE // 2, 1) * sin).astype(jnp.bfloat16)

    allowed = mask_of(seg_col_ref[...], seg_row_ref[...])
    per_group = QUERY_HEADS // KEY_VALUE_HEADS
    for group in range(KEY_VALUE_HEADS):
        key_span = slice(group * HEAD_SIZE, (group + 1) * HEAD_SIZE)
        value_span = slice(k_width + group * HEAD_SIZE, k_width + (group + 1) * HEAD_SIZE)
        key, value = keyval_ref[:, key_span], keyval_ref[:, value_span]
        grad_key = jnp.zeros(key.shape, jnp.float32)
        grad_value = jnp.zeros(key.shape, jnp.float32)
        for head in range(group * per_group, (group + 1) * per_group):
            span = slice(head * HEAD_SIZE, (head + 1) * HEAD_SIZE)
            query, grad_mixed = query_ref[:, span], mixed_grad_ref[:, span]
            probs = softmax_rows(query, key, allowed)
            grad_value += dot_tn(probs.astype(jnp.bfloat16), grad_mixed)
            grad_probs = dot_nt(grad_mixed, value)
            mean = jnp.sum(probs * grad_probs, axis=-1, keepdims=True)
            grad_scores = (probs * (grad_probs - mean)).astype(jnp.bfloat16)
            grad_proj_ref[:, span] = unrotate(dot32(grad_scores, key) * SCORE_SCALE)
            grad_key += dot_tn(grad_scores, query)
        grad_proj_ref[:, q_width + group * HEAD_SIZE : q_width + (group + 1) * HEAD_SIZE] = (
            unrotate(grad_key * SCORE_SCALE)
        )
        first = q_width + k_width + group * HEAD_SIZE
        grad_proj_ref[:, first : first + HEAD_SIZE] = grad_value.astype(jnp.bfloat16)
    gates = jnp.maximum(gates_ref[...], 0.0)
    grad_gates = grad_gates_ref[...]
    grad_logits = gates * (grad_gates - jnp.sum(gates * grad_gates, axis=-1, keepdims=True))
    high = grad_logits.astype(jnp.bfloat16).astype(jnp.float32)
    low = pltpu.roll(grad_logits - high, EXPERTS, 1)
    grad_proj_ref[:, proj_width:] = (high + low).astype(jnp.bfloat16)
    grad_xn1 = dot_nt(grad_proj_ref[...], weight_ref[...])
    tok = tok_ref[...].astype(jnp.float32)
    scale = rms_scale(tok)
    unit = tok * scale
    gain_sum_ref[0:1, :] = jnp.sum(grad_xn1 * unit, axis=0, keepdims=True)
    grad_unit = grad_xn1 * gains_ref[0:1, :]
    grad_tok_ref[...] = (
        grad_hidden
        + scale * (grad_unit - unit * jnp.mean(grad_unit * unit, axis=-1, keepdims=True))
    ).astype(jnp.bfloat16)


def ring_order(peers):
    minor = peers // 4
    walk = []
    for col in range(minor):
        line = range(4) if col % 2 == 0 else range(3, -1, -1)
        walk += [row * minor + col for row in line]
    return walk


def ring_step(part, shift, peers):
    order = ring_order(peers)
    pairs = [(order[i], order[(i + shift) % peers]) for i in range(peers)]
    return lax.ppermute(part, "expert", pairs)


class RingGather:
    def __init__(self, part, peers):
        self.peers = peers
        self.half = part.shape[0] // 2
        self.from_left, self.from_right = [part], [part]
        self.far = None
        self.sent = None

    def step(self, *earlier):
        left, right = self.from_left[-1], self.from_right[-1]
        last = len(self.from_left) == self.peers // 2
        if last:
            left, right = left[: self.half], right[self.half :]
        if earlier:
            left, right = lax.optimization_barrier((left, right) + earlier)[:2]
        self.sent = (left, right)
        left, right = ring_step(left, 1, self.peers), ring_step(right, -1, self.peers)
        if last:
            self.far = (left, right)
        else:
            self.from_left.append(left)
            self.from_right.append(right)
        return self

    def blocks(self):
        far = jnp.concatenate(self.far, axis=0)
        return self.from_left + [far] + self.from_right[:0:-1]

    def parts(self, k, micro_idx=None):
        lead = () if micro_idx is None else (micro_idx,)
        if k < len(self.from_left):
            return [(self.from_left[k], lead)]
        if k > self.peers // 2:
            return [(self.from_right[self.peers - k], lead)]
        if micro_idx is None:
            return [(part, ()) for part in self.far]
        return [(self.far[micro_idx], (0,))]


class RingScatter:
    def __init__(self, part, peers):
        self.part, self.peers = part, peers
        self.at = peers // 2
        self.sent = None

    def step(self, *earlier):
        peers, k = self.peers, self.at
        if k == peers // 2:
            block = self.part(k)
            self.half = block.shape[0] // 2
            left, right = block[: self.half], block[self.half :]
        else:
            left, right = self.part(k), self.part(peers - k)
            half = self.half
            if k == peers // 2 - 1:
                left = jnp.concatenate([add_rows(left[:half], self.left), left[half:]], axis=0)
                right = jnp.concatenate([right[:half], add_rows(right[half:], self.right)], axis=0)
            else:
                left, right = add_rows(left, self.left), add_rows(right, self.right)
        if earlier:
            left, right = lax.optimization_barrier((left, right) + earlier)[:2]
        self.sent = (left, right)
        self.left = ring_step(left, -1, peers)
        self.right = ring_step(right, 1, peers)
        self.at = k - 1
        return self

    def pieces(self):
        return self.part(0), self.left, self.right


def add_rows(left, right):
    return (left.astype(jnp.float32) + right.astype(jnp.float32)).astype(jnp.bfloat16)


def expert_kernel(sources, *refs):
    rows_refs = refs[:sources]
    grad_refs = refs[sources : 2 * sources]
    gate_ref, w_in_ref, w_out_ref = refs[2 * sources : 2 * sources + 3]
    (
        back_rows_ref,
        back_grads_ref,
        grad_gate_ref,
        picked_ref,
        grad_result_ref,
        activated_ref,
        grad_pre_ref,
    ) = refs[-7:]
    capacity, width = rows_refs[0].shape
    for k in range(sources):
        picked_ref[pl.ds(k * capacity, capacity), :] = rows_refs[k][...]
    pre_act = dot32(picked_ref[...], w_in_ref[...])
    gate_part = pre_act[:, :FF]
    up_part = pre_act[:, FF:]
    square = gate_part * gate_part
    bend = jnp.tanh(GELU_SCALE * gate_part * (1.0 + GELU_CUBE * square))
    lift = 0.5 * (1.0 + bend)
    gelu_val = gate_part * lift
    slope = lift + 0.5 * gate_part * (1.0 - bend * bend) * (
        GELU_SCALE * (1.0 + 3.0 * GELU_CUBE * square)
    )
    activated_ref[...] = (gelu_val * up_part).astype(jnp.bfloat16)
    result = dot32(activated_ref[...], w_out_ref[...])
    gates = gate_ref[...]
    for k in range(sources):
        span = slice(k * capacity, (k + 1) * capacity)
        grad_rows = grad_refs[k][...].astype(jnp.float32)
        grad_gate_ref[span, :] = jnp.sum(result[span] * grad_rows, axis=-1, keepdims=True)
        back_rows_ref[k] = (result[span] * gates[span]).astype(jnp.bfloat16)
        grad_result_ref[span, :] = (grad_rows * gates[span]).astype(jnp.bfloat16)
    grad_act = lax.dot_general(
        grad_result_ref[...],
        w_out_ref[...],
        (((1,), (1,)), ((), ())),
        preferred_element_type=jnp.float32,
    )
    grad_pre_ref[:, :FF] = (grad_act * up_part * slope).astype(jnp.bfloat16)
    grad_pre_ref[:, FF:] = (grad_act * gelu_val).astype(jnp.bfloat16)
    grad_in = lax.dot_general(
        grad_pre_ref[...],
        w_in_ref[...],
        (((1,), (1,)), ((), ())),
        preferred_element_type=jnp.float32,
    ).astype(jnp.bfloat16)
    for k in range(sources):
        back_grads_ref[k] = grad_in[k * capacity : (k + 1) * capacity]


def expert_pass(rows_list, grads_list, gate_slots, w_in, w_out, held_outs, position, first, count):
    sources = len(rows_list)
    local_experts, width, _ = w_in.shape
    slots = rows_list[0].shape[0]
    capacity = slots // local_experts
    held = sources * capacity
    block_spec = pl.BlockSpec((capacity, width), lambda e: (e + first, 0))
    back_spec = pl.BlockSpec((sources, capacity, width), lambda e: (0, e + first, 0))
    column_spec = pl.BlockSpec((None, held, 1), lambda e: (e + first, 0, 0))

    def kept_spec(columns):
        return pl.BlockSpec((None, held, columns), lambda e: (e + first, position[0], 0))

    def kept_shape(columns):
        return jax.ShapeDtypeStruct((local_experts, position[1] * held, columns), jnp.bfloat16)

    kept_widths = (width, width, FF, 2 * FF)
    first_held = 2 * sources + 3
    given = [(i, part) for i, part in enumerate(held_outs) if part is not None]
    return pl.pallas_call(
        functools.partial(expert_kernel, sources),
        grid=(count,),
        in_specs=[block_spec] * (2 * sources)
        + [
            column_spec,
            pl.BlockSpec((None, width, 2 * FF), lambda e: (e + first, 0, 0)),
            pl.BlockSpec((None, FF, width), lambda e: (e + first, 0, 0)),
        ]
        + [pl.BlockSpec(memory_space=pl.ANY)] * len(given),
        out_specs=[back_spec, back_spec, column_spec] + [kept_spec(c) for c in kept_widths],
        out_shape=[
            jax.ShapeDtypeStruct((sources, slots, width), jnp.bfloat16),
            jax.ShapeDtypeStruct((sources, slots, width), jnp.bfloat16),
            jax.ShapeDtypeStruct((local_experts, held, 1), jnp.float32),
        ]
        + [kept_shape(c) for c in kept_widths],
        input_output_aliases={first_held + at: i for at, (i, _) in enumerate(given)},
        compiler_params=pltpu.CompilerParams(vmem_limit_bytes=60 * 1024 * 1024),
        cost_estimate=SMALL_COST,
        name="expert_pass",
    )(*rows_list, *grads_list, gate_slots, w_in, w_out, *[part for _, part in given])


def block_call(kernel, operands, out_shape, name, scratch=()):
    def spec(array, lead):
        rest = array.shape[len(lead) :]
        at = lead + (0,) * len(rest)
        return pl.BlockSpec((None,) * len(lead) + rest, lambda i: at)

    return pl.pallas_call(
        kernel,
        grid=(1,),
        in_specs=[spec(*operand) for operand in operands],
        out_shape=out_shape,
        scratch_shapes=list(scratch),
        compiler_params=pltpu.CompilerParams(vmem_limit_bytes=60 * 1024 * 1024),
        cost_estimate=SMALL_COST,
        name=name,
    )(*[array for array, _ in operands])


def pick_kernel(shares, place_ref, *refs):
    at = 0
    outs = refs[sum(count for _, count in shares) :]
    for (k, count), out_ref in zip(shares, outs):
        total, row = None, 0
        for block_ref in refs[at : at + count]:
            held = block_ref.shape[0]
            part = dot32(place_ref[k, :, row : row + held], block_ref[...])
            total = part if total is None else total + part
            row += held
        out_ref[...] = total.astype(jnp.bfloat16)
        at += count


def pick_rows(place, ring, distances, micro_idx=None):
    _, slots, rows = place.shape
    parts = [ring.parts(k, micro_idx) for k in distances]
    width = parts[0][0][0].shape[-1]
    return block_call(
        functools.partial(pick_kernel, [(k, len(p)) for k, p in zip(distances, parts)]),
        [(place, ())] + [operand for p in parts for operand in p],
        [jax.ShapeDtypeStruct((slots, width), jnp.bfloat16) for _ in distances],
        "pick_rows",
    )


def spread_kernel(place_ref, rows_ref, grads_ref, gate_ref, out_ref, gate_out_ref):
    place = place_ref[...]
    out_ref[0] = dot_tn(place, grads_ref[...]).astype(jnp.bfloat16)
    out_ref[1] = dot_tn(place, rows_ref[...]).astype(jnp.bfloat16)
    capacity = gate_ref.shape[1]
    for e in range(gate_ref.shape[0]):
        hit = place[e * capacity : (e + 1) * capacity].astype(jnp.float32)
        gate_out_ref[e : e + 1, :] = jnp.sum(hit * gate_ref[e], axis=0, keepdims=True)


def spread_rows(place, rows_back, grads_back, gate_slots):
    sources, slots, rows = place.shape
    width = rows_back.shape[-1]
    local_experts = gate_slots.shape[0]
    by_source = pl.BlockSpec((None, slots, width), lambda k: (k, 0, 0))
    return pl.pallas_call(
        spread_kernel,
        grid=(sources,),
        in_specs=[
            pl.BlockSpec((None, slots, rows), lambda k: (k, 0, 0)),
            by_source,
            by_source,
            pl.BlockSpec((local_experts, slots // local_experts, 1), lambda k: (0, k, 0)),
        ],
        out_specs=[
            pl.BlockSpec((None, 2, rows, width), lambda k: (k, 0, 0, 0)),
            pl.BlockSpec((None, local_experts, rows), lambda k: (k, 0, 0)),
        ],
        out_shape=[
            jax.ShapeDtypeStruct((sources, 2, rows, width), jnp.bfloat16),
            jax.ShapeDtypeStruct((sources, local_experts, rows), jnp.float32),
        ],
        compiler_params=pltpu.CompilerParams(vmem_limit_bytes=60 * 1024 * 1024),
        cost_estimate=SMALL_COST,
        name="spread_rows",
    )(place, rows_back, grads_back, gate_slots)


def attention_forward(tokens, seg_col, seg_row, routes, gains, weight, cos, sin):
    count, rows, width = tokens.shape

    def by_micro(*shape):
        return pl.BlockSpec((None,) + shape, lambda m: (m,) + (0,) * len(shape))

    def shared(part):
        return pl.BlockSpec(part.shape, lambda m: (0, 0))

    kv_width = 2 * KEY_VALUE_HEADS * HEAD_SIZE
    shapes = [
        ((rows, width), jnp.bfloat16),
        ((rows, QUERY_HEADS * HEAD_SIZE), jnp.bfloat16),
        ((rows, kv_width), jnp.bfloat16),
        ((rows, QUERY_HEADS * HEAD_SIZE), jnp.bfloat16),
        ((rows, 128), jnp.float32),
    ]
    return pl.pallas_call(
        attention_kernel,
        grid=(count,),
        in_specs=[
            by_micro(rows, width),
            by_micro(rows, 1),
            by_micro(1, rows),
            by_micro(rows, TOPK),
            shared(gains),
            shared(weight),
            shared(cos),
            shared(sin),
        ],
        out_specs=[by_micro(*shape) for shape, _ in shapes],
        out_shape=[jax.ShapeDtypeStruct((count,) + shape, kind) for shape, kind in shapes],
        compiler_params=pltpu.CompilerParams(vmem_limit_bytes=60 * 1024 * 1024),
        cost_estimate=SMALL_COST,
        name="attention_forward",
    )(tokens, seg_col, seg_row, routes, gains, weight, cos, sin)


def attention_grad_kernel(core_ref, xn1, mixed, *refs):
    count = xn1.shape[0]
    proj, attn, sums = [refs[i * count : (i + 1) * count] for i in range(3)]
    mine_ref, other_ref = refs[-2:]
    split = proj[0].shape[1]
    span = mine_ref.shape[0]
    grad = sum(dot_tn(xn1[m], proj[m][...]) for m in range(count))
    router = grad[:, split - 128 :]
    lane = lax.broadcasted_iota(jnp.int32, router.shape, 1)
    router = router + pltpu.roll(router, 128 - EXPERTS, 1)
    gain = sum(part[...] for part in sums)
    lines = [jnp.zeros((EXPERTS, gain.shape[1]), jnp.float32), gain]
    lines.append(jnp.zeros((128 - EXPERTS - gain.shape[0], gain.shape[1]), jnp.float32))
    router = jnp.where(lane < EXPERTS, router, jnp.concatenate(lines, axis=0).T)
    first = core_ref[0] == 0

    def put(columns, value):
        value = value.astype(jnp.bfloat16)
        low, high = value[:span], value[span:]
        mine_ref[:, columns] = jnp.where(first, low, high)
        other_ref[:, columns] = jnp.where(first, high, low)

    put(slice(0, split - 128), grad[:, : split - 128])
    put(slice(split - 128, split), router)
    put(slice(split, None), sum(dot_tn(mixed[m], attn[m][...]) for m in range(count)))


def attention_grads(core, xn1, mixed, proj, attn, gain_sums, parts):
    count, rows, width = xn1.shape
    span = width // parts
    lines = parts // 2
    columns = proj[0].shape[1] + attn[0].shape[1]
    by_line = pl.BlockSpec((count, rows, 2 * span), lambda i, c: (0, 0, i))

    def shared(part):
        return pl.BlockSpec(part.shape, lambda i, c: (0, 0))

    out_spec = pl.BlockSpec((None, span, columns), lambda i, c: (i, 0, 0))
    out_shape = jax.ShapeDtypeStruct((lines, span, columns), jnp.bfloat16)
    return pl.pallas_call(
        attention_grad_kernel,
        grid_spec=pltpu.PrefetchScalarGridSpec(
            num_scalar_prefetch=1,
            grid=(lines,),
            in_specs=[by_line, by_line]
            + [shared(p) for p in proj]
            + [shared(p) for p in attn]
            + [pl.BlockSpec((p.shape[0], 2 * span), lambda i, c: (0, i)) for p in gain_sums],
            out_specs=[out_spec, out_spec],
        ),
        out_shape=[out_shape, out_shape],
        compiler_params=pltpu.CompilerParams(vmem_limit_bytes=60 * 1024 * 1024),
        cost_estimate=SMALL_COST,
        name="attention_grads",
    )(core, xn1, mixed, *proj, *attn, *gain_sums)


def per_device(
    tokens,
    segments,
    routes,
    norm_one,
    norm_two,
    w_query,
    key_value_weight,
    w_out_attn,
    w_router,
    w_in,
    w_out,
    cotangent,
):
    micro_count, rows, width = tokens.shape
    micros = range(micro_count)
    peers = lax.axis_size("expert")
    dp_count = lax.axis_size("dp")
    local_experts = w_in.shape[0]
    experts = local_experts * peers
    capacity = rows // 4
    q_width = w_query.shape[1]
    kv_width = key_value_weight.shape[1]
    proj_width = q_width + kv_width
    cosine_table, sine_values = rope_tables(rows, HEAD_SIZE)
    cos = jnp.concatenate([cosine_table, cosine_table], axis=1)
    sin = jnp.concatenate([-sine_values, sine_values], axis=1)
    order = ring_order(peers)
    spot = [order.index(dev) for dev in range(peers)]
    left_devices = [[order[(spot[me] - k) % peers] for k in range(peers)] for me in range(peers)]
    left_device = jnp.array(left_devices, jnp.int32)[lax.axis_index("expert")]
    left_distances = [[(spot[me] - spot[dev]) % peers for dev in range(peers)] for me in range(peers)]
    left_distance = jnp.array(left_distances, jnp.int32)[lax.axis_index("expert")]
    my_spot = jnp.array(spot, jnp.int32)[lax.axis_index("expert")]

    def gather_dp(part, axis=0):
        return lax.all_gather(part, "dp", axis=axis, tiled=True)

    router_pad = jnp.zeros((w_router.shape[0], 128 - 2 * experts), jnp.bfloat16)
    first_weight = jnp.concatenate(
        [w_query, key_value_weight, w_router, w_router, router_pad], axis=1
    )
    gains = gather_dp(jnp.stack([norm_one, norm_two]), axis=1).astype(jnp.float32)
    first_weight = gather_dp(first_weight)
    out_weight = gather_dp(w_out_attn)

    codes = jnp.swapaxes(
        slot_codes(routes, experts).reshape(micro_count, peers, local_experts, rows), 0, 1
    )
    codes = lax.all_to_all(codes, "expert", split_axis=0, concat_axis=0, tiled=True)
    codes = jnp.take(codes, left_device, axis=0)
    hits = [slot_hits(codes[:, m], capacity) for m in micros]
    places = [hit.astype(jnp.bfloat16).reshape(peers, -1, rows) for hit in hits]

    cot_ring = RingGather(cotangent, peers)
    steps = peers // 2
    for _ in range(steps - 2):
        cot_ring.step()

    seg_col, seg_row = segments[:, :, None], segments[:, None, :]
    xn1, query, keyval, mixed, gates = attention_forward(
        tokens, seg_col, seg_row, routes, gains, first_weight, cos, sin
    )
    gates_out = jnp.transpose(
        gates[:, :, :experts].reshape(micro_count, rows, peers, local_experts), (2, 0, 3, 1)
    )
    gates_in = lax.all_to_all(gates_out, "expert", split_axis=0, concat_axis=0, tiled=True)
    gates_in = jnp.take(gates_in, left_device, axis=0)
    cot_ring.step(gates_out)
    mixed = after(mixed, *cot_ring.sent)

    hidden, xn2 = [], []
    for m in micros:
        out = block_call(
            hidden_kernel,
            [(mixed, (m,)), (tokens, (m,)), (gains, ()), (out_weight, ())],
            [
                jax.ShapeDtypeStruct((rows, width), jnp.float32),
                jax.ShapeDtypeStruct((rows, width), jnp.bfloat16),
            ],
            "hidden_rows",
        )
        hidden.append(out[0])
        xn2.append(out[1])
    cot_ring.step()
    every = list(range(peers))
    late = [steps - 1, steps, steps + 1]
    early = [k for k in every if k not in late]
    row_rings = [RingGather(xn2[m], peers) for m in micros]
    for _ in range(steps):
        row_rings[0].step()
    groups = peers // GROUP

    class Experts:
        kept = [None] * 4

        def __init__(self, m, calls):
            self.m = m
            self.per_call = local_experts // calls
            self.outs = [[None] * 3 for _ in range(groups)]

        def pick(self, *earlier):
            m = self.m
            place = after(places[m], *earlier) if earlier else places[m]
            ring = row_rings[m]
            self.grads = pick_rows(place, cot_ring, every, m)
            rows_of = dict(zip(early, pick_rows(place, ring, early)))
            rows_of.update(zip(late, pick_rows(place, ring, late)))
            self.rows = [rows_of[k] for k in every]
            slots = jnp.sum(
                jnp.where(hits[m], gates_in[:, m][:, :, None, :], 0.0), axis=-1
            )
            self.gate_slots = jnp.swapaxes(slots, 0, 1)

        def call(self, number, *earlier):
            for g in range(groups):
                span = slice(g * GROUP, (g + 1) * GROUP)
                here = self.rows[span]
                here[0] = after(here[0], *earlier)
                done = expert_pass(
                    here,
                    self.grads[span],
                    self.gate_slots[:, span].reshape(local_experts, -1, 1),
                    w_in,
                    w_out,
                    self.outs[g] + Experts.kept,
                    (self.m * groups + g, micro_count * groups),
                    number * self.per_call,
                    self.per_call,
                )
                self.outs[g], Experts.kept = list(done[:3]), list(done[3:])
            return done[2]

        def spread(self, *earlier):
            place = places[self.m]
            place = after(place, *earlier) if earlier else place
            done = [
                spread_rows(place[g * GROUP : (g + 1) * GROUP], *self.outs[g])
                for g in range(groups)
            ]
            self.sums = [part for part, _ in done]
            return jnp.concatenate([part for _, part in done], axis=0)

        def sum_of(self, k, which=None):
            part = self.sums[k // GROUP][k % GROUP]
            return part if which is None else part[which]

    first, second = Experts(0, local_experts), Experts(1, max(1, local_experts // 2))
    row_rings[1].step(*row_rings[0].sent)
    first.pick()
    token = first.call(0, *row_rings[1].sent)
    for number in range(1, local_experts):
        row_rings[1].step(token)
        token = first.call(number, *row_rings[1].sent)
    while row_rings[1].far is None:
        row_rings[1].step(token)
    gates_first = first.spread(*row_rings[1].far)
    ring_first = RingScatter(first.sum_of, peers).step()
    second.pick(*ring_first.sent)
    token = second.call(0, *ring_first.sent)
    for number in range(1, max(1, local_experts // 2)):
        ring_first.step(token)
        token = second.call(number, *ring_first.sent)
    ring_first.step(token)
    gates_second = second.spread(*ring_first.sent)
    grad_second = RingScatter(lambda k: second.sum_of(k, 0), peers).step()
    out_second = RingScatter(lambda k: second.sum_of(k, 1), peers)
    picked, grad_result, activated, grad_pre = Experts.kept
    picked = after(picked, *grad_second.sent)
    w_in_sum = jnp.einsum(
        "erd,erf->edf", picked, grad_pre, preferred_element_type=jnp.float32
    ).astype(jnp.bfloat16)
    grad_w_in = lax.psum_scatter(w_in_sum, "dp", scatter_dimension=1, tiled=True)
    while ring_first.at > 0:
        ring_first.step(w_in_sum)
    grad_second.step(w_in_sum)
    activated = after(activated, *grad_second.sent, *ring_first.sent)
    w_out_sum = jnp.einsum(
        "erf,erd->efd", activated, grad_result, preferred_element_type=jnp.float32
    ).astype(jnp.bfloat16)
    grad_w_out = lax.psum_scatter(w_out_sum, "dp", scatter_dimension=1, tiled=True)
    grad_second.step(w_out_sum)

    grad_gates_out = jnp.take(jnp.stack([gates_first, gates_second], axis=1), left_distance, axis=0)
    grad_gates = lax.all_to_all(
        grad_gates_out, "expert", split_axis=0, concat_axis=0, tiled=True
    )
    grad_gates = jnp.transpose(grad_gates, (1, 3, 0, 2)).reshape(micro_count, rows, experts)
    grad_gates = jnp.pad(grad_gates, ((0, 0), (0, 0), (0, 128 - experts)))

    def backward(m, pieces, *earlier):
        (own, lead), left, right = pieces
        return block_call(
            backward_kernel,
            [
                (after(own, *earlier), lead),
                left,
                right,
                (cotangent, (m,)),
                (hidden[m], ()),
                (tokens, (m,)),
                (query, (m,)),
                (keyval, (m,)),
                (seg_col, (m,)),
                (seg_row, (m,)),
                (gates, (m,)),
                (grad_gates, (m,)),
                (gains, ()),
                (first_weight, ()),
                (out_weight, ()),
                (cos, ()),
                (sin, ()),
            ],
            [
                jax.ShapeDtypeStruct((rows, width), jnp.bfloat16),
                jax.ShapeDtypeStruct((rows, proj_width + 128), jnp.bfloat16),
                jax.ShapeDtypeStruct((rows, width), jnp.bfloat16),
                jax.ShapeDtypeStruct((8, width), jnp.float32),
            ],
            "attention_backward",
            [pltpu.VMEM((rows, q_width), jnp.bfloat16)],
        )

    pieces = ((first.sums[0], (0, 0)), (ring_first.left, (0,)), (ring_first.right, (0,)))
    back_first = backward(0, pieces, *grad_second.sent)
    while grad_second.at > 0:
        grad_second.step(back_first[3])
    out_second.step(grad_second.left, grad_second.right)
    pieces = ((second.sums[0], (0, 0)), (grad_second.left, ()), (grad_second.right, ()))
    back_second = backward(1, pieces, *out_second.sent)
    out_second.step(back_second[3])
    grad_tokens, grad_proj, grad_attn, gain_sums = zip(back_first, back_second)
    core = lax.rem(lax.axis_index("dp"), 2).astype(jnp.int32).reshape(1)
    mine, other = attention_grads(
        core, after(xn1, *out_second.sent), mixed, grad_proj, grad_attn, gain_sums, dp_count
    )
    out_second.step(mine)
    share, grad_w_in, grad_w_out = reduce_packed(
        mine, other, my_spot, peers, dp_count, out_second, (grad_w_in, grad_w_out)
    )

    outputs = []
    wide = jnp.float32
    own, left, right = ring_first.pieces()
    outputs.append(hidden[0] + own[1].astype(wide) + left[1].astype(wide) + right[1].astype(wide))
    own, left, right = out_second.pieces()
    outputs.append(hidden[1] + own.astype(wide) + left.astype(wide) + right.astype(wide))
    outputs = [part.astype(jnp.bfloat16) for part in outputs]
    edge = proj_width
    return (
        jnp.stack(outputs),
        jnp.stack(grad_tokens),
        share[:, edge + experts],
        share[:, edge + experts + 1],
        share[:, :q_width],
        share[:, q_width:proj_width],
        share[:, edge + 128 :],
        share[:, edge : edge + experts],
        grad_w_in,
        grad_w_out,
    )


def reduce_packed(mine, other, my_spot, peers, dp_count, out_ring, expert_grads):
    lines, span, columns = mine.shape
    swap = [(d, d ^ 1) for d in range(dp_count)]
    total = mine + lax.ppermute(other, "dp", swap)
    piece = span // peers
    while out_ring.at > 0:
        out_ring.step(total)
    total = total.reshape(lines, peers, piece, columns)

    def part(k):
        at = lax.rem(my_spot - k + peers, peers)
        return lax.dynamic_slice_in_dim(total, at, 1, axis=1).reshape(lines * piece, columns)

    ring = RingScatter(part, peers)
    while ring.at > 0:
        ring.step()
    own, left, right = [part.astype(jnp.float32) for part in ring.pieces()]
    mine = (own + left + right).astype(jnp.bfloat16).reshape(lines, piece, columns)
    line = lax.axis_index("dp") // 2

    def for_line(at):
        return lax.dynamic_index_in_dim(mine, lax.rem(at, lines), 0, keepdims=False)

    share = for_line(line).astype(jnp.float32)
    for k in range(1, lines):
        pairs = [(d, (d + 2 * k) % dp_count) for d in range(dp_count)]
        share = share + lax.ppermute(for_line(line + k), "dp", pairs)
    gather = RingGather(share.astype(jnp.bfloat16), peers)
    gather.step()
    expert_grads = [part.astype(jnp.float32) for part in expert_grads]
    gather.step(*expert_grads)
    while gather.far is None:
        gather.step()
    by_distance = jnp.stack(gather.blocks())
    distance = lax.rem(my_spot - jnp.arange(peers, dtype=jnp.int32) + peers, peers)
    by_spot = jnp.take(by_distance, distance, axis=0)
    return by_spot.reshape(span, columns).astype(jnp.float32), *expert_grads


def solution(mesh):
    return jax.shard_map(
        per_device,
        mesh=mesh,
        in_specs=(
            P(None, ("dp", "expert"), None),
            P(None, ("dp", "expert")),
            P(None, ("dp", "expert"), None),
            P("dp"),
            P("dp"),
            P("dp", None),
            P("dp", None),
            P("dp", None),
            P("dp", None),
            P("expert", None, None),
            P("expert", None, None),
            P(None, ("dp", "expert"), None),
        ),
        out_specs=(
            P(None, ("dp", "expert"), None),
            P(None, ("dp", "expert"), None),
            P("dp"),
            P("dp"),
            P("dp", None),
            P("dp", None),
            P("dp", None),
            P("dp", None),
            P("expert", "dp", None),
            P("expert", "dp", None),
        ),
        check_vma=False,
    )
```

```python
import functools
import math

import jax
import jax.numpy as jnp
from jax import lax
from jax.experimental import pallas as pl
from jax.experimental.pallas import tpu as pltpu
from jax.sharding import PartitionSpec as P

QUERY_HEADS = 12
KEY_VALUE_HEADS = 2
HEAD_SIZE = 128
FF = 768
TOPK = 4
EXPERTS = 32
EXTRA = 16
PIECES = 3
GROUP = 8

eps_norm = 1e-06
rope_base = 1000000.0
mask_fill = -1e30
highest = lax.Precision.HIGHEST


def rms_scale(tensor):
    return lax.rsqrt(jnp.mean(tensor * tensor, axis=-1, keepdims=True) + eps_norm)


def rope_tables(sequence_length, head_width):
    positions = jnp.arange(sequence_length).astype(jnp.float32)
    frequency = rope_base ** (-(jnp.arange(head_width // 2).astype(jnp.float32) * 2.0) / head_width)
    angles = positions[:, None] * frequency[None, :]
    return (jnp.cos(angles), jnp.sin(angles))

SCORE_SCALE = 1.0 / math.sqrt(HEAD_SIZE)
GELU_SCALE = math.sqrt(2.0 / math.pi)
GELU_CUBE = 0.044715
SMALL_COST = pl.CostEstimate(flops=1_000_000, bytes_accessed=1_000_000, transcendentals=0)


def after(value, *earlier):
    return lax.optimization_barrier((value,) + earlier)[0]


def slot_hits(routes_all, first_expert, local_experts, capacity):
    rows = routes_all.shape[-1]
    names = first_expert + jnp.arange(local_experts, dtype=jnp.int32)
    named = routes_all[:, None].astype(jnp.int32) == names[None, :, None, None]
    member = jnp.any(named, axis=2)
    lower = (jnp.arange(rows)[:, None] < jnp.arange(rows)[None, :]).astype(jnp.bfloat16)
    rank = dot32(member.astype(jnp.bfloat16).reshape(-1, rows), lower).reshape(member.shape)
    slots = jnp.arange(capacity, dtype=jnp.float32)
    return member[:, :, None, :] & (rank[:, :, None, :] == slots[None, None, :, None])


def pack_pieces(values, out_ref, first_row):
    rows = values.shape[1]
    rest = values
    for piece in range(PIECES):
        part = rest.astype(jnp.bfloat16)
        rest = rest - part.astype(jnp.float32)
        for half in range(EXPERTS // EXTRA):
            at = (piece * (EXPERTS // EXTRA) + half) * rows
            out_ref[first_row : first_row + EXTRA, at : at + rows] = part[
                half * EXTRA : (half + 1) * EXTRA
            ]


def dot32(left, right):
    return jnp.dot(left, right, preferred_element_type=jnp.float32)


def dot_nt(left, right):
    return lax.dot_general(
        left, right, (((1,), (1,)), ((), ())), preferred_element_type=jnp.float32
    )


def dot_tn(left, right):
    return lax.dot_general(
        left, right, (((0,), (0,)), ((), ())), preferred_element_type=jnp.float32
    )


def mask_of(seg_col, seg_row):
    rows = seg_col.shape[0]
    query_at = lax.broadcasted_iota(jnp.int32, (rows, rows), 0)
    key_at = lax.broadcasted_iota(jnp.int32, (rows, rows), 1)
    return (seg_col == seg_row) & (query_at >= key_at)


def softmax_rows(query, key, allowed):
    scores = jnp.where(allowed, dot_nt(query, key) * SCORE_SCALE, mask_fill)
    weight = jnp.exp(scores - jnp.max(scores, axis=-1, keepdims=True))
    return weight / jnp.sum(weight, axis=-1, keepdims=True)


def attention_kernel(
    tok_ref,
    seg_col_ref,
    seg_row_ref,
    routes_ref,
    gains_ref,
    weight_ref,
    cos_ref,
    sin_ref,
    xn1_ref,
    query_ref,
    keyval_ref,
    mixed_ref,
    gates_ref,
    gates_pack_ref,
):
    tok = tok_ref[...].astype(jnp.float32)
    xn1_ref[...] = (tok * rms_scale(tok) * gains_ref[0:1, :]).astype(jnp.bfloat16)
    proj = dot32(xn1_ref[...], weight_ref[...])
    cos, sin = cos_ref[...], sin_ref[...]

    def rotate(part):
        return (part * cos + pltpu.roll(part, HEAD_SIZE // 2, 1) * sin).astype(jnp.bfloat16)

    q_width = QUERY_HEADS * HEAD_SIZE
    k_width = KEY_VALUE_HEADS * HEAD_SIZE
    for head in range(QUERY_HEADS):
        span = slice(head * HEAD_SIZE, (head + 1) * HEAD_SIZE)
        query_ref[:, span] = rotate(proj[:, span])
    for head in range(KEY_VALUE_HEADS):
        span = slice(head * HEAD_SIZE, (head + 1) * HEAD_SIZE)
        keyval_ref[:, span] = rotate(proj[:, q_width:][:, span])
    keyval_ref[:, k_width:] = proj[:, q_width + k_width : q_width + 2 * k_width].astype(
        jnp.bfloat16
    )
    logits = proj[:, q_width + 2 * k_width :]
    columns = lax.broadcasted_iota(jnp.int32, logits.shape, 1)
    named = [columns == routes_ref[:, j : j + 1] for j in range(TOPK)]
    chosen = [jnp.sum(jnp.where(hit, logits, 0.0), axis=-1, keepdims=True) for hit in named]
    top = functools.reduce(jnp.maximum, chosen)
    weight = [jnp.exp(part - top) for part in chosen]
    total = functools.reduce(jnp.add, weight)
    gates = jnp.full(logits.shape, -1.0, jnp.float32)
    for hit, part in zip(named, weight):
        gates = jnp.where(hit, part / total, gates)
    gates_ref[...] = gates
    pack_pieces(gates.T[:EXPERTS], gates_pack_ref, 0)
    allowed = mask_of(seg_col_ref[...], seg_row_ref[...])
    for head in range(QUERY_HEADS):
        span = slice(head * HEAD_SIZE, (head + 1) * HEAD_SIZE)
        group = head // (QUERY_HEADS // KEY_VALUE_HEADS)
        key = keyval_ref[:, group * HEAD_SIZE : (group + 1) * HEAD_SIZE]
        value = keyval_ref[:, k_width + group * HEAD_SIZE : k_width + (group + 1) * HEAD_SIZE]
        probs = softmax_rows(query_ref[:, span], key, allowed)
        mixed_ref[:, span] = dot32(probs.astype(jnp.bfloat16), value).astype(jnp.bfloat16)


def hidden_kernel(mixed_ref, tok_ref, gains_ref, weight_ref, pack_ref, hidden_ref, xn2_ref):
    rows = tok_ref.shape[0]
    hidden = tok_ref[...].astype(jnp.float32) + dot32(mixed_ref[...], weight_ref[...])
    hidden_ref[...] = hidden
    xn2_ref[:rows, :] = (hidden * rms_scale(hidden) * gains_ref[1:2, :]).astype(jnp.bfloat16)
    xn2_ref[rows:, :] = pack_ref[...]


def backward_kernel(
    own_ref,
    left_ref,
    right_ref,
    cot_ref,
    hidden_ref,
    tok_ref,
    query_ref,
    keyval_ref,
    seg_col_ref,
    seg_row_ref,
    gates_ref,
    gains_ref,
    weight_ref,
    out_weight_ref,
    cos_ref,
    sin_ref,
    grad_tok_ref,
    grad_proj_ref,
    grad_attn_ref,
    gain_sum_ref,
    mixed_grad_ref,
):
    width = tok_ref.shape[1]
    q_width = QUERY_HEADS * HEAD_SIZE
    k_width = KEY_VALUE_HEADS * HEAD_SIZE
    proj_width = q_width + 2 * k_width
    rows = tok_ref.shape[0]
    sums = [ref[...].astype(jnp.float32) for ref in (own_ref, left_ref, right_ref)]
    sums = sums[0] + sums[1] + sums[2]
    grad_xn2, pack = sums[:rows], sums[rows:]
    halves = EXPERTS // EXTRA
    lines = [
        sum(
            pack[:, (piece * halves + half) * rows : (piece * halves + half + 1) * rows]
            for piece in range(PIECES)
        )
        for half in range(halves)
    ]
    lines.append(jnp.zeros((128 - EXPERTS, rows), jnp.float32))
    grad_gates = jnp.concatenate(lines, axis=0).T
    hidden = hidden_ref[...]
    scale = rms_scale(hidden)
    unit = hidden * scale
    gain_sum_ref[...] = jnp.zeros(gain_sum_ref.shape, jnp.float32)
    gain_sum_ref[1:2, :] = jnp.sum(grad_xn2 * unit, axis=0, keepdims=True)
    grad_unit = grad_xn2 * gains_ref[1:2, :]
    grad_hidden = cot_ref[...].astype(jnp.float32) + scale * (
        grad_unit - unit * jnp.mean(grad_unit * unit, axis=-1, keepdims=True)
    )
    grad_attn_ref[...] = grad_hidden.astype(jnp.bfloat16)
    mixed_grad_ref[...] = dot_nt(grad_attn_ref[...], out_weight_ref[...]).astype(jnp.bfloat16)
    cos, sin = cos_ref[...], sin_ref[...]

    def unrotate(part):
        return (part * cos - pltpu.roll(part, HEAD_SIZE // 2, 1) * sin).astype(jnp.bfloat16)

    allowed = mask_of(seg_col_ref[...], seg_row_ref[...])
    per_group = QUERY_HEADS // KEY_VALUE_HEADS
    for group in range(KEY_VALUE_HEADS):
        key_span = slice(group * HEAD_SIZE, (group + 1) * HEAD_SIZE)
        value_span = slice(k_width + group * HEAD_SIZE, k_width + (group + 1) * HEAD_SIZE)
        key, value = keyval_ref[:, key_span], keyval_ref[:, value_span]
        grad_key = jnp.zeros(key.shape, jnp.float32)
        grad_value = jnp.zeros(key.shape, jnp.float32)
        for head in range(group * per_group, (group + 1) * per_group):
            span = slice(head * HEAD_SIZE, (head + 1) * HEAD_SIZE)
            query, grad_mixed = query_ref[:, span], mixed_grad_ref[:, span]
            probs = softmax_rows(query, key, allowed)
            grad_value += dot_tn(probs.astype(jnp.bfloat16), grad_mixed)
            grad_probs = dot_nt(grad_mixed, value)
            mean = jnp.sum(probs * grad_probs, axis=-1, keepdims=True)
            grad_scores = (probs * (grad_probs - mean)).astype(jnp.bfloat16)
            grad_proj_ref[:, span] = unrotate(dot32(grad_scores, key) * SCORE_SCALE)
            grad_key += dot_tn(grad_scores, query)
        grad_proj_ref[:, q_width + group * HEAD_SIZE : q_width + (group + 1) * HEAD_SIZE] = (
            unrotate(grad_key * SCORE_SCALE)
        )
        first = q_width + k_width + group * HEAD_SIZE
        grad_proj_ref[:, first : first + HEAD_SIZE] = grad_value.astype(jnp.bfloat16)
    gates = jnp.maximum(gates_ref[...], 0.0)
    grad_logits = gates * (grad_gates - jnp.sum(gates * grad_gates, axis=-1, keepdims=True))
    high = grad_logits.astype(jnp.bfloat16).astype(jnp.float32)
    low = pltpu.roll(grad_logits - high, EXPERTS, 1)
    grad_proj_ref[:, proj_width:] = (high + low).astype(jnp.bfloat16)
    grad_xn1 = dot_nt(grad_proj_ref[...], weight_ref[...])
    tok = tok_ref[...].astype(jnp.float32)
    scale = rms_scale(tok)
    unit = tok * scale
    gain_sum_ref[0:1, :] = jnp.sum(grad_xn1 * unit, axis=0, keepdims=True)
    grad_unit = grad_xn1 * gains_ref[0:1, :]
    grad_tok_ref[...] = (
        grad_hidden
        + scale * (grad_unit - unit * jnp.mean(grad_unit * unit, axis=-1, keepdims=True))
    ).astype(jnp.bfloat16)


def ring_order(peers):
    minor = peers // 4
    walk = []
    for col in range(minor):
        line = range(4) if col % 2 == 0 else range(3, -1, -1)
        walk += [row * minor + col for row in line]
    return walk


def ring_step(part, shift, peers):
    order = ring_order(peers)
    pairs = [(order[i], order[(i + shift) % peers]) for i in range(peers)]
    return lax.ppermute(part, "expert", pairs)


class RingGather:
    def __init__(self, part, peers, half):
        self.peers, self.half = peers, half
        self.from_left, self.from_right = [part], [part]
        self.far = None
        self.got = ()

    def step(self, *earlier):
        left, right = self.from_left[-1], self.from_right[-1]
        last = len(self.from_left) == self.peers // 2
        if last:
            left, right = left[: self.half], right[self.half :]
        if earlier:
            left, right = lax.optimization_barrier((left, right) + earlier)[:2]
        left, right = ring_step(left, 1, self.peers), ring_step(right, -1, self.peers)
        self.got = (left, right)
        if last:
            self.far = (left, right)
        else:
            self.from_left.append(left)
            self.from_right.append(right)
        return self

    def rows(self, k, first, count):
        if k < len(self.from_left):
            return self.from_left[k], first
        if k > self.peers // 2:
            return self.from_right[self.peers - k], first
        if first < self.half:
            return self.far[0], first
        return self.far[1], first - self.half

    def stack_rows(self, first, count):
        found = [self.rows(k, first, count) for k in range(self.peers)]
        return jnp.stack([array[at : at + count] for array, at in found])


class RingScatter:
    def __init__(self, part, peers, half):
        self.part, self.peers, self.half = part, peers, half
        self.at = peers // 2
        self.got = ()

    def step(self, *earlier):
        peers, k, half = self.peers, self.at, self.half
        if earlier and k < peers // 2:
            self.left, self.right = lax.optimization_barrier((self.left, self.right) + earlier)[:2]
        if k == peers // 2:
            block = self.part(k)
            left, right = block[:half], block[half:]
        else:
            left, right = self.part(k), self.part(peers - k)
            if k == peers // 2 - 1:
                left = jnp.concatenate([add_rows(left[:half], self.left), left[half:]], axis=0)
                right = jnp.concatenate([right[:half], add_rows(right[half:], self.right)], axis=0)
            else:
                left, right = add_rows(left, self.left), add_rows(right, self.right)
        if earlier and k == peers // 2:
            left, right = lax.optimization_barrier((left, right) + earlier)[:2]
        self.left = ring_step(left, -1, peers)
        self.right = ring_step(right, 1, peers)
        self.got = (self.left, self.right)
        self.at = k - 1
        return self

    def pieces(self):
        return self.part(0), self.left, self.right


def add_rows(left, right):
    return (left.astype(jnp.float32) + right.astype(jnp.float32)).astype(jnp.bfloat16)


def expert_kernel(sources, *refs):
    rows_refs = refs[:sources]
    grad_refs = refs[sources : 2 * sources]
    gate_ref, w_in_ref, w_out_ref = refs[2 * sources : 2 * sources + 3]
    (
        back_rows_ref,
        back_grads_ref,
        grad_gate_ref,
        picked_ref,
        grad_result_ref,
        activated_ref,
        grad_pre_ref,
    ) = refs[-7:]
    capacity, width = rows_refs[0].shape
    for k in range(sources):
        picked_ref[pl.ds(k * capacity, capacity), :] = rows_refs[k][...]
    pre_act = dot32(picked_ref[...], w_in_ref[...])
    gate_part = pre_act[:, :FF]
    up_part = pre_act[:, FF:]
    square = gate_part * gate_part
    bend = jnp.tanh(GELU_SCALE * gate_part * (1.0 + GELU_CUBE * square))
    lift = 0.5 * (1.0 + bend)
    gelu_val = gate_part * lift
    slope = lift + 0.5 * gate_part * (1.0 - bend * bend) * (
        GELU_SCALE * (1.0 + 3.0 * GELU_CUBE * square)
    )
    activated_ref[...] = (gelu_val * up_part).astype(jnp.bfloat16)
    result = dot32(activated_ref[...], w_out_ref[...])
    gates = gate_ref[...]
    for k in range(sources):
        span = slice(k * capacity, (k + 1) * capacity)
        grad_rows = grad_refs[k][...].astype(jnp.float32)
        grad_gate_ref[span, :] = jnp.sum(result[span] * grad_rows, axis=-1, keepdims=True)
        back_rows_ref[k] = (result[span] * gates[span]).astype(jnp.bfloat16)
        grad_result_ref[span, :] = (grad_rows * gates[span]).astype(jnp.bfloat16)
    grad_act = lax.dot_general(
        grad_result_ref[...],
        w_out_ref[...],
        (((1,), (1,)), ((), ())),
        preferred_element_type=jnp.float32,
    )
    grad_pre_ref[:, :FF] = (grad_act * up_part * slope).astype(jnp.bfloat16)
    grad_pre_ref[:, FF:] = (grad_act * gelu_val).astype(jnp.bfloat16)
    grad_in = lax.dot_general(
        grad_pre_ref[...],
        w_in_ref[...],
        (((1,), (1,)), ((), ())),
        preferred_element_type=jnp.float32,
    ).astype(jnp.bfloat16)
    for k in range(sources):
        back_grads_ref[k] = grad_in[k * capacity : (k + 1) * capacity]


def expert_pass(rows_list, grads_list, gate_slots, w_in, w_out, held_outs, position, first, count):
    sources = len(rows_list)
    local_experts, width, _ = w_in.shape
    slots = rows_list[0].shape[0]
    capacity = slots // local_experts
    held = sources * capacity
    block_spec = pl.BlockSpec((capacity, width), lambda e: (e + first, 0))
    back_spec = pl.BlockSpec((sources, capacity, width), lambda e: (0, e + first, 0))
    column_spec = pl.BlockSpec((None, held, 1), lambda e: (e + first, 0, 0))

    def kept_spec(columns):
        return pl.BlockSpec((None, held, columns), lambda e: (e + first, position[0], 0))

    def kept_shape(columns):
        return jax.ShapeDtypeStruct((local_experts, position[1] * held, columns), jnp.bfloat16)

    kept_widths = (width, width, FF, 2 * FF)
    first_held = 2 * sources + 3
    given = [(i, part) for i, part in enumerate(held_outs) if part is not None]
    return pl.pallas_call(
        functools.partial(expert_kernel, sources),
        grid=(count,),
        in_specs=[block_spec] * (2 * sources)
        + [
            column_spec,
            pl.BlockSpec((None, width, 2 * FF), lambda e: (e + first, 0, 0)),
            pl.BlockSpec((None, FF, width), lambda e: (e + first, 0, 0)),
        ]
        + [pl.BlockSpec(memory_space=pl.ANY)] * len(given),
        out_specs=[back_spec, back_spec, column_spec] + [kept_spec(c) for c in kept_widths],
        out_shape=[
            jax.ShapeDtypeStruct((sources, slots, width), jnp.bfloat16),
            jax.ShapeDtypeStruct((sources, slots, width), jnp.bfloat16),
            jax.ShapeDtypeStruct((local_experts, held, 1), jnp.float32),
        ]
        + [kept_shape(c) for c in kept_widths],
        input_output_aliases={first_held + at: i for at, (i, _) in enumerate(given)},
        compiler_params=pltpu.CompilerParams(vmem_limit_bytes=60 * 1024 * 1024),
        cost_estimate=SMALL_COST,
        name="expert_pass",
    )(*rows_list, *grads_list, gate_slots, w_in, w_out, *[part for _, part in given])


def block_call(kernel, operands, out_shape, name, scratch=()):
    def spec(array, lead=(), rows=None):
        rest = array.shape[len(lead) :]
        at = lead + (0,) * len(rest)
        if rows is not None:
            count, block = rows if isinstance(rows, tuple) else (rows, 0)
            rest = (count,) + rest[1:]
            at = lead + (block,) + (0,) * (len(rest) - 1)
        return pl.BlockSpec((None,) * len(lead) + rest, lambda i: at)

    return pl.pallas_call(
        kernel,
        grid=(1,),
        in_specs=[spec(*operand) for operand in operands],
        out_shape=out_shape,
        scratch_shapes=list(scratch),
        compiler_params=pltpu.CompilerParams(vmem_limit_bytes=60 * 1024 * 1024),
        cost_estimate=SMALL_COST,
        name=name,
    )(*[operand[0] for operand in operands])


def pick_kernel(shares, place_ref, *refs):
    at = 0
    outs = refs[sum(count for _, count in shares) :]
    for (k, count), out_ref in zip(shares, outs):
        total, row = None, 0
        for block_ref in refs[at : at + count]:
            held = block_ref.shape[0]
            part = dot32(place_ref[k, :, row : row + held], block_ref[...])
            total = part if total is None else total + part
            row += held
        out_ref[...] = total.astype(jnp.bfloat16)
        at += count


def pick_rows(place, ring, distances, first=0):
    _, slots, rows = place.shape
    half = rows // 2
    parts = []
    for k in distances:
        spans = [(first, rows)]
        if k == ring.peers // 2 and first < ring.half < first + rows:
            spans = [(first, half), (first + half, half)]
        found = [ring.rows(k, at, count) + (count,) for at, count in spans]
        parts.append([(array, (), (count, at // count)) for array, at, count in found])
    width = parts[0][0][0].shape[-1]
    return block_call(
        functools.partial(pick_kernel, [(k, len(p)) for k, p in zip(distances, parts)]),
        [(place,)] + [operand for p in parts for operand in p],
        [jax.ShapeDtypeStruct((slots, width), jnp.bfloat16) for _ in distances],
        "pick_rows",
    )


def spread_kernel(first_ref, place_ref, rows_ref, grads_ref, gate_ref, out_ref):
    place = place_ref[...]
    rows = place.shape[1]
    out_ref[:rows, :] = dot_tn(place, grads_ref[...]).astype(jnp.bfloat16)
    out_ref[rows + EXTRA :, :] = dot_tn(place, rows_ref[...]).astype(jnp.bfloat16)
    capacity = gate_ref.shape[1]
    expert = lax.broadcasted_iota(jnp.int32, (EXPERTS, rows), 0) - first_ref[0]
    gates = jnp.zeros((EXPERTS, rows), jnp.float32)
    for e in range(gate_ref.shape[0]):
        hit = place[e * capacity : (e + 1) * capacity].astype(jnp.float32)
        line = jnp.sum(hit * gate_ref[e], axis=0, keepdims=True)
        gates = jnp.where(expert == e, line, gates)
    pack_pieces(gates, out_ref, rows)


def spread_rows(first_expert, place, rows_back, grads_back, gate_slots):
    sources, slots, rows = place.shape
    width = rows_back.shape[-1]
    local_experts = gate_slots.shape[0]
    by_source = pl.BlockSpec((None, slots, width), lambda k, f: (k, 0, 0))
    return pl.pallas_call(
        spread_kernel,
        grid_spec=pltpu.PrefetchScalarGridSpec(
            num_scalar_prefetch=1,
            grid=(sources,),
            in_specs=[
                pl.BlockSpec((None, slots, rows), lambda k, f: (k, 0, 0)),
                by_source,
                by_source,
                pl.BlockSpec((local_experts, slots // local_experts, 1), lambda k, f: (0, k, 0)),
            ],
            out_specs=pl.BlockSpec((None, 2 * rows + EXTRA, width), lambda k, f: (k, 0, 0)),
        ),
        out_shape=jax.ShapeDtypeStruct((sources, 2 * rows + EXTRA, width), jnp.bfloat16),
        compiler_params=pltpu.CompilerParams(vmem_limit_bytes=60 * 1024 * 1024),
        cost_estimate=SMALL_COST,
        name="spread_rows",
    )(first_expert, place, rows_back, grads_back, gate_slots)


def weight_grad_kernel(lines, at_ref, left_ref, right_ref, *outs):
    outs = outs[-2 * lines :]
    core, line = at_ref[0], at_ref[1]
    span = outs[0].shape[0]
    grad = dot_tn(left_ref[...], right_ref[...]).astype(jnp.bfloat16)
    here = grad.shape[0] // (2 * span)
    for i in range(here):
        low = grad[2 * i * span : (2 * i + 1) * span]
        high = grad[(2 * i + 1) * span : (2 * i + 2) * span]
        mine = jnp.where(core == 0, low, high)
        other = jnp.where(core == 0, high, low)
        away = lax.rem(pl.program_id(1) * here + i - line + lines, lines)
        for j in range(lines):

            @pl.when(away == j)
            def _():
                outs[j][...] = mine
                outs[lines + j][...] = other


def weight_grads(place_at, left, right, parts, first, count, held_outs):
    experts, held, height = left.shape
    columns = right.shape[-1]
    lines = parts // 2
    span = height // parts
    tile = min(height, 768)
    out_spec = pl.BlockSpec((None, span, columns), lambda e, i, a: (e + first, 0, 0))
    out_shape = jax.ShapeDtypeStruct((experts, span, columns), jnp.bfloat16)
    held_outs = held_outs or []
    return pl.pallas_call(
        functools.partial(weight_grad_kernel, lines),
        grid_spec=pltpu.PrefetchScalarGridSpec(
            num_scalar_prefetch=1,
            grid=(count, height // tile),
            in_specs=[
                pl.BlockSpec((None, held, tile), lambda e, i, a: (e + first, 0, i)),
                pl.BlockSpec((None, held, columns), lambda e, i, a: (e + first, 0, 0)),
            ]
            + [pl.BlockSpec(memory_space=pl.ANY)] * len(held_outs),
            out_specs=[out_spec] * (2 * lines),
        ),
        out_shape=[out_shape] * (2 * lines),
        input_output_aliases={3 + i: i for i in range(len(held_outs))},
        compiler_params=pltpu.CompilerParams(vmem_limit_bytes=60 * 1024 * 1024),
        cost_estimate=SMALL_COST,
        name="weight_grads",
    )(place_at, left, right, *held_outs)


class WeightSum:
    def __init__(self, arrays, dp_count, *earlier):
        self.dp_count = dp_count
        self.lines = len(arrays) // 2
        self.mine, other = arrays[: self.lines], arrays[self.lines :]
        swap = [(d, d ^ 1) for d in range(dp_count)]
        order = list(range(1, self.lines)) + [0]
        swapped = {j: lax.ppermute(other[j], "dp", swap) for j in order}
        self.swapped = [swapped[j] for j in range(self.lines)]
        self.send = [add_rows(self.mine[j], self.swapped[j]) for j in range(1, self.lines)]

    def along(self):
        self.got = []
        for k, part in enumerate(self.send, 1):
            pairs = [(d, (d + 2 * k) % self.dp_count) for d in range(self.dp_count)]
            self.got.append(lax.ppermute(part, "dp", pairs))
        return self

    def total(self):
        total = self.mine[0].astype(jnp.float32) + self.swapped[0].astype(jnp.float32)
        for part in self.got:
            total = total + part.astype(jnp.float32)
        return total


def attention_forward(tokens, seg_col, seg_row, routes, gains, weight, cos, sin):
    count, rows, width = tokens.shape

    def by_micro(*shape):
        return pl.BlockSpec((None,) + shape, lambda m: (m,) + (0,) * len(shape))

    def shared(part):
        return pl.BlockSpec(part.shape, lambda m: (0, 0))

    kv_width = 2 * KEY_VALUE_HEADS * HEAD_SIZE
    shapes = [
        ((rows, width), jnp.bfloat16),
        ((rows, QUERY_HEADS * HEAD_SIZE), jnp.bfloat16),
        ((rows, kv_width), jnp.bfloat16),
        ((rows, QUERY_HEADS * HEAD_SIZE), jnp.bfloat16),
        ((rows, 128), jnp.float32),
        ((EXTRA, PIECES * EXPERTS // EXTRA * rows), jnp.bfloat16),
    ]
    return pl.pallas_call(
        attention_kernel,
        grid=(count,),
        in_specs=[
            by_micro(rows, width),
            by_micro(rows, 1),
            by_micro(1, rows),
            by_micro(rows, TOPK),
            shared(gains),
            shared(weight),
            shared(cos),
            shared(sin),
        ],
        out_specs=[by_micro(*shape) for shape, _ in shapes],
        out_shape=[jax.ShapeDtypeStruct((count,) + shape, kind) for shape, kind in shapes],
        compiler_params=pltpu.CompilerParams(vmem_limit_bytes=60 * 1024 * 1024),
        cost_estimate=SMALL_COST,
        name="attention_forward",
    )(tokens, seg_col, seg_row, routes, gains, weight, cos, sin)


def attention_grad_kernel(core_ref, xn1, mixed, *refs):
    count = xn1.shape[0]
    proj, attn, sums = [refs[i * count : (i + 1) * count] for i in range(3)]
    mine_ref, other_ref = refs[-2:]
    split = proj[0].shape[1]
    span = mine_ref.shape[0]
    grad = sum(dot_tn(xn1[m], proj[m][...]) for m in range(count))
    router = grad[:, split - 128 :]
    lane = lax.broadcasted_iota(jnp.int32, router.shape, 1)
    router = router + pltpu.roll(router, 128 - EXPERTS, 1)
    gain = sum(part[...] for part in sums)
    lines = [jnp.zeros((EXPERTS, gain.shape[1]), jnp.float32), gain]
    lines.append(jnp.zeros((128 - EXPERTS - gain.shape[0], gain.shape[1]), jnp.float32))
    router = jnp.where(lane < EXPERTS, router, jnp.concatenate(lines, axis=0).T)
    first = core_ref[0] == 0

    def put(columns, value):
        value = value.astype(jnp.bfloat16)
        low, high = value[:span], value[span:]
        mine_ref[:, columns] = jnp.where(first, low, high)
        other_ref[:, columns] = jnp.where(first, high, low)

    put(slice(0, split - 128), grad[:, : split - 128])
    put(slice(split - 128, split), router)
    put(slice(split, None), sum(dot_tn(mixed[m], attn[m][...]) for m in range(count)))


def attention_grads(core, xn1, mixed, proj, attn, gain_sums, parts):
    count, rows, width = xn1.shape
    span = width // parts
    lines = parts // 2
    columns = proj[0].shape[1] + attn[0].shape[1]
    by_line = pl.BlockSpec((count, rows, 2 * span), lambda i, c: (0, 0, i))

    def shared(part):
        return pl.BlockSpec(part.shape, lambda i, c: (0, 0))

    out_spec = pl.BlockSpec((None, span, columns), lambda i, c: (i, 0, 0))
    out_shape = jax.ShapeDtypeStruct((lines, span, columns), jnp.bfloat16)
    return pl.pallas_call(
        attention_grad_kernel,
        grid_spec=pltpu.PrefetchScalarGridSpec(
            num_scalar_prefetch=1,
            grid=(lines,),
            in_specs=[by_line, by_line]
            + [shared(p) for p in proj]
            + [shared(p) for p in attn]
            + [pl.BlockSpec((p.shape[0], 2 * span), lambda i, c: (0, i)) for p in gain_sums],
            out_specs=[out_spec, out_spec],
        ),
        out_shape=[out_shape, out_shape],
        compiler_params=pltpu.CompilerParams(vmem_limit_bytes=60 * 1024 * 1024),
        cost_estimate=SMALL_COST,
        name="attention_grads",
    )(core, xn1, mixed, *proj, *attn, *gain_sums)


def per_device(
    tokens,
    segments,
    routes,
    norm_one,
    norm_two,
    w_query,
    key_value_weight,
    w_out_attn,
    w_router,
    w_in,
    w_out,
    cotangent,
):
    micro_count, rows, width = tokens.shape
    micros = range(micro_count)
    peers = lax.axis_size("expert")
    dp_count = lax.axis_size("dp")
    local_experts = w_in.shape[0]
    experts = local_experts * peers
    capacity = rows // 4
    first_expert = lax.axis_index("expert") * local_experts
    q_width = w_query.shape[1]
    kv_width = key_value_weight.shape[1]
    proj_width = q_width + kv_width
    cosine_table, sine_values = rope_tables(rows, HEAD_SIZE)
    cos = jnp.concatenate([cosine_table, cosine_table], axis=1)
    sin = jnp.concatenate([-sine_values, sine_values], axis=1)
    order = ring_order(peers)
    spot = [order.index(dev) for dev in range(peers)]
    my_spot = jnp.array(spot, jnp.int32)[lax.axis_index("expert")]

    def gather_dp(part, axis=0):
        return lax.all_gather(part, "dp", axis=axis, tiled=True)

    router_pad = jnp.zeros((w_router.shape[0], 128 - 2 * experts), jnp.bfloat16)
    first_weight = jnp.concatenate(
        [w_query, key_value_weight, w_router, w_router, router_pad], axis=1
    )
    gains = gather_dp(jnp.stack([norm_one, norm_two]), axis=1).astype(jnp.float32)
    first_weight = gather_dp(first_weight)
    out_weight = gather_dp(w_out_attn)

    routes_rows = jnp.swapaxes(routes, 1, 2).reshape(-1, rows).astype(jnp.bfloat16)
    routes_rows = jnp.pad(
        routes_rows, ((0, EXTRA - routes_rows.shape[0]), (0, width - rows))
    )
    cot_block = jnp.concatenate([cotangent.reshape(-1, width), routes_rows], axis=0)
    cot_ring = RingGather(cot_block, peers, rows)
    steps = peers // 2
    for _ in range(steps - 2):
        cot_ring.step()

    seg_col, seg_row = segments[:, :, None], segments[:, None, :]
    xn1, query, keyval, mixed, gates, gates_pack = attention_forward(
        tokens, seg_col, seg_row, routes, gains, first_weight, cos, sin
    )
    hidden, xn2 = [], []
    for m in micros:
        out = block_call(
            hidden_kernel,
            [(mixed, (m,)), (tokens, (m,)), (gains,), (out_weight,), (gates_pack, (m,))],
            [
                jax.ShapeDtypeStruct((rows, width), jnp.float32),
                jax.ShapeDtypeStruct((rows + EXTRA, width), jnp.bfloat16),
            ],
            "hidden_rows",
        )
        hidden.append(out[0])
        xn2.append(out[1])
    every = list(range(peers))
    late = [steps - 1, steps, steps + 1]
    early = [k for k in every if k not in late]
    row_rings = [RingGather(xn2[m], peers, rows // 2) for m in micros]
    cot_ring.step(mixed)
    got = cot_ring.got
    cot_ring.step()
    row_rings[0].step(*got)
    row_rings[0].step(*cot_ring.got)
    for _ in range(steps - 3):
        row_rings[0].step()
    got = row_rings[0].got
    row_rings[0].step()
    row_rings[1].step(*got)
    groups = peers // GROUP

    routes_all = cot_ring.stack_rows(micro_count * rows, micro_count * TOPK)[:, :, :rows]
    routes_all = routes_all.reshape(peers, micro_count, TOPK, rows)
    hits = [slot_hits(routes_all[:, m], first_expert, local_experts, capacity) for m in micros]
    places = [hit.astype(jnp.bfloat16).reshape(peers, -1, rows) for hit in hits]
    first_at = first_expert.astype(jnp.int32).reshape(1)

    def gates_of(ring):
        packs = ring.stack_rows(rows, EXTRA)
        packs = lax.dynamic_slice_in_dim(
            packs, lax.rem(first_expert, EXTRA), local_experts, axis=1
        )
        packs = packs.reshape(peers, local_experts, PIECES, EXPERTS // EXTRA, rows)
        packs = lax.dynamic_index_in_dim(packs, first_expert // EXTRA, 3, keepdims=False)
        return jnp.sum(packs.astype(jnp.float32), axis=2)

    class Experts:
        kept = [None] * 4

        def __init__(self, m, calls):
            self.m = m
            self.calls = calls
            self.per_call = local_experts // calls
            self.outs = [[None] * 3 for _ in range(groups)]

        def pick(self, *earlier):
            m = self.m
            place = after(places[m], *earlier) if earlier else places[m]
            ring = row_rings[m]
            self.grads = pick_rows(place, cot_ring, every, m * rows)
            rows_of = dict(zip(early, pick_rows(place, ring, early)))
            rows_of.update(zip(late, pick_rows(place, ring, late)))
            self.rows = [rows_of[k] for k in every]
            slots = jnp.sum(jnp.where(hits[m], gates_of(ring)[:, :, None, :], 0.0), axis=-1)
            self.gate_slots = jnp.swapaxes(slots, 0, 1)

        def call(self, number, *earlier):
            for g in range(groups):
                span = slice(g * GROUP, (g + 1) * GROUP)
                here = self.rows[span]
                here[0] = after(here[0], *earlier) if earlier else here[0]
                done = expert_pass(
                    here,
                    self.grads[span],
                    self.gate_slots[:, span].reshape(local_experts, -1, 1),
                    w_in,
                    w_out,
                    self.outs[g] + Experts.kept,
                    (self.m * groups + g, micro_count * groups),
                    number * self.per_call,
                    self.per_call,
                )
                self.outs[g], Experts.kept = list(done[:3]), list(done[3:])
            return done[2]

        def spread(self, *earlier):
            place = places[self.m]
            place = after(place, *earlier) if earlier else place
            self.sums = [
                spread_rows(first_at, place[g * GROUP : (g + 1) * GROUP], *self.outs[g])
                for g in range(groups)
            ]

        def sum_of(self, k):
            return self.sums[k // GROUP][k % GROUP]

    calls = 2
    first, second = Experts(0, calls), Experts(1, calls)
    first.pick()
    ring = row_rings[1]
    for number in range(calls):
        first.call(number, *ring.got)
        ring.step()
    while len(ring.from_left) < steps:
        ring.step()
    first.spread(*ring.got)
    ring.step()
    ring_first = RingScatter(first.sum_of, peers, rows + EXTRA).step()
    second.pick(first.sums[0])
    token = second.call(0)
    for number in range(1, calls):
        ring_first.step(token)
        token = second.call(number)
    second.spread()
    grad_second = RingScatter(lambda k: second.sum_of(k)[: rows + EXTRA], peers, rows // 2).step()
    out_second = RingScatter(lambda k: second.sum_of(k)[rows + EXTRA :], peers, rows // 2)
    picked, grad_result, activated, grad_pre = Experts.kept
    dp_at = lax.axis_index("dp").astype(jnp.int32)
    place_at = jnp.stack([lax.rem(dp_at, 2), dp_at // 2])
    picked = after(picked, *ring_first.got)
    ring_first.step(second.sums[0])
    w_in_parts = None
    for e in range(local_experts):
        if e == local_experts // 2:
            picked = after(picked, *grad_second.got, w_in_parts[0])
        if e == local_experts - 1:
            picked = after(picked, *ring_first.got, w_in_parts[0])
        w_in_parts = weight_grads(place_at, picked, grad_pre, dp_count, e, 1, w_in_parts)
    w_in_sum = WeightSum(w_in_parts, dp_count)
    activated = after(activated, *ring_first.got, w_in_parts[0])
    while ring_first.at > 0:
        ring_first.step()
    grad_second.step(w_in_sum.mine[0])
    w_out_sum = WeightSum(
        weight_grads(place_at, activated, grad_result, dp_count, 0, local_experts, None), dp_count
    )
    w_in_sum.along()
    got = grad_second.got
    grad_second.step(w_out_sum.mine[0])

    def backward(m, pieces, *earlier):
        own, left, right = pieces
        return block_call(
            backward_kernel,
            [
                (after(own, *earlier), (0,), rows + EXTRA),
                (left, (), rows + EXTRA),
                (right, (), rows + EXTRA),
                (cotangent, (m,)),
                (hidden[m],),
                (tokens, (m,)),
                (query, (m,)),
                (keyval, (m,)),
                (seg_col, (m,)),
                (seg_row, (m,)),
                (gates, (m,)),
                (gains,),
                (first_weight,),
                (out_weight,),
                (cos,),
                (sin,),
            ],
            [
                jax.ShapeDtypeStruct((rows, width), jnp.bfloat16),
                jax.ShapeDtypeStruct((rows, proj_width + 128), jnp.bfloat16),
                jax.ShapeDtypeStruct((rows, width), jnp.bfloat16),
                jax.ShapeDtypeStruct((8, width), jnp.float32),
            ],
            "attention_backward",
            [pltpu.VMEM((rows, q_width), jnp.bfloat16)],
        )

    back_first = backward(
        0, (first.sums[0], ring_first.left, ring_first.right), *got, *w_in_sum.send
    )
    w_out_sum.along()
    while grad_second.at > 0:
        grad_second.step(back_first[3])
    out_second.step(*grad_second.got)
    back_second = backward(
        1, (second.sums[0], grad_second.left, grad_second.right), *w_out_sum.send
    )
    out_second.step()
    grad_tokens, grad_proj, grad_attn, gain_sums = zip(back_first, back_second)
    mine, other = attention_grads(
        place_at, after(xn1, *out_second.got, *w_in_sum.got), mixed, grad_proj, grad_attn, gain_sums, dp_count
    )
    while out_second.at > 0:
        out_second.step()
    share, grad_w_in, grad_w_out = reduce_packed(
        mine, other, my_spot, peers, dp_count, out_second, w_in_sum, w_out_sum
    )

    outputs = []
    wide = jnp.float32
    own, left, right = [part[rows + EXTRA :].astype(wide) for part in ring_first.pieces()]
    outputs.append((hidden[0] + own + left + right).astype(jnp.bfloat16))
    own, left, right = [part.astype(wide) for part in out_second.pieces()]
    outputs.append((hidden[1] + own + left + right).astype(jnp.bfloat16))
    edge = proj_width
    return (
        jnp.stack(outputs),
        jnp.stack(grad_tokens),
        share[:, edge + experts],
        share[:, edge + experts + 1],
        share[:, :q_width],
        share[:, q_width:proj_width],
        share[:, edge + 128 :],
        share[:, edge : edge + experts],
        grad_w_in,
        grad_w_out,
    )


def reduce_packed(mine, other, my_spot, peers, dp_count, out_ring, w_in_sum, w_out_sum):
    lines, span, columns = mine.shape
    swap = [(d, d ^ 1) for d in range(dp_count)]
    total = mine + lax.ppermute(other, "dp", swap)
    piece = span // peers
    total = after(total, *out_ring.got, *w_out_sum.got)
    total = total.reshape(lines, peers, piece, columns)

    def part(k):
        at = lax.rem(my_spot - k + peers, peers)
        return lax.dynamic_slice_in_dim(total, at, 1, axis=1).reshape(lines * piece, columns)

    ring = RingScatter(part, peers, lines * piece // 2)
    while ring.at > 0:
        ring.step()
    own, left, right = [part.astype(jnp.float32) for part in ring.pieces()]
    mine = (own + left + right).astype(jnp.bfloat16).reshape(lines, piece, columns)
    line = lax.axis_index("dp") // 2

    def for_line(at):
        return lax.dynamic_index_in_dim(mine, lax.rem(at, lines), 0, keepdims=False)

    share = for_line(line).astype(jnp.float32)
    for k in range(1, lines):
        pairs = [(d, (d + 2 * k) % dp_count) for d in range(dp_count)]
        share = share + lax.ppermute(for_line(line + k), "dp", pairs)
    gather = RingGather(share.astype(jnp.bfloat16), peers, piece // 2)
    gather.step()
    grad_w_in = w_in_sum.total()
    gather.step(grad_w_in)
    grad_w_out = w_out_sum.total()
    gather.step(grad_w_out)
    while gather.far is None:
        gather.step()
    far = jnp.concatenate(gather.far, axis=0)
    by_distance = jnp.stack(gather.from_left + [far] + gather.from_right[:0:-1])
    distance = lax.rem(my_spot - jnp.arange(peers, dtype=jnp.int32) + peers, peers)
    by_spot = jnp.take(by_distance, distance, axis=0)
    return by_spot.reshape(span, columns).astype(jnp.float32), grad_w_in, grad_w_out


def solution(mesh):
    return jax.shard_map(
        per_device,
        mesh=mesh,
        in_specs=(
            P(None, ("dp", "expert"), None),
            P(None, ("dp", "expert")),
            P(None, ("dp", "expert"), None),
            P("dp"),
            P("dp"),
            P("dp", None),
            P("dp", None),
            P("dp", None),
            P("dp", None),
            P("expert", None, None),
            P("expert", None, None),
            P(None, ("dp", "expert"), None),
        ),
        out_specs=(
            P(None, ("dp", "expert"), None),
            P(None, ("dp", "expert"), None),
            P("dp"),
            P("dp"),
            P("dp", None),
            P("dp", None),
            P("dp", None),
            P("dp", None),
            P("expert", "dp", None),
            P("expert", "dp", None),
        ),
        check_vma=False,
    )
```

```python
import functools
import math

import jax
import jax.numpy as jnp
from jax import lax
from jax.experimental import pallas as pl
from jax.experimental.pallas import tpu as pltpu
from jax.sharding import PartitionSpec as P

QUERY_HEADS = 12
KEY_VALUE_HEADS = 2
HEAD_SIZE = 128
FF = 768
TOPK = 4
EXPERTS = 32
EXTRA = 16
PIECES = 3
GROUP = 8

eps_norm = 1e-06
rope_base = 1000000.0
mask_fill = -1e30
highest = lax.Precision.HIGHEST


def rms_scale(tensor):
    return lax.rsqrt(jnp.mean(tensor * tensor, axis=-1, keepdims=True) + eps_norm)


def rope_tables(sequence_length, head_width):
    positions = jnp.arange(sequence_length).astype(jnp.float32)
    frequency = rope_base ** (-(jnp.arange(head_width // 2).astype(jnp.float32) * 2.0) / head_width)
    angles = positions[:, None] * frequency[None, :]
    return (jnp.cos(angles), jnp.sin(angles))

SCORE_SCALE = 1.0 / math.sqrt(HEAD_SIZE)
GELU_SCALE = math.sqrt(2.0 / math.pi)
GELU_CUBE = 0.044715
SMALL_COST = pl.CostEstimate(flops=1_000_000, bytes_accessed=1_000_000, transcendentals=0)


def after(value, *earlier):
    return lax.optimization_barrier((value,) + earlier)[0]


def slot_hits(routes_all, first_expert, local_experts, capacity):
    rows = routes_all.shape[-1]
    names = first_expert + jnp.arange(local_experts, dtype=jnp.int32)
    named = routes_all[:, None].astype(jnp.int32) == names[None, :, None, None]
    member = jnp.any(named, axis=2)
    lower = (jnp.arange(rows)[:, None] < jnp.arange(rows)[None, :]).astype(jnp.bfloat16)
    rank = dot32(member.astype(jnp.bfloat16).reshape(-1, rows), lower).reshape(member.shape)
    slots = jnp.arange(capacity, dtype=jnp.float32)
    return member[:, :, None, :] & (rank[:, :, None, :] == slots[None, None, :, None])


def pack_pieces(values, out_ref, first_row):
    rows = values.shape[1]
    rest = values
    for piece in range(PIECES):
        part = rest.astype(jnp.bfloat16)
        rest = rest - part.astype(jnp.float32)
        for half in range(EXPERTS // EXTRA):
            at = (piece * (EXPERTS // EXTRA) + half) * rows
            out_ref[first_row : first_row + EXTRA, at : at + rows] = part[
                half * EXTRA : (half + 1) * EXTRA
            ]


def dot32(left, right):
    return jnp.dot(left, right, preferred_element_type=jnp.float32)


def dot_nt(left, right):
    return lax.dot_general(
        left, right, (((1,), (1,)), ((), ())), preferred_element_type=jnp.float32
    )


def dot_tn(left, right):
    return lax.dot_general(
        left, right, (((0,), (0,)), ((), ())), preferred_element_type=jnp.float32
    )


def mask_of(seg_col, seg_row):
    rows = seg_col.shape[0]
    query_at = lax.broadcasted_iota(jnp.int32, (rows, rows), 0)
    key_at = lax.broadcasted_iota(jnp.int32, (rows, rows), 1)
    return (seg_col == seg_row) & (query_at >= key_at)


def softmax_rows(query, key, allowed):
    scores = jnp.where(allowed, dot_nt(query, key) * SCORE_SCALE, mask_fill)
    weight = jnp.exp(scores - jnp.max(scores, axis=-1, keepdims=True))
    return weight / jnp.sum(weight, axis=-1, keepdims=True)


def attention_kernel(
    tok_ref,
    seg_col_ref,
    seg_row_ref,
    routes_ref,
    gains_ref,
    weight_ref,
    cos_ref,
    sin_ref,
    xn1_ref,
    query_ref,
    keyval_ref,
    mixed_ref,
    gates_ref,
    gates_pack_ref,
):
    tok = tok_ref[...].astype(jnp.float32)
    xn1_ref[...] = (tok * rms_scale(tok) * gains_ref[0:1, :]).astype(jnp.bfloat16)
    proj = dot32(xn1_ref[...], weight_ref[...])
    cos, sin = cos_ref[...], sin_ref[...]

    def rotate(part):
        return (part * cos + pltpu.roll(part, HEAD_SIZE // 2, 1) * sin).astype(jnp.bfloat16)

    q_width = QUERY_HEADS * HEAD_SIZE
    k_width = KEY_VALUE_HEADS * HEAD_SIZE
    for head in range(QUERY_HEADS):
        span = slice(head * HEAD_SIZE, (head + 1) * HEAD_SIZE)
        query_ref[:, span] = rotate(proj[:, span])
    for head in range(KEY_VALUE_HEADS):
        span = slice(head * HEAD_SIZE, (head + 1) * HEAD_SIZE)
        keyval_ref[:, span] = rotate(proj[:, q_width:][:, span])
    keyval_ref[:, k_width:] = proj[:, q_width + k_width : q_width + 2 * k_width].astype(
        jnp.bfloat16
    )
    logits = proj[:, q_width + 2 * k_width :]
    columns = lax.broadcasted_iota(jnp.int32, logits.shape, 1)
    named = [columns == routes_ref[:, j : j + 1] for j in range(TOPK)]
    chosen = [jnp.sum(jnp.where(hit, logits, 0.0), axis=-1, keepdims=True) for hit in named]
    top = functools.reduce(jnp.maximum, chosen)
    weight = [jnp.exp(part - top) for part in chosen]
    total = functools.reduce(jnp.add, weight)
    gates = jnp.full(logits.shape, -1.0, jnp.float32)
    for hit, part in zip(named, weight):
        gates = jnp.where(hit, part / total, gates)
    gates_ref[...] = gates
    pack_pieces(gates.T[:EXPERTS], gates_pack_ref, 0)
    allowed = mask_of(seg_col_ref[...], seg_row_ref[...])
    for head in range(QUERY_HEADS):
        span = slice(head * HEAD_SIZE, (head + 1) * HEAD_SIZE)
        group = head // (QUERY_HEADS // KEY_VALUE_HEADS)
        key = keyval_ref[:, group * HEAD_SIZE : (group + 1) * HEAD_SIZE]
        value = keyval_ref[:, k_width + group * HEAD_SIZE : k_width + (group + 1) * HEAD_SIZE]
        probs = softmax_rows(query_ref[:, span], key, allowed)
        mixed_ref[:, span] = dot32(probs.astype(jnp.bfloat16), value).astype(jnp.bfloat16)


def hidden_kernel(mixed_ref, tok_ref, gains_ref, weight_ref, pack_ref, hidden_ref, xn2_ref):
    rows = tok_ref.shape[0]
    hidden = tok_ref[...].astype(jnp.float32) + dot32(mixed_ref[...], weight_ref[...])
    hidden_ref[...] = hidden
    xn2_ref[:rows, :] = (hidden * rms_scale(hidden) * gains_ref[1:2, :]).astype(jnp.bfloat16)
    xn2_ref[rows:, :] = pack_ref[...]


def backward_kernel(
    own_ref,
    left_ref,
    right_ref,
    cot_ref,
    hidden_ref,
    tok_ref,
    query_ref,
    keyval_ref,
    seg_col_ref,
    seg_row_ref,
    gates_ref,
    gains_ref,
    weight_ref,
    out_weight_ref,
    cos_ref,
    sin_ref,
    grad_tok_ref,
    grad_proj_ref,
    grad_attn_ref,
    gain_sum_ref,
    mixed_grad_ref,
):
    width = tok_ref.shape[1]
    q_width = QUERY_HEADS * HEAD_SIZE
    k_width = KEY_VALUE_HEADS * HEAD_SIZE
    proj_width = q_width + 2 * k_width
    rows = tok_ref.shape[0]
    sums = [ref[...].astype(jnp.float32) for ref in (own_ref, left_ref, right_ref)]
    sums = sums[0] + sums[1] + sums[2]
    grad_xn2, pack = sums[:rows], sums[rows:]
    halves = EXPERTS // EXTRA
    lines = [
        sum(
            pack[:, (piece * halves + half) * rows : (piece * halves + half + 1) * rows]
            for piece in range(PIECES)
        )
        for half in range(halves)
    ]
    lines.append(jnp.zeros((128 - EXPERTS, rows), jnp.float32))
    grad_gates = jnp.concatenate(lines, axis=0).T
    hidden = hidden_ref[...]
    scale = rms_scale(hidden)
    unit = hidden * scale
    gain_sum_ref[...] = jnp.zeros(gain_sum_ref.shape, jnp.float32)
    gain_sum_ref[1:2, :] = jnp.sum(grad_xn2 * unit, axis=0, keepdims=True)
    grad_unit = grad_xn2 * gains_ref[1:2, :]
    grad_hidden = cot_ref[...].astype(jnp.float32) + scale * (
        grad_unit - unit * jnp.mean(grad_unit * unit, axis=-1, keepdims=True)
    )
    grad_attn_ref[...] = grad_hidden.astype(jnp.bfloat16)
    mixed_grad_ref[...] = dot_nt(grad_attn_ref[...], out_weight_ref[...]).astype(jnp.bfloat16)
    cos, sin = cos_ref[...], sin_ref[...]

    def unrotate(part):
        return (part * cos - pltpu.roll(part, HEAD_SIZE // 2, 1) * sin).astype(jnp.bfloat16)

    allowed = mask_of(seg_col_ref[...], seg_row_ref[...])
    per_group = QUERY_HEADS // KEY_VALUE_HEADS
    for group in range(KEY_VALUE_HEADS):
        key_span = slice(group * HEAD_SIZE, (group + 1) * HEAD_SIZE)
        value_span = slice(k_width + group * HEAD_SIZE, k_width + (group + 1) * HEAD_SIZE)
        key, value = keyval_ref[:, key_span], keyval_ref[:, value_span]
        grad_key = jnp.zeros(key.shape, jnp.float32)
        grad_value = jnp.zeros(key.shape, jnp.float32)
        for head in range(group * per_group, (group + 1) * per_group):
            span = slice(head * HEAD_SIZE, (head + 1) * HEAD_SIZE)
            query, grad_mixed = query_ref[:, span], mixed_grad_ref[:, span]
            probs = softmax_rows(query, key, allowed)
            grad_value += dot_tn(probs.astype(jnp.bfloat16), grad_mixed)
            grad_probs = dot_nt(grad_mixed, value)
            mean = jnp.sum(probs * grad_probs, axis=-1, keepdims=True)
            grad_scores = (probs * (grad_probs - mean)).astype(jnp.bfloat16)
            grad_proj_ref[:, span] = unrotate(dot32(grad_scores, key) * SCORE_SCALE)
            grad_key += dot_tn(grad_scores, query)
        grad_proj_ref[:, q_width + group * HEAD_SIZE : q_width + (group + 1) * HEAD_SIZE] = (
            unrotate(grad_key * SCORE_SCALE)
        )
        first = q_width + k_width + group * HEAD_SIZE
        grad_proj_ref[:, first : first + HEAD_SIZE] = grad_value.astype(jnp.bfloat16)
    gates = jnp.maximum(gates_ref[...], 0.0)
    grad_logits = gates * (grad_gates - jnp.sum(gates * grad_gates, axis=-1, keepdims=True))
    high = grad_logits.astype(jnp.bfloat16).astype(jnp.float32)
    low = pltpu.roll(grad_logits - high, EXPERTS, 1)
    grad_proj_ref[:, proj_width:] = (high + low).astype(jnp.bfloat16)
    grad_xn1 = dot_nt(grad_proj_ref[...], weight_ref[...])
    tok = tok_ref[...].astype(jnp.float32)
    scale = rms_scale(tok)
    unit = tok * scale
    gain_sum_ref[0:1, :] = jnp.sum(grad_xn1 * unit, axis=0, keepdims=True)
    grad_unit = grad_xn1 * gains_ref[0:1, :]
    grad_tok_ref[...] = (
        grad_hidden
        + scale * (grad_unit - unit * jnp.mean(grad_unit * unit, axis=-1, keepdims=True))
    ).astype(jnp.bfloat16)


def ring_order(peers):
    minor = peers // 4
    walk = []
    for col in range(minor):
        line = range(4) if col % 2 == 0 else range(3, -1, -1)
        walk += [row * minor + col for row in line]
    return walk


def ring_step(part, shift, peers):
    order = ring_order(peers)
    pairs = [(order[i], order[(i + shift) % peers]) for i in range(peers)]
    return lax.ppermute(part, "expert", pairs)


class RingGather:
    def __init__(self, part, peers, half):
        self.peers, self.half = peers, half
        self.from_left, self.from_right = [part], [part]
        self.far = None
        self.got = ()

    def step(self, *earlier):
        left, right = self.from_left[-1], self.from_right[-1]
        last = len(self.from_left) == self.peers // 2
        if last:
            left, right = left[: self.half], right[self.half :]
        if earlier:
            left, right = lax.optimization_barrier((left, right) + earlier)[:2]
        left, right = ring_step(left, 1, self.peers), ring_step(right, -1, self.peers)
        self.got = (left, right)
        if last:
            self.far = (left, right)
        else:
            self.from_left.append(left)
            self.from_right.append(right)
        return self

    def rows(self, k, first, count):
        if k < len(self.from_left):
            return self.from_left[k], first
        if k > self.peers // 2:
            return self.from_right[self.peers - k], first
        if first < self.half:
            return self.far[0], first
        return self.far[1], first - self.half

    def stack_rows(self, first, count):
        found = [self.rows(k, first, count) for k in range(self.peers)]
        return jnp.stack([array[at : at + count] for array, at in found])


class RingScatter:
    def __init__(self, parts, far, peers):
        self.parts, self.far, self.peers = parts, far, peers
        self.at = peers // 2
        self.half = far[0].shape[0]

    def step(self, *earlier):
        peers, k, half = self.peers, self.at, self.half
        if k == peers // 2:
            left, right = self.far
            if earlier:
                left, right = lax.optimization_barrier((left, right) + earlier)[:2]
        else:
            left, right = self.parts[k], self.parts[peers - k]
            if earlier:
                self.left, self.right = lax.optimization_barrier(
                    (self.left, self.right) + earlier
                )[:2]
            if k == peers // 2 - 1:
                left = jnp.concatenate([add_rows(left[:half], self.left), left[half:]], axis=0)
                right = jnp.concatenate([right[:half], add_rows(right[half:], self.right)], axis=0)
            else:
                left, right = add_rows(left, self.left), add_rows(right, self.right)
        self.left = ring_step(left, -1, peers)
        self.right = ring_step(right, 1, peers)
        self.got = (self.left, self.right)
        self.at = k - 1
        return self


def add_rows(left, right):
    return (left.astype(jnp.float32) + right.astype(jnp.float32)).astype(jnp.bfloat16)


def expert_kernel(sources, *refs):
    rows_refs = refs[:sources]
    grad_refs = refs[sources : 2 * sources]
    gate_refs = refs[2 * sources : 3 * sources]
    w_in_ref, w_out_ref = refs[3 * sources : 3 * sources + 2]
    (
        back_rows_ref,
        back_grads_ref,
        grad_gate_ref,
        picked_ref,
        grad_result_ref,
        activated_ref,
        grad_pre_ref,
    ) = refs[-7:]
    capacity, width = rows_refs[0].shape
    for k in range(sources):
        picked_ref[pl.ds(k * capacity, capacity), :] = rows_refs[k][...]
    pre_act = dot32(picked_ref[...], w_in_ref[...])
    gate_part = pre_act[:, :FF]
    up_part = pre_act[:, FF:]
    square = gate_part * gate_part
    bend = jnp.tanh(GELU_SCALE * gate_part * (1.0 + GELU_CUBE * square))
    lift = 0.5 * (1.0 + bend)
    gelu_val = gate_part * lift
    slope = lift + 0.5 * gate_part * (1.0 - bend * bend) * (
        GELU_SCALE * (1.0 + 3.0 * GELU_CUBE * square)
    )
    activated_ref[...] = (gelu_val * up_part).astype(jnp.bfloat16)
    result = dot32(activated_ref[...], w_out_ref[...])
    for k in range(sources):
        gates = gate_refs[k][...]
        span = slice(k * capacity, (k + 1) * capacity)
        grad_rows = grad_refs[k][...].astype(jnp.float32)
        grad_gate_ref[span, :] = jnp.sum(result[span] * grad_rows, axis=-1, keepdims=True)
        back_rows_ref[k] = (result[span] * gates).astype(jnp.bfloat16)
        grad_result_ref[span, :] = (grad_rows * gates).astype(jnp.bfloat16)
    grad_act = lax.dot_general(
        grad_result_ref[...],
        w_out_ref[...],
        (((1,), (1,)), ((), ())),
        preferred_element_type=jnp.float32,
    )
    grad_pre_ref[:, :FF] = (grad_act * up_part * slope).astype(jnp.bfloat16)
    grad_pre_ref[:, FF:] = (grad_act * gelu_val).astype(jnp.bfloat16)
    grad_in = lax.dot_general(
        grad_pre_ref[...],
        w_in_ref[...],
        (((1,), (1,)), ((), ())),
        preferred_element_type=jnp.float32,
    ).astype(jnp.bfloat16)
    for k in range(sources):
        back_grads_ref[k] = grad_in[k * capacity : (k + 1) * capacity]


def expert_pass(rows_list, grads_list, gate_slots, w_in, w_out, held_outs, position, first, count):
    sources = len(rows_list)
    local_experts, width, _ = w_in.shape
    slots = rows_list[0].shape[0]
    capacity = slots // local_experts
    held = sources * capacity
    block_spec = pl.BlockSpec((capacity, width), lambda e: (e + first, 0))
    back_spec = pl.BlockSpec((sources, capacity, width), lambda e: (0, e + first, 0))
    column_spec = pl.BlockSpec((None, held, 1), lambda e: (e + first, 0, 0))

    def kept_spec(columns):
        return pl.BlockSpec((None, held, columns), lambda e: (e + first, position[0], 0))

    def kept_shape(columns):
        return jax.ShapeDtypeStruct((local_experts, position[1] * held, columns), jnp.bfloat16)

    kept_widths = (width, width, FF, 2 * FF)
    first_held = 3 * sources + 2
    given = [(i, part) for i, part in enumerate(held_outs) if part is not None]
    return pl.pallas_call(
        functools.partial(expert_kernel, sources),
        grid=(count,),
        in_specs=[block_spec] * (2 * sources)
        + [pl.BlockSpec((capacity, 1), lambda e: (e + first, 0))] * sources
        + [
            pl.BlockSpec((None, width, 2 * FF), lambda e: (e + first, 0, 0)),
            pl.BlockSpec((None, FF, width), lambda e: (e + first, 0, 0)),
        ]
        + [pl.BlockSpec(memory_space=pl.ANY)] * len(given),
        out_specs=[back_spec, back_spec, column_spec] + [kept_spec(c) for c in kept_widths],
        out_shape=[
            jax.ShapeDtypeStruct((sources, slots, width), jnp.bfloat16),
            jax.ShapeDtypeStruct((sources, slots, width), jnp.bfloat16),
            jax.ShapeDtypeStruct((local_experts, held, 1), jnp.float32),
        ]
        + [kept_shape(c) for c in kept_widths],
        input_output_aliases={first_held + at: i for at, (i, _) in enumerate(given)},
        compiler_params=pltpu.CompilerParams(vmem_limit_bytes=60 * 1024 * 1024),
        cost_estimate=SMALL_COST,
        name="expert_pass",
    )(*rows_list, *grads_list, *gate_slots, w_in, w_out, *[part for _, part in given])


def block_call(kernel, operands, out_shape, name, scratch=(), prefetch=None):
    def spec(array, lead=(), rows=None):
        rest = array.shape[len(lead) :]
        at = lead + (0,) * len(rest)
        if rows is not None:
            count, block = rows if isinstance(rows, tuple) else (rows, 0)
            rest = (count,) + rest[1:]
            at = lead + (block,) + (0,) * (len(rest) - 1)
        return pl.BlockSpec((None,) * len(lead) + rest, lambda *_: at)

    scalars = [] if prefetch is None else [prefetch]
    return pl.pallas_call(
        kernel,
        grid_spec=pltpu.PrefetchScalarGridSpec(
            num_scalar_prefetch=len(scalars),
            grid=(1,),
            in_specs=[spec(*operand) for operand in operands],
            out_specs=[spec(shape) for shape in out_shape],
            scratch_shapes=list(scratch),
        ),
        out_shape=out_shape,
        compiler_params=pltpu.CompilerParams(vmem_limit_bytes=60 * 1024 * 1024),
        cost_estimate=SMALL_COST,
        name=name,
    )(*scalars, *[operand[0] for operand in operands])


def pick_kernel(shares, gated, first_ref, place_ref, *refs):
    at = 0
    outs = refs[sum(count for _, count in shares) + (len(shares) if gated else 0) :]
    for number, (k, count) in enumerate(shares):
        total, row = None, 0
        for block_ref in refs[at : at + count]:
            held = block_ref.shape[0]
            part = dot32(place_ref[k, :, row : row + held], block_ref[...])
            total = part if total is None else total + part
            row += held
        outs[number][...] = total.astype(jnp.bfloat16)
        at += count
        if gated:
            slot_gates(first_ref[0], place_ref[k], refs[at], outs[len(shares) + number])
            at += 1


def slot_gates(first_expert, place, pack_ref, out_ref):
    slots, rows = place.shape
    pack = pack_ref[...].astype(jnp.float32)
    halves = EXPERTS // EXTRA
    line = lax.broadcasted_iota(jnp.int32, (EXTRA, rows), 0)
    local_experts = slots * 4 // rows
    capacity = rows // 4
    for e in range(local_experts):
        gate = jnp.zeros((1, rows), jnp.float32)
        for half in range(halves):
            hit = line + half * EXTRA == first_expert + e
            for piece in range(PIECES):
                at = (piece * halves + half) * rows
                gate += jnp.sum(
                    jnp.where(hit, pack[:, at : at + rows], 0.0), axis=0, keepdims=True
                )
        span = slice(e * capacity, (e + 1) * capacity)
        out_ref[span, :] = jnp.sum(
            place[span].astype(jnp.float32) * gate, axis=-1, keepdims=True
        )


def pick_rows(first_expert, place, ring, distances, gated):
    _, slots, rows = place.shape
    half = rows // 2
    operands, shares = [], []
    for k in distances:
        spans = [(0, rows)]
        if k == ring.peers // 2 and ring.half < rows:
            spans = [(0, half), (half, half)]
        shares.append((k, len(spans)))
        for at, count in spans + ([(rows, EXTRA)] if gated else []):
            array, at = ring.rows(k, at, count)
            operands.append((array, (), (count, at // count)))
    width = operands[0][0].shape[-1]
    out_shape = [jax.ShapeDtypeStruct((slots, width), jnp.bfloat16) for _ in distances]
    if gated:
        out_shape += [jax.ShapeDtypeStruct((slots, 1), jnp.float32) for _ in distances]
    return block_call(
        functools.partial(pick_kernel, shares, gated),
        [(place,)] + operands,
        out_shape,
        "pick_rows",
        prefetch=first_expert,
    )


def spread_kernel(middle, half, refs_held, first_ref, devices_ref, place_ref, rows_ref, grads_ref, gate_ref, *refs):
    sums_ref, out_ref, far_left_ref, far_right_ref = refs[refs_held:]
    place = place_ref[...]
    rows = place.shape[1]
    grads = dot_tn(place, grads_ref[...]).astype(jnp.bfloat16)
    sums_ref[:rows, :] = grads
    out_ref[...] = dot_tn(place, rows_ref[...]).astype(jnp.bfloat16)
    capacity = gate_ref.shape[1]
    expert = lax.broadcasted_iota(jnp.int32, (EXPERTS, rows), 0) - first_ref[0]
    gates = jnp.zeros((EXPERTS, rows), jnp.float32)
    for e in range(gate_ref.shape[0]):
        hit = place[e * capacity : (e + 1) * capacity].astype(jnp.float32)
        line = jnp.sum(hit * gate_ref[e], axis=0, keepdims=True)
        gates = jnp.where(expert == e, line, gates)
    pack_pieces(gates, sums_ref, rows)

    @pl.when(pl.program_id(0) == middle)
    def _():
        far_left_ref[...] = grads[:half]
        far_right_ref[: rows - half, :] = grads[half:]
        far_right_ref[rows - half :, :] = sums_ref[rows:, :]


def spread_rows(first_expert, devices, place, rows_back, grads_back, gate_slots, group, half, held):
    sources, slots, rows = place.shape
    width = rows_back.shape[-1]
    local_experts = gate_slots.shape[0]
    base = group * GROUP
    by_source = pl.BlockSpec((None, slots, width), lambda k, f, d: (k, 0, 0))
    held = held or []
    out_shape = [
        jax.ShapeDtypeStruct((sources, rows + EXTRA, width), jnp.bfloat16),
        jax.ShapeDtypeStruct((sources, rows, width), jnp.bfloat16),
        jax.ShapeDtypeStruct((half, width), jnp.bfloat16),
        jax.ShapeDtypeStruct((rows + EXTRA - half, width), jnp.bfloat16),
    ]
    return pl.pallas_call(
        functools.partial(spread_kernel, sources // 2 - base, half, len(held)),
        grid_spec=pltpu.PrefetchScalarGridSpec(
            num_scalar_prefetch=2,
            grid=(GROUP,),
            in_specs=[
                pl.BlockSpec((None, slots, rows), lambda k, f, d: (base + k, 0, 0)),
                by_source,
                by_source,
                pl.BlockSpec((local_experts, slots // local_experts, 1), lambda k, f, d: (0, k, 0)),
            ]
            + [pl.BlockSpec(memory_space=pl.ANY)] * len(held),
            out_specs=[
                pl.BlockSpec((None, rows + EXTRA, width), lambda k, f, d: (base + k, 0, 0)),
                pl.BlockSpec((None, rows, width), lambda k, f, d: (d[base + k], 0, 0)),
                pl.BlockSpec(out_shape[2].shape, lambda k, f, d: (0, 0)),
                pl.BlockSpec(out_shape[3].shape, lambda k, f, d: (0, 0)),
            ],
        ),
        out_shape=out_shape,
        input_output_aliases={6 + i: i for i in range(len(held))},
        compiler_params=pltpu.CompilerParams(vmem_limit_bytes=60 * 1024 * 1024),
        cost_estimate=SMALL_COST,
        name="spread_rows",
    )(first_expert, devices, place, rows_back, grads_back, gate_slots, *held)


def weight_grad_kernel(lines, at_ref, left_ref, right_ref, *outs):
    outs = outs[-2 * lines :]
    core, line = at_ref[0], at_ref[1]
    span = outs[0].shape[0]
    grad = dot_tn(left_ref[...], right_ref[...]).astype(jnp.bfloat16)
    here = grad.shape[0] // (2 * span)
    for i in range(here):
        low = grad[2 * i * span : (2 * i + 1) * span]
        high = grad[(2 * i + 1) * span : (2 * i + 2) * span]
        mine = jnp.where(core == 0, low, high)
        other = jnp.where(core == 0, high, low)
        away = lax.rem(pl.program_id(1) * here + i - line + lines, lines)
        for j in range(lines):

            @pl.when(away == j)
            def _():
                outs[j][...] = mine
                outs[lines + j][...] = other


def weight_grads(place_at, left, right, parts, first, count, held_outs):
    experts, held, height = left.shape
    columns = right.shape[-1]
    lines = parts // 2
    span = height // parts
    tile = min(height, 768)
    out_spec = pl.BlockSpec((None, span, columns), lambda e, i, a: (e + first, 0, 0))
    out_shape = jax.ShapeDtypeStruct((experts, span, columns), jnp.bfloat16)
    held_outs = held_outs or []
    return pl.pallas_call(
        functools.partial(weight_grad_kernel, lines),
        grid_spec=pltpu.PrefetchScalarGridSpec(
            num_scalar_prefetch=1,
            grid=(count, height // tile),
            in_specs=[
                pl.BlockSpec((None, held, tile), lambda e, i, a: (e + first, 0, i)),
                pl.BlockSpec((None, held, columns), lambda e, i, a: (e + first, 0, 0)),
            ]
            + [pl.BlockSpec(memory_space=pl.ANY)] * len(held_outs),
            out_specs=[out_spec] * (2 * lines),
        ),
        out_shape=[out_shape] * (2 * lines),
        input_output_aliases={3 + i: i for i in range(len(held_outs))},
        compiler_params=pltpu.CompilerParams(vmem_limit_bytes=60 * 1024 * 1024),
        cost_estimate=SMALL_COST,
        name="weight_grads",
    )(place_at, left, right, *held_outs)


class WeightSum:
    def __init__(self, arrays, dp_count, *earlier):
        self.dp_count = dp_count
        self.lines = len(arrays) // 2
        self.mine, other = arrays[: self.lines], arrays[self.lines :]
        swap = [(d, d ^ 1) for d in range(dp_count)]
        order = list(range(1, self.lines)) + [0]
        swapped = {j: lax.ppermute(other[j], "dp", swap) for j in order}
        self.swapped = [swapped[j] for j in range(self.lines)]
        self.send = [add_rows(self.mine[j], self.swapped[j]) for j in range(1, self.lines)]

    def along(self):
        self.got = []
        for k, part in enumerate(self.send, 1):
            pairs = [(d, (d + 2 * k) % self.dp_count) for d in range(self.dp_count)]
            self.got.append(lax.ppermute(part, "dp", pairs))
        return self

    def total(self):
        total = self.mine[0].astype(jnp.float32) + self.swapped[0].astype(jnp.float32)
        for part in self.got:
            total = total + part.astype(jnp.float32)
        return total


def attention_forward(tokens, seg_col, seg_row, routes, gains, weight, cos, sin):
    count, rows, width = tokens.shape

    def by_micro(*shape):
        return pl.BlockSpec((None,) + shape, lambda m: (m,) + (0,) * len(shape))

    def shared(part):
        return pl.BlockSpec(part.shape, lambda m: (0, 0))

    kv_width = 2 * KEY_VALUE_HEADS * HEAD_SIZE
    shapes = [
        ((rows, width), jnp.bfloat16),
        ((rows, QUERY_HEADS * HEAD_SIZE), jnp.bfloat16),
        ((rows, kv_width), jnp.bfloat16),
        ((rows, QUERY_HEADS * HEAD_SIZE), jnp.bfloat16),
        ((rows, 128), jnp.float32),
        ((EXTRA, PIECES * EXPERTS // EXTRA * rows), jnp.bfloat16),
    ]
    return pl.pallas_call(
        attention_kernel,
        grid=(count,),
        in_specs=[
            by_micro(rows, width),
            by_micro(rows, 1),
            by_micro(1, rows),
            by_micro(rows, TOPK),
            shared(gains),
            shared(weight),
            shared(cos),
            shared(sin),
        ],
        out_specs=[by_micro(*shape) for shape, _ in shapes],
        out_shape=[jax.ShapeDtypeStruct((count,) + shape, kind) for shape, kind in shapes],
        compiler_params=pltpu.CompilerParams(vmem_limit_bytes=60 * 1024 * 1024),
        cost_estimate=SMALL_COST,
        name="attention_forward",
    )(tokens, seg_col, seg_row, routes, gains, weight, cos, sin)


def attention_grad_kernel(core_ref, xn1, mixed, *refs):
    count = xn1.shape[0]
    proj, attn, sums = [refs[i * count : (i + 1) * count] for i in range(3)]
    mine_ref, other_ref = refs[-2:]
    split = proj[0].shape[1]
    span = mine_ref.shape[0]
    grad = sum(dot_tn(xn1[m], proj[m][...]) for m in range(count))
    router = grad[:, split - 128 :]
    lane = lax.broadcasted_iota(jnp.int32, router.shape, 1)
    router = router + pltpu.roll(router, 128 - EXPERTS, 1)
    gain = sum(part[...] for part in sums)
    lines = [jnp.zeros((EXPERTS, gain.shape[1]), jnp.float32), gain]
    lines.append(jnp.zeros((128 - EXPERTS - gain.shape[0], gain.shape[1]), jnp.float32))
    router = jnp.where(lane < EXPERTS, router, jnp.concatenate(lines, axis=0).T)
    first = core_ref[0] == 0

    def put(columns, value):
        value = value.astype(jnp.bfloat16)
        low, high = value[:span], value[span:]
        mine_ref[:, columns] = jnp.where(first, low, high)
        other_ref[:, columns] = jnp.where(first, high, low)

    put(slice(0, split - 128), grad[:, : split - 128])
    put(slice(split - 128, split), router)
    put(slice(split, None), sum(dot_tn(mixed[m], attn[m][...]) for m in range(count)))


def attention_grads(core, xn1, mixed, proj, attn, gain_sums, parts):
    count, rows, width = xn1.shape
    span = width // parts
    lines = parts // 2
    columns = proj[0].shape[1] + attn[0].shape[1]
    by_line = pl.BlockSpec((count, rows, 2 * span), lambda i, c: (0, 0, i))

    def shared(part):
        return pl.BlockSpec(part.shape, lambda i, c: (0, 0))

    out_spec = pl.BlockSpec((None, span, columns), lambda i, c: (i, 0, 0))
    out_shape = jax.ShapeDtypeStruct((lines, span, columns), jnp.bfloat16)
    return pl.pallas_call(
        attention_grad_kernel,
        grid_spec=pltpu.PrefetchScalarGridSpec(
            num_scalar_prefetch=1,
            grid=(lines,),
            in_specs=[by_line, by_line]
            + [shared(p) for p in proj]
            + [shared(p) for p in attn]
            + [pl.BlockSpec((p.shape[0], 2 * span), lambda i, c: (0, i)) for p in gain_sums],
            out_specs=[out_spec, out_spec],
        ),
        out_shape=[out_shape, out_shape],
        compiler_params=pltpu.CompilerParams(vmem_limit_bytes=60 * 1024 * 1024),
        cost_estimate=SMALL_COST,
        name="attention_grads",
    )(core, xn1, mixed, *proj, *attn, *gain_sums)


def per_device(
    tokens,
    segments,
    routes,
    norm_one,
    norm_two,
    w_query,
    key_value_weight,
    w_out_attn,
    w_router,
    w_in,
    w_out,
    cotangent,
):
    micro_count, rows, width = tokens.shape
    micros = range(micro_count)
    peers = lax.axis_size("expert")
    dp_count = lax.axis_size("dp")
    local_experts = w_in.shape[0]
    experts = local_experts * peers
    capacity = rows // 4
    first_expert = lax.axis_index("expert") * local_experts
    q_width = w_query.shape[1]
    kv_width = key_value_weight.shape[1]
    proj_width = q_width + kv_width
    cosine_table, sine_values = rope_tables(rows, HEAD_SIZE)
    cos = jnp.concatenate([cosine_table, cosine_table], axis=1)
    sin = jnp.concatenate([-sine_values, sine_values], axis=1)
    order = ring_order(peers)
    spot = [order.index(dev) for dev in range(peers)]
    left_devices = [[order[(spot[me] - k) % peers] for k in range(peers)] for me in range(peers)]
    left_device = jnp.array(left_devices, jnp.int32)[lax.axis_index("expert")]
    my_spot = jnp.array(spot, jnp.int32)[lax.axis_index("expert")]

    def gather_dp(part, axis=0):
        return lax.all_gather(part, "dp", axis=axis, tiled=True)

    router_pad = jnp.zeros((w_router.shape[0], 128 - 2 * experts), jnp.bfloat16)
    first_weight = jnp.concatenate(
        [w_query, key_value_weight, w_router, w_router, router_pad], axis=1
    )
    gains = gather_dp(jnp.stack([norm_one, norm_two]), axis=1).astype(jnp.float32)
    first_weight = gather_dp(first_weight)
    out_weight = gather_dp(w_out_attn)

    routes_rows = jnp.swapaxes(routes, 1, 2).reshape(-1, rows).astype(jnp.bfloat16)
    routes_rows = jnp.pad(
        routes_rows, ((0, EXTRA - routes_rows.shape[0]), (0, width - rows))
    )
    cot_rings = [
        RingGather(jnp.concatenate([cotangent[0], routes_rows], axis=0), peers, rows // 2),
        RingGather(cotangent[1], peers, rows // 2),
    ]
    steps = peers // 2
    for _ in range(steps):
        cot_rings[0].step()
    cot_rings[1].step(*cot_rings[0].got)
    first_at = first_expert.astype(jnp.int32).reshape(1)
    routes_all = cot_rings[0].stack_rows(rows, micro_count * TOPK)[:, :, :rows]
    routes_all = routes_all.reshape(peers, micro_count, TOPK, rows)
    places = [
        slot_hits(routes_all[:, m], first_expert, local_experts, capacity)
        .astype(jnp.bfloat16)
        .reshape(peers, -1, rows)
        for m in micros
    ]

    seg_col, seg_row = segments[:, :, None], segments[:, None, :]
    xn1, query, keyval, mixed, gates, gates_pack = attention_forward(
        tokens, seg_col, seg_row, routes, gains, first_weight, cos, sin
    )
    cot_rings[1].step(mixed)
    mixed_late = after(mixed, *places)
    hidden, xn2 = [], []
    for m in micros:
        out = block_call(
            hidden_kernel,
            [(mixed_late, (m,)), (tokens, (m,)), (gains,), (out_weight,), (gates_pack, (m,))],
            [
                jax.ShapeDtypeStruct((rows, width), jnp.float32),
                jax.ShapeDtypeStruct((rows + EXTRA, width), jnp.bfloat16),
            ],
            "hidden_rows",
        )
        hidden.append(out[0])
        xn2.append(out[1])
    every = list(range(peers))
    late = [steps - 1, steps, steps + 1]
    early = [k for k in every if k not in late]
    row_rings = [RingGather(xn2[m], peers, rows // 2) for m in micros]
    row_rings[0].step(*cot_rings[1].got)
    groups = peers // GROUP

    class Experts:
        kept = [None] * 4

        def __init__(self, m, calls):
            self.m = m
            self.calls = calls
            self.per_call = local_experts // calls
            self.outs = [[None] * 3 for _ in range(groups)]
            self.found = {}

        def pick_grads(self):
            place = places[self.m]
            self.grads = pick_rows(first_at, place, cot_rings[self.m], every, False)
            return self.grads[0]

        def pick(self, distances):
            out = pick_rows(first_at, places[self.m], row_rings[self.m], distances, True)
            self.found.update(zip(distances, zip(out, out[len(distances) :])))
            self.rows = [self.found[k][0] for k in every if k in self.found]
            self.gate_slots = [self.found[k][1] for k in every if k in self.found]
            return out[0]

        def call(self, number, *earlier):
            for g in range(groups):
                span = slice(g * GROUP, (g + 1) * GROUP)
                here = self.rows[span]
                here[0] = after(here[0], *earlier) if earlier else here[0]
                done = expert_pass(
                    here,
                    self.grads[span],
                    self.gate_slots[span],
                    w_in,
                    w_out,
                    self.outs[g] + Experts.kept,
                    (self.m * groups + g, micro_count * groups),
                    number * self.per_call,
                    self.per_call,
                )
                self.outs[g], Experts.kept = list(done[:3]), list(done[3:])
            return done[2]

        def spread(self, *earlier):
            place = places[self.m]
            place = after(place, *earlier) if earlier else place
            held = None
            for g in range(groups):
                out = spread_rows(
                    first_at, left_device, place, *self.outs[g], g, rows // 2, held
                )
                held = out[:2]
                if g == groups // 2:
                    far = out[2:]
            self.sums = held[0]
            self.ring = RingScatter(self.sums, far, peers)
            self.result = lax.psum_scatter(
                held[1].reshape(-1, width), "expert", scatter_dimension=0, tiled=True
            )

    calls = 2
    first, second = Experts(0, calls), Experts(1, calls)
    ring, ring_next, cot_next = row_rings[0], row_rings[1], cot_rings[1]
    while len(ring.from_left) < steps - 1:
        ring.step(xn2[1])
    ring.step(first.pick_grads())
    ring.step(first.pick(early))
    first.pick(late)
    ring_next.step(*ring.got)
    cot_next.step(*ring.got)
    token = first.call(0)
    for number in range(1, calls):
        got = ring_next.got + cot_next.got
        ring_next.step(token)
        if cot_next.far is None:
            cot_next.step(token)
        token = first.call(number, *got)
    while cot_next.far is None:
        cot_next.step()
    got = ring_next.got + cot_next.got
    while len(ring_next.from_left) < steps:
        ring_next.step(token)
    first.spread(*got)
    ring_next.step(first.sums, second.pick_grads())
    first.ring.step()
    second.pick(early)
    second.pick(late)
    token = second.call(0)
    for number in range(1, calls):
        got = first.ring.got
        first.ring.step(token)
        token = second.call(number, *got)
    got = first.ring.got
    first.ring.step(token)
    second.spread(*got)
    second.ring.step()
    got = first.ring.got
    while first.ring.at > 0:
        first.ring.step(second.sums)
    picked, grad_result, activated, grad_pre = Experts.kept
    dp_at = lax.axis_index("dp").astype(jnp.int32)
    place_at = jnp.stack([lax.rem(dp_at, 2), dp_at // 2])
    w_out_sum = WeightSum(
        weight_grads(
            place_at,
            after(activated, second.sums, *got),
            grad_result,
            dp_count,
            0,
            local_experts,
            None,
        ),
        dp_count,
    )

    def in_grads(first_one, count, held, *earlier):
        return weight_grads(
            place_at, after(picked, *earlier), grad_pre, dp_count, first_one, count, held
        )

    def backward(m, pieces, *earlier):
        own, left, right = pieces
        return block_call(
            backward_kernel,
            [
                (after(own, *earlier), (0,), rows + EXTRA),
                (left, (), rows + EXTRA),
                (right, (), rows + EXTRA),
                (cotangent, (m,)),
                (hidden[m],),
                (tokens, (m,)),
                (query, (m,)),
                (keyval, (m,)),
                (seg_col, (m,)),
                (seg_row, (m,)),
                (gates, (m,)),
                (gains,),
                (first_weight,),
                (out_weight,),
                (cos,),
                (sin,),
            ],
            [
                jax.ShapeDtypeStruct((rows, width), jnp.bfloat16),
                jax.ShapeDtypeStruct((rows, proj_width + 128), jnp.bfloat16),
                jax.ShapeDtypeStruct((rows, width), jnp.bfloat16),
                jax.ShapeDtypeStruct((8, width), jnp.float32),
            ],
            "attention_backward",
            [pltpu.VMEM((rows, q_width), jnp.bfloat16)],
        )

    got = second.ring.got
    second.ring.step(w_out_sum.mine[0])
    back_first = backward(0, (first.sums, first.ring.left, first.ring.right), *got)
    got = second.ring.got
    second.ring.step(back_first[3])
    half = max(1, local_experts // 2)
    w_in_parts = in_grads(0, half, None, back_first[3], *got)
    got = second.ring.got
    while second.ring.at > 0:
        second.ring.step(w_in_parts[0])
    w_out_sum.along()
    w_in_parts = in_grads(half, local_experts - half, w_in_parts, *got, *w_out_sum.send)
    w_in_sum = WeightSum(w_in_parts, dp_count)
    back_second = backward(
        1, (second.sums, second.ring.left, second.ring.right), w_in_parts[0]
    )
    grad_tokens, grad_proj, grad_attn, gain_sums = zip(back_first, back_second)
    mine, other = attention_grads(
        place_at, after(xn1, first.result), mixed, grad_proj, grad_attn, gain_sums, dp_count
    )
    grads, grad_w_in, grad_w_out = reduce_packed(
        mine, other, my_spot, peers, dp_count, w_in_sum, w_out_sum, second.result, (q_width, kv_width)
    )
    grad_query, grad_keyval, grad_small, grad_attn_out = grads
    outputs = [
        (hidden[m] + part.result.astype(jnp.float32)).astype(jnp.bfloat16)
        for m, part in enumerate((first, second))
    ]
    return (
        jnp.stack(outputs),
        jnp.stack(grad_tokens),
        grad_small[:, experts],
        grad_small[:, experts + 1],
        grad_query,
        grad_keyval,
        grad_attn_out,
        grad_small[:, :experts],
        grad_w_in,
        grad_w_out,
    )


def last_kernel(spot_ref, *refs):
    outs = refs[-4:]
    blocks = refs[:-4]
    peers = len(blocks) - 1
    piece = blocks[0].shape[0]
    for k, block_ref in enumerate(blocks):
        distance = k if k <= peers // 2 else k - 1
        spot = lax.rem(spot_ref[0] - distance + peers, peers)
        held = block_ref.shape[0]
        row = spot * piece + (held if k == peers // 2 + 1 else 0)
        at = 0
        for out_ref in outs:
            columns = out_ref.shape[1]
            out_ref[pl.ds(pl.multiple_of(row, 8), held), :] = block_ref[
                :, at : at + columns
            ].astype(jnp.float32)
            at += columns


def reduce_packed(mine, other, my_spot, peers, dp_count, w_in_sum, w_out_sum, result, widths):
    lines, span, columns = mine.shape
    swap = [(d, d ^ 1) for d in range(dp_count)]
    total = mine + lax.ppermute(other, "dp", swap)
    piece = span // peers
    total = after(total, *w_in_sum.send, *w_out_sum.got)
    w_in_sum.along()
    total = total.reshape(lines, peers, piece, columns)

    def part(k):
        at = lax.rem(my_spot - k + peers, peers)
        return lax.dynamic_slice_in_dim(total, at, 1, axis=1).reshape(lines * piece, columns)

    parts = [part(k) for k in range(peers)]
    half = lines * piece // 2
    ring = RingScatter(parts, (parts[peers // 2][:half], parts[peers // 2][half:]), peers)
    while ring.at > 0:
        ring.step()
    own, left, right = [part.astype(jnp.float32) for part in (parts[0], ring.left, ring.right)]
    mine = (own + left + right).astype(jnp.bfloat16).reshape(lines, piece, columns)
    line = lax.axis_index("dp") // 2

    def for_line(at):
        return lax.dynamic_index_in_dim(mine, lax.rem(at, lines), 0, keepdims=False)

    share = for_line(line).astype(jnp.float32)
    for k in range(1, lines):
        pairs = [(d, (d + 2 * k) % dp_count) for d in range(dp_count)]
        share = share + lax.ppermute(for_line(line + k), "dp", pairs)
    gather = RingGather(share.astype(jnp.bfloat16), peers, piece // 2)
    gather.step()
    grad_w_out = w_out_sum.total()
    gather.step(grad_w_out)
    grad_w_in = w_in_sum.total()
    gather.step(grad_w_in, result)
    while gather.far is None:
        gather.step()
    blocks = gather.from_left + list(gather.far) + gather.from_right[:0:-1]
    columns = (widths[0], widths[1], 128, columns - sum(widths) - 128)
    if piece % 16 == 0:
        grads = block_call(
            last_kernel,
            [(block,) for block in blocks],
            [jax.ShapeDtypeStruct((span, count), jnp.float32) for count in columns],
            "last_rows",
            prefetch=my_spot.astype(jnp.int32).reshape(1),
        )
    else:
        far = jnp.concatenate(gather.far, axis=0)
        by_distance = jnp.stack(gather.from_left + [far] + gather.from_right[:0:-1])
        distance = lax.rem(my_spot - jnp.arange(peers, dtype=jnp.int32) + peers, peers)
        by_spot = jnp.take(by_distance, distance, axis=0).reshape(span, -1).astype(jnp.float32)
        edges = [sum(columns[:i]) for i in range(5)]
        grads = [by_spot[:, edges[i] : edges[i + 1]] for i in range(4)]
    return grads, grad_w_in, grad_w_out


def solution(mesh):
    return jax.shard_map(
        per_device,
        mesh=mesh,
        in_specs=(
            P(None, ("dp", "expert"), None),
            P(None, ("dp", "expert")),
            P(None, ("dp", "expert"), None),
            P("dp"),
            P("dp"),
            P("dp", None),
            P("dp", None),
            P("dp", None),
            P("dp", None),
            P("expert", None, None),
            P("expert", None, None),
            P(None, ("dp", "expert"), None),
        ),
        out_specs=(
            P(None, ("dp", "expert"), None),
            P(None, ("dp", "expert"), None),
            P("dp"),
            P("dp"),
            P("dp", None),
            P("dp", None),
            P("dp", None),
            P("dp", None),
            P("expert", "dp", None),
            P("expert", "dp", None),
        ),
        check_vma=False,
    )
```

```python
import functools
import math

import jax
import jax.numpy as jnp
from jax import lax
from jax.experimental import pallas as pl
from jax.experimental.pallas import tpu as pltpu
from jax.sharding import PartitionSpec as P

QUERY_HEADS = 12
KEY_VALUE_HEADS = 2
HEAD_SIZE = 128
FF = 768
TOPK = 4
EXPERTS = 32
EXTRA = 16
PIECES = 3
GROUP = 8

eps_norm = 1e-06
rope_base = 1000000.0
mask_fill = -1e30
highest = lax.Precision.HIGHEST


def rms_scale(tensor):
    return lax.rsqrt(jnp.mean(tensor * tensor, axis=-1, keepdims=True) + eps_norm)


def rope_tables(sequence_length, head_width):
    positions = jnp.arange(sequence_length).astype(jnp.float32)
    frequency = rope_base ** (-(jnp.arange(head_width // 2).astype(jnp.float32) * 2.0) / head_width)
    angles = positions[:, None] * frequency[None, :]
    return (jnp.cos(angles), jnp.sin(angles))

SCORE_SCALE = 1.0 / math.sqrt(HEAD_SIZE)
GELU_SCALE = math.sqrt(2.0 / math.pi)
GELU_CUBE = 0.044715
SMALL_COST = pl.CostEstimate(flops=1_000_000, bytes_accessed=1_000_000, transcendentals=0)


def after(value, *earlier):
    return lax.optimization_barrier((value,) + earlier)[0]


def slot_hits(routes_all, first_expert, local_experts, capacity):
    rows = routes_all.shape[-1]
    names = first_expert + jnp.arange(local_experts, dtype=jnp.int32)
    named = routes_all[:, None].astype(jnp.int32) == names[None, :, None, None]
    member = jnp.any(named, axis=2)
    lower = (jnp.arange(rows)[:, None] < jnp.arange(rows)[None, :]).astype(jnp.bfloat16)
    rank = dot32(member.astype(jnp.bfloat16).reshape(-1, rows), lower).reshape(member.shape)
    slots = jnp.arange(capacity, dtype=jnp.float32)
    return member[:, :, None, :] & (rank[:, :, None, :] == slots[None, None, :, None])


def pack_pieces(values, out_ref, first_row):
    rows = values.shape[1]
    rest = values
    for piece in range(PIECES):
        part = rest.astype(jnp.bfloat16)
        rest = rest - part.astype(jnp.float32)
        for half in range(EXPERTS // EXTRA):
            at = (piece * (EXPERTS // EXTRA) + half) * rows
            out_ref[first_row : first_row + EXTRA, at : at + rows] = part[
                half * EXTRA : (half + 1) * EXTRA
            ]


def dot32(left, right):
    return jnp.dot(left, right, preferred_element_type=jnp.float32)


def dot_nt(left, right):
    return lax.dot_general(
        left, right, (((1,), (1,)), ((), ())), preferred_element_type=jnp.float32
    )


def dot_tn(left, right):
    return lax.dot_general(
        left, right, (((0,), (0,)), ((), ())), preferred_element_type=jnp.float32
    )


def mask_of(seg_col, seg_row):
    rows = seg_col.shape[0]
    query_at = lax.broadcasted_iota(jnp.int32, (rows, rows), 0)
    key_at = lax.broadcasted_iota(jnp.int32, (rows, rows), 1)
    return (seg_col == seg_row) & (query_at >= key_at)


def softmax_rows(query, key, allowed):
    scores = jnp.where(allowed, dot_nt(query, key) * SCORE_SCALE, mask_fill)
    weight = jnp.exp(scores - jnp.max(scores, axis=-1, keepdims=True))
    return weight / jnp.sum(weight, axis=-1, keepdims=True)


def from_blocks(starts_ref, rows_ref, blocks):
    total = None
    for at, block_ref in enumerate(blocks):
        span = block_ref.shape[0]
        columns = pl.ds(pl.multiple_of(starts_ref[at], 128), span)
        part = dot32(rows_ref[:, columns], block_ref[...])
        total = part if total is None else total + part
    return total


def into_blocks(starts_ref, rows, blocks, out_ref):
    for at, block_ref in enumerate(blocks):
        span = block_ref.shape[0]
        columns = pl.ds(pl.multiple_of(starts_ref[at], 128), span)
        out_ref[:, columns] = dot_nt(rows, block_ref[...]).astype(out_ref.dtype)


def attention_kernel(
    starts_ref,
    tok_ref,
    seg_col_ref,
    seg_row_ref,
    routes_ref,
    gains_ref,
    cos_ref,
    sin_ref,
    *refs,
):
    weight_refs = refs[:-6]
    xn1_ref, query_ref, keyval_ref, mixed_ref, gates_ref, gates_pack_ref = refs[-6:]
    tok = tok_ref[...].astype(jnp.float32)
    xn1_ref[...] = (tok * rms_scale(tok) * gains_ref[0:1, :]).astype(jnp.bfloat16)
    proj = from_blocks(starts_ref, xn1_ref, weight_refs)
    cos, sin = cos_ref[...], sin_ref[...]

    def rotate(part):
        return (part * cos + pltpu.roll(part, HEAD_SIZE // 2, 1) * sin).astype(jnp.bfloat16)

    q_width = QUERY_HEADS * HEAD_SIZE
    k_width = KEY_VALUE_HEADS * HEAD_SIZE
    for head in range(QUERY_HEADS):
        span = slice(head * HEAD_SIZE, (head + 1) * HEAD_SIZE)
        query_ref[:, span] = rotate(proj[:, span])
    for head in range(KEY_VALUE_HEADS):
        span = slice(head * HEAD_SIZE, (head + 1) * HEAD_SIZE)
        keyval_ref[:, span] = rotate(proj[:, q_width:][:, span])
    keyval_ref[:, k_width:] = proj[:, q_width + k_width : q_width + 2 * k_width].astype(
        jnp.bfloat16
    )
    logits = proj[:, q_width + 2 * k_width :]
    columns = lax.broadcasted_iota(jnp.int32, logits.shape, 1)
    named = [columns == routes_ref[:, j : j + 1] for j in range(TOPK)]
    chosen = [jnp.sum(jnp.where(hit, logits, 0.0), axis=-1, keepdims=True) for hit in named]
    top = functools.reduce(jnp.maximum, chosen)
    weight = [jnp.exp(part - top) for part in chosen]
    total = functools.reduce(jnp.add, weight)
    gates = jnp.full(logits.shape, -1.0, jnp.float32)
    for hit, part in zip(named, weight):
        gates = jnp.where(hit, part / total, gates)
    gates_ref[...] = gates
    pack_pieces(gates.T[:EXPERTS], gates_pack_ref, 0)
    allowed = mask_of(seg_col_ref[...], seg_row_ref[...])
    for head in range(QUERY_HEADS):
        span = slice(head * HEAD_SIZE, (head + 1) * HEAD_SIZE)
        group = head // (QUERY_HEADS // KEY_VALUE_HEADS)
        key = keyval_ref[:, group * HEAD_SIZE : (group + 1) * HEAD_SIZE]
        value = keyval_ref[:, k_width + group * HEAD_SIZE : k_width + (group + 1) * HEAD_SIZE]
        probs = softmax_rows(query_ref[:, span], key, allowed)
        mixed_ref[:, span] = dot32(probs.astype(jnp.bfloat16), value).astype(jnp.bfloat16)


def hidden_kernel(starts_ref, mixed_ref, tok_ref, gains_ref, pack_ref, *refs):
    weight_refs = refs[:-2]
    hidden_ref, xn2_ref = refs[-2:]
    rows = tok_ref.shape[0]
    hidden = tok_ref[...].astype(jnp.float32) + from_blocks(
        starts_ref, mixed_ref, weight_refs
    )
    hidden_ref[...] = hidden
    xn2_ref[:rows, :] = (hidden * rms_scale(hidden) * gains_ref[1:2, :]).astype(jnp.bfloat16)
    xn2_ref[rows:, :] = pack_ref[...]


def backward_kernel(
    starts_ref,
    own_ref,
    left_ref,
    right_ref,
    cot_ref,
    hidden_ref,
    tok_ref,
    query_ref,
    keyval_ref,
    seg_col_ref,
    seg_row_ref,
    gates_ref,
    gains_ref,
    cos_ref,
    sin_ref,
    *refs,
):
    blocks = (len(refs) - 6) // 2
    weight_refs, out_weight_refs = refs[:blocks], refs[blocks : 2 * blocks]
    grad_tok_ref, grad_proj_ref, grad_attn_ref, gain_sum_ref, mixed_grad_ref, wide_ref = refs[-6:]
    width = tok_ref.shape[1]
    q_width = QUERY_HEADS * HEAD_SIZE
    k_width = KEY_VALUE_HEADS * HEAD_SIZE
    proj_width = q_width + 2 * k_width
    rows = tok_ref.shape[0]
    sums = [ref[...].astype(jnp.float32) for ref in (own_ref, left_ref, right_ref)]
    sums = sums[0] + sums[1] + sums[2]
    grad_xn2, pack = sums[:rows], sums[rows:]
    halves = EXPERTS // EXTRA
    lines = [
        sum(
            pack[:, (piece * halves + half) * rows : (piece * halves + half + 1) * rows]
            for piece in range(PIECES)
        )
        for half in range(halves)
    ]
    lines.append(jnp.zeros((128 - EXPERTS, rows), jnp.float32))
    grad_gates = jnp.concatenate(lines, axis=0).T
    hidden = hidden_ref[...]
    scale = rms_scale(hidden)
    unit = hidden * scale
    gain_sum_ref[...] = jnp.zeros(gain_sum_ref.shape, jnp.float32)
    gain_sum_ref[1:2, :] = jnp.sum(grad_xn2 * unit, axis=0, keepdims=True)
    grad_unit = grad_xn2 * gains_ref[1:2, :]
    grad_hidden = cot_ref[...].astype(jnp.float32) + scale * (
        grad_unit - unit * jnp.mean(grad_unit * unit, axis=-1, keepdims=True)
    )
    grad_attn_ref[...] = grad_hidden.astype(jnp.bfloat16)
    into_blocks(starts_ref, grad_attn_ref[...], out_weight_refs, mixed_grad_ref)
    cos, sin = cos_ref[...], sin_ref[...]

    def unrotate(part):
        return (part * cos - pltpu.roll(part, HEAD_SIZE // 2, 1) * sin).astype(jnp.bfloat16)

    allowed = mask_of(seg_col_ref[...], seg_row_ref[...])
    per_group = QUERY_HEADS // KEY_VALUE_HEADS
    for group in range(KEY_VALUE_HEADS):
        key_span = slice(group * HEAD_SIZE, (group + 1) * HEAD_SIZE)
        value_span = slice(k_width + group * HEAD_SIZE, k_width + (group + 1) * HEAD_SIZE)
        key, value = keyval_ref[:, key_span], keyval_ref[:, value_span]
        grad_key = jnp.zeros(key.shape, jnp.float32)
        grad_value = jnp.zeros(key.shape, jnp.float32)
        for head in range(group * per_group, (group + 1) * per_group):
            span = slice(head * HEAD_SIZE, (head + 1) * HEAD_SIZE)
            query, grad_mixed = query_ref[:, span], mixed_grad_ref[:, span]
            probs = softmax_rows(query, key, allowed)
            grad_value += dot_tn(probs.astype(jnp.bfloat16), grad_mixed)
            grad_probs = dot_nt(grad_mixed, value)
            mean = jnp.sum(probs * grad_probs, axis=-1, keepdims=True)
            grad_scores = (probs * (grad_probs - mean)).astype(jnp.bfloat16)
            grad_proj_ref[:, span] = unrotate(dot32(grad_scores, key) * SCORE_SCALE)
            grad_key += dot_tn(grad_scores, query)
        grad_proj_ref[:, q_width + group * HEAD_SIZE : q_width + (group + 1) * HEAD_SIZE] = (
            unrotate(grad_key * SCORE_SCALE)
        )
        first = q_width + k_width + group * HEAD_SIZE
        grad_proj_ref[:, first : first + HEAD_SIZE] = grad_value.astype(jnp.bfloat16)
    gates = jnp.maximum(gates_ref[...], 0.0)
    grad_logits = gates * (grad_gates - jnp.sum(gates * grad_gates, axis=-1, keepdims=True))
    high = grad_logits.astype(jnp.bfloat16).astype(jnp.float32)
    low = pltpu.roll(grad_logits - high, EXPERTS, 1)
    grad_proj_ref[:, proj_width:] = (high + low).astype(jnp.bfloat16)
    into_blocks(starts_ref, grad_proj_ref[...], weight_refs, wide_ref)
    grad_xn1 = wide_ref[...]
    tok = tok_ref[...].astype(jnp.float32)
    scale = rms_scale(tok)
    unit = tok * scale
    gain_sum_ref[0:1, :] = jnp.sum(grad_xn1 * unit, axis=0, keepdims=True)
    grad_unit = grad_xn1 * gains_ref[0:1, :]
    grad_tok_ref[...] = (
        grad_hidden
        + scale * (grad_unit - unit * jnp.mean(grad_unit * unit, axis=-1, keepdims=True))
    ).astype(jnp.bfloat16)


def ring_order(peers):
    minor = peers // 4
    walk = []
    for col in range(minor):
        line = range(4) if col % 2 == 0 else range(3, -1, -1)
        walk += [row * minor + col for row in line]
    return walk


def ring_step(part, shift, peers):
    order = ring_order(peers)
    pairs = [(order[i], order[(i + shift) % peers]) for i in range(peers)]
    return lax.ppermute(part, "expert", pairs)


class RingGather:
    def __init__(self, part, peers, half):
        self.peers, self.half = peers, half
        self.from_left, self.from_right = [part], [part]
        self.far = None
        self.got = ()

    def step(self, *earlier):
        left, right = self.from_left[-1], self.from_right[-1]
        last = len(self.from_left) == self.peers // 2
        if last:
            left, right = left[: self.half], right[self.half :]
        left, right = self.sent = lax.optimization_barrier((left, right) + earlier)[:2]
        left, right = ring_step(left, 1, self.peers), ring_step(right, -1, self.peers)
        self.got = (left, right)
        if last:
            self.far = (left, right)
        else:
            self.from_left.append(left)
            self.from_right.append(right)
        return self

    def rows(self, k, first, count):
        if k < len(self.from_left):
            return self.from_left[k], first
        if k > self.peers // 2:
            return self.from_right[self.peers - k], first
        if first < self.half:
            return self.far[0], first
        return self.far[1], first - self.half

    def stack_rows(self, first, count):
        found = [self.rows(k, first, count) for k in range(self.peers)]
        return jnp.stack([array[at : at + count] for array, at in found])


class RingScatter:
    def __init__(self, part, far, peers):
        self.part, self.far, self.peers = part, far, peers
        self.at = peers // 2
        self.half = far[0].shape[0]

    def step(self, *earlier):
        peers, k, half = self.peers, self.at, self.half
        if k == peers // 2:
            left, right = lax.optimization_barrier(tuple(self.far) + earlier)[:2]
        else:
            left, right = self.part(k), self.part(peers - k)
            if earlier:
                self.left, self.right = lax.optimization_barrier(
                    (self.left, self.right) + earlier
                )[:2]
            if k == peers // 2 - 1:
                left = jnp.concatenate([add_rows(left[:half], self.left), left[half:]], axis=0)
                right = jnp.concatenate([right[:half], add_rows(right[half:], self.right)], axis=0)
            else:
                left, right = add_rows(left, self.left), add_rows(right, self.right)
        left, right = self.sent = lax.optimization_barrier((left, right))
        self.left = ring_step(left, -1, peers)
        self.right = ring_step(right, 1, peers)
        self.got = (self.left, self.right)
        self.at = k - 1
        return self


def add_rows(left, right):
    return (left.astype(jnp.float32) + right.astype(jnp.float32)).astype(jnp.bfloat16)


def expert_kernel(sources, *refs):
    rows_refs = refs[:sources]
    grad_refs = refs[sources : 2 * sources]
    gate_refs = refs[2 * sources : 3 * sources]
    w_in_ref, w_out_ref = refs[3 * sources : 3 * sources + 2]
    (
        back_rows_ref,
        back_grads_ref,
        grad_gate_ref,
        picked_ref,
        grad_result_ref,
        activated_ref,
        grad_pre_ref,
    ) = refs[-7:]
    capacity, width = rows_refs[0].shape
    for k in range(sources):
        picked_ref[pl.ds(k * capacity, capacity), :] = rows_refs[k][...]
    pre_act = dot32(picked_ref[...], w_in_ref[...])
    gate_part = pre_act[:, :FF]
    up_part = pre_act[:, FF:]
    square = gate_part * gate_part
    bend = jnp.tanh(GELU_SCALE * gate_part * (1.0 + GELU_CUBE * square))
    lift = 0.5 * (1.0 + bend)
    gelu_val = gate_part * lift
    slope = lift + 0.5 * gate_part * (1.0 - bend * bend) * (
        GELU_SCALE * (1.0 + 3.0 * GELU_CUBE * square)
    )
    activated_ref[...] = (gelu_val * up_part).astype(jnp.bfloat16)
    result = dot32(activated_ref[...], w_out_ref[...])
    for k in range(sources):
        gates = gate_refs[k][...]
        span = slice(k * capacity, (k + 1) * capacity)
        grad_rows = grad_refs[k][...].astype(jnp.float32)
        grad_gate_ref[span, :] = jnp.sum(result[span] * grad_rows, axis=-1, keepdims=True)
        back_rows_ref[k] = (result[span] * gates).astype(jnp.bfloat16)
        grad_result_ref[span, :] = (grad_rows * gates).astype(jnp.bfloat16)
    grad_act = lax.dot_general(
        grad_result_ref[...],
        w_out_ref[...],
        (((1,), (1,)), ((), ())),
        preferred_element_type=jnp.float32,
    )
    grad_pre_ref[:, :FF] = (grad_act * up_part * slope).astype(jnp.bfloat16)
    grad_pre_ref[:, FF:] = (grad_act * gelu_val).astype(jnp.bfloat16)
    grad_in = lax.dot_general(
        grad_pre_ref[...],
        w_in_ref[...],
        (((1,), (1,)), ((), ())),
        preferred_element_type=jnp.float32,
    ).astype(jnp.bfloat16)
    for k in range(sources):
        back_grads_ref[k] = grad_in[k * capacity : (k + 1) * capacity]


def expert_pass(rows_list, grads_list, gate_slots, w_in, w_out, held_outs, position, first, count):
    sources = len(rows_list)
    local_experts, width, _ = w_in.shape
    slots = rows_list[0].shape[0]
    capacity = slots // local_experts
    held = sources * capacity
    block_spec = pl.BlockSpec((capacity, width), lambda e: (e + first, 0))
    back_spec = pl.BlockSpec((sources, capacity, width), lambda e: (0, e + first, 0))
    column_spec = pl.BlockSpec((None, held, 1), lambda e: (e + first, 0, 0))

    def kept_spec(columns):
        return pl.BlockSpec((None, held, columns), lambda e: (e + first, position[0], 0))

    def kept_shape(columns):
        return jax.ShapeDtypeStruct((local_experts, position[1] * held, columns), jnp.bfloat16)

    kept_widths = (width, width, FF, 2 * FF)
    first_held = 3 * sources + 2
    given = [(i, part) for i, part in enumerate(held_outs) if part is not None]
    return pl.pallas_call(
        functools.partial(expert_kernel, sources),
        grid=(count,),
        in_specs=[block_spec] * (2 * sources)
        + [pl.BlockSpec((capacity, 1), lambda e: (e + first, 0))] * sources
        + [
            pl.BlockSpec((None, width, 2 * FF), lambda e: (e + first, 0, 0)),
            pl.BlockSpec((None, FF, width), lambda e: (e + first, 0, 0)),
        ]
        + [pl.BlockSpec(memory_space=pl.ANY)] * len(given),
        out_specs=[back_spec, back_spec, column_spec] + [kept_spec(c) for c in kept_widths],
        out_shape=[
            jax.ShapeDtypeStruct((sources, slots, width), jnp.bfloat16),
            jax.ShapeDtypeStruct((sources, slots, width), jnp.bfloat16),
            jax.ShapeDtypeStruct((local_experts, held, 1), jnp.float32),
        ]
        + [kept_shape(c) for c in kept_widths],
        input_output_aliases={first_held + at: i for at, (i, _) in enumerate(given)},
        compiler_params=pltpu.CompilerParams(vmem_limit_bytes=60 * 1024 * 1024),
        cost_estimate=SMALL_COST,
        name="expert_pass",
    )(*rows_list, *grads_list, *gate_slots, w_in, w_out, *[part for _, part in given])


def block_call(kernel, operands, out_shape, name, scratch=(), prefetch=None):
    def spec(array, lead=(), rows=None):
        rest = array.shape[len(lead) :]
        at = lead + (0,) * len(rest)
        if rows is not None:
            count, block = rows if isinstance(rows, tuple) else (rows, 0)
            rest = (count,) + rest[1:]
            at = lead + (block,) + (0,) * (len(rest) - 1)
        return pl.BlockSpec((None,) * len(lead) + rest, lambda *_: at)

    scalars = [] if prefetch is None else [prefetch]
    return pl.pallas_call(
        kernel,
        grid_spec=pltpu.PrefetchScalarGridSpec(
            num_scalar_prefetch=len(scalars),
            grid=(1,),
            in_specs=[spec(*operand) for operand in operands],
            out_specs=[spec(shape) for shape in out_shape],
            scratch_shapes=list(scratch),
        ),
        out_shape=out_shape,
        compiler_params=pltpu.CompilerParams(vmem_limit_bytes=60 * 1024 * 1024),
        cost_estimate=SMALL_COST,
        name=name,
    )(*scalars, *[operand[0] for operand in operands])


def pick_kernel(shares, gated, first_ref, place_ref, *refs):
    at = 0
    outs = refs[sum(count for _, count in shares) + (len(shares) if gated else 0) :]
    for number, (k, count) in enumerate(shares):
        total, row = None, 0
        for block_ref in refs[at : at + count]:
            held = block_ref.shape[0]
            part = dot32(place_ref[k, :, row : row + held], block_ref[...])
            total = part if total is None else total + part
            row += held
        outs[number][...] = total.astype(jnp.bfloat16)
        at += count
        if gated:
            slot_gates(first_ref[0], place_ref[k], refs[at], outs[len(shares) + number])
            at += 1


def slot_gates(first_expert, place, pack_ref, out_ref):
    slots, rows = place.shape
    pack = pack_ref[...].astype(jnp.float32)
    halves = EXPERTS // EXTRA
    line = lax.broadcasted_iota(jnp.int32, (EXTRA, rows), 0)
    local_experts = slots * 4 // rows
    capacity = rows // 4
    for e in range(local_experts):
        gate = jnp.zeros((1, rows), jnp.float32)
        for half in range(halves):
            hit = line + half * EXTRA == first_expert + e
            for piece in range(PIECES):
                at = (piece * halves + half) * rows
                gate += jnp.sum(
                    jnp.where(hit, pack[:, at : at + rows], 0.0), axis=0, keepdims=True
                )
        span = slice(e * capacity, (e + 1) * capacity)
        out_ref[span, :] = jnp.sum(
            place[span].astype(jnp.float32) * gate, axis=-1, keepdims=True
        )


def pick_rows(first_expert, place, ring, distances, gated):
    _, slots, rows = place.shape
    half = rows // 2
    operands, shares = [], []
    for k in distances:
        spans = [(0, rows)]
        if k == ring.peers // 2 and ring.half < rows:
            spans = [(0, half), (half, half)]
        shares.append((k, len(spans)))
        for at, count in spans + ([(rows, EXTRA)] if gated else []):
            array, at = ring.rows(k, at, count)
            operands.append((array, (), (count, at // count)))
    width = operands[0][0].shape[-1]
    out_shape = [jax.ShapeDtypeStruct((slots, width), jnp.bfloat16) for _ in distances]
    if gated:
        out_shape += [jax.ShapeDtypeStruct((slots, 1), jnp.float32) for _ in distances]
    return block_call(
        functools.partial(pick_kernel, shares, gated),
        [(place,)] + operands,
        out_shape,
        "pick_rows",
        prefetch=first_expert,
    )


def spread_kernel(middle, spans, held, first_ref, place_ref, rows_ref, grads_ref, gate_ref, *refs):
    out_ref, *far_refs = refs[held:]
    place = place_ref[...]
    rows = place.shape[1]
    out_ref[:rows, :] = dot_tn(place, grads_ref[...]).astype(jnp.bfloat16)
    out_ref[rows + EXTRA :, :] = dot_tn(place, rows_ref[...]).astype(jnp.bfloat16)
    capacity = gate_ref.shape[1]
    expert = lax.broadcasted_iota(jnp.int32, (EXPERTS, rows), 0) - first_ref[0]
    gates = jnp.zeros((EXPERTS, rows), jnp.float32)
    for e in range(gate_ref.shape[0]):
        hit = place[e * capacity : (e + 1) * capacity].astype(jnp.float32)
        line = jnp.sum(hit * gate_ref[e], axis=0, keepdims=True)
        gates = jnp.where(expert == e, line, gates)
    pack_pieces(gates, out_ref, rows)

    @pl.when(pl.program_id(0) == middle)
    def _():
        for far_ref, (row, count) in zip(far_refs, spans):
            far_ref[...] = out_ref[row : row + count, :]


def spread_rows(first_expert, place, rows_back, grads_back, gate_slots, group, spans, held):
    sources, slots, rows = place.shape
    width = rows_back.shape[-1]
    local_experts = gate_slots.shape[0]
    base = group * GROUP
    by_source = pl.BlockSpec((None, slots, width), lambda k, f: (k, 0, 0))
    held = [] if held is None else [held]
    out_shape = [jax.ShapeDtypeStruct((sources, 2 * rows + EXTRA, width), jnp.bfloat16)]
    out_shape += [jax.ShapeDtypeStruct((count, width), jnp.bfloat16) for _, count in spans]
    out_specs = [pl.BlockSpec((None, 2 * rows + EXTRA, width), lambda k, f: (base + k, 0, 0))]
    out_specs += [pl.BlockSpec((count, width), lambda k, f: (0, 0)) for _, count in spans]
    return pl.pallas_call(
        functools.partial(spread_kernel, sources // 2 - base, spans, len(held)),
        grid_spec=pltpu.PrefetchScalarGridSpec(
            num_scalar_prefetch=1,
            grid=(GROUP,),
            in_specs=[
                pl.BlockSpec((None, slots, rows), lambda k, f: (base + k, 0, 0)),
                by_source,
                by_source,
                pl.BlockSpec((local_experts, slots // local_experts, 1), lambda k, f: (0, k, 0)),
            ]
            + [pl.BlockSpec(memory_space=pl.ANY)] * len(held),
            out_specs=out_specs,
        ),
        out_shape=out_shape,
        input_output_aliases={5 + i: i for i in range(len(held))},
        compiler_params=pltpu.CompilerParams(vmem_limit_bytes=60 * 1024 * 1024),
        cost_estimate=SMALL_COST,
        name="spread_rows",
    )(first_expert, place, rows_back, grads_back, gate_slots, *held)


def weight_grad_kernel(left_ref, right_ref, *refs):
    refs[-1][...] = dot_tn(left_ref[...], right_ref[...]).astype(jnp.bfloat16)


def weight_grads(left, right, first, count, held_out):
    experts, held, height = left.shape
    columns = right.shape[-1]
    tile = min(height, 768)
    given = [] if held_out is None else [held_out]
    return pl.pallas_call(
        weight_grad_kernel,
        grid=(count, height // tile),
        in_specs=[
            pl.BlockSpec((None, held, tile), lambda e, i: (e + first, 0, i)),
            pl.BlockSpec((None, held, columns), lambda e, i: (e + first, 0, 0)),
        ]
        + [pl.BlockSpec(memory_space=pl.ANY)] * len(given),
        out_specs=pl.BlockSpec((None, tile, columns), lambda e, i: (e + first, i, 0)),
        out_shape=jax.ShapeDtypeStruct((experts, height, columns), jnp.bfloat16),
        input_output_aliases={2: 0} if given else {},
        compiler_params=pltpu.CompilerParams(vmem_limit_bytes=60 * 1024 * 1024),
        cost_estimate=SMALL_COST,
        name="weight_grads",
    )(left, right, *given)


def attention_forward(starts, tokens, seg_col, seg_row, routes, gains, cos, sin, weights):
    count, rows, width = tokens.shape

    def by_micro(*shape):
        return pl.BlockSpec((None,) + shape, lambda m, s: (m,) + (0,) * len(shape))

    def shared(part):
        return pl.BlockSpec(part.shape, lambda m, s: (0, 0))

    kv_width = 2 * KEY_VALUE_HEADS * HEAD_SIZE
    shapes = [
        ((rows, width), jnp.bfloat16),
        ((rows, QUERY_HEADS * HEAD_SIZE), jnp.bfloat16),
        ((rows, kv_width), jnp.bfloat16),
        ((rows, QUERY_HEADS * HEAD_SIZE), jnp.bfloat16),
        ((rows, 128), jnp.float32),
        ((EXTRA, PIECES * EXPERTS // EXTRA * rows), jnp.bfloat16),
    ]
    return pl.pallas_call(
        attention_kernel,
        grid_spec=pltpu.PrefetchScalarGridSpec(
            num_scalar_prefetch=1,
            grid=(count,),
            in_specs=[
                by_micro(rows, width),
                by_micro(rows, 1),
                by_micro(1, rows),
                by_micro(rows, TOPK),
                shared(gains),
                shared(cos),
                shared(sin),
            ]
            + [shared(part) for part in weights],
            out_specs=[by_micro(*shape) for shape, _ in shapes],
        ),
        out_shape=[jax.ShapeDtypeStruct((count,) + shape, kind) for shape, kind in shapes],
        compiler_params=pltpu.CompilerParams(vmem_limit_bytes=60 * 1024 * 1024),
        cost_estimate=SMALL_COST,
        name="attention_forward",
    )(starts, tokens, seg_col, seg_row, routes, gains, cos, sin, *weights)


def attention_grad_kernel(core_ref, xn1, mixed, *refs):
    count = xn1.shape[0]
    proj, attn, sums = [refs[i * count : (i + 1) * count] for i in range(3)]
    mine_ref, other_ref = refs[-2:]
    split = proj[0].shape[1]
    span = mine_ref.shape[0]
    grad = sum(dot_tn(xn1[m], proj[m][...]) for m in range(count))
    router = grad[:, split - 128 :]
    lane = lax.broadcasted_iota(jnp.int32, router.shape, 1)
    router = router + pltpu.roll(router, 128 - EXPERTS, 1)
    gain = sum(part[...] for part in sums)
    lines = [jnp.zeros((EXPERTS, gain.shape[1]), jnp.float32), gain]
    lines.append(jnp.zeros((128 - EXPERTS - gain.shape[0], gain.shape[1]), jnp.float32))
    router = jnp.where(lane < EXPERTS, router, jnp.concatenate(lines, axis=0).T)
    first = core_ref[0] == 0

    def put(columns, value):
        value = value.astype(jnp.bfloat16)
        low, high = value[:span], value[span:]
        mine_ref[:, columns] = jnp.where(first, low, high)
        other_ref[:, columns] = jnp.where(first, high, low)

    put(slice(0, split - 128), grad[:, : split - 128])
    put(slice(split - 128, split), router)
    put(slice(split, None), sum(dot_tn(mixed[m], attn[m][...]) for m in range(count)))


def attention_grads(core, xn1, mixed, proj, attn, gain_sums, parts):
    count, rows, width = xn1.shape
    span = width // parts
    lines = parts // 2
    columns = proj[0].shape[1] + attn[0].shape[1]
    by_line = pl.BlockSpec((count, rows, 2 * span), lambda i, c: (0, 0, i))

    def shared(part):
        return pl.BlockSpec(part.shape, lambda i, c: (0, 0))

    out_spec = pl.BlockSpec((None, span, columns), lambda i, c: (i, 0, 0))
    out_shape = jax.ShapeDtypeStruct((lines, span, columns), jnp.bfloat16)
    return pl.pallas_call(
        attention_grad_kernel,
        grid_spec=pltpu.PrefetchScalarGridSpec(
            num_scalar_prefetch=1,
            grid=(lines,),
            in_specs=[by_line, by_line]
            + [shared(p) for p in proj]
            + [shared(p) for p in attn]
            + [pl.BlockSpec((p.shape[0], 2 * span), lambda i, c: (0, i)) for p in gain_sums],
            out_specs=[out_spec, out_spec],
        ),
        out_shape=[out_shape, out_shape],
        compiler_params=pltpu.CompilerParams(vmem_limit_bytes=60 * 1024 * 1024),
        cost_estimate=SMALL_COST,
        name="attention_grads",
    )(core, xn1, mixed, *proj, *attn, *gain_sums)


def gather_blocks(part, dp_at, dp_count):
    span = part.shape[0]
    if span % 128 or dp_count != 4:
        whole = lax.all_gather(part, "dp", axis=0, tiled=True)
        return [whole], jnp.zeros((1,), jnp.int32)
    line = [(d, (d + 2) % 4) for d in range(4)]
    core = [(d, d ^ 1) for d in range(4)]
    across = lax.ppermute(part, "dp", line)
    beside = lax.ppermute(part, "dp", core)
    both = lax.ppermute(across, "dp", core)
    far = lax.rem(dp_at + 2, 4)
    owners = jnp.stack([dp_at, dp_at + 1 - 2 * lax.rem(dp_at, 2), far, far + 1 - 2 * lax.rem(far, 2)])
    return [part, beside, across, both], owners * span


def per_device(
    tokens,
    segments,
    routes,
    norm_one,
    norm_two,
    w_query,
    key_value_weight,
    w_out_attn,
    w_router,
    w_in,
    w_out,
    cotangent,
):
    micro_count, rows, width = tokens.shape
    micros = range(micro_count)
    peers = lax.axis_size("expert")
    dp_count = lax.axis_size("dp")
    local_experts = w_in.shape[0]
    experts = local_experts * peers
    capacity = rows // 4
    first_expert = lax.axis_index("expert") * local_experts
    q_width = w_query.shape[1]
    kv_width = key_value_weight.shape[1]
    proj_width = q_width + kv_width
    cosine_table, sine_values = rope_tables(rows, HEAD_SIZE)
    cos = jnp.concatenate([cosine_table, cosine_table], axis=1)
    sin = jnp.concatenate([-sine_values, sine_values], axis=1)
    order = ring_order(peers)
    spot = [order.index(dev) for dev in range(peers)]
    my_spot = jnp.array(spot, jnp.int32)[lax.axis_index("expert")]

    router_pad = jnp.zeros((w_router.shape[0], 128 - 2 * experts), jnp.bfloat16)
    first_weight = jnp.concatenate(
        [w_query, key_value_weight, w_router, w_router, router_pad], axis=1
    )
    dp_at = lax.axis_index("dp").astype(jnp.int32)
    first_weights, starts = gather_blocks(first_weight, dp_at, dp_count)
    out_weights, _ = gather_blocks(w_out_attn, dp_at, dp_count)
    gains = lax.all_gather(jnp.stack([norm_one, norm_two]), "dp", axis=1, tiled=True)
    gains = gains.astype(jnp.float32)

    routes_rows = jnp.swapaxes(routes, 1, 2).reshape(-1, rows).astype(jnp.bfloat16)
    routes_rows = jnp.pad(
        routes_rows, ((0, EXTRA - routes_rows.shape[0]), (0, width - rows))
    )
    cot_rings = [
        RingGather(jnp.concatenate([cotangent[0], routes_rows], axis=0), peers, rows // 2),
        RingGather(cotangent[1], peers, rows // 2),
    ]
    steps = peers // 2
    for _ in range(steps):
        cot_rings[0].step()
    first_at = first_expert.astype(jnp.int32).reshape(1)
    routes_all = cot_rings[0].stack_rows(rows, micro_count * TOPK)[:, :, :rows]
    routes_all = routes_all.reshape(peers, micro_count, TOPK, rows)
    places = [
        slot_hits(routes_all[:, m], first_expert, local_experts, capacity)
        .astype(jnp.bfloat16)
        .reshape(peers, -1, rows)
        for m in micros
    ]

    seg_col, seg_row = segments[:, :, None], segments[:, None, :]
    xn1, query, keyval, mixed, gates, gates_pack = attention_forward(
        starts, tokens, seg_col, seg_row, routes, gains, cos, sin, first_weights
    )
    mixed_late = after(mixed, *places)
    hidden, xn2 = [], []
    for m in micros:
        out = block_call(
            hidden_kernel,
            [(mixed_late, (m,)), (tokens, (m,)), (gains,), (gates_pack, (m,))]
            + [(part,) for part in out_weights],
            [
                jax.ShapeDtypeStruct((rows, width), jnp.float32),
                jax.ShapeDtypeStruct((rows + EXTRA, width), jnp.bfloat16),
            ],
            "hidden_rows",
            prefetch=starts,
        )
        hidden.append(out[0])
        xn2.append(out[1])
    every = list(range(peers))
    late = [steps - 1, steps, steps + 1]
    early = [k for k in every if k not in late]
    row_rings = [RingGather(xn2[m], peers, rows // 2) for m in micros]
    row_rings[0].step(*cot_rings[0].got)
    groups = peers // GROUP

    class Experts:
        kept = [None] * 4

        def __init__(self, m, calls):
            self.m = m
            self.calls = calls
            self.per_call = local_experts // calls
            self.outs = [[None] * 3 for _ in range(groups)]
            self.found = {}

        def pick_grads(self):
            place = places[self.m]
            self.grads = pick_rows(first_at, place, cot_rings[self.m], every, False)
            return self.grads[0]

        def pick(self, distances):
            out = pick_rows(first_at, places[self.m], row_rings[self.m], distances, True)
            self.found.update(zip(distances, zip(out, out[len(distances) :])))
            self.rows = [self.found[k][0] for k in every if k in self.found]
            self.gate_slots = [self.found[k][1] for k in every if k in self.found]
            return out[0]

        def call(self, number, *earlier):
            for g in range(groups):
                span = slice(g * GROUP, (g + 1) * GROUP)
                here = self.rows[span]
                here[0] = after(here[0], *earlier) if earlier else here[0]
                done = expert_pass(
                    here,
                    self.grads[span],
                    self.gate_slots[span],
                    w_in,
                    w_out,
                    self.outs[g] + Experts.kept,
                    (self.m * groups + g, micro_count * groups),
                    number * self.per_call,
                    self.per_call,
                )
                self.outs[g], Experts.kept = list(done[:3]), list(done[3:])
            return done[2]

        def spread(self, spans, *earlier):
            place = places[self.m]
            place = after(place, *earlier) if earlier else place
            self.sums = None
            for g in range(groups):
                out = spread_rows(first_at, place, *self.outs[g], g, spans, self.sums)
                self.sums = out[0]
                if g == groups // 2:
                    far = out[1:]
            return far

    calls = 2
    first, second = Experts(0, calls), Experts(1, calls)
    ring, ring_next, cot_next = row_rings[0], row_rings[1], cot_rings[1]
    while len(ring.from_left) < steps - 1:
        ring.step(xn2[1])
    ring.step(first.pick_grads())
    ring.step(first.pick(early))
    first.pick(late)
    ring_next.step(*ring.got)
    cot_next.step(*ring.got)
    token = first.call(0)
    for number in range(1, calls):
        got = ring_next.got + cot_next.got
        ring_next.step(token)
        cot_next.step(token)
        token = first.call(number, *got)
    block = rows + EXTRA
    got = ring_next.got + cot_next.got
    far = first.spread([(0, block), (block, rows)], *got)
    while cot_next.far is None:
        got = ring_next.got
        cot_next.step(token)
        ring_next.step(token)
    ring_first = RingScatter(lambda k: first.sums[k], far, peers)
    ring_first.step(*got)
    second.pick_grads()
    second.pick(early)
    second.pick(late)
    token = second.call(0)
    for number in range(1, calls):
        ring_first.step(token)
        token = second.call(number, *ring_first.sent)
    half = rows // 2
    spans = [(0, half), (half, block - half), (block, half), (block + half, half)]
    far = second.spread(spans)
    ring_grads = RingScatter(lambda k: second.sums[k, :block], far[:2], peers)
    ring_results = RingScatter(lambda k: second.sums[k, block:], far[2:], peers)
    ring_grads.step()
    picked, grad_result, activated, grad_pre = Experts.kept
    place_at = jnp.stack([lax.rem(dp_at, 2), dp_at // 2])
    ring_grads.step()
    w_out_sum = weight_grads(
        after(activated, *ring_grads.sent, *ring_first.got), grad_result, 0, local_experts, None
    )
    def backward(m, pieces, *earlier):
        own, left, right = pieces
        return block_call(
            backward_kernel,
            [
                (after(own, *earlier), (0,), block),
                (left, (), block),
                (right, (), block),
                (cotangent, (m,)),
                (hidden[m],),
                (tokens, (m,)),
                (query, (m,)),
                (keyval, (m,)),
                (seg_col, (m,)),
                (seg_row, (m,)),
                (gates, (m,)),
                (gains,),
                (cos,),
                (sin,),
            ]
            + [(part,) for part in first_weights + out_weights],
            [
                jax.ShapeDtypeStruct((rows, width), jnp.bfloat16),
                jax.ShapeDtypeStruct((rows, proj_width + 128), jnp.bfloat16),
                jax.ShapeDtypeStruct((rows, width), jnp.bfloat16),
                jax.ShapeDtypeStruct((8, width), jnp.float32),
            ],
            "attention_backward",
            [pltpu.VMEM((rows, q_width), jnp.bfloat16), pltpu.VMEM((rows, width), jnp.float32)],
            prefetch=starts,
        )

    half = max(1, local_experts // 2)
    got = ring_grads.got
    ring_grads.step(w_out_sum)
    picked = after(picked, w_out_sum, *got, *ring_grads.sent)
    w_in_sum = weight_grads(picked, grad_pre, 0, half, None)
    while ring_grads.at > 0:
        got = ring_grads.got
        ring_grads.step(w_in_sum)
    picked = after(picked, w_in_sum, *got, *ring_grads.sent)
    w_in_sum = weight_grads(picked, grad_pre, half, local_experts - half, w_in_sum)
    while ring_first.at > 1:
        ring_first.step(w_in_sum)
    grad_w_in, grad_w_out = [
        lax.psum_scatter(after(part, *ring_grads.got), "dp", scatter_dimension=1, tiled=True)
        for part in (w_in_sum, w_out_sum)
    ]
    back_second = backward(1, (second.sums, ring_grads.left, ring_grads.right), *ring_first.sent)
    got = ring_first.got
    ring_first.step(back_second[3])
    ring_results.step(*got)
    ring_results.step(*ring_first.got)
    back_first = backward(
        0, (first.sums, ring_first.left, ring_first.right), *ring_results.sent
    )
    ring_results.step(back_first[3])
    grad_tokens, grad_proj, grad_attn, gain_sums = zip(back_first, back_second)
    mine, other = attention_grads(
        place_at, after(xn1, *ring_results.sent), mixed, grad_proj, grad_attn, gain_sums, dp_count
    )
    grads, grad_w_in, grad_w_out = reduce_packed(
        mine, other, my_spot, peers, dp_count, grad_w_in, grad_w_out, ring_results, (q_width, kv_width)
    )
    grad_query, grad_keyval, grad_small, grad_attn_out = grads
    wide = jnp.float32
    outputs = []
    for m, (own, ring, at) in enumerate(
        ((first.sums, ring_first, block), (second.sums, ring_results, 0))
    ):
        total = hidden[m] + own[0, block:].astype(wide)
        total = total + ring.left[at:].astype(wide) + ring.right[at:].astype(wide)
        outputs.append(total.astype(jnp.bfloat16))
    return (
        jnp.stack(outputs),
        jnp.stack(grad_tokens),
        grad_small[:, experts],
        grad_small[:, experts + 1],
        grad_query,
        grad_keyval,
        grad_attn_out,
        grad_small[:, :experts],
        grad_w_in,
        grad_w_out,
    )


def last_kernel(spot_ref, *refs):
    outs = refs[-4:]
    blocks = refs[:-4]
    peers = len(blocks) - 1
    piece = blocks[0].shape[0]
    for k, block_ref in enumerate(blocks):
        distance = k if k <= peers // 2 else k - 1
        spot = lax.rem(spot_ref[0] - distance + peers, peers)
        held = block_ref.shape[0]
        row = spot * piece + (held if k == peers // 2 + 1 else 0)
        at = 0
        for out_ref in outs:
            columns = out_ref.shape[1]
            out_ref[pl.ds(pl.multiple_of(row, 8), held), :] = block_ref[
                :, at : at + columns
            ].astype(jnp.float32)
            at += columns


def reduce_packed(mine, other, my_spot, peers, dp_count, grad_w_in, grad_w_out, ring_results, widths):
    lines, span, columns = mine.shape
    swap = [(d, d ^ 1) for d in range(dp_count)]
    total = mine + lax.ppermute(other, "dp", swap)
    piece = span // peers
    got = ring_results.got
    while ring_results.at > 0:
        ring_results.step()
    total = after(total, *got, *ring_results.sent)
    total = total.reshape(lines, peers, piece, columns)

    def part(k):
        at = lax.rem(my_spot - k + peers, peers)
        return lax.dynamic_slice_in_dim(total, at, 1, axis=1).reshape(lines * piece, columns)

    parts = [part(k) for k in range(peers)]
    half = lines * piece // 2
    ring = RingScatter(lambda k: parts[k], (parts[peers // 2][:half], parts[peers // 2][half:]), peers)
    ring.step()
    while ring.at > 0:
        ring.step()
    own, left, right = [part.astype(jnp.float32) for part in (parts[0], ring.left, ring.right)]
    mine = (own + left + right).astype(jnp.bfloat16).reshape(lines, piece, columns)
    line = lax.axis_index("dp") // 2

    def for_line(at):
        return lax.dynamic_index_in_dim(mine, lax.rem(at, lines), 0, keepdims=False)

    share = for_line(line).astype(jnp.float32)
    for k in range(1, lines):
        pairs = [(d, (d + 2 * k) % dp_count) for d in range(dp_count)]
        share = share + lax.ppermute(for_line(line + k), "dp", pairs)
    gather = RingGather(share.astype(jnp.bfloat16), peers, piece // 2)
    gather.step()
    grad_w_out = grad_w_out.astype(jnp.float32)
    gather.step(grad_w_out)
    grad_w_in = grad_w_in.astype(jnp.float32)
    gather.step(grad_w_in, *ring_results.got)
    while gather.far is None:
        gather.step()
    blocks = gather.from_left + list(gather.far) + gather.from_right[:0:-1]
    columns = (widths[0], widths[1], 128, columns - sum(widths) - 128)
    if piece % 16 == 0:
        grads = block_call(
            last_kernel,
            [(block,) for block in blocks],
            [jax.ShapeDtypeStruct((span, count), jnp.float32) for count in columns],
            "last_rows",
            prefetch=my_spot.astype(jnp.int32).reshape(1),
        )
    else:
        far = jnp.concatenate(gather.far, axis=0)
        by_distance = jnp.stack(gather.from_left + [far] + gather.from_right[:0:-1])
        distance = lax.rem(my_spot - jnp.arange(peers, dtype=jnp.int32) + peers, peers)
        by_spot = jnp.take(by_distance, distance, axis=0).reshape(span, -1).astype(jnp.float32)
        edges = [sum(columns[:i]) for i in range(5)]
        grads = [by_spot[:, edges[i] : edges[i + 1]] for i in range(4)]
    return grads, grad_w_in, grad_w_out


def solution(mesh):
    return jax.shard_map(
        per_device,
        mesh=mesh,
        in_specs=(
            P(None, ("dp", "expert"), None),
            P(None, ("dp", "expert")),
            P(None, ("dp", "expert"), None),
            P("dp"),
            P("dp"),
            P("dp", None),
            P("dp", None),
            P("dp", None),
            P("dp", None),
            P("expert", None, None),
            P("expert", None, None),
            P(None, ("dp", "expert"), None),
        ),
        out_specs=(
            P(None, ("dp", "expert"), None),
            P(None, ("dp", "expert"), None),
            P("dp"),
            P("dp"),
            P("dp", None),
            P("dp", None),
            P("dp", None),
            P("dp", None),
            P("expert", "dp", None),
            P("expert", "dp", None),
        ),
        check_vma=False,
    )
```

```python
import functools
import math

import jax
import jax.numpy as jnp
from jax import lax
from jax.experimental import pallas as pl
from jax.experimental.pallas import tpu as pltpu
from jax.sharding import PartitionSpec as P

QUERY_HEADS = 12
KEY_VALUE_HEADS = 2
HEAD_SIZE = 128
FF = 768
TOPK = 4
EXPERTS = 32
EXTRA = 16
PIECES = 3
GROUP = 8

eps_norm = 1e-06
rope_base = 1000000.0
mask_fill = -1e30
highest = lax.Precision.HIGHEST


def rms_scale(tensor):
    return lax.rsqrt(jnp.mean(tensor * tensor, axis=-1, keepdims=True) + eps_norm)


def rope_tables(sequence_length, head_width):
    positions = jnp.arange(sequence_length).astype(jnp.float32)
    frequency = rope_base ** (-(jnp.arange(head_width // 2).astype(jnp.float32) * 2.0) / head_width)
    angles = positions[:, None] * frequency[None, :]
    return (jnp.cos(angles), jnp.sin(angles))

SCORE_SCALE = 1.0 / math.sqrt(HEAD_SIZE)
GELU_SCALE = math.sqrt(2.0 / math.pi)
GELU_CUBE = 0.044715
SMALL_COST = pl.CostEstimate(flops=1_000_000, bytes_accessed=1_000_000, transcendentals=0)


def after(value, *earlier):
    return lax.optimization_barrier((value,) + earlier)[0]


def slot_hits(routes_all, first_expert, local_experts, capacity):
    rows = routes_all.shape[-1]
    names = first_expert + jnp.arange(local_experts, dtype=jnp.int32)
    named = routes_all[:, None].astype(jnp.int32) == names[None, :, None, None]
    member = jnp.any(named, axis=2)
    lower = (jnp.arange(rows)[:, None] < jnp.arange(rows)[None, :]).astype(jnp.bfloat16)
    rank = dot32(member.astype(jnp.bfloat16).reshape(-1, rows), lower).reshape(member.shape)
    slots = jnp.arange(capacity, dtype=jnp.float32)
    return member[:, :, None, :] & (rank[:, :, None, :] == slots[None, None, :, None])


def pack_pieces(values, out_ref, first_row):
    rows = values.shape[1]
    rest = values
    for piece in range(PIECES):
        part = rest.astype(jnp.bfloat16)
        rest = rest - part.astype(jnp.float32)
        for half in range(EXPERTS // EXTRA):
            at = (piece * (EXPERTS // EXTRA) + half) * rows
            out_ref[first_row : first_row + EXTRA, at : at + rows] = part[
                half * EXTRA : (half + 1) * EXTRA
            ]


def dot32(left, right):
    return jnp.dot(left, right, preferred_element_type=jnp.float32)


def dot_nt(left, right):
    return lax.dot_general(
        left, right, (((1,), (1,)), ((), ())), preferred_element_type=jnp.float32
    )


def dot_tn(left, right):
    return lax.dot_general(
        left, right, (((0,), (0,)), ((), ())), preferred_element_type=jnp.float32
    )


def mask_of(seg_col, seg_row):
    rows = seg_col.shape[0]
    query_at = lax.broadcasted_iota(jnp.int32, (rows, rows), 0)
    key_at = lax.broadcasted_iota(jnp.int32, (rows, rows), 1)
    return (seg_col == seg_row) & (query_at >= key_at)


def softmax_rows(query, key, allowed):
    scores = jnp.where(allowed, dot_nt(query, key) * SCORE_SCALE, mask_fill)
    weight = jnp.exp(scores - jnp.max(scores, axis=-1, keepdims=True))
    return weight / jnp.sum(weight, axis=-1, keepdims=True)


def from_blocks(starts_ref, rows_ref, blocks):
    total = None
    for at, block_ref in enumerate(blocks):
        span = block_ref.shape[0]
        columns = pl.ds(pl.multiple_of(starts_ref[at], 128), span)
        part = dot32(rows_ref[:, columns], block_ref[...])
        total = part if total is None else total + part
    return total


def attention_kernel(
    starts_ref,
    tok_ref,
    seg_col_ref,
    seg_row_ref,
    routes_ref,
    cos_ref,
    sin_ref,
    *refs,
):
    weight_refs = refs[:-7]
    xn1_ref, query_ref, keyval_ref, mixed_ref, gates_ref, gates_pack_ref, gains_ref = refs[-7:]

    @pl.when(pl.program_id(0) == 0)
    def _():
        for at, block_ref in enumerate(weight_refs):
            span, columns = block_ref.shape
            pad = block_ref[:, columns - 128 :].astype(jnp.float32).T
            place = pl.ds(pl.multiple_of(starts_ref[at], 128), span)
            gains_ref[:, place] = pad[2 * EXPERTS : 2 * EXPERTS + 8]

    tok = tok_ref[...].astype(jnp.float32)
    xn1_ref[...] = (tok * rms_scale(tok) * gains_ref[0:1, :]).astype(jnp.bfloat16)
    proj = from_blocks(starts_ref, xn1_ref, weight_refs)
    cos, sin = cos_ref[...], sin_ref[...]

    def rotate(part):
        return (part * cos + pltpu.roll(part, HEAD_SIZE // 2, 1) * sin).astype(jnp.bfloat16)

    q_width = QUERY_HEADS * HEAD_SIZE
    k_width = KEY_VALUE_HEADS * HEAD_SIZE
    for head in range(QUERY_HEADS):
        span = slice(head * HEAD_SIZE, (head + 1) * HEAD_SIZE)
        query_ref[:, span] = rotate(proj[:, span])
    for head in range(KEY_VALUE_HEADS):
        span = slice(head * HEAD_SIZE, (head + 1) * HEAD_SIZE)
        keyval_ref[:, span] = rotate(proj[:, q_width:][:, span])
    keyval_ref[:, k_width:] = proj[:, q_width + k_width : q_width + 2 * k_width].astype(
        jnp.bfloat16
    )
    logits = proj[:, q_width + 2 * k_width :]
    columns = lax.broadcasted_iota(jnp.int32, logits.shape, 1)
    named = [columns == routes_ref[:, j : j + 1] for j in range(TOPK)]
    chosen = [jnp.sum(jnp.where(hit, logits, 0.0), axis=-1, keepdims=True) for hit in named]
    top = functools.reduce(jnp.maximum, chosen)
    weight = [jnp.exp(part - top) for part in chosen]
    total = functools.reduce(jnp.add, weight)
    gates = jnp.full(logits.shape, -1.0, jnp.float32)
    for hit, part in zip(named, weight):
        gates = jnp.where(hit, part / total, gates)
    gates_ref[...] = gates
    pack_pieces(gates.T[:EXPERTS], gates_pack_ref, 0)
    allowed = mask_of(seg_col_ref[...], seg_row_ref[...])
    for head in range(QUERY_HEADS):
        span = slice(head * HEAD_SIZE, (head + 1) * HEAD_SIZE)
        group = head // (QUERY_HEADS // KEY_VALUE_HEADS)
        key = keyval_ref[:, group * HEAD_SIZE : (group + 1) * HEAD_SIZE]
        value = keyval_ref[:, k_width + group * HEAD_SIZE : k_width + (group + 1) * HEAD_SIZE]
        probs = softmax_rows(query_ref[:, span], key, allowed)
        mixed_ref[:, span] = dot32(probs.astype(jnp.bfloat16), value).astype(jnp.bfloat16)


def hidden_kernel(starts_ref, mixed_ref, tok_ref, gains_ref, pack_ref, *refs):
    weight_refs = refs[:-2]
    hidden_ref, xn2_ref = refs[-2:]
    rows = tok_ref.shape[0]
    hidden = tok_ref[...].astype(jnp.float32) + from_blocks(
        starts_ref, mixed_ref, weight_refs
    )
    hidden_ref[...] = hidden
    xn2_ref[:rows, :] = (hidden * rms_scale(hidden) * gains_ref[1:2, :]).astype(jnp.bfloat16)
    xn2_ref[rows:, :] = pack_ref[...]


def backward_kernel(
    own_ref,
    left_ref,
    right_ref,
    cot_ref,
    hidden_ref,
    tok_ref,
    query_ref,
    keyval_ref,
    seg_col_ref,
    seg_row_ref,
    gates_ref,
    gains_ref,
    cos_ref,
    sin_ref,
    *refs,
):
    weight_ref, out_weight_ref = refs[:2]
    grad_tok_ref, grad_proj_ref, grad_attn_ref, gain_sum_ref, mixed_grad_ref = refs[2:]
    width = tok_ref.shape[1]
    q_width = QUERY_HEADS * HEAD_SIZE
    k_width = KEY_VALUE_HEADS * HEAD_SIZE
    proj_width = q_width + 2 * k_width
    rows = tok_ref.shape[0]
    sums = [ref[...].astype(jnp.float32) for ref in (own_ref, left_ref, right_ref)]
    sums = sums[0] + sums[1] + sums[2]
    grad_xn2, pack = sums[:rows], sums[rows:]
    halves = EXPERTS // EXTRA
    lines = [
        sum(
            pack[:, (piece * halves + half) * rows : (piece * halves + half + 1) * rows]
            for piece in range(PIECES)
        )
        for half in range(halves)
    ]
    lines.append(jnp.zeros((128 - EXPERTS, rows), jnp.float32))
    grad_gates = jnp.concatenate(lines, axis=0).T
    hidden = hidden_ref[...]
    scale = rms_scale(hidden)
    unit = hidden * scale
    gain_sum_ref[...] = jnp.zeros(gain_sum_ref.shape, jnp.float32)
    gain_sum_ref[1:2, :] = jnp.sum(grad_xn2 * unit, axis=0, keepdims=True)
    grad_unit = grad_xn2 * gains_ref[1:2, :]
    grad_hidden = cot_ref[...].astype(jnp.float32) + scale * (
        grad_unit - unit * jnp.mean(grad_unit * unit, axis=-1, keepdims=True)
    )
    grad_attn_ref[...] = grad_hidden.astype(jnp.bfloat16)
    mixed_grad_ref[...] = dot_nt(grad_attn_ref[...], out_weight_ref[...]).astype(jnp.bfloat16)
    cos, sin = cos_ref[...], sin_ref[...]

    def unrotate(part):
        return (part * cos - pltpu.roll(part, HEAD_SIZE // 2, 1) * sin).astype(jnp.bfloat16)

    allowed = mask_of(seg_col_ref[...], seg_row_ref[...])
    per_group = QUERY_HEADS // KEY_VALUE_HEADS
    for group in range(KEY_VALUE_HEADS):
        key_span = slice(group * HEAD_SIZE, (group + 1) * HEAD_SIZE)
        value_span = slice(k_width + group * HEAD_SIZE, k_width + (group + 1) * HEAD_SIZE)
        key, value = keyval_ref[:, key_span], keyval_ref[:, value_span]
        grad_key = jnp.zeros(key.shape, jnp.float32)
        grad_value = jnp.zeros(key.shape, jnp.float32)
        for head in range(group * per_group, (group + 1) * per_group):
            span = slice(head * HEAD_SIZE, (head + 1) * HEAD_SIZE)
            query, grad_mixed = query_ref[:, span], mixed_grad_ref[:, span]
            probs = softmax_rows(query, key, allowed)
            grad_value += dot_tn(probs.astype(jnp.bfloat16), grad_mixed)
            grad_probs = dot_nt(grad_mixed, value)
            mean = jnp.sum(probs * grad_probs, axis=-1, keepdims=True)
            grad_scores = (probs * (grad_probs - mean)).astype(jnp.bfloat16)
            grad_proj_ref[:, span] = unrotate(dot32(grad_scores, key) * SCORE_SCALE)
            grad_key += dot_tn(grad_scores, query)
        grad_proj_ref[:, q_width + group * HEAD_SIZE : q_width + (group + 1) * HEAD_SIZE] = (
            unrotate(grad_key * SCORE_SCALE)
        )
        first = q_width + k_width + group * HEAD_SIZE
        grad_proj_ref[:, first : first + HEAD_SIZE] = grad_value.astype(jnp.bfloat16)
    gates = jnp.maximum(gates_ref[...], 0.0)
    grad_logits = gates * (grad_gates - jnp.sum(gates * grad_gates, axis=-1, keepdims=True))
    high = grad_logits.astype(jnp.bfloat16).astype(jnp.float32)
    low = pltpu.roll(grad_logits - high, EXPERTS, 1)
    grad_proj_ref[:, proj_width:] = (high + low).astype(jnp.bfloat16)
    grad_xn1 = dot_nt(grad_proj_ref[...], weight_ref[...])
    tok = tok_ref[...].astype(jnp.float32)
    scale = rms_scale(tok)
    unit = tok * scale
    gain_sum_ref[0:1, :] = jnp.sum(grad_xn1 * unit, axis=0, keepdims=True)
    grad_unit = grad_xn1 * gains_ref[0:1, :]
    grad_tok_ref[...] = (
        grad_hidden
        + scale * (grad_unit - unit * jnp.mean(grad_unit * unit, axis=-1, keepdims=True))
    ).astype(jnp.bfloat16)


def ring_order(peers):
    minor = peers // 4
    walk = []
    for col in range(minor):
        line = range(4) if col % 2 == 0 else range(3, -1, -1)
        walk += [row * minor + col for row in line]
    return walk


def ring_step(part, shift, peers):
    order = ring_order(peers)
    pairs = [(order[i], order[(i + shift) % peers]) for i in range(peers)]
    return lax.ppermute(part, "expert", pairs)


class RingGather:
    def __init__(self, part, peers, half):
        self.peers, self.half = peers, half
        self.from_left, self.from_right = [part], [part]
        self.far = None
        self.got = ()

    def step(self, *earlier):
        left, right = self.from_left[-1], self.from_right[-1]
        last = len(self.from_left) == self.peers // 2
        if last:
            left, right = left[: self.half], right[self.half :]
        left, right = self.sent = lax.optimization_barrier((left, right) + earlier)[:2]
        left, right = ring_step(left, 1, self.peers), ring_step(right, -1, self.peers)
        self.got = (left, right)
        if last:
            self.far = (left, right)
        else:
            self.from_left.append(left)
            self.from_right.append(right)
        return self

    def rows(self, k, first, count):
        if k < len(self.from_left):
            return self.from_left[k], first
        if k > self.peers // 2:
            return self.from_right[self.peers - k], first
        if first < self.half:
            return self.far[0], first
        return self.far[1], first - self.half

    def stack_rows(self, first, count):
        found = [self.rows(k, first, count) for k in range(self.peers)]
        return jnp.stack([array[at : at + count] for array, at in found])


class RingScatter:
    def __init__(self, part, far, peers):
        self.part, self.far, self.peers = part, far, peers
        self.at = peers // 2
        self.half = far[0].shape[0]

    def step(self, *earlier):
        peers, k, half = self.peers, self.at, self.half
        if k == peers // 2:
            left, right = lax.optimization_barrier(tuple(self.far) + earlier)[:2]
        else:
            left, right = self.part(k), self.part(peers - k)
            if earlier:
                self.left, self.right = lax.optimization_barrier(
                    (self.left, self.right) + earlier
                )[:2]
            if k == peers // 2 - 1:
                kept = left[half:].astype(jnp.bfloat16), right[:half].astype(jnp.bfloat16)
                left = jnp.concatenate([add_rows(left[:half], self.left), kept[0]], axis=0)
                right = jnp.concatenate([kept[1], add_rows(right[half:], self.right)], axis=0)
            else:
                left, right = add_rows(left, self.left), add_rows(right, self.right)
        left, right = self.sent = lax.optimization_barrier((left, right))
        self.left = ring_step(left, -1, peers)
        self.right = ring_step(right, 1, peers)
        self.got = (self.left, self.right)
        self.at = k - 1
        return self


def add_rows(left, right):
    return (left.astype(jnp.float32) + right.astype(jnp.float32)).astype(jnp.bfloat16)


def expert_kernel(sources, *refs):
    rows_refs = refs[:sources]
    grad_refs = refs[sources : 2 * sources]
    gate_refs = refs[2 * sources : 3 * sources]
    w_in_ref, w_out_ref = refs[3 * sources : 3 * sources + 2]
    (
        back_rows_ref,
        back_grads_ref,
        grad_gate_ref,
        picked_ref,
        grad_result_ref,
        activated_ref,
        grad_pre_ref,
    ) = refs[-7:]
    capacity, width = rows_refs[0].shape
    for k in range(sources):
        picked_ref[pl.ds(k * capacity, capacity), :] = rows_refs[k][...]
    pre_act = dot32(picked_ref[...], w_in_ref[...])
    gate_part = pre_act[:, :FF]
    up_part = pre_act[:, FF:]
    square = gate_part * gate_part
    bend = jnp.tanh(GELU_SCALE * gate_part * (1.0 + GELU_CUBE * square))
    lift = 0.5 * (1.0 + bend)
    gelu_val = gate_part * lift
    slope = lift + 0.5 * gate_part * (1.0 - bend * bend) * (
        GELU_SCALE * (1.0 + 3.0 * GELU_CUBE * square)
    )
    activated_ref[...] = (gelu_val * up_part).astype(jnp.bfloat16)
    result = dot32(activated_ref[...], w_out_ref[...])
    for k in range(sources):
        gates = gate_refs[k][...]
        span = slice(k * capacity, (k + 1) * capacity)
        grad_rows = grad_refs[k][...].astype(jnp.float32)
        grad_gate_ref[span, :] = jnp.sum(result[span] * grad_rows, axis=-1, keepdims=True)
        back_rows_ref[k] = (result[span] * gates).astype(jnp.bfloat16)
        grad_result_ref[span, :] = (grad_rows * gates).astype(jnp.bfloat16)
    grad_act = lax.dot_general(
        grad_result_ref[...],
        w_out_ref[...],
        (((1,), (1,)), ((), ())),
        preferred_element_type=jnp.float32,
    )
    grad_pre_ref[:, :FF] = (grad_act * up_part * slope).astype(jnp.bfloat16)
    grad_pre_ref[:, FF:] = (grad_act * gelu_val).astype(jnp.bfloat16)
    grad_in = lax.dot_general(
        grad_pre_ref[...],
        w_in_ref[...],
        (((1,), (1,)), ((), ())),
        preferred_element_type=jnp.float32,
    ).astype(jnp.bfloat16)
    for k in range(sources):
        back_grads_ref[k] = grad_in[k * capacity : (k + 1) * capacity]


def expert_pass(rows_list, grads_list, gate_slots, w_in, w_out, held_outs, position, first, count):
    sources = len(rows_list)
    local_experts, width, _ = w_in.shape
    slots = rows_list[0].shape[0]
    capacity = slots // local_experts
    held = sources * capacity
    block_spec = pl.BlockSpec((capacity, width), lambda e: (e + first, 0))
    back_spec = pl.BlockSpec((sources, capacity, width), lambda e: (0, e + first, 0))
    column_spec = pl.BlockSpec((None, held, 1), lambda e: (e + first, 0, 0))

    def kept_spec(columns):
        return pl.BlockSpec((None, held, columns), lambda e: (e + first, position[0], 0))

    def kept_shape(columns):
        return jax.ShapeDtypeStruct((local_experts, position[1] * held, columns), jnp.bfloat16)

    kept_widths = (width, width, FF, 2 * FF)
    first_held = 3 * sources + 2
    given = [(i, part) for i, part in enumerate(held_outs) if part is not None]
    return pl.pallas_call(
        functools.partial(expert_kernel, sources),
        grid=(count,),
        in_specs=[block_spec] * (2 * sources)
        + [pl.BlockSpec((capacity, 1), lambda e: (e + first, 0))] * sources
        + [
            pl.BlockSpec((None, width, 2 * FF), lambda e: (e + first, 0, 0)),
            pl.BlockSpec((None, FF, width), lambda e: (e + first, 0, 0)),
        ]
        + [pl.BlockSpec(memory_space=pl.ANY)] * len(given),
        out_specs=[back_spec, back_spec, column_spec] + [kept_spec(c) for c in kept_widths],
        out_shape=[
            jax.ShapeDtypeStruct((sources, slots, width), jnp.bfloat16),
            jax.ShapeDtypeStruct((sources, slots, width), jnp.bfloat16),
            jax.ShapeDtypeStruct((local_experts, held, 1), jnp.float32),
        ]
        + [kept_shape(c) for c in kept_widths],
        input_output_aliases={first_held + at: i for at, (i, _) in enumerate(given)},
        compiler_params=pltpu.CompilerParams(vmem_limit_bytes=60 * 1024 * 1024),
        cost_estimate=SMALL_COST,
        name="expert_pass",
    )(*rows_list, *grads_list, *gate_slots, w_in, w_out, *[part for _, part in given])


def block_call(kernel, operands, out_shape, name, scratch=(), prefetch=None):
    def spec(array, lead=(), rows=None):
        rest = array.shape[len(lead) :]
        at = lead + (0,) * len(rest)
        if rows is not None:
            count, block = rows if isinstance(rows, tuple) else (rows, 0)
            rest = (count,) + rest[1:]
            at = lead + (block,) + (0,) * (len(rest) - 1)
        return pl.BlockSpec((None,) * len(lead) + rest, lambda *_: at)

    scalars = [] if prefetch is None else [prefetch]
    return pl.pallas_call(
        kernel,
        grid_spec=pltpu.PrefetchScalarGridSpec(
            num_scalar_prefetch=len(scalars),
            grid=(1,),
            in_specs=[spec(*operand) for operand in operands],
            out_specs=[spec(shape) for shape in out_shape],
            scratch_shapes=list(scratch),
        ),
        out_shape=out_shape,
        compiler_params=pltpu.CompilerParams(vmem_limit_bytes=60 * 1024 * 1024),
        cost_estimate=SMALL_COST,
        name=name,
    )(*scalars, *[operand[0] for operand in operands])


def pick_kernel(shares, gated, first_ref, place_ref, *refs):
    at = 0
    outs = refs[sum(count for _, count in shares) + (len(shares) if gated else 0) :]
    for number, (k, count) in enumerate(shares):
        total, row = None, 0
        for block_ref in refs[at : at + count]:
            held = block_ref.shape[0]
            part = dot32(place_ref[k, :, row : row + held], block_ref[...])
            total = part if total is None else total + part
            row += held
        outs[number][...] = total.astype(jnp.bfloat16)
        at += count
        if gated:
            slot_gates(first_ref[0], place_ref[k], refs[at], outs[len(shares) + number])
            at += 1


def slot_gates(first_expert, place, pack_ref, out_ref):
    slots, rows = place.shape
    pack = pack_ref[...].astype(jnp.float32)
    halves = EXPERTS // EXTRA
    line = lax.broadcasted_iota(jnp.int32, (EXTRA, rows), 0)
    local_experts = slots * 4 // rows
    capacity = rows // 4
    for e in range(local_experts):
        gate = jnp.zeros((1, rows), jnp.float32)
        for half in range(halves):
            hit = line + half * EXTRA == first_expert + e
            for piece in range(PIECES):
                at = (piece * halves + half) * rows
                gate += jnp.sum(
                    jnp.where(hit, pack[:, at : at + rows], 0.0), axis=0, keepdims=True
                )
        span = slice(e * capacity, (e + 1) * capacity)
        out_ref[span, :] = jnp.sum(
            place[span].astype(jnp.float32) * gate, axis=-1, keepdims=True
        )


def pick_rows(first_expert, place, ring, distances, gated):
    _, slots, rows = place.shape
    half = rows // 2
    operands, shares = [], []
    for k in distances:
        spans = [(0, rows)]
        if k == ring.peers // 2 and ring.half < rows:
            spans = [(0, half), (half, half)]
        shares.append((k, len(spans)))
        for at, count in spans + ([(rows, EXTRA)] if gated else []):
            array, at = ring.rows(k, at, count)
            operands.append((array, (), (count, at // count)))
    width = operands[0][0].shape[-1]
    out_shape = [jax.ShapeDtypeStruct((slots, width), jnp.bfloat16) for _ in distances]
    if gated:
        out_shape += [jax.ShapeDtypeStruct((slots, 1), jnp.float32) for _ in distances]
    return block_call(
        functools.partial(pick_kernel, shares, gated),
        [(place,)] + operands,
        out_shape,
        "pick_rows",
        prefetch=first_expert,
    )


def spread_kernel(middle, spans, held, first_ref, place_ref, rows_ref, grads_ref, gate_ref, *refs):
    out_ref, *far_refs = refs[held:]
    place = place_ref[...]
    rows = place.shape[1]
    out_ref[:rows, :] = dot_tn(place, grads_ref[...]).astype(jnp.bfloat16)
    out_ref[rows + EXTRA :, :] = dot_tn(place, rows_ref[...]).astype(jnp.bfloat16)
    capacity = gate_ref.shape[1]
    expert = lax.broadcasted_iota(jnp.int32, (EXPERTS, rows), 0) - first_ref[0]
    gates = jnp.zeros((EXPERTS, rows), jnp.float32)
    for e in range(gate_ref.shape[0]):
        hit = place[e * capacity : (e + 1) * capacity].astype(jnp.float32)
        line = jnp.sum(hit * gate_ref[e], axis=0, keepdims=True)
        gates = jnp.where(expert == e, line, gates)
    pack_pieces(gates, out_ref, rows)

    @pl.when(pl.program_id(0) == middle)
    def _():
        for far_ref, (row, count) in zip(far_refs, spans):
            far_ref[...] = out_ref[row : row + count, :]


def spread_rows(first_expert, place, rows_back, grads_back, gate_slots, group, spans, held):
    sources, slots, rows = place.shape
    width = rows_back.shape[-1]
    local_experts = gate_slots.shape[0]
    base = group * GROUP
    by_source = pl.BlockSpec((None, slots, width), lambda k, f: (k, 0, 0))
    held = [] if held is None else [held]
    out_shape = [jax.ShapeDtypeStruct((sources, 2 * rows + EXTRA, width), jnp.bfloat16)]
    out_shape += [jax.ShapeDtypeStruct((count, width), jnp.bfloat16) for _, count in spans]
    out_specs = [pl.BlockSpec((None, 2 * rows + EXTRA, width), lambda k, f: (base + k, 0, 0))]
    out_specs += [pl.BlockSpec((count, width), lambda k, f: (0, 0)) for _, count in spans]
    return pl.pallas_call(
        functools.partial(spread_kernel, sources // 2 - base, spans, len(held)),
        grid_spec=pltpu.PrefetchScalarGridSpec(
            num_scalar_prefetch=1,
            grid=(GROUP,),
            in_specs=[
                pl.BlockSpec((None, slots, rows), lambda k, f: (base + k, 0, 0)),
                by_source,
                by_source,
                pl.BlockSpec((local_experts, slots // local_experts, 1), lambda k, f: (0, k, 0)),
            ]
            + [pl.BlockSpec(memory_space=pl.ANY)] * len(held),
            out_specs=out_specs,
        ),
        out_shape=out_shape,
        input_output_aliases={5 + i: i for i in range(len(held))},
        compiler_params=pltpu.CompilerParams(vmem_limit_bytes=60 * 1024 * 1024),
        cost_estimate=SMALL_COST,
        name="spread_rows",
    )(first_expert, place, rows_back, grads_back, gate_slots, *held)


def weight_grad_kernel(left_ref, right_ref, *refs):
    refs[-1][...] = dot_tn(left_ref[...], right_ref[...]).astype(jnp.bfloat16)


def weight_grads(left, right, first, count, held_out):
    experts, held, height = left.shape
    columns = right.shape[-1]
    tile = min(height, 768)
    given = [] if held_out is None else [held_out]
    return pl.pallas_call(
        weight_grad_kernel,
        grid=(count, height // tile),
        in_specs=[
            pl.BlockSpec((None, held, tile), lambda e, i: (e + first, 0, i)),
            pl.BlockSpec((None, held, columns), lambda e, i: (e + first, 0, 0)),
        ]
        + [pl.BlockSpec(memory_space=pl.ANY)] * len(given),
        out_specs=pl.BlockSpec((None, tile, columns), lambda e, i: (e + first, i, 0)),
        out_shape=jax.ShapeDtypeStruct((experts, height, columns), jnp.bfloat16),
        input_output_aliases={2: 0} if given else {},
        compiler_params=pltpu.CompilerParams(vmem_limit_bytes=60 * 1024 * 1024),
        cost_estimate=SMALL_COST,
        name="weight_grads",
    )(left, right, *given)


def attention_forward(starts, tokens, seg_col, seg_row, routes, cos, sin, weights):
    count, rows, width = tokens.shape

    def by_micro(*shape):
        return pl.BlockSpec((None,) + shape, lambda m, s: (m,) + (0,) * len(shape))

    def shared(part):
        return pl.BlockSpec(part.shape, lambda m, s: (0, 0))

    kv_width = 2 * KEY_VALUE_HEADS * HEAD_SIZE
    shapes = [
        ((rows, width), jnp.bfloat16),
        ((rows, QUERY_HEADS * HEAD_SIZE), jnp.bfloat16),
        ((rows, kv_width), jnp.bfloat16),
        ((rows, QUERY_HEADS * HEAD_SIZE), jnp.bfloat16),
        ((rows, 128), jnp.float32),
        ((EXTRA, PIECES * EXPERTS // EXTRA * rows), jnp.bfloat16),
    ]
    return pl.pallas_call(
        attention_kernel,
        grid_spec=pltpu.PrefetchScalarGridSpec(
            num_scalar_prefetch=1,
            grid=(count,),
            in_specs=[
                by_micro(rows, width),
                by_micro(rows, 1),
                by_micro(1, rows),
                by_micro(rows, TOPK),
                shared(cos),
                shared(sin),
            ]
            + [shared(part) for part in weights],
            out_specs=[by_micro(*shape) for shape, _ in shapes]
            + [pl.BlockSpec((8, width), lambda m, s: (0, 0))],
        ),
        out_shape=[jax.ShapeDtypeStruct((count,) + shape, kind) for shape, kind in shapes]
        + [jax.ShapeDtypeStruct((8, width), jnp.float32)],
        compiler_params=pltpu.CompilerParams(vmem_limit_bytes=60 * 1024 * 1024),
        cost_estimate=SMALL_COST,
        name="attention_forward",
    )(starts, tokens, seg_col, seg_row, routes, cos, sin, *weights)


def join_kernel(starts_ref, *refs):
    for at, block_ref in enumerate(refs[:-1]):

        @pl.when(pl.program_id(0) == at)
        def _():
            refs[-1][...] = block_ref[...]


def join_blocks(starts, blocks):
    if len(blocks) == 1:
        return blocks[0]
    span, columns = blocks[0].shape
    return pl.pallas_call(
        join_kernel,
        grid_spec=pltpu.PrefetchScalarGridSpec(
            num_scalar_prefetch=1,
            grid=(len(blocks),),
            in_specs=[pl.BlockSpec((span, columns), lambda i, s: (0, 0)) for _ in blocks],
            out_specs=pl.BlockSpec((span, columns), lambda i, s: (s[i] // span, 0)),
        ),
        out_shape=jax.ShapeDtypeStruct((len(blocks) * span, columns), blocks[0].dtype),
        compiler_params=pltpu.CompilerParams(vmem_limit_bytes=60 * 1024 * 1024),
        cost_estimate=SMALL_COST,
        name="join_blocks",
    )(starts, *blocks)


def attention_grad_kernel(core_ref, xn1, mixed, *refs):
    count = xn1.shape[0]
    proj, attn, sums = [refs[i * count : (i + 1) * count] for i in range(3)]
    mine_ref, other_ref = refs[-2:]
    split = proj[0].shape[1]
    span = mine_ref.shape[0]
    grad = sum(dot_tn(xn1[m], proj[m][...]) for m in range(count))
    router = grad[:, split - 128 :]
    lane = lax.broadcasted_iota(jnp.int32, router.shape, 1)
    router = router + pltpu.roll(router, 128 - EXPERTS, 1)
    gain = sum(part[...] for part in sums)
    lines = [jnp.zeros((EXPERTS, gain.shape[1]), jnp.float32), gain]
    lines.append(jnp.zeros((128 - EXPERTS - gain.shape[0], gain.shape[1]), jnp.float32))
    router = jnp.where(lane < EXPERTS, router, jnp.concatenate(lines, axis=0).T)
    first = core_ref[0] == 0

    def put(columns, value):
        value = value.astype(jnp.bfloat16)
        low, high = value[:span], value[span:]
        mine_ref[:, columns] = jnp.where(first, low, high)
        other_ref[:, columns] = jnp.where(first, high, low)

    put(slice(0, split - 128), grad[:, : split - 128])
    put(slice(split - 128, split), router)
    put(slice(split, None), sum(dot_tn(mixed[m], attn[m][...]) for m in range(count)))


def attention_grads(core, xn1, mixed, proj, attn, gain_sums, parts):
    count, rows, width = xn1.shape
    span = width // parts
    lines = parts // 2
    columns = proj[0].shape[1] + attn[0].shape[1]
    by_line = pl.BlockSpec((count, rows, 2 * span), lambda i, c: (0, 0, i))

    def shared(part):
        return pl.BlockSpec(part.shape, lambda i, c: (0, 0))

    out_spec = pl.BlockSpec((None, span, columns), lambda i, c: (i, 0, 0))
    out_shape = jax.ShapeDtypeStruct((lines, span, columns), jnp.bfloat16)
    return pl.pallas_call(
        attention_grad_kernel,
        grid_spec=pltpu.PrefetchScalarGridSpec(
            num_scalar_prefetch=1,
            grid=(lines,),
            in_specs=[by_line, by_line]
            + [shared(p) for p in proj]
            + [shared(p) for p in attn]
            + [pl.BlockSpec((p.shape[0], 2 * span), lambda i, c: (0, i)) for p in gain_sums],
            out_specs=[out_spec, out_spec],
        ),
        out_shape=[out_shape, out_shape],
        compiler_params=pltpu.CompilerParams(vmem_limit_bytes=60 * 1024 * 1024),
        cost_estimate=SMALL_COST,
        name="attention_grads",
    )(core, xn1, mixed, *proj, *attn, *gain_sums)


def gather_blocks(part, dp_at, dp_count):
    span = part.shape[0]
    if span % 128 or dp_count != 4:
        whole = lax.all_gather(part, "dp", axis=0, tiled=True)
        return [whole], jnp.zeros((1,), jnp.int32)
    line = [(d, (d + 2) % 4) for d in range(4)]
    core = [(d, d ^ 1) for d in range(4)]
    across = lax.ppermute(part, "dp", line)
    beside = lax.ppermute(part, "dp", core)
    both = lax.ppermute(across, "dp", core)
    far = lax.rem(dp_at + 2, 4)
    owners = jnp.stack([dp_at, dp_at + 1 - 2 * lax.rem(dp_at, 2), far, far + 1 - 2 * lax.rem(far, 2)])
    return [part, beside, across, both], owners * span


def per_device(
    tokens,
    segments,
    routes,
    norm_one,
    norm_two,
    w_query,
    key_value_weight,
    w_out_attn,
    w_router,
    w_in,
    w_out,
    cotangent,
):
    micro_count, rows, width = tokens.shape
    micros = range(micro_count)
    peers = lax.axis_size("expert")
    dp_count = lax.axis_size("dp")
    local_experts = w_in.shape[0]
    experts = local_experts * peers
    capacity = rows // 4
    first_expert = lax.axis_index("expert") * local_experts
    q_width = w_query.shape[1]
    kv_width = key_value_weight.shape[1]
    proj_width = q_width + kv_width
    cosine_table, sine_values = rope_tables(rows, HEAD_SIZE)
    cos = jnp.concatenate([cosine_table, cosine_table], axis=1)
    sin = jnp.concatenate([-sine_values, sine_values], axis=1)
    order = ring_order(peers)
    spot = [order.index(dev) for dev in range(peers)]
    my_spot = jnp.array(spot, jnp.int32)[lax.axis_index("expert")]

    router_pad = jnp.zeros((w_router.shape[0], 126 - 2 * experts), jnp.bfloat16)
    first_weight = jnp.concatenate(
        [
            w_query,
            key_value_weight,
            w_router,
            w_router,
            norm_one[:, None],
            norm_two[:, None],
            router_pad,
        ],
        axis=1,
    )
    dp_at = lax.axis_index("dp").astype(jnp.int32)
    first_weights, starts = gather_blocks(first_weight, dp_at, dp_count)
    out_weights, _ = gather_blocks(w_out_attn, dp_at, dp_count)

    routes_rows = jnp.swapaxes(routes, 1, 2).reshape(-1, rows).astype(jnp.bfloat16)
    routes_rows = jnp.pad(
        routes_rows, ((0, EXTRA - routes_rows.shape[0]), (0, width - rows))
    )
    cot_rings = [
        RingGather(jnp.concatenate([cotangent[0], routes_rows], axis=0), peers, rows // 2),
        RingGather(cotangent[1], peers, rows // 2),
    ]
    steps = peers // 2
    for _ in range(steps):
        cot_rings[0].step()
    cot_rings[1].step(*cot_rings[0].got)
    first_at = first_expert.astype(jnp.int32).reshape(1)
    routes_all = cot_rings[0].stack_rows(rows, micro_count * TOPK)[:, :, :rows]
    routes_all = routes_all.reshape(peers, micro_count, TOPK, rows)
    places = [
        slot_hits(routes_all[:, m], first_expert, local_experts, capacity)
        .astype(jnp.bfloat16)
        .reshape(peers, -1, rows)
        for m in micros
    ]

    seg_col, seg_row = segments[:, :, None], segments[:, None, :]
    xn1, query, keyval, mixed, gates, gates_pack, gains = attention_forward(
        starts, tokens, seg_col, seg_row, routes, cos, sin, first_weights
    )
    cot_rings[1].step(mixed)
    mixed_late = after(mixed, *places)
    hidden, xn2 = [], []
    for m in micros:
        out = block_call(
            hidden_kernel,
            [(mixed_late, (m,)), (tokens, (m,)), (gains,), (gates_pack, (m,))]
            + [(part,) for part in out_weights],
            [
                jax.ShapeDtypeStruct((rows, width), jnp.float32),
                jax.ShapeDtypeStruct((rows + EXTRA, width), jnp.bfloat16),
            ],
            "hidden_rows",
            prefetch=starts,
        )
        hidden.append(out[0])
        xn2.append(out[1])
    every = list(range(peers))
    late = [steps - 1, steps, steps + 1]
    early = [k for k in every if k not in late]
    row_rings = [RingGather(xn2[m], peers, rows // 2) for m in micros]
    row_rings[0].step(*cot_rings[1].got)
    groups = peers // GROUP

    class Experts:
        kept = [None] * 4

        def __init__(self, m, calls):
            self.m = m
            self.calls = calls
            self.per_call = local_experts // calls
            self.outs = [[None] * 3 for _ in range(groups)]
            self.found = {}

        def pick_grads(self):
            place = places[self.m]
            self.grads = pick_rows(first_at, place, cot_rings[self.m], every, False)
            return self.grads[0]

        def pick(self, distances):
            out = pick_rows(first_at, places[self.m], row_rings[self.m], distances, True)
            self.found.update(zip(distances, zip(out, out[len(distances) :])))
            self.rows = [self.found[k][0] for k in every if k in self.found]
            self.gate_slots = [self.found[k][1] for k in every if k in self.found]
            return out[0]

        def call(self, number, *earlier):
            for g in range(groups):
                span = slice(g * GROUP, (g + 1) * GROUP)
                here = self.rows[span]
                here[0] = after(here[0], *earlier) if earlier else here[0]
                done = expert_pass(
                    here,
                    self.grads[span],
                    self.gate_slots[span],
                    w_in,
                    w_out,
                    self.outs[g] + Experts.kept,
                    (self.m * groups + g, micro_count * groups),
                    number * self.per_call,
                    self.per_call,
                )
                self.outs[g], Experts.kept = list(done[:3]), list(done[3:])
            return done[2]

        def spread(self, spans, *earlier):
            place = places[self.m]
            place = after(place, *earlier) if earlier else place
            self.sums = None
            for g in range(groups):
                out = spread_rows(first_at, place, *self.outs[g], g, spans, self.sums)
                self.sums = out[0]
                if g == groups // 2:
                    far = out[1:]
            return far

    calls = 2
    first, second = Experts(0, calls), Experts(1, calls)
    ring, ring_next, cot_next = row_rings[0], row_rings[1], cot_rings[1]
    first_whole = join_blocks(starts, [after(first_weights[0], xn2[1])] + first_weights[1:])
    out_whole = join_blocks(starts, [after(out_weights[0], first_whole)] + out_weights[1:])
    while len(ring.from_left) < steps - 1:
        ring.step(xn2[1], out_whole)
    ring.step(first.pick_grads())
    ring.step(first.pick(early))
    first.pick(late)
    ring_next.step(*ring.got)
    cot_next.step(*ring.got)
    token = first.call(0)
    for number in range(1, calls):
        got = ring_next.got + cot_next.got
        ring_next.step(token)
        cot_next.step(token)
        token = first.call(number, *got)
    block = rows + EXTRA
    got = ring_next.got + cot_next.got
    while cot_next.far is None:
        cot_next.step(token)
    while len(ring_next.from_left) < steps:
        ring_next.step(token)
    far = first.spread([(0, block), (block, rows)], *got)
    got = ring_next.got
    while ring_next.far is None:
        ring_next.step()
    ring_first = RingScatter(lambda k: first.sums[k], far, peers)
    ring_first.step(*got)
    second.pick_grads()
    second.pick(early)
    second.pick(late)
    token = second.call(0)
    for number in range(1, calls):
        ring_first.step(token)
        token = second.call(number, *ring_first.sent)
    half = rows // 2
    spans = [(0, half), (half, block - half), (block, half), (block + half, half)]
    far = second.spread(spans)
    ring_grads = RingScatter(lambda k: second.sums[k, :block], far[:2], peers)
    ring_results = RingScatter(lambda k: second.sums[k, block:], far[2:], peers)
    ring_grads.step()
    picked, grad_result, activated, grad_pre = Experts.kept
    place_at = jnp.stack([lax.rem(dp_at, 2), dp_at // 2])
    ring_grads.step()
    w_out_sum = weight_grads(
        after(activated, *ring_grads.sent, *ring_first.got), grad_result, 0, local_experts, None
    )
    def backward(m, pieces, *earlier):
        own, left, right = pieces
        return block_call(
            backward_kernel,
            [
                (after(own, *earlier), (0,), block),
                (left, (), block),
                (right, (), block),
                (cotangent, (m,)),
                (hidden[m],),
                (tokens, (m,)),
                (query, (m,)),
                (keyval, (m,)),
                (seg_col, (m,)),
                (seg_row, (m,)),
                (gates, (m,)),
                (gains,),
                (cos,),
                (sin,),
                (first_whole,),
                (out_whole,),
            ],
            [
                jax.ShapeDtypeStruct((rows, width), jnp.bfloat16),
                jax.ShapeDtypeStruct((rows, proj_width + 128), jnp.bfloat16),
                jax.ShapeDtypeStruct((rows, width), jnp.bfloat16),
                jax.ShapeDtypeStruct((8, width), jnp.float32),
            ],
            "attention_backward",
            [pltpu.VMEM((rows, q_width), jnp.bfloat16)],
        )

    half = max(1, local_experts // 2)
    got = ring_grads.got
    ring_grads.step(w_out_sum)
    picked = after(picked, w_out_sum, *got, *ring_grads.sent)
    while ring_first.at > 1:
        ring_first.step(w_out_sum)
    picked = after(picked, *ring_first.sent)
    w_in_sum = weight_grads(picked, grad_pre, 0, half, None)
    while ring_grads.at > 0:
        got = ring_grads.got
        ring_grads.step(w_in_sum)
    last = ring_first.got
    while ring_first.at > 0:
        ring_first.step(*ring_grads.sent)
    picked = after(picked, w_in_sum, *got, *ring_grads.sent, *ring_first.sent)
    w_in_sum = weight_grads(picked, grad_pre, half, local_experts - half, w_in_sum)
    got = last
    ring_results.step(*got)
    grad_w_in, grad_w_out = [
        lax.psum_scatter(
            after(part, w_in_sum, *ring_grads.got), "dp", scatter_dimension=1, tiled=True
        )
        for part in (w_in_sum, w_out_sum)
    ]
    back_second = backward(1, (second.sums, ring_grads.left, ring_grads.right), *ring_first.sent)
    ring_results.step(back_second[3], *got)
    back_first = backward(
        0, (first.sums, ring_first.left, ring_first.right), *ring_results.sent
    )
    ring_results.step(back_first[3])
    grad_tokens, grad_proj, grad_attn, gain_sums = zip(back_first, back_second)
    mine, other = attention_grads(
        place_at, after(xn1, *ring_results.sent), mixed, grad_proj, grad_attn, gain_sums, dp_count
    )
    grads, grad_w_in, grad_w_out = reduce_packed(
        mine, other, my_spot, peers, dp_count, grad_w_in, grad_w_out, ring_results, (q_width, kv_width)
    )
    grad_query, grad_keyval, grad_small, grad_attn_out = grads
    wide = jnp.float32
    outputs = []
    for m, (own, ring, at) in enumerate(
        ((first.sums, ring_first, block), (second.sums, ring_results, 0))
    ):
        total = hidden[m] + own[0, block:].astype(wide)
        total = total + ring.left[at:].astype(wide) + ring.right[at:].astype(wide)
        outputs.append(total.astype(jnp.bfloat16))
    return (
        jnp.stack(outputs),
        jnp.stack(grad_tokens),
        grad_small[:, experts],
        grad_small[:, experts + 1],
        grad_query,
        grad_keyval,
        grad_attn_out,
        grad_small[:, :experts],
        grad_w_in,
        grad_w_out,
    )


def last_kernel(spot_ref, *refs):
    outs = refs[-4:]
    blocks = refs[:-4]
    peers = len(blocks) - 1
    piece = blocks[0].shape[0]
    for k, block_ref in enumerate(blocks):
        distance = k if k <= peers // 2 else k - 1
        spot = lax.rem(spot_ref[0] - distance + peers, peers)
        held = block_ref.shape[0]
        row = spot * piece + (held if k == peers // 2 + 1 else 0)
        at = 0
        for out_ref in outs:
            columns = out_ref.shape[1]
            out_ref[pl.ds(pl.multiple_of(row, 8), held), :] = block_ref[
                :, at : at + columns
            ].astype(jnp.float32)
            at += columns


def reduce_packed(mine, other, my_spot, peers, dp_count, grad_w_in, grad_w_out, ring_results, widths):
    lines, span, columns = mine.shape
    swap = [(d, d ^ 1) for d in range(dp_count)]
    got = ring_results.got
    while ring_results.at > 0:
        ring_results.step()
    swapped = after(lax.ppermute(other, "dp", swap), *got, *ring_results.sent)
    piece = span // peers
    shape = (lines, peers, piece, columns)
    mine, swapped = mine.reshape(shape), swapped.reshape(shape)

    def part(k):
        at = lax.rem(my_spot - k + peers, peers)
        both = [
            lax.dynamic_slice_in_dim(held, at, 1, axis=1).astype(jnp.float32)
            for held in (mine, swapped)
        ]
        return (both[0] + both[1]).reshape(lines * piece, columns)

    half = lines * piece // 2
    farthest = part(peers // 2).astype(jnp.bfloat16)
    ring = RingScatter(part, (farthest[:half], farthest[half:]), peers)
    ring.step()
    while ring.at > 0:
        ring.step()
    own, left, right = [held.astype(jnp.float32) for held in (part(0), ring.left, ring.right)]
    mine = (own + left + right).astype(jnp.bfloat16).reshape(lines, piece, columns)
    line = lax.axis_index("dp") // 2

    def for_line(at):
        return lax.dynamic_index_in_dim(mine, lax.rem(at, lines), 0, keepdims=False)

    share = for_line(line).astype(jnp.float32)
    for k in range(1, lines):
        pairs = [(d, (d + 2 * k) % dp_count) for d in range(dp_count)]
        share = share + lax.ppermute(for_line(line + k), "dp", pairs)
    gather = RingGather(share.astype(jnp.bfloat16), peers, piece // 2)
    gather.step()
    grad_w_out = grad_w_out.astype(jnp.float32)
    gather.step(grad_w_out)
    grad_w_in = grad_w_in.astype(jnp.float32)
    gather.step(grad_w_in, *ring_results.got)
    while gather.far is None:
        gather.step()
    blocks = gather.from_left + list(gather.far) + gather.from_right[:0:-1]
    columns = (widths[0], widths[1], 128, columns - sum(widths) - 128)
    if piece % 16 == 0:
        grads = block_call(
            last_kernel,
            [(block,) for block in blocks],
            [jax.ShapeDtypeStruct((span, count), jnp.float32) for count in columns],
            "last_rows",
            prefetch=my_spot.astype(jnp.int32).reshape(1),
        )
    else:
        far = jnp.concatenate(gather.far, axis=0)
        by_distance = jnp.stack(gather.from_left + [far] + gather.from_right[:0:-1])
        distance = lax.rem(my_spot - jnp.arange(peers, dtype=jnp.int32) + peers, peers)
        by_spot = jnp.take(by_distance, distance, axis=0).reshape(span, -1).astype(jnp.float32)
        edges = [sum(columns[:i]) for i in range(5)]
        grads = [by_spot[:, edges[i] : edges[i + 1]] for i in range(4)]
    return grads, grad_w_in, grad_w_out


def solution(mesh):
    return jax.shard_map(
        per_device,
        mesh=mesh,
        in_specs=(
            P(None, ("dp", "expert"), None),
            P(None, ("dp", "expert")),
            P(None, ("dp", "expert"), None),
            P("dp"),
            P("dp"),
            P("dp", None),
            P("dp", None),
            P("dp", None),
            P("dp", None),
            P("expert", None, None),
            P("expert", None, None),
            P(None, ("dp", "expert"), None),
        ),
        out_specs=(
            P(None, ("dp", "expert"), None),
            P(None, ("dp", "expert"), None),
            P("dp"),
            P("dp"),
            P("dp", None),
            P("dp", None),
            P("dp", None),
            P("dp", None),
            P("expert", "dp", None),
            P("expert", "dp", None),
        ),
        check_vma=False,
    )
```

```python
import functools
import math

import jax
import jax.numpy as jnp
from jax import lax
from jax.experimental import pallas as pl
from jax.experimental.pallas import tpu as pltpu
from jax.sharding import PartitionSpec as P

QUERY_HEADS = 12
KEY_VALUE_HEADS = 2
HEAD_SIZE = 128
FF = 768
TOPK = 4
EXPERTS = 32
EXTRA = 16
PIECES = 3
GROUP = 8

eps_norm = 1e-06
rope_base = 1000000.0
mask_fill = -1e30
highest = lax.Precision.HIGHEST


def rms_scale(tensor):
    return lax.rsqrt(jnp.mean(tensor * tensor, axis=-1, keepdims=True) + eps_norm)


def rope_tables(sequence_length, head_width):
    positions = jnp.arange(sequence_length).astype(jnp.float32)
    frequency = rope_base ** (-(jnp.arange(head_width // 2).astype(jnp.float32) * 2.0) / head_width)
    angles = positions[:, None] * frequency[None, :]
    return (jnp.cos(angles), jnp.sin(angles))

SCORE_SCALE = 1.0 / math.sqrt(HEAD_SIZE)
GELU_SCALE = math.sqrt(2.0 / math.pi)
GELU_CUBE = 0.044715
SMALL_COST = pl.CostEstimate(flops=1_000_000, bytes_accessed=1_000_000, transcendentals=0)


def after(value, *earlier):
    return lax.optimization_barrier((value,) + earlier)[0]


def slot_hits(routes_all, first_expert, local_experts, capacity):
    rows = routes_all.shape[-1]
    names = first_expert + jnp.arange(local_experts, dtype=jnp.int32)
    named = routes_all[:, None].astype(jnp.int32) == names[None, :, None, None]
    member = jnp.any(named, axis=2)
    lower = (jnp.arange(rows)[:, None] < jnp.arange(rows)[None, :]).astype(jnp.bfloat16)
    rank = dot32(member.astype(jnp.bfloat16).reshape(-1, rows), lower).reshape(member.shape)
    slots = jnp.arange(capacity, dtype=jnp.float32)
    return member[:, :, None, :] & (rank[:, :, None, :] == slots[None, None, :, None])


def pack_pieces(values, out_ref, first_row):
    rows = values.shape[1]
    rest = values
    for piece in range(PIECES):
        part = rest.astype(jnp.bfloat16)
        rest = rest - part.astype(jnp.float32)
        for half in range(EXPERTS // EXTRA):
            at = (piece * (EXPERTS // EXTRA) + half) * rows
            out_ref[first_row : first_row + EXTRA, at : at + rows] = part[
                half * EXTRA : (half + 1) * EXTRA
            ]


def dot32(left, right):
    return jnp.dot(left, right, preferred_element_type=jnp.float32)


def dot_nt(left, right):
    return lax.dot_general(
        left, right, (((1,), (1,)), ((), ())), preferred_element_type=jnp.float32
    )


def dot_tn(left, right):
    return lax.dot_general(
        left, right, (((0,), (0,)), ((), ())), preferred_element_type=jnp.float32
    )


def mask_of(seg_col, seg_row):
    rows = seg_col.shape[0]
    query_at = lax.broadcasted_iota(jnp.int32, (rows, rows), 0)
    key_at = lax.broadcasted_iota(jnp.int32, (rows, rows), 1)
    return (seg_col == seg_row) & (query_at >= key_at)


def softmax_rows(query, key, allowed):
    scores = jnp.where(allowed, dot_nt(query, key) * SCORE_SCALE, mask_fill)
    weight = jnp.exp(scores - jnp.max(scores, axis=-1, keepdims=True))
    return weight / jnp.sum(weight, axis=-1, keepdims=True)


def from_blocks(starts_ref, rows_ref, blocks):
    total = None
    for at, block_ref in enumerate(blocks):
        span = block_ref.shape[0]
        columns = pl.ds(pl.multiple_of(starts_ref[at], 128), span)
        part = dot32(rows_ref[:, columns], block_ref[...])
        total = part if total is None else total + part
    return total


def attention_kernel(
    starts_ref,
    tok_ref,
    seg_col_ref,
    seg_row_ref,
    routes_ref,
    cos_ref,
    sin_ref,
    *refs,
):
    weight_refs = refs[:-7]
    xn1_ref, query_ref, keyval_ref, mixed_ref, gates_ref, gates_pack_ref, gains_ref = refs[-7:]

    @pl.when(pl.program_id(0) == 0)
    def _():
        for at, block_ref in enumerate(weight_refs):
            span, columns = block_ref.shape
            pad = block_ref[:, columns - 128 :].astype(jnp.float32).T
            place = pl.ds(pl.multiple_of(starts_ref[at], 128), span)
            gains_ref[:, place] = pad[2 * EXPERTS : 2 * EXPERTS + 8]

    tok = tok_ref[...].astype(jnp.float32)
    xn1_ref[...] = (tok * rms_scale(tok) * gains_ref[0:1, :]).astype(jnp.bfloat16)
    proj = from_blocks(starts_ref, xn1_ref, weight_refs)
    cos, sin = cos_ref[...], sin_ref[...]

    def rotate(part):
        return (part * cos + pltpu.roll(part, HEAD_SIZE // 2, 1) * sin).astype(jnp.bfloat16)

    q_width = QUERY_HEADS * HEAD_SIZE
    k_width = KEY_VALUE_HEADS * HEAD_SIZE
    for head in range(QUERY_HEADS):
        span = slice(head * HEAD_SIZE, (head + 1) * HEAD_SIZE)
        query_ref[:, span] = rotate(proj[:, span])
    for head in range(KEY_VALUE_HEADS):
        span = slice(head * HEAD_SIZE, (head + 1) * HEAD_SIZE)
        keyval_ref[:, span] = rotate(proj[:, q_width:][:, span])
    keyval_ref[:, k_width:] = proj[:, q_width + k_width : q_width + 2 * k_width].astype(
        jnp.bfloat16
    )
    logits = proj[:, q_width + 2 * k_width :]
    columns = lax.broadcasted_iota(jnp.int32, logits.shape, 1)
    named = [columns == routes_ref[:, j : j + 1] for j in range(TOPK)]
    chosen = [jnp.sum(jnp.where(hit, logits, 0.0), axis=-1, keepdims=True) for hit in named]
    top = functools.reduce(jnp.maximum, chosen)
    weight = [jnp.exp(part - top) for part in chosen]
    total = functools.reduce(jnp.add, weight)
    gates = jnp.full(logits.shape, -1.0, jnp.float32)
    for hit, part in zip(named, weight):
        gates = jnp.where(hit, part / total, gates)
    gates_ref[...] = gates
    pack_pieces(gates.T[:EXPERTS], gates_pack_ref, 0)
    allowed = mask_of(seg_col_ref[...], seg_row_ref[...])
    for head in range(QUERY_HEADS):
        span = slice(head * HEAD_SIZE, (head + 1) * HEAD_SIZE)
        group = head // (QUERY_HEADS // KEY_VALUE_HEADS)
        key = keyval_ref[:, group * HEAD_SIZE : (group + 1) * HEAD_SIZE]
        value = keyval_ref[:, k_width + group * HEAD_SIZE : k_width + (group + 1) * HEAD_SIZE]
        probs = softmax_rows(query_ref[:, span], key, allowed)
        mixed_ref[:, span] = dot32(probs.astype(jnp.bfloat16), value).astype(jnp.bfloat16)


def hidden_kernel(starts_ref, mixed_ref, tok_ref, gains_ref, pack_ref, *refs):
    weight_refs = refs[:-2]
    hidden_ref, xn2_ref = refs[-2:]
    rows = tok_ref.shape[0]
    hidden = tok_ref[...].astype(jnp.float32) + from_blocks(
        starts_ref, mixed_ref, weight_refs
    )
    hidden_ref[...] = hidden
    xn2_ref[:rows, :] = (hidden * rms_scale(hidden) * gains_ref[1:2, :]).astype(jnp.bfloat16)
    xn2_ref[rows:, :] = pack_ref[...]


def backward_kernel(
    own_ref,
    left_ref,
    right_ref,
    cot_ref,
    hidden_ref,
    tok_ref,
    query_ref,
    keyval_ref,
    seg_col_ref,
    seg_row_ref,
    gates_ref,
    gains_ref,
    cos_ref,
    sin_ref,
    *refs,
):
    weight_ref, out_weight_ref = refs[:2]
    grad_tok_ref, grad_proj_ref, grad_attn_ref, gain_sum_ref, mixed_grad_ref = refs[2:]
    width = tok_ref.shape[1]
    q_width = QUERY_HEADS * HEAD_SIZE
    k_width = KEY_VALUE_HEADS * HEAD_SIZE
    proj_width = q_width + 2 * k_width
    rows = tok_ref.shape[0]
    sums = [ref[...].astype(jnp.float32) for ref in (own_ref, left_ref, right_ref)]
    sums = sums[0] + sums[1] + sums[2]
    grad_xn2, pack = sums[:rows], sums[rows:]
    halves = EXPERTS // EXTRA
    lines = [
        sum(
            pack[:, (piece * halves + half) * rows : (piece * halves + half + 1) * rows]
            for piece in range(PIECES)
        )
        for half in range(halves)
    ]
    lines.append(jnp.zeros((128 - EXPERTS, rows), jnp.float32))
    grad_gates = jnp.concatenate(lines, axis=0).T
    hidden = hidden_ref[...]
    scale = rms_scale(hidden)
    unit = hidden * scale
    gain_sum_ref[...] = jnp.zeros(gain_sum_ref.shape, jnp.float32)
    gain_sum_ref[1:2, :] = jnp.sum(grad_xn2 * unit, axis=0, keepdims=True)
    grad_unit = grad_xn2 * gains_ref[1:2, :]
    grad_hidden = cot_ref[...].astype(jnp.float32) + scale * (
        grad_unit - unit * jnp.mean(grad_unit * unit, axis=-1, keepdims=True)
    )
    grad_attn_ref[...] = grad_hidden.astype(jnp.bfloat16)
    mixed_grad_ref[...] = dot_nt(grad_attn_ref[...], out_weight_ref[...]).astype(jnp.bfloat16)
    cos, sin = cos_ref[...], sin_ref[...]

    def unrotate(part):
        return (part * cos - pltpu.roll(part, HEAD_SIZE // 2, 1) * sin).astype(jnp.bfloat16)

    allowed = mask_of(seg_col_ref[...], seg_row_ref[...])
    per_group = QUERY_HEADS // KEY_VALUE_HEADS
    for group in range(KEY_VALUE_HEADS):
        key_span = slice(group * HEAD_SIZE, (group + 1) * HEAD_SIZE)
        value_span = slice(k_width + group * HEAD_SIZE, k_width + (group + 1) * HEAD_SIZE)
        key, value = keyval_ref[:, key_span], keyval_ref[:, value_span]
        grad_key = jnp.zeros(key.shape, jnp.float32)
        grad_value = jnp.zeros(key.shape, jnp.float32)
        for head in range(group * per_group, (group + 1) * per_group):
            span = slice(head * HEAD_SIZE, (head + 1) * HEAD_SIZE)
            query, grad_mixed = query_ref[:, span], mixed_grad_ref[:, span]
            probs = softmax_rows(query, key, allowed)
            grad_value += dot_tn(probs.astype(jnp.bfloat16), grad_mixed)
            grad_probs = dot_nt(grad_mixed, value)
            mean = jnp.sum(probs * grad_probs, axis=-1, keepdims=True)
            grad_scores = (probs * (grad_probs - mean)).astype(jnp.bfloat16)
            grad_proj_ref[:, span] = unrotate(dot32(grad_scores, key) * SCORE_SCALE)
            grad_key += dot_tn(grad_scores, query)
        grad_proj_ref[:, q_width + group * HEAD_SIZE : q_width + (group + 1) * HEAD_SIZE] = (
            unrotate(grad_key * SCORE_SCALE)
        )
        first = q_width + k_width + group * HEAD_SIZE
        grad_proj_ref[:, first : first + HEAD_SIZE] = grad_value.astype(jnp.bfloat16)
    gates = jnp.maximum(gates_ref[...], 0.0)
    grad_logits = gates * (grad_gates - jnp.sum(gates * grad_gates, axis=-1, keepdims=True))
    high = grad_logits.astype(jnp.bfloat16).astype(jnp.float32)
    low = pltpu.roll(grad_logits - high, EXPERTS, 1)
    grad_proj_ref[:, proj_width:] = (high + low).astype(jnp.bfloat16)
    grad_xn1 = dot_nt(grad_proj_ref[...], weight_ref[...])
    tok = tok_ref[...].astype(jnp.float32)
    scale = rms_scale(tok)
    unit = tok * scale
    gain_sum_ref[0:1, :] = jnp.sum(grad_xn1 * unit, axis=0, keepdims=True)
    grad_unit = grad_xn1 * gains_ref[0:1, :]
    grad_tok_ref[...] = (
        grad_hidden
        + scale * (grad_unit - unit * jnp.mean(grad_unit * unit, axis=-1, keepdims=True))
    ).astype(jnp.bfloat16)


def ring_order(peers):
    minor = peers // 4
    walk = []
    for col in range(minor):
        line = range(4) if col % 2 == 0 else range(3, -1, -1)
        walk += [row * minor + col for row in line]
    return walk


def ring_step(part, shift, peers):
    order = ring_order(peers)
    pairs = [(order[i], order[(i + shift) % peers]) for i in range(peers)]
    return lax.ppermute(part, "expert", pairs)


class RingGather:
    def __init__(self, part, peers, half):
        self.peers, self.half = peers, half
        self.from_left, self.from_right = [part], [part]
        self.far = None
        self.got = ()

    def step(self, *earlier):
        left, right = self.from_left[-1], self.from_right[-1]
        last = len(self.from_left) == self.peers // 2
        if last:
            left, right = left[: self.half], right[self.half :]
        left, right = self.sent = lax.optimization_barrier((left, right) + earlier)[:2]
        left, right = ring_step(left, 1, self.peers), ring_step(right, -1, self.peers)
        self.got = (left, right)
        if last:
            self.far = (left, right)
        else:
            self.from_left.append(left)
            self.from_right.append(right)
        return self

    def rows(self, k, first, count):
        if k < len(self.from_left):
            return self.from_left[k], first
        if k > self.peers // 2:
            return self.from_right[self.peers - k], first
        if first < self.half:
            return self.far[0], first
        return self.far[1], first - self.half

    def stack_rows(self, first, count):
        found = [self.rows(k, first, count) for k in range(self.peers)]
        return jnp.stack([array[at : at + count] for array, at in found])


class RingScatter:
    def __init__(self, part, far, peers):
        self.part, self.far, self.peers = part, far, peers
        self.at = peers // 2
        self.half = far[0].shape[0]

    def step(self, *earlier):
        peers, k, half = self.peers, self.at, self.half
        if k == peers // 2:
            left, right = lax.optimization_barrier(tuple(self.far) + earlier)[:2]
        else:
            left, right = self.part(k), self.part(peers - k)
            if earlier:
                self.left, self.right = lax.optimization_barrier(
                    (self.left, self.right) + earlier
                )[:2]
            if k == peers // 2 - 1:
                kept = left[half:].astype(jnp.bfloat16), right[:half].astype(jnp.bfloat16)
                left = jnp.concatenate([add_rows(left[:half], self.left), kept[0]], axis=0)
                right = jnp.concatenate([kept[1], add_rows(right[half:], self.right)], axis=0)
            else:
                left, right = add_rows(left, self.left), add_rows(right, self.right)
        left, right = self.sent = lax.optimization_barrier((left, right))
        self.left = ring_step(left, -1, peers)
        self.right = ring_step(right, 1, peers)
        self.got = (self.left, self.right)
        self.at = k - 1
        return self


def add_rows(left, right):
    return (left.astype(jnp.float32) + right.astype(jnp.float32)).astype(jnp.bfloat16)


def expert_kernel(sources, *refs):
    rows_refs = refs[:sources]
    grad_refs = refs[sources : 2 * sources]
    gate_refs = refs[2 * sources : 3 * sources]
    w_in_ref, w_out_ref = refs[3 * sources : 3 * sources + 2]
    (
        back_rows_ref,
        back_grads_ref,
        grad_gate_ref,
        picked_ref,
        grad_result_ref,
        activated_ref,
        grad_pre_ref,
    ) = refs[-7:]
    capacity, width = rows_refs[0].shape
    for k in range(sources):
        picked_ref[pl.ds(k * capacity, capacity), :] = rows_refs[k][...]
    pre_act = dot32(picked_ref[...], w_in_ref[...])
    gate_part = pre_act[:, :FF]
    up_part = pre_act[:, FF:]
    square = gate_part * gate_part
    bend = jnp.tanh(GELU_SCALE * gate_part * (1.0 + GELU_CUBE * square))
    lift = 0.5 * (1.0 + bend)
    gelu_val = gate_part * lift
    slope = lift + 0.5 * gate_part * (1.0 - bend * bend) * (
        GELU_SCALE * (1.0 + 3.0 * GELU_CUBE * square)
    )
    activated_ref[...] = (gelu_val * up_part).astype(jnp.bfloat16)
    result = dot32(activated_ref[...], w_out_ref[...])
    for k in range(sources):
        gates = gate_refs[k][...]
        span = slice(k * capacity, (k + 1) * capacity)
        grad_rows = grad_refs[k][...].astype(jnp.float32)
        grad_gate_ref[span, :] = jnp.sum(result[span] * grad_rows, axis=-1, keepdims=True)
        back_rows_ref[k] = (result[span] * gates).astype(jnp.bfloat16)
        grad_result_ref[span, :] = (grad_rows * gates).astype(jnp.bfloat16)
    grad_act = lax.dot_general(
        grad_result_ref[...],
        w_out_ref[...],
        (((1,), (1,)), ((), ())),
        preferred_element_type=jnp.float32,
    )
    grad_pre_ref[:, :FF] = (grad_act * up_part * slope).astype(jnp.bfloat16)
    grad_pre_ref[:, FF:] = (grad_act * gelu_val).astype(jnp.bfloat16)
    grad_in = lax.dot_general(
        grad_pre_ref[...],
        w_in_ref[...],
        (((1,), (1,)), ((), ())),
        preferred_element_type=jnp.float32,
    ).astype(jnp.bfloat16)
    for k in range(sources):
        back_grads_ref[k] = grad_in[k * capacity : (k + 1) * capacity]


def expert_pass(rows_list, grads_list, gate_slots, w_in, w_out, held_outs, position, first, count):
    sources = len(rows_list)
    local_experts, width, _ = w_in.shape
    slots = rows_list[0].shape[0]
    capacity = slots // local_experts
    held = sources * capacity
    block_spec = pl.BlockSpec((capacity, width), lambda e: (e + first, 0))
    back_spec = pl.BlockSpec((sources, capacity, width), lambda e: (0, e + first, 0))
    column_spec = pl.BlockSpec((None, held, 1), lambda e: (e + first, 0, 0))

    def kept_spec(columns):
        return pl.BlockSpec((None, held, columns), lambda e: (e + first, position[0], 0))

    def kept_shape(columns):
        return jax.ShapeDtypeStruct((local_experts, position[1] * held, columns), jnp.bfloat16)

    kept_widths = (width, width, FF, 2 * FF)
    first_held = 3 * sources + 2
    given = [(i, part) for i, part in enumerate(held_outs) if part is not None]
    return pl.pallas_call(
        functools.partial(expert_kernel, sources),
        grid=(count,),
        in_specs=[block_spec] * (2 * sources)
        + [pl.BlockSpec((capacity, 1), lambda e: (e + first, 0))] * sources
        + [
            pl.BlockSpec((None, width, 2 * FF), lambda e: (e + first, 0, 0)),
            pl.BlockSpec((None, FF, width), lambda e: (e + first, 0, 0)),
        ]
        + [pl.BlockSpec(memory_space=pl.ANY)] * len(given),
        out_specs=[back_spec, back_spec, column_spec] + [kept_spec(c) for c in kept_widths],
        out_shape=[
            jax.ShapeDtypeStruct((sources, slots, width), jnp.bfloat16),
            jax.ShapeDtypeStruct((sources, slots, width), jnp.bfloat16),
            jax.ShapeDtypeStruct((local_experts, held, 1), jnp.float32),
        ]
        + [kept_shape(c) for c in kept_widths],
        input_output_aliases={first_held + at: i for at, (i, _) in enumerate(given)},
        compiler_params=pltpu.CompilerParams(vmem_limit_bytes=60 * 1024 * 1024),
        cost_estimate=SMALL_COST,
        name="expert_pass",
    )(*rows_list, *grads_list, *gate_slots, w_in, w_out, *[part for _, part in given])


def block_call(kernel, operands, out_shape, name, scratch=(), prefetch=None):
    def spec(array, lead=(), rows=None):
        rest = array.shape[len(lead) :]
        at = lead + (0,) * len(rest)
        if rows is not None:
            count, block = rows if isinstance(rows, tuple) else (rows, 0)
            rest = (count,) + rest[1:]
            at = lead + (block,) + (0,) * (len(rest) - 1)
        return pl.BlockSpec((None,) * len(lead) + rest, lambda *_: at)

    scalars = [] if prefetch is None else [prefetch]
    return pl.pallas_call(
        kernel,
        grid_spec=pltpu.PrefetchScalarGridSpec(
            num_scalar_prefetch=len(scalars),
            grid=(1,),
            in_specs=[spec(*operand) for operand in operands],
            out_specs=[spec(shape) for shape in out_shape],
            scratch_shapes=list(scratch),
        ),
        out_shape=out_shape,
        compiler_params=pltpu.CompilerParams(vmem_limit_bytes=60 * 1024 * 1024),
        cost_estimate=SMALL_COST,
        name=name,
    )(*scalars, *[operand[0] for operand in operands])


def pick_kernel(shares, gated, first_ref, place_ref, *refs):
    at = 0
    outs = refs[sum(count for _, count in shares) + (len(shares) if gated else 0) :]
    for number, (k, count) in enumerate(shares):
        total, row = None, 0
        for block_ref in refs[at : at + count]:
            held = block_ref.shape[0]
            part = dot32(place_ref[k, :, row : row + held], block_ref[...])
            total = part if total is None else total + part
            row += held
        outs[number][...] = total.astype(jnp.bfloat16)
        at += count
        if gated:
            slot_gates(first_ref[0], place_ref[k], refs[at], outs[len(shares) + number])
            at += 1


def slot_gates(first_expert, place, pack_ref, out_ref):
    slots, rows = place.shape
    pack = pack_ref[...].astype(jnp.float32)
    halves = EXPERTS // EXTRA
    line = lax.broadcasted_iota(jnp.int32, (EXTRA, rows), 0)
    local_experts = slots * 4 // rows
    capacity = rows // 4
    for e in range(local_experts):
        gate = jnp.zeros((1, rows), jnp.float32)
        for half in range(halves):
            hit = line + half * EXTRA == first_expert + e
            for piece in range(PIECES):
                at = (piece * halves + half) * rows
                gate += jnp.sum(
                    jnp.where(hit, pack[:, at : at + rows], 0.0), axis=0, keepdims=True
                )
        span = slice(e * capacity, (e + 1) * capacity)
        out_ref[span, :] = jnp.sum(
            place[span].astype(jnp.float32) * gate, axis=-1, keepdims=True
        )


def pick_rows(first_expert, place, ring, distances, gated):
    _, slots, rows = place.shape
    half = rows // 2
    operands, shares = [], []
    for k in distances:
        spans = [(0, rows)]
        if k == ring.peers // 2 and ring.half < rows:
            spans = [(0, half), (half, half)]
        shares.append((k, len(spans)))
        for at, count in spans + ([(rows, EXTRA)] if gated else []):
            array, at = ring.rows(k, at, count)
            operands.append((array, (), (count, at // count)))
    width = operands[0][0].shape[-1]
    out_shape = [jax.ShapeDtypeStruct((slots, width), jnp.bfloat16) for _ in distances]
    if gated:
        out_shape += [jax.ShapeDtypeStruct((slots, 1), jnp.float32) for _ in distances]
    return block_call(
        functools.partial(pick_kernel, shares, gated),
        [(place,)] + operands,
        out_shape,
        "pick_rows",
        prefetch=first_expert,
    )


def spread_kernel(middle, spans, held, first_ref, place_ref, rows_ref, grads_ref, gate_ref, *refs):
    out_ref, *far_refs = refs[held:]
    place = place_ref[...]
    rows = place.shape[1]
    out_ref[:rows, :] = dot_tn(place, grads_ref[...]).astype(jnp.bfloat16)
    out_ref[rows + EXTRA :, :] = dot_tn(place, rows_ref[...]).astype(jnp.bfloat16)
    capacity = gate_ref.shape[1]
    expert = lax.broadcasted_iota(jnp.int32, (EXPERTS, rows), 0) - first_ref[0]
    gates = jnp.zeros((EXPERTS, rows), jnp.float32)
    for e in range(gate_ref.shape[0]):
        hit = place[e * capacity : (e + 1) * capacity].astype(jnp.float32)
        line = jnp.sum(hit * gate_ref[e], axis=0, keepdims=True)
        gates = jnp.where(expert == e, line, gates)
    pack_pieces(gates, out_ref, rows)

    @pl.when(pl.program_id(0) == middle)
    def _():
        for far_ref, (row, count) in zip(far_refs, spans):
            far_ref[...] = out_ref[row : row + count, :]


def spread_rows(first_expert, place, rows_back, grads_back, gate_slots, group, spans, held):
    sources, slots, rows = place.shape
    width = rows_back.shape[-1]
    local_experts = gate_slots.shape[0]
    base = group * GROUP
    by_source = pl.BlockSpec((None, slots, width), lambda k, f: (k, 0, 0))
    held = [] if held is None else [held]
    out_shape = [jax.ShapeDtypeStruct((sources, 2 * rows + EXTRA, width), jnp.bfloat16)]
    out_shape += [jax.ShapeDtypeStruct((count, width), jnp.bfloat16) for _, count in spans]
    out_specs = [pl.BlockSpec((None, 2 * rows + EXTRA, width), lambda k, f: (base + k, 0, 0))]
    out_specs += [pl.BlockSpec((count, width), lambda k, f: (0, 0)) for _, count in spans]
    return pl.pallas_call(
        functools.partial(spread_kernel, sources // 2 - base, spans, len(held)),
        grid_spec=pltpu.PrefetchScalarGridSpec(
            num_scalar_prefetch=1,
            grid=(GROUP,),
            in_specs=[
                pl.BlockSpec((None, slots, rows), lambda k, f: (base + k, 0, 0)),
                by_source,
                by_source,
                pl.BlockSpec((local_experts, slots // local_experts, 1), lambda k, f: (0, k, 0)),
            ]
            + [pl.BlockSpec(memory_space=pl.ANY)] * len(held),
            out_specs=out_specs,
        ),
        out_shape=out_shape,
        input_output_aliases={5 + i: i for i in range(len(held))},
        compiler_params=pltpu.CompilerParams(vmem_limit_bytes=60 * 1024 * 1024),
        cost_estimate=SMALL_COST,
        name="spread_rows",
    )(first_expert, place, rows_back, grads_back, gate_slots, *held)


def weight_grad_kernel(left_ref, right_ref, *refs):
    refs[-1][...] = dot_tn(left_ref[...], right_ref[...]).astype(jnp.bfloat16)


def weight_grads(left, right, first, count, held_out):
    experts, held, height = left.shape
    columns = right.shape[-1]
    tile = min(height, 768)
    given = [] if held_out is None else [held_out]
    return pl.pallas_call(
        weight_grad_kernel,
        grid=(count, height // tile),
        in_specs=[
            pl.BlockSpec((None, held, tile), lambda e, i: (e + first, 0, i)),
            pl.BlockSpec((None, held, columns), lambda e, i: (e + first, 0, 0)),
        ]
        + [pl.BlockSpec(memory_space=pl.ANY)] * len(given),
        out_specs=pl.BlockSpec((None, tile, columns), lambda e, i: (e + first, i, 0)),
        out_shape=jax.ShapeDtypeStruct((experts, height, columns), jnp.bfloat16),
        input_output_aliases={2: 0} if given else {},
        compiler_params=pltpu.CompilerParams(vmem_limit_bytes=60 * 1024 * 1024),
        cost_estimate=SMALL_COST,
        name="weight_grads",
    )(left, right, *given)


def attention_forward(starts, tokens, seg_col, seg_row, routes, cos, sin, weights):
    count, rows, width = tokens.shape

    def by_micro(*shape):
        return pl.BlockSpec((None,) + shape, lambda m, s: (m,) + (0,) * len(shape))

    def shared(part):
        return pl.BlockSpec(part.shape, lambda m, s: (0, 0))

    kv_width = 2 * KEY_VALUE_HEADS * HEAD_SIZE
    shapes = [
        ((rows, width), jnp.bfloat16),
        ((rows, QUERY_HEADS * HEAD_SIZE), jnp.bfloat16),
        ((rows, kv_width), jnp.bfloat16),
        ((rows, QUERY_HEADS * HEAD_SIZE), jnp.bfloat16),
        ((rows, 128), jnp.float32),
        ((EXTRA, PIECES * EXPERTS // EXTRA * rows), jnp.bfloat16),
    ]
    return pl.pallas_call(
        attention_kernel,
        grid_spec=pltpu.PrefetchScalarGridSpec(
            num_scalar_prefetch=1,
            grid=(count,),
            in_specs=[
                by_micro(rows, width),
                by_micro(rows, 1),
                by_micro(1, rows),
                by_micro(rows, TOPK),
                shared(cos),
                shared(sin),
            ]
            + [shared(part) for part in weights],
            out_specs=[by_micro(*shape) for shape, _ in shapes]
            + [pl.BlockSpec((8, width), lambda m, s: (0, 0))],
        ),
        out_shape=[jax.ShapeDtypeStruct((count,) + shape, kind) for shape, kind in shapes]
        + [jax.ShapeDtypeStruct((8, width), jnp.float32)],
        compiler_params=pltpu.CompilerParams(vmem_limit_bytes=60 * 1024 * 1024),
        cost_estimate=SMALL_COST,
        name="attention_forward",
    )(starts, tokens, seg_col, seg_row, routes, cos, sin, *weights)


def join_kernel(starts_ref, *refs):
    for at, block_ref in enumerate(refs[:-1]):

        @pl.when(pl.program_id(0) == at)
        def _():
            refs[-1][...] = block_ref[...]


def join_blocks(starts, blocks):
    if len(blocks) == 1:
        return blocks[0]
    span, columns = blocks[0].shape
    return pl.pallas_call(
        join_kernel,
        grid_spec=pltpu.PrefetchScalarGridSpec(
            num_scalar_prefetch=1,
            grid=(len(blocks),),
            in_specs=[pl.BlockSpec((span, columns), lambda i, s: (0, 0)) for _ in blocks],
            out_specs=pl.BlockSpec((span, columns), lambda i, s: (s[i] // span, 0)),
        ),
        out_shape=jax.ShapeDtypeStruct((len(blocks) * span, columns), blocks[0].dtype),
        compiler_params=pltpu.CompilerParams(vmem_limit_bytes=60 * 1024 * 1024),
        cost_estimate=SMALL_COST,
        name="join_blocks",
    )(starts, *blocks)


def attention_grad_kernel(core_ref, xn1, mixed, *refs):
    count = xn1.shape[0]
    proj, attn, sums = [refs[i * count : (i + 1) * count] for i in range(3)]
    mine_ref, other_ref = refs[-2:]
    split = proj[0].shape[1]
    span = mine_ref.shape[0]
    grad = sum(dot_tn(xn1[m], proj[m][...]) for m in range(count))
    router = grad[:, split - 128 :]
    lane = lax.broadcasted_iota(jnp.int32, router.shape, 1)
    router = router + pltpu.roll(router, 128 - EXPERTS, 1)
    gain = sum(part[...] for part in sums)
    lines = [jnp.zeros((EXPERTS, gain.shape[1]), jnp.float32), gain]
    lines.append(jnp.zeros((128 - EXPERTS - gain.shape[0], gain.shape[1]), jnp.float32))
    router = jnp.where(lane < EXPERTS, router, jnp.concatenate(lines, axis=0).T)
    first = core_ref[0] == 0

    def put(columns, value):
        value = value.astype(jnp.bfloat16)
        low, high = value[:span], value[span:]
        mine_ref[:, columns] = jnp.where(first, low, high)
        other_ref[:, columns] = jnp.where(first, high, low)

    put(slice(0, split - 128), grad[:, : split - 128])
    put(slice(split - 128, split), router)
    put(slice(split, None), sum(dot_tn(mixed[m], attn[m][...]) for m in range(count)))


def attention_grads(core, xn1, mixed, proj, attn, gain_sums, parts):
    count, rows, width = xn1.shape
    span = width // parts
    lines = parts // 2
    columns = proj[0].shape[1] + attn[0].shape[1]
    by_line = pl.BlockSpec((count, rows, 2 * span), lambda i, c: (0, 0, i))

    def shared(part):
        return pl.BlockSpec(part.shape, lambda i, c: (0, 0))

    out_spec = pl.BlockSpec((None, span, columns), lambda i, c: (i, 0, 0))
    out_shape = jax.ShapeDtypeStruct((lines, span, columns), jnp.bfloat16)
    return pl.pallas_call(
        attention_grad_kernel,
        grid_spec=pltpu.PrefetchScalarGridSpec(
            num_scalar_prefetch=1,
            grid=(lines,),
            in_specs=[by_line, by_line]
            + [shared(p) for p in proj]
            + [shared(p) for p in attn]
            + [pl.BlockSpec((p.shape[0], 2 * span), lambda i, c: (0, i)) for p in gain_sums],
            out_specs=[out_spec, out_spec],
        ),
        out_shape=[out_shape, out_shape],
        compiler_params=pltpu.CompilerParams(vmem_limit_bytes=60 * 1024 * 1024),
        cost_estimate=SMALL_COST,
        name="attention_grads",
    )(core, xn1, mixed, *proj, *attn, *gain_sums)


def gather_blocks(part, dp_at, dp_count):
    span = part.shape[0]
    if span % 128 or dp_count != 4:
        whole = lax.all_gather(part, "dp", axis=0, tiled=True)
        return [whole], jnp.zeros((1,), jnp.int32)
    line = [(d, (d + 2) % 4) for d in range(4)]
    core = [(d, d ^ 1) for d in range(4)]
    across = lax.ppermute(part, "dp", line)
    beside = lax.ppermute(part, "dp", core)
    both = lax.ppermute(across, "dp", core)
    far = lax.rem(dp_at + 2, 4)
    owners = jnp.stack([dp_at, dp_at + 1 - 2 * lax.rem(dp_at, 2), far, far + 1 - 2 * lax.rem(far, 2)])
    return [part, beside, across, both], owners * span


def per_device(
    tokens,
    segments,
    routes,
    norm_one,
    norm_two,
    w_query,
    key_value_weight,
    w_out_attn,
    w_router,
    w_in,
    w_out,
    cotangent,
):
    micro_count, rows, width = tokens.shape
    micros = range(micro_count)
    peers = lax.axis_size("expert")
    dp_count = lax.axis_size("dp")
    local_experts = w_in.shape[0]
    experts = local_experts * peers
    capacity = rows // 4
    first_expert = lax.axis_index("expert") * local_experts
    q_width = w_query.shape[1]
    kv_width = key_value_weight.shape[1]
    proj_width = q_width + kv_width
    cosine_table, sine_values = rope_tables(rows, HEAD_SIZE)
    cos = jnp.concatenate([cosine_table, cosine_table], axis=1)
    sin = jnp.concatenate([-sine_values, sine_values], axis=1)
    order = ring_order(peers)
    spot = [order.index(dev) for dev in range(peers)]
    my_spot = jnp.array(spot, jnp.int32)[lax.axis_index("expert")]

    router_pad = jnp.zeros((w_router.shape[0], 126 - 2 * experts), jnp.bfloat16)
    first_weight = jnp.concatenate(
        [
            w_query,
            key_value_weight,
            w_router,
            w_router,
            norm_one[:, None],
            norm_two[:, None],
            router_pad,
        ],
        axis=1,
    )
    dp_at = lax.axis_index("dp").astype(jnp.int32)
    first_weights, starts = gather_blocks(first_weight, dp_at, dp_count)
    out_weights, _ = gather_blocks(w_out_attn, dp_at, dp_count)

    routes_rows = jnp.swapaxes(routes, 1, 2).reshape(-1, rows).astype(jnp.bfloat16)
    routes_rows = jnp.pad(
        routes_rows, ((0, EXTRA - routes_rows.shape[0]), (0, width - rows))
    )
    cot_rings = [
        RingGather(jnp.concatenate([cotangent[0], routes_rows], axis=0), peers, rows // 2),
        RingGather(cotangent[1], peers, rows // 2),
    ]
    steps = peers // 2
    for _ in range(steps - 2):
        for ring in cot_rings:
            ring.step()
    first_at = first_expert.astype(jnp.int32).reshape(1)
    seg_col, seg_row = segments[:, :, None], segments[:, None, :]
    xn1, query, keyval, mixed, gates, gates_pack, gains = attention_forward(
        starts, tokens, seg_col, seg_row, routes, cos, sin, first_weights
    )
    for ring in cot_rings:
        ring.step(mixed)
    first_whole = join_blocks(starts, [after(first_weights[0], gates)] + first_weights[1:])
    out_whole = join_blocks(starts, [after(out_weights[0], first_whole)] + out_weights[1:])
    hidden, xn2 = [], []
    for m in micros:
        out = block_call(
            hidden_kernel,
            [(mixed, (m,)), (tokens, (m,)), (gains,), (gates_pack, (m,))]
            + [(part,) for part in out_weights],
            [
                jax.ShapeDtypeStruct((rows, width), jnp.float32),
                jax.ShapeDtypeStruct((rows + EXTRA, width), jnp.bfloat16),
            ],
            "hidden_rows",
            prefetch=starts,
        )
        hidden.append(out[0])
        xn2.append(out[1])
    cot_rings[0].step(xn2[1])
    cot_rings[1].step(xn2[1], out_whole)
    routes_all = cot_rings[0].stack_rows(rows, micro_count * TOPK)[:, :, :rows]
    routes_all = routes_all.reshape(peers, micro_count, TOPK, rows)
    places = [
        slot_hits(routes_all[:, m], first_expert, local_experts, capacity)
        .astype(jnp.bfloat16)
        .reshape(peers, -1, rows)
        for m in micros
    ]
    every = list(range(peers))
    late = [steps - 1, steps, steps + 1]
    early = [k for k in every if k not in late]
    row_rings = [RingGather(xn2[m], peers, rows // 2) for m in micros]
    row_rings[0].step(*cot_rings[0].got, *cot_rings[1].got)
    groups = peers // GROUP

    class Experts:
        kept = [None] * 4

        def __init__(self, m, calls):
            self.m = m
            self.calls = calls
            self.per_call = local_experts // calls
            self.outs = [[None] * 3 for _ in range(groups)]
            self.found = {}

        def pick_grads(self):
            place = places[self.m]
            self.grads = pick_rows(first_at, place, cot_rings[self.m], every, False)
            return self.grads[0]

        def pick(self, distances):
            out = pick_rows(first_at, places[self.m], row_rings[self.m], distances, True)
            self.found.update(zip(distances, zip(out, out[len(distances) :])))
            self.rows = [self.found[k][0] for k in every if k in self.found]
            self.gate_slots = [self.found[k][1] for k in every if k in self.found]
            return out[0]

        def call(self, number, *earlier):
            for g in range(groups):
                span = slice(g * GROUP, (g + 1) * GROUP)
                here = self.rows[span]
                here[0] = after(here[0], *earlier) if earlier else here[0]
                done = expert_pass(
                    here,
                    self.grads[span],
                    self.gate_slots[span],
                    w_in,
                    w_out,
                    self.outs[g] + Experts.kept,
                    (self.m * groups + g, micro_count * groups),
                    number * self.per_call,
                    self.per_call,
                )
                self.outs[g], Experts.kept = list(done[:3]), list(done[3:])
            return done[2]

        def spread(self, spans, *earlier):
            place = places[self.m]
            place = after(place, *earlier) if earlier else place
            self.sums = None
            for g in range(groups):
                out = spread_rows(first_at, place, *self.outs[g], g, spans, self.sums)
                self.sums = out[0]
                if g == groups // 2:
                    far = out[1:]
            return far

    calls = 2
    first, second = Experts(0, calls), Experts(1, calls)
    ring, ring_next = row_rings
    while len(ring.from_left) < steps - 1:
        ring.step(*places)
    ring.step(first.pick_grads())
    ring.step(first.pick(early))
    first.pick(late)
    ring_next.step(*ring.got)
    token = first.call(0)
    for number in range(1, calls):
        got = ring_next.got
        ring_next.step(token)
        token = first.call(number, *got)
    block = rows + EXTRA
    got = ring_next.got
    while len(ring_next.from_left) < steps:
        ring_next.step(token)
    far = first.spread([(0, block), (block, rows)], *got)
    got = ring_next.got
    while ring_next.far is None:
        ring_next.step()
    ring_first = RingScatter(lambda k: first.sums[k], far, peers)
    ring_first.step(*got)
    second.pick_grads()
    second.pick(early)
    second.pick(late)
    token = second.call(0)
    for number in range(1, calls):
        ring_first.step(token)
        token = second.call(number, *ring_first.sent)
    half = rows // 2
    spans = [(0, half), (half, block - half), (block, half), (block + half, half)]
    far = second.spread(spans)
    ring_grads = RingScatter(lambda k: second.sums[k, :block], far[:2], peers)
    ring_results = RingScatter(lambda k: second.sums[k, block:], far[2:], peers)
    ring_grads.step()
    picked, grad_result, activated, grad_pre = Experts.kept
    place_at = jnp.stack([lax.rem(dp_at, 2), dp_at // 2])
    ring_grads.step()
    w_out_sum = weight_grads(
        after(activated, *ring_grads.sent, *ring_first.got), grad_result, 0, local_experts, None
    )
    def backward(m, pieces, *earlier):
        own, left, right = pieces
        return block_call(
            backward_kernel,
            [
                (after(own, *earlier), (0,), block),
                (left, (), block),
                (right, (), block),
                (cotangent, (m,)),
                (hidden[m],),
                (tokens, (m,)),
                (query, (m,)),
                (keyval, (m,)),
                (seg_col, (m,)),
                (seg_row, (m,)),
                (gates, (m,)),
                (gains,),
                (cos,),
                (sin,),
                (first_whole,),
                (out_whole,),
            ],
            [
                jax.ShapeDtypeStruct((rows, width), jnp.bfloat16),
                jax.ShapeDtypeStruct((rows, proj_width + 128), jnp.bfloat16),
                jax.ShapeDtypeStruct((rows, width), jnp.bfloat16),
                jax.ShapeDtypeStruct((8, width), jnp.float32),
            ],
            "attention_backward",
            [pltpu.VMEM((rows, q_width), jnp.bfloat16)],
        )

    half = max(1, local_experts // 2)
    got = second_got = ring_grads.got
    ring_grads.step(w_out_sum)
    picked = after(picked, w_out_sum, *got, *ring_grads.sent)
    while ring_first.at > 1:
        ring_first.step(w_out_sum)
    picked = after(picked, *ring_first.sent)
    w_in_sum = weight_grads(picked, grad_pre, 0, half, None)
    while ring_grads.at > 0:
        got = ring_grads.got
        ring_grads.step(w_in_sum)
    last = ring_first.got
    while ring_first.at > 0:
        ring_first.step(*ring_grads.sent)
    picked = after(picked, w_in_sum, *got, *ring_grads.sent, *ring_first.sent)
    w_in_sum = weight_grads(picked, grad_pre, half, local_experts - half, w_in_sum)
    got = last
    ring_results.step(*got)
    grad_w_out = lax.psum_scatter(
        after(w_out_sum, *second_got), "dp", scatter_dimension=1, tiled=True
    )
    grad_w_in = lax.psum_scatter(
        after(w_in_sum, *ring_grads.got), "dp", scatter_dimension=1, tiled=True
    )
    back_second = backward(1, (second.sums, ring_grads.left, ring_grads.right), w_in_sum)
    ring_results.step(back_second[3], *got)
    back_first = backward(
        0, (first.sums, ring_first.left, ring_first.right), *ring_results.sent
    )
    ring_results.step(back_first[3])
    grad_tokens, grad_proj, grad_attn, gain_sums = zip(back_first, back_second)
    mine, other = attention_grads(
        place_at, after(xn1, *ring_results.sent), mixed, grad_proj, grad_attn, gain_sums, dp_count
    )
    grads, grad_w_in, grad_w_out = reduce_packed(
        mine, other, my_spot, peers, dp_count, grad_w_in, grad_w_out, ring_results, (q_width, kv_width)
    )
    grad_query, grad_keyval, grad_small, grad_attn_out = grads
    wide = jnp.float32
    outputs = []
    for m, (own, ring, at) in enumerate(
        ((first.sums, ring_first, block), (second.sums, ring_results, 0))
    ):
        total = hidden[m] + own[0, block:].astype(wide)
        total = total + ring.left[at:].astype(wide) + ring.right[at:].astype(wide)
        outputs.append(total.astype(jnp.bfloat16))
    return (
        jnp.stack(outputs),
        jnp.stack(grad_tokens),
        grad_small[:, experts],
        grad_small[:, experts + 1],
        grad_query,
        grad_keyval,
        grad_attn_out,
        grad_small[:, :experts],
        grad_w_in,
        grad_w_out,
    )


def last_kernel(spot_ref, *refs):
    outs = refs[-4:]
    blocks = refs[:-4]
    peers = len(blocks) - 1
    piece = blocks[0].shape[0]
    for k, block_ref in enumerate(blocks):
        distance = k if k <= peers // 2 else k - 1
        spot = lax.rem(spot_ref[0] - distance + peers, peers)
        held = block_ref.shape[0]
        row = spot * piece + (held if k == peers // 2 + 1 else 0)
        at = 0
        for out_ref in outs:
            columns = out_ref.shape[1]
            out_ref[pl.ds(pl.multiple_of(row, 8), held), :] = block_ref[
                :, at : at + columns
            ].astype(jnp.float32)
            at += columns


def reduce_packed(mine, other, my_spot, peers, dp_count, grad_w_in, grad_w_out, ring_results, widths):
    lines, span, columns = mine.shape
    swap = [(d, d ^ 1) for d in range(dp_count)]
    while ring_results.at > 0:
        ring_results.step()
    total = add_rows(mine, lax.ppermute(other, "dp", swap))
    piece = span // peers
    total = total.reshape(lines, peers, piece, columns)

    def part(k):
        at = lax.rem(my_spot - k + peers, peers)
        return lax.dynamic_slice_in_dim(total, at, 1, axis=1).reshape(lines * piece, columns)

    half = lines * piece // 2
    farthest = part(peers // 2)
    ring = RingScatter(part, (farthest[:half], farthest[half:]), peers)
    ring.step()
    while ring.at > 0:
        ring.step()
    own, left, right = [held.astype(jnp.float32) for held in (part(0), ring.left, ring.right)]
    mine = (own + left + right).astype(jnp.bfloat16).reshape(lines, piece, columns)
    mine = after(mine, grad_w_in, grad_w_out)
    line = lax.axis_index("dp") // 2

    def for_line(at):
        return lax.dynamic_index_in_dim(mine, lax.rem(at, lines), 0, keepdims=False)

    share = for_line(line).astype(jnp.float32)
    for k in range(1, lines):
        pairs = [(d, (d + 2 * k) % dp_count) for d in range(dp_count)]
        share = share + lax.ppermute(for_line(line + k), "dp", pairs)
    gather = RingGather(share.astype(jnp.bfloat16), peers, piece // 2)
    gather.step()
    grad_w_out = grad_w_out.astype(jnp.float32)
    gather.step(grad_w_out)
    grad_w_in = grad_w_in.astype(jnp.float32)
    gather.step(grad_w_in, *ring_results.got)
    while gather.far is None:
        gather.step()
    blocks = gather.from_left + list(gather.far) + gather.from_right[:0:-1]
    columns = (widths[0], widths[1], 128, columns - sum(widths) - 128)
    if piece % 16 == 0:
        grads = block_call(
            last_kernel,
            [(block,) for block in blocks],
            [jax.ShapeDtypeStruct((span, count), jnp.float32) for count in columns],
            "last_rows",
            prefetch=my_spot.astype(jnp.int32).reshape(1),
        )
    else:
        far = jnp.concatenate(gather.far, axis=0)
        by_distance = jnp.stack(gather.from_left + [far] + gather.from_right[:0:-1])
        distance = lax.rem(my_spot - jnp.arange(peers, dtype=jnp.int32) + peers, peers)
        by_spot = jnp.take(by_distance, distance, axis=0).reshape(span, -1).astype(jnp.float32)
        edges = [sum(columns[:i]) for i in range(5)]
        grads = [by_spot[:, edges[i] : edges[i + 1]] for i in range(4)]
    return grads, grad_w_in, grad_w_out


def solution(mesh):
    return jax.shard_map(
        per_device,
        mesh=mesh,
        in_specs=(
            P(None, ("dp", "expert"), None),
            P(None, ("dp", "expert")),
            P(None, ("dp", "expert"), None),
            P("dp"),
            P("dp"),
            P("dp", None),
            P("dp", None),
            P("dp", None),
            P("dp", None),
            P("expert", None, None),
            P("expert", None, None),
            P(None, ("dp", "expert"), None),
        ),
        out_specs=(
            P(None, ("dp", "expert"), None),
            P(None, ("dp", "expert"), None),
            P("dp"),
            P("dp"),
            P("dp", None),
            P("dp", None),
            P("dp", None),
            P("dp", None),
            P("expert", "dp", None),
            P("expert", "dp", None),
        ),
        check_vma=False,
    )
```

```python
import functools
import math

import jax
import jax.numpy as jnp
from jax import lax
from jax.experimental import pallas as pl
from jax.experimental.pallas import tpu as pltpu
from jax.sharding import PartitionSpec as P

QUERY_HEADS = 12
KEY_VALUE_HEADS = 2
HEAD_SIZE = 128
FF = 768
TOPK = 4
EXPERTS = 32
EXTRA = 16
PIECES = 3
GROUP = 8

eps_norm = 1e-06
rope_base = 1000000.0
mask_fill = -1e30
highest = lax.Precision.HIGHEST


def rms_scale(tensor):
    return lax.rsqrt(jnp.mean(tensor * tensor, axis=-1, keepdims=True) + eps_norm)


def rope_tables(sequence_length, head_width):
    positions = jnp.arange(sequence_length).astype(jnp.float32)
    frequency = rope_base ** (-(jnp.arange(head_width // 2).astype(jnp.float32) * 2.0) / head_width)
    angles = positions[:, None] * frequency[None, :]
    return (jnp.cos(angles), jnp.sin(angles))

SCORE_SCALE = 1.0 / math.sqrt(HEAD_SIZE)
GELU_SCALE = math.sqrt(2.0 / math.pi)
GELU_CUBE = 0.044715
SMALL_COST = pl.CostEstimate(flops=1_000_000, bytes_accessed=1_000_000, transcendentals=0)


def after(value, *earlier):
    return lax.optimization_barrier((value,) + earlier)[0]


def slot_hits(routes_all, first_expert, local_experts, capacity):
    rows = routes_all.shape[-1]
    names = first_expert + jnp.arange(local_experts, dtype=jnp.int32)
    named = routes_all[:, None].astype(jnp.int32) == names[None, :, None, None]
    member = jnp.any(named, axis=2)
    lower = (jnp.arange(rows)[:, None] < jnp.arange(rows)[None, :]).astype(jnp.bfloat16)
    rank = dot32(member.astype(jnp.bfloat16).reshape(-1, rows), lower).reshape(member.shape)
    slots = jnp.arange(capacity, dtype=jnp.float32)
    return member[:, :, None, :] & (rank[:, :, None, :] == slots[None, None, :, None])


def pack_pieces(values, out_ref, first_row):
    rows = values.shape[1]
    rest = values
    for piece in range(PIECES):
        part = rest.astype(jnp.bfloat16)
        rest = rest - part.astype(jnp.float32)
        for half in range(EXPERTS // EXTRA):
            at = (piece * (EXPERTS // EXTRA) + half) * rows
            out_ref[first_row : first_row + EXTRA, at : at + rows] = part[
                half * EXTRA : (half + 1) * EXTRA
            ]


def dot32(left, right):
    return jnp.dot(left, right, preferred_element_type=jnp.float32)


def dot_nt(left, right):
    return lax.dot_general(
        left, right, (((1,), (1,)), ((), ())), preferred_element_type=jnp.float32
    )


def dot_tn(left, right):
    return lax.dot_general(
        left, right, (((0,), (0,)), ((), ())), preferred_element_type=jnp.float32
    )


def mask_of(seg_col, seg_row):
    rows = seg_col.shape[0]
    query_at = lax.broadcasted_iota(jnp.int32, (rows, rows), 0)
    key_at = lax.broadcasted_iota(jnp.int32, (rows, rows), 1)
    return (seg_col == seg_row) & (query_at >= key_at)


def softmax_rows(query, key, allowed):
    scores = jnp.where(allowed, dot_nt(query, key) * SCORE_SCALE, mask_fill)
    weight = jnp.exp(scores - jnp.max(scores, axis=-1, keepdims=True))
    return weight / jnp.sum(weight, axis=-1, keepdims=True)


def from_blocks(starts_ref, rows_ref, blocks):
    total = None
    for at, block_ref in enumerate(blocks):
        span = block_ref.shape[0]
        columns = pl.ds(pl.multiple_of(starts_ref[at], 128), span)
        part = dot32(rows_ref[:, columns], block_ref[...])
        total = part if total is None else total + part
    return total


def attention_kernel(
    starts_ref,
    tok_ref,
    seg_col_ref,
    seg_row_ref,
    routes_ref,
    cos_ref,
    sin_ref,
    *refs,
):
    weight_refs = refs[:-7]
    xn1_ref, query_ref, keyval_ref, mixed_ref, gates_ref, gates_pack_ref, gains_ref = refs[-7:]

    @pl.when(pl.program_id(0) == 0)
    def _():
        for at, block_ref in enumerate(weight_refs):
            span, columns = block_ref.shape
            pad = block_ref[:, columns - 128 :].astype(jnp.float32).T
            place = pl.ds(pl.multiple_of(starts_ref[at], 128), span)
            gains_ref[:, place] = pad[2 * EXPERTS : 2 * EXPERTS + 8]

    tok = tok_ref[...].astype(jnp.float32)
    xn1_ref[...] = (tok * rms_scale(tok) * gains_ref[0:1, :]).astype(jnp.bfloat16)
    proj = from_blocks(starts_ref, xn1_ref, weight_refs)
    cos, sin = cos_ref[...], sin_ref[...]

    def rotate(part):
        return (part * cos + pltpu.roll(part, HEAD_SIZE // 2, 1) * sin).astype(jnp.bfloat16)

    q_width = QUERY_HEADS * HEAD_SIZE
    k_width = KEY_VALUE_HEADS * HEAD_SIZE
    for head in range(QUERY_HEADS):
        span = slice(head * HEAD_SIZE, (head + 1) * HEAD_SIZE)
        query_ref[:, span] = rotate(proj[:, span])
    for head in range(KEY_VALUE_HEADS):
        span = slice(head * HEAD_SIZE, (head + 1) * HEAD_SIZE)
        keyval_ref[:, span] = rotate(proj[:, q_width:][:, span])
    keyval_ref[:, k_width:] = proj[:, q_width + k_width : q_width + 2 * k_width].astype(
        jnp.bfloat16
    )
    logits = proj[:, q_width + 2 * k_width :]
    columns = lax.broadcasted_iota(jnp.int32, logits.shape, 1)
    named = [columns == routes_ref[:, j : j + 1] for j in range(TOPK)]
    chosen = [jnp.sum(jnp.where(hit, logits, 0.0), axis=-1, keepdims=True) for hit in named]
    top = functools.reduce(jnp.maximum, chosen)
    weight = [jnp.exp(part - top) for part in chosen]
    total = functools.reduce(jnp.add, weight)
    gates = jnp.full(logits.shape, -1.0, jnp.float32)
    for hit, part in zip(named, weight):
        gates = jnp.where(hit, part / total, gates)
    gates_ref[...] = gates
    pack_pieces(gates.T[:EXPERTS], gates_pack_ref, 0)
    allowed = mask_of(seg_col_ref[...], seg_row_ref[...])
    for head in range(QUERY_HEADS):
        span = slice(head * HEAD_SIZE, (head + 1) * HEAD_SIZE)
        group = head // (QUERY_HEADS // KEY_VALUE_HEADS)
        key = keyval_ref[:, group * HEAD_SIZE : (group + 1) * HEAD_SIZE]
        value = keyval_ref[:, k_width + group * HEAD_SIZE : k_width + (group + 1) * HEAD_SIZE]
        probs = softmax_rows(query_ref[:, span], key, allowed)
        mixed_ref[:, span] = dot32(probs.astype(jnp.bfloat16), value).astype(jnp.bfloat16)


def hidden_kernel(starts_ref, mixed_ref, tok_ref, gains_ref, pack_ref, *refs):
    weight_refs = refs[:-2]
    hidden_ref, xn2_ref = refs[-2:]
    rows = tok_ref.shape[0]
    hidden = tok_ref[...].astype(jnp.float32) + from_blocks(
        starts_ref, mixed_ref, weight_refs
    )
    hidden_ref[...] = hidden
    xn2_ref[:rows, :] = (hidden * rms_scale(hidden) * gains_ref[1:2, :]).astype(jnp.bfloat16)
    xn2_ref[rows:, :] = pack_ref[...]


def backward_kernel(
    own_ref,
    left_ref,
    right_ref,
    cot_ref,
    hidden_ref,
    tok_ref,
    query_ref,
    keyval_ref,
    seg_col_ref,
    seg_row_ref,
    gates_ref,
    gains_ref,
    cos_ref,
    sin_ref,
    *refs,
):
    weight_ref, out_weight_ref = refs[:2]
    grad_tok_ref, grad_proj_ref, grad_attn_ref, gain_sum_ref, mixed_grad_ref = refs[2:]
    width = tok_ref.shape[1]
    q_width = QUERY_HEADS * HEAD_SIZE
    k_width = KEY_VALUE_HEADS * HEAD_SIZE
    proj_width = q_width + 2 * k_width
    rows = tok_ref.shape[0]
    sums = [ref[...].astype(jnp.float32) for ref in (own_ref, left_ref, right_ref)]
    sums = sums[0] + sums[1] + sums[2]
    grad_xn2, pack = sums[:rows], sums[rows:]
    halves = EXPERTS // EXTRA
    lines = [
        sum(
            pack[:, (piece * halves + half) * rows : (piece * halves + half + 1) * rows]
            for piece in range(PIECES)
        )
        for half in range(halves)
    ]
    lines.append(jnp.zeros((128 - EXPERTS, rows), jnp.float32))
    grad_gates = jnp.concatenate(lines, axis=0).T
    hidden = hidden_ref[...]
    scale = rms_scale(hidden)
    unit = hidden * scale
    gain_sum_ref[...] = jnp.zeros(gain_sum_ref.shape, jnp.float32)
    gain_sum_ref[1:2, :] = jnp.sum(grad_xn2 * unit, axis=0, keepdims=True)
    grad_unit = grad_xn2 * gains_ref[1:2, :]
    grad_hidden = cot_ref[...].astype(jnp.float32) + scale * (
        grad_unit - unit * jnp.mean(grad_unit * unit, axis=-1, keepdims=True)
    )
    grad_attn_ref[...] = grad_hidden.astype(jnp.bfloat16)
    mixed_grad_ref[...] = dot_nt(grad_attn_ref[...], out_weight_ref[...]).astype(jnp.bfloat16)
    cos, sin = cos_ref[...], sin_ref[...]

    def unrotate(part):
        return (part * cos - pltpu.roll(part, HEAD_SIZE // 2, 1) * sin).astype(jnp.bfloat16)

    allowed = mask_of(seg_col_ref[...], seg_row_ref[...])
    per_group = QUERY_HEADS // KEY_VALUE_HEADS
    for group in range(KEY_VALUE_HEADS):
        key_span = slice(group * HEAD_SIZE, (group + 1) * HEAD_SIZE)
        value_span = slice(k_width + group * HEAD_SIZE, k_width + (group + 1) * HEAD_SIZE)
        key, value = keyval_ref[:, key_span], keyval_ref[:, value_span]
        grad_key = jnp.zeros(key.shape, jnp.float32)
        grad_value = jnp.zeros(key.shape, jnp.float32)
        for head in range(group * per_group, (group + 1) * per_group):
            span = slice(head * HEAD_SIZE, (head + 1) * HEAD_SIZE)
            query, grad_mixed = query_ref[:, span], mixed_grad_ref[:, span]
            probs = softmax_rows(query, key, allowed)
            grad_value += dot_tn(probs.astype(jnp.bfloat16), grad_mixed)
            grad_probs = dot_nt(grad_mixed, value)
            mean = jnp.sum(probs * grad_probs, axis=-1, keepdims=True)
            grad_scores = (probs * (grad_probs - mean)).astype(jnp.bfloat16)
            grad_proj_ref[:, span] = unrotate(dot32(grad_scores, key) * SCORE_SCALE)
            grad_key += dot_tn(grad_scores, query)
        grad_proj_ref[:, q_width + group * HEAD_SIZE : q_width + (group + 1) * HEAD_SIZE] = (
            unrotate(grad_key * SCORE_SCALE)
        )
        first = q_width + k_width + group * HEAD_SIZE
        grad_proj_ref[:, first : first + HEAD_SIZE] = grad_value.astype(jnp.bfloat16)
    gates = jnp.maximum(gates_ref[...], 0.0)
    grad_logits = gates * (grad_gates - jnp.sum(gates * grad_gates, axis=-1, keepdims=True))
    high = grad_logits.astype(jnp.bfloat16).astype(jnp.float32)
    low = pltpu.roll(grad_logits - high, EXPERTS, 1)
    grad_proj_ref[:, proj_width:] = (high + low).astype(jnp.bfloat16)
    grad_xn1 = dot_nt(grad_proj_ref[...], weight_ref[...])
    tok = tok_ref[...].astype(jnp.float32)
    scale = rms_scale(tok)
    unit = tok * scale
    gain_sum_ref[0:1, :] = jnp.sum(grad_xn1 * unit, axis=0, keepdims=True)
    grad_unit = grad_xn1 * gains_ref[0:1, :]
    grad_tok_ref[...] = (
        grad_hidden
        + scale * (grad_unit - unit * jnp.mean(grad_unit * unit, axis=-1, keepdims=True))
    ).astype(jnp.bfloat16)


def ring_order(peers):
    minor = peers // 4
    walk = []
    for col in range(minor):
        line = range(4) if col % 2 == 0 else range(3, -1, -1)
        walk += [row * minor + col for row in line]
    return walk


def ring_step(part, shift, peers):
    order = ring_order(peers)
    pairs = [(order[i], order[(i + shift) % peers]) for i in range(peers)]
    return lax.ppermute(part, "expert", pairs)


class RingGather:
    def __init__(self, part, peers, half):
        self.peers, self.half = peers, half
        self.from_left, self.from_right = [part], [part]
        self.far = None
        self.got = ()

    def step(self, *earlier):
        left, right = self.from_left[-1], self.from_right[-1]
        last = len(self.from_left) == self.peers // 2
        if last:
            left, right = left[: self.half], right[self.half :]
        left, right = self.sent = lax.optimization_barrier((left, right) + earlier)[:2]
        left, right = ring_step(left, 1, self.peers), ring_step(right, -1, self.peers)
        self.got = (left, right)
        if last:
            self.far = (left, right)
        else:
            self.from_left.append(left)
            self.from_right.append(right)
        return self

    def rows(self, k, first, count):
        if k < len(self.from_left):
            return self.from_left[k], first
        if k > self.peers // 2:
            return self.from_right[self.peers - k], first
        if first < self.half:
            return self.far[0], first
        return self.far[1], first - self.half

    def stack_rows(self, first, count):
        found = [self.rows(k, first, count) for k in range(self.peers)]
        return jnp.stack([array[at : at + count] for array, at in found])


class RingScatter:
    def __init__(self, part, far, peers):
        self.part, self.far, self.peers = part, far, peers
        self.at = peers // 2
        self.half = far[0].shape[0]

    def step(self, *earlier):
        peers, k, half = self.peers, self.at, self.half
        if k == peers // 2:
            left, right = lax.optimization_barrier(tuple(self.far) + earlier)[:2]
        else:
            left, right = self.part(k), self.part(peers - k)
            if earlier:
                self.left, self.right = lax.optimization_barrier(
                    (self.left, self.right) + earlier
                )[:2]
            if k == peers // 2 - 1:
                kept = left[half:].astype(jnp.bfloat16), right[:half].astype(jnp.bfloat16)
                left = jnp.concatenate([add_rows(left[:half], self.left), kept[0]], axis=0)
                right = jnp.concatenate([kept[1], add_rows(right[half:], self.right)], axis=0)
            else:
                left, right = add_rows(left, self.left), add_rows(right, self.right)
        left, right = self.sent = lax.optimization_barrier((left, right))
        self.left = ring_step(left, -1, peers)
        self.right = ring_step(right, 1, peers)
        self.got = (self.left, self.right)
        self.at = k - 1
        return self


def add_rows(left, right):
    return (left.astype(jnp.float32) + right.astype(jnp.float32)).astype(jnp.bfloat16)


def expert_kernel(sources, *refs):
    rows_refs = refs[:sources]
    grad_refs = refs[sources : 2 * sources]
    gate_refs = refs[2 * sources : 3 * sources]
    w_in_ref, w_out_ref = refs[3 * sources : 3 * sources + 2]
    (
        back_rows_ref,
        back_grads_ref,
        grad_gate_ref,
        picked_ref,
        grad_result_ref,
        activated_ref,
        grad_pre_ref,
    ) = refs[-7:]
    capacity, width = rows_refs[0].shape
    for k in range(sources):
        picked_ref[pl.ds(k * capacity, capacity), :] = rows_refs[k][...]
    pre_act = dot32(picked_ref[...], w_in_ref[...])
    gate_part = pre_act[:, :FF]
    up_part = pre_act[:, FF:]
    square = gate_part * gate_part
    bend = jnp.tanh(GELU_SCALE * gate_part * (1.0 + GELU_CUBE * square))
    lift = 0.5 * (1.0 + bend)
    gelu_val = gate_part * lift
    slope = lift + 0.5 * gate_part * (1.0 - bend * bend) * (
        GELU_SCALE * (1.0 + 3.0 * GELU_CUBE * square)
    )
    activated_ref[...] = (gelu_val * up_part).astype(jnp.bfloat16)
    result = dot32(activated_ref[...], w_out_ref[...])
    for k in range(sources):
        gates = gate_refs[k][...]
        span = slice(k * capacity, (k + 1) * capacity)
        grad_rows = grad_refs[k][...].astype(jnp.float32)
        grad_gate_ref[span, :] = jnp.sum(result[span] * grad_rows, axis=-1, keepdims=True)
        back_rows_ref[k] = (result[span] * gates).astype(jnp.bfloat16)
        grad_result_ref[span, :] = (grad_rows * gates).astype(jnp.bfloat16)
    grad_act = lax.dot_general(
        grad_result_ref[...],
        w_out_ref[...],
        (((1,), (1,)), ((), ())),
        preferred_element_type=jnp.float32,
    )
    grad_pre_ref[:, :FF] = (grad_act * up_part * slope).astype(jnp.bfloat16)
    grad_pre_ref[:, FF:] = (grad_act * gelu_val).astype(jnp.bfloat16)
    grad_in = lax.dot_general(
        grad_pre_ref[...],
        w_in_ref[...],
        (((1,), (1,)), ((), ())),
        preferred_element_type=jnp.float32,
    ).astype(jnp.bfloat16)
    for k in range(sources):
        back_grads_ref[k] = grad_in[k * capacity : (k + 1) * capacity]


def expert_pass(rows_list, grads_list, gate_slots, w_in, w_out, held_outs, position, first, count):
    sources = len(rows_list)
    local_experts, width, _ = w_in.shape
    slots = rows_list[0].shape[0]
    capacity = slots // local_experts
    held = sources * capacity
    block_spec = pl.BlockSpec((capacity, width), lambda e: (e + first, 0))
    back_spec = pl.BlockSpec((sources, capacity, width), lambda e: (0, e + first, 0))
    column_spec = pl.BlockSpec((None, held, 1), lambda e: (e + first, 0, 0))

    def kept_spec(columns):
        return pl.BlockSpec((None, held, columns), lambda e: (e + first, position[0], 0))

    def kept_shape(columns):
        return jax.ShapeDtypeStruct((local_experts, position[1] * held, columns), jnp.bfloat16)

    kept_widths = (width, width, FF, 2 * FF)
    first_held = 3 * sources + 2
    given = [(i, part) for i, part in enumerate(held_outs) if part is not None]
    return pl.pallas_call(
        functools.partial(expert_kernel, sources),
        grid=(count,),
        in_specs=[block_spec] * (2 * sources)
        + [pl.BlockSpec((capacity, 1), lambda e: (e + first, 0))] * sources
        + [
            pl.BlockSpec((None, width, 2 * FF), lambda e: (e + first, 0, 0)),
            pl.BlockSpec((None, FF, width), lambda e: (e + first, 0, 0)),
        ]
        + [pl.BlockSpec(memory_space=pl.ANY)] * len(given),
        out_specs=[back_spec, back_spec, column_spec] + [kept_spec(c) for c in kept_widths],
        out_shape=[
            jax.ShapeDtypeStruct((sources, slots, width), jnp.bfloat16),
            jax.ShapeDtypeStruct((sources, slots, width), jnp.bfloat16),
            jax.ShapeDtypeStruct((local_experts, held, 1), jnp.float32),
        ]
        + [kept_shape(c) for c in kept_widths],
        input_output_aliases={first_held + at: i for at, (i, _) in enumerate(given)},
        compiler_params=pltpu.CompilerParams(vmem_limit_bytes=60 * 1024 * 1024),
        cost_estimate=SMALL_COST,
        name="expert_pass",
    )(*rows_list, *grads_list, *gate_slots, w_in, w_out, *[part for _, part in given])


def block_call(kernel, operands, out_shape, name, scratch=(), prefetch=None):
    def spec(array, lead=(), rows=None):
        rest = array.shape[len(lead) :]
        at = lead + (0,) * len(rest)
        if rows is not None:
            count, block = rows if isinstance(rows, tuple) else (rows, 0)
            rest = (count,) + rest[1:]
            at = lead + (block,) + (0,) * (len(rest) - 1)
        return pl.BlockSpec((None,) * len(lead) + rest, lambda *_: at)

    scalars = [] if prefetch is None else [prefetch]
    return pl.pallas_call(
        kernel,
        grid_spec=pltpu.PrefetchScalarGridSpec(
            num_scalar_prefetch=len(scalars),
            grid=(1,),
            in_specs=[spec(*operand) for operand in operands],
            out_specs=[spec(shape) for shape in out_shape],
            scratch_shapes=list(scratch),
        ),
        out_shape=out_shape,
        compiler_params=pltpu.CompilerParams(vmem_limit_bytes=60 * 1024 * 1024),
        cost_estimate=SMALL_COST,
        name=name,
    )(*scalars, *[operand[0] for operand in operands])


def pick_kernel(shares, gated, first_ref, place_ref, *refs):
    at = 0
    outs = refs[sum(count for _, count in shares) + (len(shares) if gated else 0) :]
    for number, (k, count) in enumerate(shares):
        total, row = None, 0
        for block_ref in refs[at : at + count]:
            held = block_ref.shape[0]
            part = dot32(place_ref[k, :, row : row + held], block_ref[...])
            total = part if total is None else total + part
            row += held
        outs[number][...] = total.astype(jnp.bfloat16)
        at += count
        if gated:
            slot_gates(first_ref[0], place_ref[k], refs[at], outs[len(shares) + number])
            at += 1


def slot_gates(first_expert, place, pack_ref, out_ref):
    slots, rows = place.shape
    pack = pack_ref[...].astype(jnp.float32)
    halves = EXPERTS // EXTRA
    line = lax.broadcasted_iota(jnp.int32, (EXTRA, rows), 0)
    local_experts = slots * 4 // rows
    capacity = rows // 4
    for e in range(local_experts):
        gate = jnp.zeros((1, rows), jnp.float32)
        for half in range(halves):
            hit = line + half * EXTRA == first_expert + e
            for piece in range(PIECES):
                at = (piece * halves + half) * rows
                gate += jnp.sum(
                    jnp.where(hit, pack[:, at : at + rows], 0.0), axis=0, keepdims=True
                )
        span = slice(e * capacity, (e + 1) * capacity)
        out_ref[span, :] = jnp.sum(
            place[span].astype(jnp.float32) * gate, axis=-1, keepdims=True
        )


def pick_rows(first_expert, place, ring, distances, gated):
    _, slots, rows = place.shape
    half = rows // 2
    operands, shares = [], []
    for k in distances:
        spans = [(0, rows)]
        if k == ring.peers // 2 and ring.half < rows:
            spans = [(0, half), (half, half)]
        shares.append((k, len(spans)))
        for at, count in spans + ([(rows, EXTRA)] if gated else []):
            array, at = ring.rows(k, at, count)
            operands.append((array, (), (count, at // count)))
    width = operands[0][0].shape[-1]
    out_shape = [jax.ShapeDtypeStruct((slots, width), jnp.bfloat16) for _ in distances]
    if gated:
        out_shape += [jax.ShapeDtypeStruct((slots, 1), jnp.float32) for _ in distances]
    return block_call(
        functools.partial(pick_kernel, shares, gated),
        [(place,)] + operands,
        out_shape,
        "pick_rows",
        prefetch=first_expert,
    )


def spread_kernel(middle, spans, held, first_ref, place_ref, rows_ref, grads_ref, gate_ref, *refs):
    out_ref, *far_refs = refs[held:]
    place = place_ref[...]
    rows = place.shape[1]
    out_ref[:rows, :] = dot_tn(place, grads_ref[...]).astype(jnp.bfloat16)
    out_ref[rows + EXTRA :, :] = dot_tn(place, rows_ref[...]).astype(jnp.bfloat16)
    capacity = gate_ref.shape[1]
    expert = lax.broadcasted_iota(jnp.int32, (EXPERTS, rows), 0) - first_ref[0]
    gates = jnp.zeros((EXPERTS, rows), jnp.float32)
    for e in range(gate_ref.shape[0]):
        hit = place[e * capacity : (e + 1) * capacity].astype(jnp.float32)
        line = jnp.sum(hit * gate_ref[e], axis=0, keepdims=True)
        gates = jnp.where(expert == e, line, gates)
    pack_pieces(gates, out_ref, rows)

    @pl.when(pl.program_id(0) == middle)
    def _():
        for far_ref, (row, count) in zip(far_refs, spans):
            far_ref[...] = out_ref[row : row + count, :]


def spread_rows(first_expert, place, rows_back, grads_back, gate_slots, group, spans, held):
    sources, slots, rows = place.shape
    width = rows_back.shape[-1]
    local_experts = gate_slots.shape[0]
    base = group * GROUP
    by_source = pl.BlockSpec((None, slots, width), lambda k, f: (k, 0, 0))
    held = [] if held is None else [held]
    out_shape = [jax.ShapeDtypeStruct((sources, 2 * rows + EXTRA, width), jnp.bfloat16)]
    out_shape += [jax.ShapeDtypeStruct((count, width), jnp.bfloat16) for _, count in spans]
    out_specs = [pl.BlockSpec((None, 2 * rows + EXTRA, width), lambda k, f: (base + k, 0, 0))]
    out_specs += [pl.BlockSpec((count, width), lambda k, f: (0, 0)) for _, count in spans]
    return pl.pallas_call(
        functools.partial(spread_kernel, sources // 2 - base, spans, len(held)),
        grid_spec=pltpu.PrefetchScalarGridSpec(
            num_scalar_prefetch=1,
            grid=(GROUP,),
            in_specs=[
                pl.BlockSpec((None, slots, rows), lambda k, f: (base + k, 0, 0)),
                by_source,
                by_source,
                pl.BlockSpec((local_experts, slots // local_experts, 1), lambda k, f: (0, k, 0)),
            ]
            + [pl.BlockSpec(memory_space=pl.ANY)] * len(held),
            out_specs=out_specs,
        ),
        out_shape=out_shape,
        input_output_aliases={5 + i: i for i in range(len(held))},
        compiler_params=pltpu.CompilerParams(vmem_limit_bytes=60 * 1024 * 1024),
        cost_estimate=SMALL_COST,
        name="spread_rows",
    )(first_expert, place, rows_back, grads_back, gate_slots, *held)


def weight_grad_kernel(left_ref, right_ref, *refs):
    refs[-1][...] = dot_tn(left_ref[...], right_ref[...]).astype(jnp.bfloat16)


def weight_grads(left, right, first, count, held_out):
    experts, held, height = left.shape
    columns = right.shape[-1]
    tile = min(height, 768)
    given = [] if held_out is None else [held_out]
    return pl.pallas_call(
        weight_grad_kernel,
        grid=(count, height // tile),
        in_specs=[
            pl.BlockSpec((None, held, tile), lambda e, i: (e + first, 0, i)),
            pl.BlockSpec((None, held, columns), lambda e, i: (e + first, 0, 0)),
        ]
        + [pl.BlockSpec(memory_space=pl.ANY)] * len(given),
        out_specs=pl.BlockSpec((None, tile, columns), lambda e, i: (e + first, i, 0)),
        out_shape=jax.ShapeDtypeStruct((experts, height, columns), jnp.bfloat16),
        input_output_aliases={2: 0} if given else {},
        compiler_params=pltpu.CompilerParams(vmem_limit_bytes=60 * 1024 * 1024),
        cost_estimate=SMALL_COST,
        name="weight_grads",
    )(left, right, *given)


def attention_forward(starts, tokens, seg_col, seg_row, routes, cos, sin, weights):
    count, rows, width = tokens.shape

    def by_micro(*shape):
        return pl.BlockSpec((None,) + shape, lambda m, s: (m,) + (0,) * len(shape))

    def shared(part):
        return pl.BlockSpec(part.shape, lambda m, s: (0, 0))

    kv_width = 2 * KEY_VALUE_HEADS * HEAD_SIZE
    shapes = [
        ((rows, width), jnp.bfloat16),
        ((rows, QUERY_HEADS * HEAD_SIZE), jnp.bfloat16),
        ((rows, kv_width), jnp.bfloat16),
        ((rows, QUERY_HEADS * HEAD_SIZE), jnp.bfloat16),
        ((rows, 128), jnp.float32),
        ((EXTRA, PIECES * EXPERTS // EXTRA * rows), jnp.bfloat16),
    ]
    return pl.pallas_call(
        attention_kernel,
        grid_spec=pltpu.PrefetchScalarGridSpec(
            num_scalar_prefetch=1,
            grid=(count,),
            in_specs=[
                by_micro(rows, width),
                by_micro(rows, 1),
                by_micro(1, rows),
                by_micro(rows, TOPK),
                shared(cos),
                shared(sin),
            ]
            + [shared(part) for part in weights],
            out_specs=[by_micro(*shape) for shape, _ in shapes]
            + [pl.BlockSpec((8, width), lambda m, s: (0, 0))],
        ),
        out_shape=[jax.ShapeDtypeStruct((count,) + shape, kind) for shape, kind in shapes]
        + [jax.ShapeDtypeStruct((8, width), jnp.float32)],
        compiler_params=pltpu.CompilerParams(vmem_limit_bytes=60 * 1024 * 1024),
        cost_estimate=SMALL_COST,
        name="attention_forward",
    )(starts, tokens, seg_col, seg_row, routes, cos, sin, *weights)


def join_kernel(starts_ref, *refs):
    for at, block_ref in enumerate(refs[:-1]):

        @pl.when(pl.program_id(0) == at)
        def _():
            refs[-1][...] = block_ref[...]


def join_blocks(starts, blocks):
    if len(blocks) == 1:
        return blocks[0]
    span, columns = blocks[0].shape
    return pl.pallas_call(
        join_kernel,
        grid_spec=pltpu.PrefetchScalarGridSpec(
            num_scalar_prefetch=1,
            grid=(len(blocks),),
            in_specs=[pl.BlockSpec((span, columns), lambda i, s: (0, 0)) for _ in blocks],
            out_specs=pl.BlockSpec((span, columns), lambda i, s: (s[i] // span, 0)),
        ),
        out_shape=jax.ShapeDtypeStruct((len(blocks) * span, columns), blocks[0].dtype),
        compiler_params=pltpu.CompilerParams(vmem_limit_bytes=60 * 1024 * 1024),
        cost_estimate=SMALL_COST,
        name="join_blocks",
    )(starts, *blocks)


def attention_grad_kernel(core_ref, xn1, mixed, *refs):
    count = xn1.shape[0]
    proj, attn, sums = [refs[i * count : (i + 1) * count] for i in range(3)]
    mine_ref, other_ref = refs[-2:]
    split = proj[0].shape[1]
    span = mine_ref.shape[0]
    grad = sum(dot_tn(xn1[m], proj[m][...]) for m in range(count))
    router = grad[:, split - 128 :]
    lane = lax.broadcasted_iota(jnp.int32, router.shape, 1)
    router = router + pltpu.roll(router, 128 - EXPERTS, 1)
    gain = sum(part[...] for part in sums)
    lines = [jnp.zeros((EXPERTS, gain.shape[1]), jnp.float32), gain]
    lines.append(jnp.zeros((128 - EXPERTS - gain.shape[0], gain.shape[1]), jnp.float32))
    router = jnp.where(lane < EXPERTS, router, jnp.concatenate(lines, axis=0).T)
    first = core_ref[0] == 0

    def put(columns, value):
        value = value.astype(jnp.bfloat16)
        low, high = value[:span], value[span:]
        mine_ref[:, columns] = jnp.where(first, low, high)
        other_ref[:, columns] = jnp.where(first, high, low)

    put(slice(0, split - 128), grad[:, : split - 128])
    put(slice(split - 128, split), router)
    put(slice(split, None), sum(dot_tn(mixed[m], attn[m][...]) for m in range(count)))


def attention_grads(core, xn1, mixed, proj, attn, gain_sums, parts):
    count, rows, width = xn1.shape
    span = width // parts
    lines = parts // 2
    columns = proj[0].shape[1] + attn[0].shape[1]
    by_line = pl.BlockSpec((count, rows, 2 * span), lambda i, c: (0, 0, i))

    def shared(part):
        return pl.BlockSpec(part.shape, lambda i, c: (0, 0))

    out_spec = pl.BlockSpec((None, span, columns), lambda i, c: (i, 0, 0))
    out_shape = jax.ShapeDtypeStruct((lines, span, columns), jnp.bfloat16)
    return pl.pallas_call(
        attention_grad_kernel,
        grid_spec=pltpu.PrefetchScalarGridSpec(
            num_scalar_prefetch=1,
            grid=(lines,),
            in_specs=[by_line, by_line]
            + [shared(p) for p in proj]
            + [shared(p) for p in attn]
            + [pl.BlockSpec((p.shape[0], 2 * span), lambda i, c: (0, i)) for p in gain_sums],
            out_specs=[out_spec, out_spec],
        ),
        out_shape=[out_shape, out_shape],
        compiler_params=pltpu.CompilerParams(vmem_limit_bytes=60 * 1024 * 1024),
        cost_estimate=SMALL_COST,
        name="attention_grads",
    )(core, xn1, mixed, *proj, *attn, *gain_sums)


def gather_blocks(part, dp_at, dp_count):
    span = part.shape[0]
    if span % 128 or dp_count != 4:
        whole = lax.all_gather(part, "dp", axis=0, tiled=True)
        return lambda *earlier: [whole], jnp.zeros((1,), jnp.int32)
    line = [(d, (d + 2) % 4) for d in range(4)]
    core = [(d, d ^ 1) for d in range(4)]
    across = lax.ppermute(part, "dp", line)
    beside = lax.ppermute(part, "dp", core)
    far = lax.rem(dp_at + 2, 4)
    owners = jnp.stack([dp_at, dp_at + 1 - 2 * lax.rem(dp_at, 2), far, far + 1 - 2 * lax.rem(far, 2)])

    def blocks(*earlier):
        moved = after(across, *earlier) if earlier else across
        return [part, beside, moved, lax.ppermute(moved, "dp", core)]

    return blocks, owners * span


def per_device(
    tokens,
    segments,
    routes,
    norm_one,
    norm_two,
    w_query,
    key_value_weight,
    w_out_attn,
    w_router,
    w_in,
    w_out,
    cotangent,
):
    micro_count, rows, width = tokens.shape
    micros = range(micro_count)
    peers = lax.axis_size("expert")
    dp_count = lax.axis_size("dp")
    local_experts = w_in.shape[0]
    experts = local_experts * peers
    capacity = rows // 4
    first_expert = lax.axis_index("expert") * local_experts
    q_width = w_query.shape[1]
    kv_width = key_value_weight.shape[1]
    proj_width = q_width + kv_width
    cosine_table, sine_values = rope_tables(rows, HEAD_SIZE)
    cos = jnp.concatenate([cosine_table, cosine_table], axis=1)
    sin = jnp.concatenate([-sine_values, sine_values], axis=1)
    order = ring_order(peers)
    spot = [order.index(dev) for dev in range(peers)]
    my_spot = jnp.array(spot, jnp.int32)[lax.axis_index("expert")]

    router_pad = jnp.zeros((w_router.shape[0], 126 - 2 * experts), jnp.bfloat16)
    first_weight = jnp.concatenate(
        [
            w_query,
            key_value_weight,
            w_router,
            w_router,
            norm_one[:, None],
            norm_two[:, None],
            router_pad,
        ],
        axis=1,
    )
    dp_at = lax.axis_index("dp").astype(jnp.int32)
    first_weights, starts = gather_blocks(first_weight, dp_at, dp_count)
    out_weights, _ = gather_blocks(w_out_attn, dp_at, dp_count)

    routes_rows = jnp.swapaxes(routes, 1, 2).reshape(-1, rows).astype(jnp.bfloat16)
    routes_rows = jnp.pad(
        routes_rows, ((0, EXTRA - routes_rows.shape[0]), (0, width - rows))
    )
    cot_rings = [
        RingGather(jnp.concatenate([cotangent[0], routes_rows], axis=0), peers, rows // 2),
        RingGather(cotangent[1], peers, rows // 2),
    ]
    steps = peers // 2
    for at in range(steps - 2):
        for ring in cot_rings:
            ring.step()
        if at == 0:
            first_weights = first_weights(*cot_rings[0].got, *cot_rings[1].got)
    first_at = first_expert.astype(jnp.int32).reshape(1)
    seg_col, seg_row = segments[:, :, None], segments[:, None, :]
    xn1, query, keyval, mixed, gates, gates_pack, gains = attention_forward(
        starts, tokens, seg_col, seg_row, routes, cos, sin, first_weights
    )
    for ring in cot_rings:
        ring.step(mixed)
    out_weights = out_weights(mixed)
    hidden, xn2 = [], []
    for m in micros:
        out = block_call(
            hidden_kernel,
            [(mixed, (m,)), (tokens, (m,)), (gains,), (gates_pack, (m,))]
            + [(part,) for part in out_weights],
            [
                jax.ShapeDtypeStruct((rows, width), jnp.float32),
                jax.ShapeDtypeStruct((rows + EXTRA, width), jnp.bfloat16),
            ],
            "hidden_rows",
            prefetch=starts,
        )
        hidden.append(out[0])
        xn2.append(out[1])
    for ring in cot_rings:
        ring.step()
    first_whole = join_blocks(starts, [after(first_weights[0], xn2[1])] + first_weights[1:])
    out_whole = join_blocks(starts, [after(out_weights[0], first_whole)] + out_weights[1:])
    routes_all = cot_rings[0].stack_rows(rows, micro_count * TOPK)[:, :, :rows]
    routes_all = routes_all.reshape(peers, micro_count, TOPK, rows)
    places = [
        slot_hits(routes_all[:, m], first_expert, local_experts, capacity)
        .astype(jnp.bfloat16)
        .reshape(peers, -1, rows)
        for m in micros
    ]
    every = list(range(peers))
    late = [steps - 1, steps, steps + 1]
    early = [k for k in every if k not in late]
    row_rings = [RingGather(xn2[m], peers, rows // 2) for m in micros]
    row_rings[0].step(*cot_rings[0].got, *cot_rings[1].got)
    groups = peers // GROUP

    class Experts:
        kept = [None] * 4

        def __init__(self, m, calls):
            self.m = m
            self.calls = calls
            self.per_call = local_experts // calls
            self.outs = [[None] * 3 for _ in range(groups)]
            self.found = {}

        def pick_grads(self):
            place = places[self.m]
            self.grads = pick_rows(first_at, place, cot_rings[self.m], every, False)
            return self.grads[0]

        def pick(self, distances):
            out = pick_rows(first_at, places[self.m], row_rings[self.m], distances, True)
            self.found.update(zip(distances, zip(out, out[len(distances) :])))
            self.rows = [self.found[k][0] for k in every if k in self.found]
            self.gate_slots = [self.found[k][1] for k in every if k in self.found]
            return out[0]

        def call(self, number, *earlier):
            for g in range(groups):
                span = slice(g * GROUP, (g + 1) * GROUP)
                here = self.rows[span]
                here[0] = after(here[0], *earlier) if earlier else here[0]
                done = expert_pass(
                    here,
                    self.grads[span],
                    self.gate_slots[span],
                    w_in,
                    w_out,
                    self.outs[g] + Experts.kept,
                    (self.m * groups + g, micro_count * groups),
                    number * self.per_call,
                    self.per_call,
                )
                self.outs[g], Experts.kept = list(done[:3]), list(done[3:])
            return done[2]

        def spread(self, spans, *earlier):
            place = places[self.m]
            place = after(place, *earlier) if earlier else place
            self.sums = None
            for g in range(groups):
                out = spread_rows(first_at, place, *self.outs[g], g, spans, self.sums)
                self.sums = out[0]
                if g == groups // 2:
                    far = out[1:]
            return far

    calls = 2
    first, second = Experts(0, calls), Experts(1, calls)
    ring, ring_next = row_rings
    while len(ring.from_left) < steps - 1:
        ring.step(*places, out_whole)
    ring.step(first.pick_grads())
    ring.step(first.pick(early))
    places[0] = after(places[0], second.pick_grads())
    first.pick(late)
    ring_next.step(*ring.got)
    token = first.call(0)
    for number in range(1, calls):
        got = ring_next.got
        ring_next.step(token)
        token = first.call(number, *got)
    block = rows + EXTRA
    got = ring_next.got
    while len(ring_next.from_left) < steps:
        ring_next.step(token)
    far = first.spread([(0, block), (block, rows)], *got)
    got = ring_next.got
    while ring_next.far is None:
        ring_next.step()
    ring_first = RingScatter(lambda k: first.sums[k], far, peers)
    ring_first.step(*got)
    second.pick(early)
    second.pick(late)
    token = second.call(0)
    for number in range(1, calls):
        ring_first.step(token)
        token = second.call(number, *ring_first.sent)
    half = rows // 2
    spans = [(0, half), (half, block - half), (block, half), (block + half, half)]
    far = second.spread(spans)
    ring_grads = RingScatter(lambda k: second.sums[k, :block], far[:2], peers)
    ring_results = RingScatter(lambda k: second.sums[k, block:], far[2:], peers)
    ring_grads.step()
    got = ring_first.got
    while ring_first.at > 1:
        ring_first.step(second.sums)
    picked, grad_result, activated, grad_pre = Experts.kept
    place_at = jnp.stack([lax.rem(dp_at, 2), dp_at // 2])
    ring_grads.step()
    w_out_sum = weight_grads(
        after(activated, *ring_grads.sent, *ring_first.sent), grad_result, 0, local_experts, None
    )
    def backward(m, pieces, *earlier):
        own, left, right = pieces
        return block_call(
            backward_kernel,
            [
                (after(own, *earlier), (0,), block),
                (left, (), block),
                (right, (), block),
                (cotangent, (m,)),
                (hidden[m],),
                (tokens, (m,)),
                (query, (m,)),
                (keyval, (m,)),
                (seg_col, (m,)),
                (seg_row, (m,)),
                (gates, (m,)),
                (gains,),
                (cos,),
                (sin,),
                (first_whole,),
                (out_whole,),
            ],
            [
                jax.ShapeDtypeStruct((rows, width), jnp.bfloat16),
                jax.ShapeDtypeStruct((rows, proj_width + 128), jnp.bfloat16),
                jax.ShapeDtypeStruct((rows, width), jnp.bfloat16),
                jax.ShapeDtypeStruct((8, width), jnp.float32),
            ],
            "attention_backward",
            [pltpu.VMEM((rows, q_width), jnp.bfloat16)],
        )

    half = max(1, local_experts // 2)
    got = second_got = ring_grads.got
    ring_grads.step(w_out_sum)
    picked = after(picked, w_out_sum, *got, *ring_grads.sent)
    w_in_sum = weight_grads(picked, grad_pre, 0, half, None)
    while ring_grads.at > 0:
        got = ring_grads.got
        ring_grads.step(w_in_sum)
    last = ring_first.got
    while ring_first.at > 0:
        ring_first.step(*ring_grads.sent)
    picked = after(picked, w_in_sum, *got, *ring_grads.sent, *ring_first.sent)
    w_in_sum = weight_grads(picked, grad_pre, half, local_experts - half, w_in_sum)
    got = last
    ring_results.step(*got)
    grad_w_out = lax.psum_scatter(
        after(w_out_sum, *second_got), "dp", scatter_dimension=1, tiled=True
    )
    grad_w_in = lax.psum_scatter(
        after(w_in_sum, *ring_grads.got), "dp", scatter_dimension=1, tiled=True
    )
    back_second = backward(1, (second.sums, ring_grads.left, ring_grads.right), w_in_sum)
    ring_results.step(back_second[3], *got)
    back_first = backward(
        0, (first.sums, ring_first.left, ring_first.right), *ring_results.sent
    )
    ring_results.step(back_first[3])
    grad_tokens, grad_proj, grad_attn, gain_sums = zip(back_first, back_second)
    mine, other = attention_grads(
        place_at, after(xn1, *ring_results.sent), mixed, grad_proj, grad_attn, gain_sums, dp_count
    )
    grads, grad_w_in, grad_w_out = reduce_packed(
        mine, other, my_spot, peers, dp_count, grad_w_in, grad_w_out, ring_results, (q_width, kv_width)
    )
    grad_query, grad_keyval, grad_small, grad_attn_out = grads
    wide = jnp.float32
    outputs = []
    for m, (own, ring, at) in enumerate(
        ((first.sums, ring_first, block), (second.sums, ring_results, 0))
    ):
        total = hidden[m] + own[0, block:].astype(wide)
        total = total + ring.left[at:].astype(wide) + ring.right[at:].astype(wide)
        outputs.append(total.astype(jnp.bfloat16))
    return (
        jnp.stack(outputs),
        jnp.stack(grad_tokens),
        grad_small[:, experts],
        grad_small[:, experts + 1],
        grad_query,
        grad_keyval,
        grad_attn_out,
        grad_small[:, :experts],
        grad_w_in,
        grad_w_out,
    )


def last_kernel(spot_ref, *refs):
    outs = refs[-4:]
    blocks = refs[:-4]
    peers = len(blocks) - 1
    piece = blocks[0].shape[0]
    for k, block_ref in enumerate(blocks):
        distance = k if k <= peers // 2 else k - 1
        spot = lax.rem(spot_ref[0] - distance + peers, peers)
        held = block_ref.shape[0]
        row = spot * piece + (held if k == peers // 2 + 1 else 0)
        at = 0
        for out_ref in outs:
            columns = out_ref.shape[1]
            out_ref[pl.ds(pl.multiple_of(row, 8), held), :] = block_ref[
                :, at : at + columns
            ].astype(jnp.float32)
            at += columns


def reduce_packed(mine, other, my_spot, peers, dp_count, grad_w_in, grad_w_out, ring_results, widths):
    lines, span, columns = mine.shape
    swap = [(d, d ^ 1) for d in range(dp_count)]
    while ring_results.at > 1:
        ring_results.step()
    total = add_rows(mine, lax.ppermute(other, "dp", swap))
    total = after(total, *ring_results.got)
    piece = span // peers
    total = total.reshape(lines, peers, piece, columns)

    def part(k):
        at = lax.rem(my_spot - k + peers, peers)
        return lax.dynamic_slice_in_dim(total, at, 1, axis=1).reshape(lines * piece, columns)

    half = lines * piece // 2
    farthest = part(peers // 2)
    ring = RingScatter(part, (farthest[:half], farthest[half:]), peers)
    ring.step()
    ring_results.step()
    ring.step(*ring_results.sent)
    while ring.at > 0:
        ring.step()
    own, left, right = [held.astype(jnp.float32) for held in (part(0), ring.left, ring.right)]
    mine = (own + left + right).astype(jnp.bfloat16).reshape(lines, piece, columns)
    mine = after(mine, grad_w_in, grad_w_out, *ring_results.got)
    line = lax.axis_index("dp") // 2

    def for_line(at):
        return lax.dynamic_index_in_dim(mine, lax.rem(at, lines), 0, keepdims=False)

    share = for_line(line).astype(jnp.float32)
    for k in range(1, lines):
        pairs = [(d, (d + 2 * k) % dp_count) for d in range(dp_count)]
        share = share + lax.ppermute(for_line(line + k), "dp", pairs)
    gather = RingGather(share.astype(jnp.bfloat16), peers, piece // 2)
    gather.step()
    grad_w_out = grad_w_out.astype(jnp.float32)
    gather.step(grad_w_out)
    grad_w_in = grad_w_in.astype(jnp.float32)
    gather.step(grad_w_in, *ring_results.got)
    while gather.far is None:
        gather.step()
    blocks = gather.from_left + list(gather.far) + gather.from_right[:0:-1]
    columns = (widths[0], widths[1], 128, columns - sum(widths) - 128)
    if piece % 16 == 0:
        grads = block_call(
            last_kernel,
            [(block,) for block in blocks],
            [jax.ShapeDtypeStruct((span, count), jnp.float32) for count in columns],
            "last_rows",
            prefetch=my_spot.astype(jnp.int32).reshape(1),
        )
    else:
        far = jnp.concatenate(gather.far, axis=0)
        by_distance = jnp.stack(gather.from_left + [far] + gather.from_right[:0:-1])
        distance = lax.rem(my_spot - jnp.arange(peers, dtype=jnp.int32) + peers, peers)
        by_spot = jnp.take(by_distance, distance, axis=0).reshape(span, -1).astype(jnp.float32)
        edges = [sum(columns[:i]) for i in range(5)]
        grads = [by_spot[:, edges[i] : edges[i + 1]] for i in range(4)]
    return grads, grad_w_in, grad_w_out


def solution(mesh):
    return jax.shard_map(
        per_device,
        mesh=mesh,
        in_specs=(
            P(None, ("dp", "expert"), None),
            P(None, ("dp", "expert")),
            P(None, ("dp", "expert"), None),
            P("dp"),
            P("dp"),
            P("dp", None),
            P("dp", None),
            P("dp", None),
            P("dp", None),
            P("expert", None, None),
            P("expert", None, None),
            P(None, ("dp", "expert"), None),
        ),
        out_specs=(
            P(None, ("dp", "expert"), None),
            P(None, ("dp", "expert"), None),
            P("dp"),
            P("dp"),
            P("dp", None),
            P("dp", None),
            P("dp", None),
            P("dp", None),
            P("expert", "dp", None),
            P("expert", "dp", None),
        ),
        check_vma=False,
    )
```

```python
import functools
import math

import jax
import jax.numpy as jnp
from jax import lax
from jax.experimental import pallas as pl
from jax.experimental.pallas import tpu as pltpu
from jax.sharding import PartitionSpec as P

QUERY_HEADS = 12
KEY_VALUE_HEADS = 2
HEAD_SIZE = 128
FF = 768
TOPK = 4
EXPERTS = 32
EXTRA = 16
PIECES = 3
GROUP = 8

eps_norm = 1e-06
rope_base = 1000000.0
mask_fill = -1e30
highest = lax.Precision.HIGHEST


def rms_scale(tensor):
    return lax.rsqrt(jnp.mean(tensor * tensor, axis=-1, keepdims=True) + eps_norm)


def rope_tables(sequence_length, head_width):
    positions = jnp.arange(sequence_length).astype(jnp.float32)
    frequency = rope_base ** (-(jnp.arange(head_width // 2).astype(jnp.float32) * 2.0) / head_width)
    angles = positions[:, None] * frequency[None, :]
    return (jnp.cos(angles), jnp.sin(angles))

SCORE_SCALE = 1.0 / math.sqrt(HEAD_SIZE)
GELU_SCALE = math.sqrt(2.0 / math.pi)
GELU_CUBE = 0.044715
SMALL_COST = pl.CostEstimate(flops=1_000_000, bytes_accessed=1_000_000, transcendentals=0)


def after(value, *earlier):
    return lax.optimization_barrier((value,) + earlier)[0]


def slot_hits(routes_all, first_expert, local_experts, capacity):
    rows = routes_all.shape[-1]
    names = first_expert + jnp.arange(local_experts, dtype=jnp.int32)
    named = routes_all[:, None].astype(jnp.int32) == names[None, :, None, None]
    member = jnp.any(named, axis=2)
    lower = (jnp.arange(rows)[:, None] < jnp.arange(rows)[None, :]).astype(jnp.bfloat16)
    rank = dot32(member.astype(jnp.bfloat16).reshape(-1, rows), lower).reshape(member.shape)
    slots = jnp.arange(capacity, dtype=jnp.float32)
    return member[:, :, None, :] & (rank[:, :, None, :] == slots[None, None, :, None])


def pack_pieces(values, out_ref, first_row):
    rows = values.shape[1]
    rest = values
    for piece in range(PIECES):
        part = rest.astype(jnp.bfloat16)
        rest = rest - part.astype(jnp.float32)
        for half in range(EXPERTS // EXTRA):
            at = (piece * (EXPERTS // EXTRA) + half) * rows
            out_ref[first_row : first_row + EXTRA, at : at + rows] = part[
                half * EXTRA : (half + 1) * EXTRA
            ]


def dot32(left, right):
    return jnp.dot(left, right, preferred_element_type=jnp.float32)


def dot_nt(left, right):
    return lax.dot_general(
        left, right, (((1,), (1,)), ((), ())), preferred_element_type=jnp.float32
    )


def dot_tn(left, right):
    return lax.dot_general(
        left, right, (((0,), (0,)), ((), ())), preferred_element_type=jnp.float32
    )


def mask_of(seg_col, seg_row):
    rows = seg_col.shape[0]
    query_at = lax.broadcasted_iota(jnp.int32, (rows, rows), 0)
    key_at = lax.broadcasted_iota(jnp.int32, (rows, rows), 1)
    return (seg_col == seg_row) & (query_at >= key_at)


def softmax_rows(query, key, allowed):
    scores = jnp.where(allowed, dot_nt(query, key) * SCORE_SCALE, mask_fill)
    weight = jnp.exp(scores - jnp.max(scores, axis=-1, keepdims=True))
    return weight / jnp.sum(weight, axis=-1, keepdims=True)


def from_blocks(starts_ref, rows_ref, blocks):
    total = None
    for at, block_ref in enumerate(blocks):
        span = block_ref.shape[0]
        columns = pl.ds(pl.multiple_of(starts_ref[at], 128), span)
        part = dot32(rows_ref[:, columns], block_ref[...])
        total = part if total is None else total + part
    return total


def attention_kernel(
    starts_ref,
    tok_ref,
    seg_col_ref,
    seg_row_ref,
    routes_ref,
    cos_ref,
    sin_ref,
    *refs,
):
    weight_refs = refs[:-7]
    xn1_ref, query_ref, keyval_ref, mixed_ref, gates_ref, gates_pack_ref, gains_ref = refs[-7:]

    @pl.when(pl.program_id(0) == 0)
    def _():
        for at, block_ref in enumerate(weight_refs):
            span, columns = block_ref.shape
            pad = block_ref[:, columns - 128 :].astype(jnp.float32).T
            place = pl.ds(pl.multiple_of(starts_ref[at], 128), span)
            gains_ref[:, place] = pad[2 * EXPERTS : 2 * EXPERTS + 8]

    tok = tok_ref[...].astype(jnp.float32)
    xn1_ref[...] = (tok * rms_scale(tok) * gains_ref[0:1, :]).astype(jnp.bfloat16)
    proj = from_blocks(starts_ref, xn1_ref, weight_refs)
    cos, sin = cos_ref[...], sin_ref[...]

    def rotate(part):
        return (part * cos + pltpu.roll(part, HEAD_SIZE // 2, 1) * sin).astype(jnp.bfloat16)

    q_width = QUERY_HEADS * HEAD_SIZE
    k_width = KEY_VALUE_HEADS * HEAD_SIZE
    for head in range(QUERY_HEADS):
        span = slice(head * HEAD_SIZE, (head + 1) * HEAD_SIZE)
        query_ref[:, span] = rotate(proj[:, span])
    for head in range(KEY_VALUE_HEADS):
        span = slice(head * HEAD_SIZE, (head + 1) * HEAD_SIZE)
        keyval_ref[:, span] = rotate(proj[:, q_width:][:, span])
    keyval_ref[:, k_width:] = proj[:, q_width + k_width : q_width + 2 * k_width].astype(
        jnp.bfloat16
    )
    logits = proj[:, q_width + 2 * k_width :]
    columns = lax.broadcasted_iota(jnp.int32, logits.shape, 1)
    named = [columns == routes_ref[:, j : j + 1] for j in range(TOPK)]
    chosen = [jnp.sum(jnp.where(hit, logits, 0.0), axis=-1, keepdims=True) for hit in named]
    top = functools.reduce(jnp.maximum, chosen)
    weight = [jnp.exp(part - top) for part in chosen]
    total = functools.reduce(jnp.add, weight)
    gates = jnp.full(logits.shape, -1.0, jnp.float32)
    for hit, part in zip(named, weight):
        gates = jnp.where(hit, part / total, gates)
    gates_ref[...] = gates
    pack_pieces(gates.T[:EXPERTS], gates_pack_ref, 0)
    allowed = mask_of(seg_col_ref[...], seg_row_ref[...])
    for head in range(QUERY_HEADS):
        span = slice(head * HEAD_SIZE, (head + 1) * HEAD_SIZE)
        group = head // (QUERY_HEADS // KEY_VALUE_HEADS)
        key = keyval_ref[:, group * HEAD_SIZE : (group + 1) * HEAD_SIZE]
        value = keyval_ref[:, k_width + group * HEAD_SIZE : k_width + (group + 1) * HEAD_SIZE]
        probs = softmax_rows(query_ref[:, span], key, allowed)
        mixed_ref[:, span] = dot32(probs.astype(jnp.bfloat16), value).astype(jnp.bfloat16)


def hidden_kernel(starts_ref, mixed_ref, tok_ref, gains_ref, pack_ref, *refs):
    weight_refs = refs[:-2]
    hidden_ref, xn2_ref = refs[-2:]
    rows = tok_ref.shape[0]
    hidden = tok_ref[...].astype(jnp.float32) + from_blocks(
        starts_ref, mixed_ref, weight_refs
    )
    hidden_ref[...] = hidden
    xn2_ref[:rows, :] = (hidden * rms_scale(hidden) * gains_ref[1:2, :]).astype(jnp.bfloat16)
    xn2_ref[rows:, :] = pack_ref[...]


def backward_kernel(
    own_ref,
    left_ref,
    right_ref,
    cot_ref,
    hidden_ref,
    tok_ref,
    query_ref,
    keyval_ref,
    seg_col_ref,
    seg_row_ref,
    gates_ref,
    gains_ref,
    cos_ref,
    sin_ref,
    *refs,
):
    weight_ref, out_weight_ref = refs[:2]
    grad_tok_ref, grad_proj_ref, grad_attn_ref, gain_sum_ref, mixed_grad_ref = refs[2:]
    width = tok_ref.shape[1]
    q_width = QUERY_HEADS * HEAD_SIZE
    k_width = KEY_VALUE_HEADS * HEAD_SIZE
    proj_width = q_width + 2 * k_width
    rows = tok_ref.shape[0]
    sums = [ref[...].astype(jnp.float32) for ref in (own_ref, left_ref, right_ref)]
    sums = sums[0] + sums[1] + sums[2]
    grad_xn2, pack = sums[:rows], sums[rows:]
    halves = EXPERTS // EXTRA
    lines = [
        sum(
            pack[:, (piece * halves + half) * rows : (piece * halves + half + 1) * rows]
            for piece in range(PIECES)
        )
        for half in range(halves)
    ]
    lines.append(jnp.zeros((128 - EXPERTS, rows), jnp.float32))
    grad_gates = jnp.concatenate(lines, axis=0).T
    hidden = hidden_ref[...]
    scale = rms_scale(hidden)
    unit = hidden * scale
    gain_sum_ref[...] = jnp.zeros(gain_sum_ref.shape, jnp.float32)
    gain_sum_ref[1:2, :] = jnp.sum(grad_xn2 * unit, axis=0, keepdims=True)
    grad_unit = grad_xn2 * gains_ref[1:2, :]
    grad_hidden = cot_ref[...].astype(jnp.float32) + scale * (
        grad_unit - unit * jnp.mean(grad_unit * unit, axis=-1, keepdims=True)
    )
    grad_attn_ref[...] = grad_hidden.astype(jnp.bfloat16)
    mixed_grad_ref[...] = dot_nt(grad_attn_ref[...], out_weight_ref[...]).astype(jnp.bfloat16)
    cos, sin = cos_ref[...], sin_ref[...]

    def unrotate(part):
        return (part * cos - pltpu.roll(part, HEAD_SIZE // 2, 1) * sin).astype(jnp.bfloat16)

    allowed = mask_of(seg_col_ref[...], seg_row_ref[...])
    per_group = QUERY_HEADS // KEY_VALUE_HEADS
    for group in range(KEY_VALUE_HEADS):
        key_span = slice(group * HEAD_SIZE, (group + 1) * HEAD_SIZE)
        value_span = slice(k_width + group * HEAD_SIZE, k_width + (group + 1) * HEAD_SIZE)
        key, value = keyval_ref[:, key_span], keyval_ref[:, value_span]
        grad_key = jnp.zeros(key.shape, jnp.float32)
        grad_value = jnp.zeros(key.shape, jnp.float32)
        for head in range(group * per_group, (group + 1) * per_group):
            span = slice(head * HEAD_SIZE, (head + 1) * HEAD_SIZE)
            query, grad_mixed = query_ref[:, span], mixed_grad_ref[:, span]
            probs = softmax_rows(query, key, allowed)
            grad_value += dot_tn(probs.astype(jnp.bfloat16), grad_mixed)
            grad_probs = dot_nt(grad_mixed, value)
            mean = jnp.sum(probs * grad_probs, axis=-1, keepdims=True)
            grad_scores = (probs * (grad_probs - mean)).astype(jnp.bfloat16)
            grad_proj_ref[:, span] = unrotate(dot32(grad_scores, key) * SCORE_SCALE)
            grad_key += dot_tn(grad_scores, query)
        grad_proj_ref[:, q_width + group * HEAD_SIZE : q_width + (group + 1) * HEAD_SIZE] = (
            unrotate(grad_key * SCORE_SCALE)
        )
        first = q_width + k_width + group * HEAD_SIZE
        grad_proj_ref[:, first : first + HEAD_SIZE] = grad_value.astype(jnp.bfloat16)
    gates = jnp.maximum(gates_ref[...], 0.0)
    grad_logits = gates * (grad_gates - jnp.sum(gates * grad_gates, axis=-1, keepdims=True))
    high = grad_logits.astype(jnp.bfloat16).astype(jnp.float32)
    low = pltpu.roll(grad_logits - high, EXPERTS, 1)
    grad_proj_ref[:, proj_width:] = (high + low).astype(jnp.bfloat16)
    grad_xn1 = dot_nt(grad_proj_ref[...], weight_ref[...])
    tok = tok_ref[...].astype(jnp.float32)
    scale = rms_scale(tok)
    unit = tok * scale
    gain_sum_ref[0:1, :] = jnp.sum(grad_xn1 * unit, axis=0, keepdims=True)
    grad_unit = grad_xn1 * gains_ref[0:1, :]
    grad_tok_ref[...] = (
        grad_hidden
        + scale * (grad_unit - unit * jnp.mean(grad_unit * unit, axis=-1, keepdims=True))
    ).astype(jnp.bfloat16)


def ring_order(peers):
    minor = peers // 4
    walk = []
    for col in range(minor):
        line = range(4) if col % 2 == 0 else range(3, -1, -1)
        walk += [row * minor + col for row in line]
    return walk


def ring_step(part, shift, peers):
    order = ring_order(peers)
    pairs = [(order[i], order[(i + shift) % peers]) for i in range(peers)]
    return lax.ppermute(part, "expert", pairs)


class RingGather:
    def __init__(self, part, peers, half):
        self.peers, self.half = peers, half
        self.from_left, self.from_right = [part], [part]
        self.far = None
        self.got = ()

    def step(self, *earlier):
        left, right = self.from_left[-1], self.from_right[-1]
        last = len(self.from_left) == self.peers // 2
        if last:
            left, right = left[: self.half], right[self.half :]
        left, right = self.sent = lax.optimization_barrier((left, right) + earlier)[:2]
        left, right = ring_step(left, 1, self.peers), ring_step(right, -1, self.peers)
        self.got = (left, right)
        if last:
            self.far = (left, right)
        else:
            self.from_left.append(left)
            self.from_right.append(right)
        return self

    def rows(self, k, first, count):
        if k < len(self.from_left):
            return self.from_left[k], first
        if k > self.peers // 2:
            return self.from_right[self.peers - k], first
        if first < self.half:
            return self.far[0], first
        return self.far[1], first - self.half

    def stack_rows(self, first, count):
        found = [self.rows(k, first, count) for k in range(self.peers)]
        return jnp.stack([array[at : at + count] for array, at in found])


class RingScatter:
    def __init__(self, part, far, peers):
        self.part, self.far, self.peers = part, far, peers
        self.at = peers // 2
        self.half = far[0].shape[0]

    def step(self, *earlier):
        peers, k, half = self.peers, self.at, self.half
        if k == peers // 2:
            left, right = lax.optimization_barrier(tuple(self.far) + earlier)[:2]
        else:
            left, right = self.part(k), self.part(peers - k)
            if earlier:
                self.left, self.right = lax.optimization_barrier(
                    (self.left, self.right) + earlier
                )[:2]
            if k == peers // 2 - 1:
                kept = left[half:].astype(jnp.bfloat16), right[:half].astype(jnp.bfloat16)
                left = jnp.concatenate([add_rows(left[:half], self.left), kept[0]], axis=0)
                right = jnp.concatenate([kept[1], add_rows(right[half:], self.right)], axis=0)
            else:
                left, right = add_rows(left, self.left), add_rows(right, self.right)
        left, right = self.sent = lax.optimization_barrier((left, right))
        self.left = ring_step(left, -1, peers)
        self.right = ring_step(right, 1, peers)
        self.got = (self.left, self.right)
        self.at = k - 1
        return self


def add_rows(left, right):
    return (left.astype(jnp.float32) + right.astype(jnp.float32)).astype(jnp.bfloat16)


def expert_kernel(sources, *refs):
    rows_refs = refs[:sources]
    grad_refs = refs[sources : 2 * sources]
    gate_refs = refs[2 * sources : 3 * sources]
    w_in_ref, w_out_ref = refs[3 * sources : 3 * sources + 2]
    (
        back_rows_ref,
        back_grads_ref,
        grad_gate_ref,
        picked_ref,
        grad_result_ref,
        activated_ref,
        grad_pre_ref,
    ) = refs[-7:]
    capacity, width = rows_refs[0].shape
    for k in range(sources):
        picked_ref[pl.ds(k * capacity, capacity), :] = rows_refs[k][...]
    pre_act = dot32(picked_ref[...], w_in_ref[...])
    gate_part = pre_act[:, :FF]
    up_part = pre_act[:, FF:]
    square = gate_part * gate_part
    bend = jnp.tanh(GELU_SCALE * gate_part * (1.0 + GELU_CUBE * square))
    lift = 0.5 * (1.0 + bend)
    gelu_val = gate_part * lift
    slope = lift + 0.5 * gate_part * (1.0 - bend * bend) * (
        GELU_SCALE * (1.0 + 3.0 * GELU_CUBE * square)
    )
    activated_ref[...] = (gelu_val * up_part).astype(jnp.bfloat16)
    result = dot32(activated_ref[...], w_out_ref[...])
    for k in range(sources):
        gates = gate_refs[k][...]
        span = slice(k * capacity, (k + 1) * capacity)
        grad_rows = grad_refs[k][...].astype(jnp.float32)
        grad_gate_ref[span, :] = jnp.sum(result[span] * grad_rows, axis=-1, keepdims=True)
        back_rows_ref[k] = (result[span] * gates).astype(jnp.bfloat16)
        grad_result_ref[span, :] = (grad_rows * gates).astype(jnp.bfloat16)
    grad_act = lax.dot_general(
        grad_result_ref[...],
        w_out_ref[...],
        (((1,), (1,)), ((), ())),
        preferred_element_type=jnp.float32,
    )
    grad_pre_ref[:, :FF] = (grad_act * up_part * slope).astype(jnp.bfloat16)
    grad_pre_ref[:, FF:] = (grad_act * gelu_val).astype(jnp.bfloat16)
    grad_in = lax.dot_general(
        grad_pre_ref[...],
        w_in_ref[...],
        (((1,), (1,)), ((), ())),
        preferred_element_type=jnp.float32,
    ).astype(jnp.bfloat16)
    for k in range(sources):
        back_grads_ref[k] = grad_in[k * capacity : (k + 1) * capacity]


def expert_pass(rows_list, grads_list, gate_slots, w_in, w_out, held_outs, position, first, count):
    sources = len(rows_list)
    local_experts, width, _ = w_in.shape
    slots = rows_list[0].shape[0]
    capacity = slots // local_experts
    held = sources * capacity
    block_spec = pl.BlockSpec((capacity, width), lambda e: (e + first, 0))
    back_spec = pl.BlockSpec((sources, capacity, width), lambda e: (0, e + first, 0))
    column_spec = pl.BlockSpec((None, held, 1), lambda e: (e + first, 0, 0))

    def kept_spec(columns):
        return pl.BlockSpec((None, held, columns), lambda e: (e + first, position[0], 0))

    def kept_shape(columns):
        return jax.ShapeDtypeStruct((local_experts, position[1] * held, columns), jnp.bfloat16)

    kept_widths = (width, width, FF, 2 * FF)
    first_held = 3 * sources + 2
    given = [(i, part) for i, part in enumerate(held_outs) if part is not None]
    return pl.pallas_call(
        functools.partial(expert_kernel, sources),
        grid=(count,),
        in_specs=[block_spec] * (2 * sources)
        + [pl.BlockSpec((capacity, 1), lambda e: (e + first, 0))] * sources
        + [
            pl.BlockSpec((None, width, 2 * FF), lambda e: (e + first, 0, 0)),
            pl.BlockSpec((None, FF, width), lambda e: (e + first, 0, 0)),
        ]
        + [pl.BlockSpec(memory_space=pl.ANY)] * len(given),
        out_specs=[back_spec, back_spec, column_spec] + [kept_spec(c) for c in kept_widths],
        out_shape=[
            jax.ShapeDtypeStruct((sources, slots, width), jnp.bfloat16),
            jax.ShapeDtypeStruct((sources, slots, width), jnp.bfloat16),
            jax.ShapeDtypeStruct((local_experts, held, 1), jnp.float32),
        ]
        + [kept_shape(c) for c in kept_widths],
        input_output_aliases={first_held + at: i for at, (i, _) in enumerate(given)},
        compiler_params=pltpu.CompilerParams(vmem_limit_bytes=60 * 1024 * 1024),
        cost_estimate=SMALL_COST,
        name="expert_pass",
    )(*rows_list, *grads_list, *gate_slots, w_in, w_out, *[part for _, part in given])


def block_call(kernel, operands, out_shape, name, scratch=(), prefetch=None):
    def spec(array, lead=(), rows=None):
        rest = array.shape[len(lead) :]
        at = lead + (0,) * len(rest)
        if rows is not None:
            count, block = rows if isinstance(rows, tuple) else (rows, 0)
            rest = (count,) + rest[1:]
            at = lead + (block,) + (0,) * (len(rest) - 1)
        return pl.BlockSpec((None,) * len(lead) + rest, lambda *_: at)

    scalars = [] if prefetch is None else [prefetch]
    return pl.pallas_call(
        kernel,
        grid_spec=pltpu.PrefetchScalarGridSpec(
            num_scalar_prefetch=len(scalars),
            grid=(1,),
            in_specs=[spec(*operand) for operand in operands],
            out_specs=[spec(shape) for shape in out_shape],
            scratch_shapes=list(scratch),
        ),
        out_shape=out_shape,
        compiler_params=pltpu.CompilerParams(vmem_limit_bytes=60 * 1024 * 1024),
        cost_estimate=SMALL_COST,
        name=name,
    )(*scalars, *[operand[0] for operand in operands])


def pick_kernel(shares, gated, first_ref, place_ref, *refs):
    at = 0
    outs = refs[sum(count for _, count in shares) + (len(shares) if gated else 0) :]
    for number, (k, count) in enumerate(shares):
        total, row = None, 0
        for block_ref in refs[at : at + count]:
            held = block_ref.shape[0]
            part = dot32(place_ref[k, :, row : row + held], block_ref[...])
            total = part if total is None else total + part
            row += held
        outs[number][...] = total.astype(jnp.bfloat16)
        at += count
        if gated:
            slot_gates(first_ref[0], place_ref[k], refs[at], outs[len(shares) + number])
            at += 1


def slot_gates(first_expert, place, pack_ref, out_ref):
    slots, rows = place.shape
    pack = pack_ref[...].astype(jnp.float32)
    halves = EXPERTS // EXTRA
    line = lax.broadcasted_iota(jnp.int32, (EXTRA, rows), 0)
    local_experts = slots * 4 // rows
    capacity = rows // 4
    for e in range(local_experts):
        gate = jnp.zeros((1, rows), jnp.float32)
        for half in range(halves):
            hit = line + half * EXTRA == first_expert + e
            for piece in range(PIECES):
                at = (piece * halves + half) * rows
                gate += jnp.sum(
                    jnp.where(hit, pack[:, at : at + rows], 0.0), axis=0, keepdims=True
                )
        span = slice(e * capacity, (e + 1) * capacity)
        out_ref[span, :] = jnp.sum(
            place[span].astype(jnp.float32) * gate, axis=-1, keepdims=True
        )


def pick_rows(first_expert, place, ring, distances, gated):
    _, slots, rows = place.shape
    half = rows // 2
    operands, shares = [], []
    for k in distances:
        spans = [(0, rows)]
        if k == ring.peers // 2 and ring.half < rows:
            spans = [(0, half), (half, half)]
        shares.append((k, len(spans)))
        for at, count in spans + ([(rows, EXTRA)] if gated else []):
            array, at = ring.rows(k, at, count)
            operands.append((array, (), (count, at // count)))
    width = operands[0][0].shape[-1]
    out_shape = [jax.ShapeDtypeStruct((slots, width), jnp.bfloat16) for _ in distances]
    if gated:
        out_shape += [jax.ShapeDtypeStruct((slots, 1), jnp.float32) for _ in distances]
    return block_call(
        functools.partial(pick_kernel, shares, gated),
        [(place,)] + operands,
        out_shape,
        "pick_rows",
        prefetch=first_expert,
    )


def spread_kernel(middle, spans, held, first_ref, place_ref, rows_ref, grads_ref, gate_ref, *refs):
    out_ref, *far_refs = refs[held:]
    place = place_ref[...]
    rows = place.shape[1]
    out_ref[:rows, :] = dot_tn(place, grads_ref[...]).astype(jnp.bfloat16)
    out_ref[rows + EXTRA :, :] = dot_tn(place, rows_ref[...]).astype(jnp.bfloat16)
    capacity = gate_ref.shape[1]
    expert = lax.broadcasted_iota(jnp.int32, (EXPERTS, rows), 0) - first_ref[0]
    gates = jnp.zeros((EXPERTS, rows), jnp.float32)
    for e in range(gate_ref.shape[0]):
        hit = place[e * capacity : (e + 1) * capacity].astype(jnp.float32)
        line = jnp.sum(hit * gate_ref[e], axis=0, keepdims=True)
        gates = jnp.where(expert == e, line, gates)
    pack_pieces(gates, out_ref, rows)

    @pl.when(pl.program_id(0) == middle)
    def _():
        for far_ref, (row, count) in zip(far_refs, spans):
            far_ref[...] = out_ref[row : row + count, :]


def spread_rows(first_expert, place, rows_back, grads_back, gate_slots, group, spans, held):
    sources, slots, rows = place.shape
    width = rows_back.shape[-1]
    local_experts = gate_slots.shape[0]
    base = group * GROUP
    by_source = pl.BlockSpec((None, slots, width), lambda k, f: (k, 0, 0))
    held = [] if held is None else [held]
    out_shape = [jax.ShapeDtypeStruct((sources, 2 * rows + EXTRA, width), jnp.bfloat16)]
    out_shape += [jax.ShapeDtypeStruct((count, width), jnp.bfloat16) for _, count in spans]
    out_specs = [pl.BlockSpec((None, 2 * rows + EXTRA, width), lambda k, f: (base + k, 0, 0))]
    out_specs += [pl.BlockSpec((count, width), lambda k, f: (0, 0)) for _, count in spans]
    return pl.pallas_call(
        functools.partial(spread_kernel, sources // 2 - base, spans, len(held)),
        grid_spec=pltpu.PrefetchScalarGridSpec(
            num_scalar_prefetch=1,
            grid=(GROUP,),
            in_specs=[
                pl.BlockSpec((None, slots, rows), lambda k, f: (base + k, 0, 0)),
                by_source,
                by_source,
                pl.BlockSpec((local_experts, slots // local_experts, 1), lambda k, f: (0, k, 0)),
            ]
            + [pl.BlockSpec(memory_space=pl.ANY)] * len(held),
            out_specs=out_specs,
        ),
        out_shape=out_shape,
        input_output_aliases={5 + i: i for i in range(len(held))},
        compiler_params=pltpu.CompilerParams(vmem_limit_bytes=60 * 1024 * 1024),
        cost_estimate=SMALL_COST,
        name="spread_rows",
    )(first_expert, place, rows_back, grads_back, gate_slots, *held)


def weight_grad_kernel(left_ref, right_ref, *refs):
    refs[-1][...] = dot_tn(left_ref[...], right_ref[...]).astype(jnp.bfloat16)


def weight_grads(left, right, first, count, held_out):
    experts, held, height = left.shape
    columns = right.shape[-1]
    tile = min(height, 768)
    given = [] if held_out is None else [held_out]
    return pl.pallas_call(
        weight_grad_kernel,
        grid=(count, height // tile),
        in_specs=[
            pl.BlockSpec((None, held, tile), lambda e, i: (e + first, 0, i)),
            pl.BlockSpec((None, held, columns), lambda e, i: (e + first, 0, 0)),
        ]
        + [pl.BlockSpec(memory_space=pl.ANY)] * len(given),
        out_specs=pl.BlockSpec((None, tile, columns), lambda e, i: (e + first, i, 0)),
        out_shape=jax.ShapeDtypeStruct((experts, height, columns), jnp.bfloat16),
        input_output_aliases={2: 0} if given else {},
        compiler_params=pltpu.CompilerParams(vmem_limit_bytes=60 * 1024 * 1024),
        cost_estimate=SMALL_COST,
        name="weight_grads",
    )(left, right, *given)


def attention_forward(starts, tokens, seg_col, seg_row, routes, cos, sin, weights):
    count, rows, width = tokens.shape

    def by_micro(*shape):
        return pl.BlockSpec((None,) + shape, lambda m, s: (m,) + (0,) * len(shape))

    def shared(part):
        return pl.BlockSpec(part.shape, lambda m, s: (0, 0))

    kv_width = 2 * KEY_VALUE_HEADS * HEAD_SIZE
    shapes = [
        ((rows, width), jnp.bfloat16),
        ((rows, QUERY_HEADS * HEAD_SIZE), jnp.bfloat16),
        ((rows, kv_width), jnp.bfloat16),
        ((rows, QUERY_HEADS * HEAD_SIZE), jnp.bfloat16),
        ((rows, 128), jnp.float32),
        ((EXTRA, PIECES * EXPERTS // EXTRA * rows), jnp.bfloat16),
    ]
    return pl.pallas_call(
        attention_kernel,
        grid_spec=pltpu.PrefetchScalarGridSpec(
            num_scalar_prefetch=1,
            grid=(count,),
            in_specs=[
                by_micro(rows, width),
                by_micro(rows, 1),
                by_micro(1, rows),
                by_micro(rows, TOPK),
                shared(cos),
                shared(sin),
            ]
            + [shared(part) for part in weights],
            out_specs=[by_micro(*shape) for shape, _ in shapes]
            + [pl.BlockSpec((8, width), lambda m, s: (0, 0))],
        ),
        out_shape=[jax.ShapeDtypeStruct((count,) + shape, kind) for shape, kind in shapes]
        + [jax.ShapeDtypeStruct((8, width), jnp.float32)],
        compiler_params=pltpu.CompilerParams(vmem_limit_bytes=60 * 1024 * 1024),
        cost_estimate=SMALL_COST,
        name="attention_forward",
    )(starts, tokens, seg_col, seg_row, routes, cos, sin, *weights)


def join_kernel(starts_ref, *refs):
    for at, block_ref in enumerate(refs[:-1]):

        @pl.when(pl.program_id(0) == at)
        def _():
            refs[-1][...] = block_ref[...]


def join_blocks(starts, blocks):
    if len(blocks) == 1:
        return blocks[0]
    span, columns = blocks[0].shape
    return pl.pallas_call(
        join_kernel,
        grid_spec=pltpu.PrefetchScalarGridSpec(
            num_scalar_prefetch=1,
            grid=(len(blocks),),
            in_specs=[pl.BlockSpec((span, columns), lambda i, s: (0, 0)) for _ in blocks],
            out_specs=pl.BlockSpec((span, columns), lambda i, s: (s[i] // span, 0)),
        ),
        out_shape=jax.ShapeDtypeStruct((len(blocks) * span, columns), blocks[0].dtype),
        compiler_params=pltpu.CompilerParams(vmem_limit_bytes=60 * 1024 * 1024),
        cost_estimate=SMALL_COST,
        name="join_blocks",
    )(starts, *blocks)


def attention_grad_kernel(core_ref, xn1, mixed, *refs):
    count = xn1.shape[0]
    proj, attn, sums = [refs[i * count : (i + 1) * count] for i in range(3)]
    mine_ref, other_ref = refs[-2:]
    split = proj[0].shape[1]
    span = mine_ref.shape[0]
    grad = sum(dot_tn(xn1[m], proj[m][...]) for m in range(count))
    router = grad[:, split - 128 :]
    lane = lax.broadcasted_iota(jnp.int32, router.shape, 1)
    router = router + pltpu.roll(router, 128 - EXPERTS, 1)
    gain = sum(part[...] for part in sums)
    lines = [jnp.zeros((EXPERTS, gain.shape[1]), jnp.float32), gain]
    lines.append(jnp.zeros((128 - EXPERTS - gain.shape[0], gain.shape[1]), jnp.float32))
    router = jnp.where(lane < EXPERTS, router, jnp.concatenate(lines, axis=0).T)
    first = core_ref[0] == 0

    def put(columns, value):
        value = value.astype(jnp.bfloat16)
        low, high = value[:span], value[span:]
        mine_ref[:, columns] = jnp.where(first, low, high)
        other_ref[:, columns] = jnp.where(first, high, low)

    put(slice(0, split - 128), grad[:, : split - 128])
    put(slice(split - 128, split), router)
    put(slice(split, None), sum(dot_tn(mixed[m], attn[m][...]) for m in range(count)))


def attention_grads(core, xn1, mixed, proj, attn, gain_sums, parts):
    count, rows, width = xn1.shape
    span = width // parts
    lines = parts // 2
    columns = proj[0].shape[1] + attn[0].shape[1]
    by_line = pl.BlockSpec((count, rows, 2 * span), lambda i, c: (0, 0, i))

    def shared(part):
        return pl.BlockSpec(part.shape, lambda i, c: (0, 0))

    out_spec = pl.BlockSpec((None, span, columns), lambda i, c: (i, 0, 0))
    out_shape = jax.ShapeDtypeStruct((lines, span, columns), jnp.bfloat16)
    return pl.pallas_call(
        attention_grad_kernel,
        grid_spec=pltpu.PrefetchScalarGridSpec(
            num_scalar_prefetch=1,
            grid=(lines,),
            in_specs=[by_line, by_line]
            + [shared(p) for p in proj]
            + [shared(p) for p in attn]
            + [pl.BlockSpec((p.shape[0], 2 * span), lambda i, c: (0, i)) for p in gain_sums],
            out_specs=[out_spec, out_spec],
        ),
        out_shape=[out_shape, out_shape],
        compiler_params=pltpu.CompilerParams(vmem_limit_bytes=60 * 1024 * 1024),
        cost_estimate=SMALL_COST,
        name="attention_grads",
    )(core, xn1, mixed, *proj, *attn, *gain_sums)


def gather_blocks(part, dp_at, dp_count):
    span = part.shape[0]
    if span % 128 or dp_count != 4:
        whole = lax.all_gather(part, "dp", axis=0, tiled=True)
        return lambda *earlier: [whole], jnp.zeros((1,), jnp.int32)
    line = [(d, (d + 2) % 4) for d in range(4)]
    core = [(d, d ^ 1) for d in range(4)]
    across = lax.ppermute(part, "dp", line)
    beside = lax.ppermute(part, "dp", core)
    far = lax.rem(dp_at + 2, 4)
    owners = jnp.stack([dp_at, dp_at + 1 - 2 * lax.rem(dp_at, 2), far, far + 1 - 2 * lax.rem(far, 2)])

    def blocks(*earlier):
        moved = after(across, *earlier) if earlier else across
        return [part, beside, moved, lax.ppermute(moved, "dp", core)]

    return blocks, owners * span


def per_device(
    tokens,
    segments,
    routes,
    norm_one,
    norm_two,
    w_query,
    key_value_weight,
    w_out_attn,
    w_router,
    w_in,
    w_out,
    cotangent,
):
    micro_count, rows, width = tokens.shape
    micros = range(micro_count)
    peers = lax.axis_size("expert")
    dp_count = lax.axis_size("dp")
    local_experts = w_in.shape[0]
    experts = local_experts * peers
    capacity = rows // 4
    first_expert = lax.axis_index("expert") * local_experts
    q_width = w_query.shape[1]
    kv_width = key_value_weight.shape[1]
    proj_width = q_width + kv_width
    cosine_table, sine_values = rope_tables(rows, HEAD_SIZE)
    cos = jnp.concatenate([cosine_table, cosine_table], axis=1)
    sin = jnp.concatenate([-sine_values, sine_values], axis=1)
    order = ring_order(peers)
    spot = [order.index(dev) for dev in range(peers)]
    my_spot = jnp.array(spot, jnp.int32)[lax.axis_index("expert")]

    router_pad = jnp.zeros((w_router.shape[0], 126 - 2 * experts), jnp.bfloat16)
    first_weight = jnp.concatenate(
        [
            w_query,
            key_value_weight,
            w_router,
            w_router,
            norm_one[:, None],
            norm_two[:, None],
            router_pad,
        ],
        axis=1,
    )
    dp_at = lax.axis_index("dp").astype(jnp.int32)
    first_weights, starts = gather_blocks(first_weight, dp_at, dp_count)
    out_weights, _ = gather_blocks(w_out_attn, dp_at, dp_count)

    routes_rows = jnp.swapaxes(routes, 1, 2).reshape(-1, rows).astype(jnp.bfloat16)
    routes_rows = jnp.pad(
        routes_rows, ((0, EXTRA - routes_rows.shape[0]), (0, width - rows))
    )
    cot_rings = [
        RingGather(jnp.concatenate([cotangent[0], routes_rows], axis=0), peers, rows // 2),
        RingGather(cotangent[1], peers, rows // 2),
    ]
    steps = peers // 2
    for at in range(steps - 2):
        for ring in cot_rings:
            ring.step()
        if at == 0:
            first_weights = first_weights(*cot_rings[0].got, *cot_rings[1].got)
    first_at = first_expert.astype(jnp.int32).reshape(1)
    seg_col, seg_row = segments[:, :, None], segments[:, None, :]
    xn1, query, keyval, mixed, gates, gates_pack, gains = attention_forward(
        starts, tokens, seg_col, seg_row, routes, cos, sin, first_weights
    )
    for ring in cot_rings:
        ring.step(mixed)
    out_weights = out_weights(mixed)
    hidden, xn2 = [], []
    for m in micros:
        out = block_call(
            hidden_kernel,
            [(mixed, (m,)), (tokens, (m,)), (gains,), (gates_pack, (m,))]
            + [(part,) for part in out_weights],
            [
                jax.ShapeDtypeStruct((rows, width), jnp.float32),
                jax.ShapeDtypeStruct((rows + EXTRA, width), jnp.bfloat16),
            ],
            "hidden_rows",
            prefetch=starts,
        )
        hidden.append(out[0])
        xn2.append(out[1])
    for ring in cot_rings:
        ring.step(xn2[1])
    got = cot_rings[0].got + cot_rings[1].got
    first_whole = join_blocks(starts, [after(first_weights[0], *got)] + first_weights[1:])
    out_whole = join_blocks(starts, [after(out_weights[0], first_whole)] + out_weights[1:])
    routes_all = cot_rings[0].stack_rows(rows, micro_count * TOPK)[:, :, :rows]
    routes_all = routes_all.reshape(peers, micro_count, TOPK, rows)
    places = [
        slot_hits(routes_all[:, m], first_expert, local_experts, capacity)
        .astype(jnp.bfloat16)
        .reshape(peers, -1, rows)
        for m in micros
    ]
    every = list(range(peers))
    late = [steps - 1, steps, steps + 1]
    early = [k for k in every if k not in late]
    row_rings = [RingGather(xn2[m], peers, rows // 2) for m in micros]
    row_rings[0].step(*cot_rings[0].got, *cot_rings[1].got)
    groups = peers // GROUP

    class Experts:
        kept = [None] * 4

        def __init__(self, m, calls):
            self.m = m
            self.calls = calls
            self.per_call = local_experts // calls
            self.outs = [[None] * 3 for _ in range(groups)]
            self.found = {}

        def pick_grads(self):
            place = places[self.m]
            self.grads = pick_rows(first_at, place, cot_rings[self.m], every, False)
            return self.grads[0]

        def pick(self, distances):
            out = pick_rows(first_at, places[self.m], row_rings[self.m], distances, True)
            self.found.update(zip(distances, zip(out, out[len(distances) :])))
            self.rows = [self.found[k][0] for k in every if k in self.found]
            self.gate_slots = [self.found[k][1] for k in every if k in self.found]
            return out[0]

        def call(self, number, *earlier):
            for g in range(groups):
                span = slice(g * GROUP, (g + 1) * GROUP)
                here = self.rows[span]
                here[0] = after(here[0], *earlier) if earlier else here[0]
                done = expert_pass(
                    here,
                    self.grads[span],
                    self.gate_slots[span],
                    w_in,
                    w_out,
                    self.outs[g] + Experts.kept,
                    (self.m * groups + g, micro_count * groups),
                    number * self.per_call,
                    self.per_call,
                )
                self.outs[g], Experts.kept = list(done[:3]), list(done[3:])
            return done[2]

        def spread(self, spans, *earlier):
            place = places[self.m]
            place = after(place, *earlier) if earlier else place
            self.sums = None
            for g in range(groups):
                out = spread_rows(first_at, place, *self.outs[g], g, spans, self.sums)
                self.sums = out[0]
                if g == groups // 2:
                    far = out[1:]
            return far

    calls = 2
    first, second = Experts(0, local_experts), Experts(1, calls)
    ring, ring_next = row_rings
    while len(ring.from_left) < steps - 1:
        ring.step(*places, out_whole)
    ring.step(first.pick_grads())
    ring.step(first.pick(early))
    places[0] = after(places[0], second.pick_grads())
    first.pick(late)
    ring_next.step(*ring.got)
    token = first.call(0)
    for number in range(1, local_experts):
        got = ring_next.got
        ring_next.step(token)
        token = first.call(number, *got)
    block = rows + EXTRA
    got = ring_next.got
    while len(ring_next.from_left) < steps:
        ring_next.step(token)
    far = first.spread([(0, block), (block, rows)], *got)
    got = ring_next.got
    while ring_next.far is None:
        ring_next.step()
    ring_first = RingScatter(lambda k: first.sums[k], far, peers)
    ring_first.step(*got)
    second.pick(early)
    second.pick(late)
    token = second.call(0)
    for number in range(1, calls):
        ring_first.step(token)
        token = second.call(number, *ring_first.sent)
    half = rows // 2
    spans = [(0, half), (half, block - half), (block, half), (block + half, half)]
    far = second.spread(spans)
    ring_grads = RingScatter(lambda k: second.sums[k, :block], far[:2], peers)
    ring_results = RingScatter(lambda k: second.sums[k, block:], far[2:], peers)
    ring_grads.step()
    got = ring_first.got
    while ring_first.at > 1:
        ring_first.step(second.sums)
    picked, grad_result, activated, grad_pre = Experts.kept
    place_at = jnp.stack([lax.rem(dp_at, 2), dp_at // 2])
    ring_grads.step()
    w_out_sum = weight_grads(
        after(activated, *ring_grads.sent, *ring_first.sent), grad_result, 0, local_experts, None
    )
    def backward(m, pieces, *earlier):
        own, left, right = pieces
        return block_call(
            backward_kernel,
            [
                (after(own, *earlier), (0,), block),
                (left, (), block),
                (right, (), block),
                (cotangent, (m,)),
                (hidden[m],),
                (tokens, (m,)),
                (query, (m,)),
                (keyval, (m,)),
                (seg_col, (m,)),
                (seg_row, (m,)),
                (gates, (m,)),
                (gains,),
                (cos,),
                (sin,),
                (first_whole,),
                (out_whole,),
            ],
            [
                jax.ShapeDtypeStruct((rows, width), jnp.bfloat16),
                jax.ShapeDtypeStruct((rows, proj_width + 128), jnp.bfloat16),
                jax.ShapeDtypeStruct((rows, width), jnp.bfloat16),
                jax.ShapeDtypeStruct((8, width), jnp.float32),
            ],
            "attention_backward",
            [pltpu.VMEM((rows, q_width), jnp.bfloat16)],
        )

    half = max(1, local_experts // 2)
    got = second_got = ring_grads.got
    ring_grads.step(w_out_sum)
    picked = after(picked, w_out_sum, *got, *ring_grads.sent)
    w_in_sum = weight_grads(picked, grad_pre, 0, half, None)
    while ring_grads.at > 0:
        got = ring_grads.got
        ring_grads.step(w_in_sum)
    last = ring_first.got
    while ring_first.at > 0:
        ring_first.step(*ring_grads.sent)
    got = last
    ring_results.step(*got)
    grad_w_out = lax.psum_scatter(
        after(w_out_sum, *second_got), "dp", scatter_dimension=1, tiled=True
    )
    back_second = backward(
        1, (second.sums, ring_grads.left, ring_grads.right), w_in_sum, *ring_first.sent
    )
    picked = after(picked, w_in_sum, back_second[3])
    w_in_sum = weight_grads(picked, grad_pre, half, local_experts - half, w_in_sum)
    grad_w_in = lax.psum_scatter(w_in_sum, "dp", scatter_dimension=1, tiled=True)
    ring_results.step(back_second[3], *got)
    back_first = backward(
        0, (first.sums, ring_first.left, ring_first.right), w_in_sum, *ring_results.sent
    )
    ring_results.step(back_first[3])
    grad_tokens, grad_proj, grad_attn, gain_sums = zip(back_first, back_second)
    mine, other = attention_grads(
        place_at, after(xn1, *ring_results.sent), mixed, grad_proj, grad_attn, gain_sums, dp_count
    )
    grads, grad_w_in, grad_w_out = reduce_packed(
        mine, other, my_spot, peers, dp_count, grad_w_in, grad_w_out, ring_results, (q_width, kv_width)
    )
    grad_query, grad_keyval, grad_small, grad_attn_out = grads
    wide = jnp.float32
    outputs = []
    for m, (own, ring, at) in enumerate(
        ((first.sums, ring_first, block), (second.sums, ring_results, 0))
    ):
        total = hidden[m] + own[0, block:].astype(wide)
        total = total + ring.left[at:].astype(wide) + ring.right[at:].astype(wide)
        outputs.append(total.astype(jnp.bfloat16))
    return (
        jnp.stack(outputs),
        jnp.stack(grad_tokens),
        grad_small[:, experts],
        grad_small[:, experts + 1],
        grad_query,
        grad_keyval,
        grad_attn_out,
        grad_small[:, :experts],
        grad_w_in,
        grad_w_out,
    )


def last_kernel(spot_ref, *refs):
    outs = refs[-4:]
    blocks = refs[:-4]
    peers = len(blocks) - 1
    piece = blocks[0].shape[0]
    for k, block_ref in enumerate(blocks):
        distance = k if k <= peers // 2 else k - 1
        spot = lax.rem(spot_ref[0] - distance + peers, peers)
        held = block_ref.shape[0]
        row = spot * piece + (held if k == peers // 2 + 1 else 0)
        at = 0
        for out_ref in outs:
            columns = out_ref.shape[1]
            out_ref[pl.ds(pl.multiple_of(row, 8), held), :] = block_ref[
                :, at : at + columns
            ].astype(jnp.float32)
            at += columns


def reduce_packed(mine, other, my_spot, peers, dp_count, grad_w_in, grad_w_out, ring_results, widths):
    lines, span, columns = mine.shape
    swap = [(d, d ^ 1) for d in range(dp_count)]
    while ring_results.at > 1:
        ring_results.step()
    total = add_rows(mine, lax.ppermute(other, "dp", swap))
    total = after(total, *ring_results.got)
    piece = span // peers
    total = total.reshape(lines, peers, piece, columns)

    def part(k):
        at = lax.rem(my_spot - k + peers, peers)
        return lax.dynamic_slice_in_dim(total, at, 1, axis=1).reshape(lines * piece, columns)

    half = lines * piece // 2
    farthest = part(peers // 2)
    ring = RingScatter(part, (farthest[:half], farthest[half:]), peers)
    ring.step()
    ring_results.step()
    ring.step(*ring_results.sent)
    while ring.at > 0:
        ring.step()
    own, left, right = [held.astype(jnp.float32) for held in (part(0), ring.left, ring.right)]
    mine = (own + left + right).astype(jnp.bfloat16).reshape(lines, piece, columns)
    mine = after(mine, grad_w_in, grad_w_out, *ring_results.got)
    line = lax.axis_index("dp") // 2

    def for_line(at):
        return lax.dynamic_index_in_dim(mine, lax.rem(at, lines), 0, keepdims=False)

    share = for_line(line).astype(jnp.float32)
    for k in range(1, lines):
        pairs = [(d, (d + 2 * k) % dp_count) for d in range(dp_count)]
        share = share + lax.ppermute(for_line(line + k), "dp", pairs)
    gather = RingGather(share.astype(jnp.bfloat16), peers, piece // 2)
    gather.step()
    grad_w_out = grad_w_out.astype(jnp.float32)
    gather.step(grad_w_out)
    grad_w_in = grad_w_in.astype(jnp.float32)
    gather.step(grad_w_in, *ring_results.got)
    while gather.far is None:
        gather.step()
    blocks = gather.from_left + list(gather.far) + gather.from_right[:0:-1]
    columns = (widths[0], widths[1], 128, columns - sum(widths) - 128)
    if piece % 16 == 0:
        grads = block_call(
            last_kernel,
            [(block,) for block in blocks],
            [jax.ShapeDtypeStruct((span, count), jnp.float32) for count in columns],
            "last_rows",
            prefetch=my_spot.astype(jnp.int32).reshape(1),
        )
    else:
        far = jnp.concatenate(gather.far, axis=0)
        by_distance = jnp.stack(gather.from_left + [far] + gather.from_right[:0:-1])
        distance = lax.rem(my_spot - jnp.arange(peers, dtype=jnp.int32) + peers, peers)
        by_spot = jnp.take(by_distance, distance, axis=0).reshape(span, -1).astype(jnp.float32)
        edges = [sum(columns[:i]) for i in range(5)]
        grads = [by_spot[:, edges[i] : edges[i + 1]] for i in range(4)]
    return grads, grad_w_in, grad_w_out


def solution(mesh):
    return jax.shard_map(
        per_device,
        mesh=mesh,
        in_specs=(
            P(None, ("dp", "expert"), None),
            P(None, ("dp", "expert")),
            P(None, ("dp", "expert"), None),
            P("dp"),
            P("dp"),
            P("dp", None),
            P("dp", None),
            P("dp", None),
            P("dp", None),
            P("expert", None, None),
            P("expert", None, None),
            P(None, ("dp", "expert"), None),
        ),
        out_specs=(
            P(None, ("dp", "expert"), None),
            P(None, ("dp", "expert"), None),
            P("dp"),
            P("dp"),
            P("dp", None),
            P("dp", None),
            P("dp", None),
            P("dp", None),
            P("expert", "dp", None),
            P("expert", "dp", None),
        ),
        check_vma=False,
    )
```

```python
import functools
import math

import jax
import jax.numpy as jnp
from jax import lax
from jax.experimental import pallas as pl
from jax.experimental.pallas import tpu as pltpu
from jax.sharding import PartitionSpec as P

QUERY_HEADS = 12
KEY_VALUE_HEADS = 2
HEAD_SIZE = 128
FF = 768
TOPK = 4
EXPERTS = 32
EXTRA = 16
PIECES = 3
GROUP = 8

eps_norm = 1e-06
rope_base = 1000000.0
mask_fill = -1e30
highest = lax.Precision.HIGHEST


def rms_scale(tensor):
    return lax.rsqrt(jnp.mean(tensor * tensor, axis=-1, keepdims=True) + eps_norm)


def rope_tables(sequence_length, head_width):
    positions = jnp.arange(sequence_length).astype(jnp.float32)
    frequency = rope_base ** (-(jnp.arange(head_width // 2).astype(jnp.float32) * 2.0) / head_width)
    angles = positions[:, None] * frequency[None, :]
    return (jnp.cos(angles), jnp.sin(angles))

SCORE_SCALE = 1.0 / math.sqrt(HEAD_SIZE)
GELU_SCALE = math.sqrt(2.0 / math.pi)
GELU_CUBE = 0.044715
SMALL_COST = pl.CostEstimate(flops=1_000_000, bytes_accessed=1_000_000, transcendentals=0)


def after(value, *earlier):
    return lax.optimization_barrier((value,) + earlier)[0]


def slot_hits(routes_all, first_expert, local_experts, capacity):
    rows = routes_all.shape[-1]
    names = first_expert + jnp.arange(local_experts, dtype=jnp.int32)
    named = routes_all[:, None].astype(jnp.int32) == names[None, :, None, None]
    member = jnp.any(named, axis=2)
    lower = (jnp.arange(rows)[:, None] < jnp.arange(rows)[None, :]).astype(jnp.bfloat16)
    rank = dot32(member.astype(jnp.bfloat16).reshape(-1, rows), lower).reshape(member.shape)
    slots = jnp.arange(capacity, dtype=jnp.float32)
    return member[:, :, None, :] & (rank[:, :, None, :] == slots[None, None, :, None])


def pack_pieces(values, out_ref, first_row):
    rows = values.shape[1]
    rest = values
    for piece in range(PIECES):
        part = rest.astype(jnp.bfloat16)
        rest = rest - part.astype(jnp.float32)
        for half in range(EXPERTS // EXTRA):
            at = (piece * (EXPERTS // EXTRA) + half) * rows
            out_ref[first_row : first_row + EXTRA, at : at + rows] = part[
                half * EXTRA : (half + 1) * EXTRA
            ]


def dot32(left, right):
    return jnp.dot(left, right, preferred_element_type=jnp.float32)


def dot_nt(left, right):
    return lax.dot_general(
        left, right, (((1,), (1,)), ((), ())), preferred_element_type=jnp.float32
    )


def dot_tn(left, right):
    return lax.dot_general(
        left, right, (((0,), (0,)), ((), ())), preferred_element_type=jnp.float32
    )


def mask_of(seg_col, seg_row):
    rows = seg_col.shape[0]
    query_at = lax.broadcasted_iota(jnp.int32, (rows, rows), 0)
    key_at = lax.broadcasted_iota(jnp.int32, (rows, rows), 1)
    return (seg_col == seg_row) & (query_at >= key_at)


def softmax_rows(query, key, allowed):
    scores = jnp.where(allowed, dot_nt(query, key) * SCORE_SCALE, mask_fill)
    weight = jnp.exp(scores - jnp.max(scores, axis=-1, keepdims=True))
    return weight / jnp.sum(weight, axis=-1, keepdims=True)


def from_blocks(starts_ref, rows_ref, blocks):
    total = None
    for at, block_ref in enumerate(blocks):
        span = block_ref.shape[0]
        columns = pl.ds(pl.multiple_of(starts_ref[at], 128), span)
        part = dot32(rows_ref[:, columns], block_ref[...])
        total = part if total is None else total + part
    return total


def attention_kernel(
    starts_ref,
    tok_ref,
    seg_col_ref,
    seg_row_ref,
    routes_ref,
    cos_ref,
    sin_ref,
    *refs,
):
    weight_refs = refs[:-7]
    xn1_ref, query_ref, keyval_ref, mixed_ref, gates_ref, gates_pack_ref, gains_ref = refs[-7:]

    @pl.when(pl.program_id(0) == 0)
    def _():
        for at, block_ref in enumerate(weight_refs):
            span, columns = block_ref.shape
            pad = block_ref[:, columns - 128 :].astype(jnp.float32).T
            place = pl.ds(pl.multiple_of(starts_ref[at], 128), span)
            gains_ref[:, place] = pad[2 * EXPERTS : 2 * EXPERTS + 8]

    tok = tok_ref[...].astype(jnp.float32)
    xn1_ref[...] = (tok * rms_scale(tok) * gains_ref[0:1, :]).astype(jnp.bfloat16)
    proj = from_blocks(starts_ref, xn1_ref, weight_refs)
    cos, sin = cos_ref[...], sin_ref[...]

    def rotate(part):
        return (part * cos + pltpu.roll(part, HEAD_SIZE // 2, 1) * sin).astype(jnp.bfloat16)

    q_width = QUERY_HEADS * HEAD_SIZE
    k_width = KEY_VALUE_HEADS * HEAD_SIZE
    for head in range(QUERY_HEADS):
        span = slice(head * HEAD_SIZE, (head + 1) * HEAD_SIZE)
        query_ref[:, span] = rotate(proj[:, span])
    for head in range(KEY_VALUE_HEADS):
        span = slice(head * HEAD_SIZE, (head + 1) * HEAD_SIZE)
        keyval_ref[:, span] = rotate(proj[:, q_width:][:, span])
    keyval_ref[:, k_width:] = proj[:, q_width + k_width : q_width + 2 * k_width].astype(
        jnp.bfloat16
    )
    logits = proj[:, q_width + 2 * k_width :]
    columns = lax.broadcasted_iota(jnp.int32, logits.shape, 1)
    named = [columns == routes_ref[:, j : j + 1] for j in range(TOPK)]
    chosen = [jnp.sum(jnp.where(hit, logits, 0.0), axis=-1, keepdims=True) for hit in named]
    top = functools.reduce(jnp.maximum, chosen)
    weight = [jnp.exp(part - top) for part in chosen]
    total = functools.reduce(jnp.add, weight)
    gates = jnp.full(logits.shape, -1.0, jnp.float32)
    for hit, part in zip(named, weight):
        gates = jnp.where(hit, part / total, gates)
    gates_ref[...] = gates
    pack_pieces(gates.T[:EXPERTS], gates_pack_ref, 0)
    allowed = mask_of(seg_col_ref[...], seg_row_ref[...])
    for head in range(QUERY_HEADS):
        span = slice(head * HEAD_SIZE, (head + 1) * HEAD_SIZE)
        group = head // (QUERY_HEADS // KEY_VALUE_HEADS)
        key = keyval_ref[:, group * HEAD_SIZE : (group + 1) * HEAD_SIZE]
        value = keyval_ref[:, k_width + group * HEAD_SIZE : k_width + (group + 1) * HEAD_SIZE]
        probs = softmax_rows(query_ref[:, span], key, allowed)
        mixed_ref[:, span] = dot32(probs.astype(jnp.bfloat16), value).astype(jnp.bfloat16)


def hidden_kernel(starts_ref, mixed_ref, tok_ref, gains_ref, pack_ref, *refs):
    weight_refs = refs[:-2]
    hidden_ref, xn2_ref = refs[-2:]
    rows = tok_ref.shape[0]
    hidden = tok_ref[...].astype(jnp.float32) + from_blocks(
        starts_ref, mixed_ref, weight_refs
    )
    hidden_ref[...] = hidden
    xn2_ref[:rows, :] = (hidden * rms_scale(hidden) * gains_ref[1:2, :]).astype(jnp.bfloat16)
    xn2_ref[rows:, :] = pack_ref[...]


def backward_kernel(
    own_ref,
    left_ref,
    right_ref,
    cot_ref,
    hidden_ref,
    tok_ref,
    query_ref,
    keyval_ref,
    seg_col_ref,
    seg_row_ref,
    gates_ref,
    gains_ref,
    cos_ref,
    sin_ref,
    *refs,
):
    weight_ref, out_weight_ref = refs[:2]
    grad_tok_ref, grad_proj_ref, grad_attn_ref, gain_sum_ref, mixed_grad_ref = refs[2:]
    width = tok_ref.shape[1]
    q_width = QUERY_HEADS * HEAD_SIZE
    k_width = KEY_VALUE_HEADS * HEAD_SIZE
    proj_width = q_width + 2 * k_width
    rows = tok_ref.shape[0]
    sums = [ref[...].astype(jnp.float32) for ref in (own_ref, left_ref, right_ref)]
    sums = sums[0] + sums[1] + sums[2]
    grad_xn2, pack = sums[:rows], sums[rows:]
    halves = EXPERTS // EXTRA
    lines = [
        sum(
            pack[:, (piece * halves + half) * rows : (piece * halves + half + 1) * rows]
            for piece in range(PIECES)
        )
        for half in range(halves)
    ]
    lines.append(jnp.zeros((128 - EXPERTS, rows), jnp.float32))
    grad_gates = jnp.concatenate(lines, axis=0).T
    hidden = hidden_ref[...]
    scale = rms_scale(hidden)
    unit = hidden * scale
    gain_sum_ref[...] = jnp.zeros(gain_sum_ref.shape, jnp.float32)
    gain_sum_ref[1:2, :] = jnp.sum(grad_xn2 * unit, axis=0, keepdims=True)
    grad_unit = grad_xn2 * gains_ref[1:2, :]
    grad_hidden = cot_ref[...].astype(jnp.float32) + scale * (
        grad_unit - unit * jnp.mean(grad_unit * unit, axis=-1, keepdims=True)
    )
    grad_attn_ref[...] = grad_hidden.astype(jnp.bfloat16)
    mixed_grad_ref[...] = dot_nt(grad_attn_ref[...], out_weight_ref[...]).astype(jnp.bfloat16)
    cos, sin = cos_ref[...], sin_ref[...]

    def unrotate(part):
        return (part * cos - pltpu.roll(part, HEAD_SIZE // 2, 1) * sin).astype(jnp.bfloat16)

    allowed = mask_of(seg_col_ref[...], seg_row_ref[...])
    per_group = QUERY_HEADS // KEY_VALUE_HEADS
    for group in range(KEY_VALUE_HEADS):
        key_span = slice(group * HEAD_SIZE, (group + 1) * HEAD_SIZE)
        value_span = slice(k_width + group * HEAD_SIZE, k_width + (group + 1) * HEAD_SIZE)
        key, value = keyval_ref[:, key_span], keyval_ref[:, value_span]
        grad_key = jnp.zeros(key.shape, jnp.float32)
        grad_value = jnp.zeros(key.shape, jnp.float32)
        for head in range(group * per_group, (group + 1) * per_group):
            span = slice(head * HEAD_SIZE, (head + 1) * HEAD_SIZE)
            query, grad_mixed = query_ref[:, span], mixed_grad_ref[:, span]
            probs = softmax_rows(query, key, allowed)
            grad_value += dot_tn(probs.astype(jnp.bfloat16), grad_mixed)
            grad_probs = dot_nt(grad_mixed, value)
            mean = jnp.sum(probs * grad_probs, axis=-1, keepdims=True)
            grad_scores = (probs * (grad_probs - mean)).astype(jnp.bfloat16)
            grad_proj_ref[:, span] = unrotate(dot32(grad_scores, key) * SCORE_SCALE)
            grad_key += dot_tn(grad_scores, query)
        grad_proj_ref[:, q_width + group * HEAD_SIZE : q_width + (group + 1) * HEAD_SIZE] = (
            unrotate(grad_key * SCORE_SCALE)
        )
        first = q_width + k_width + group * HEAD_SIZE
        grad_proj_ref[:, first : first + HEAD_SIZE] = grad_value.astype(jnp.bfloat16)
    gates = jnp.maximum(gates_ref[...], 0.0)
    grad_logits = gates * (grad_gates - jnp.sum(gates * grad_gates, axis=-1, keepdims=True))
    high = grad_logits.astype(jnp.bfloat16).astype(jnp.float32)
    low = pltpu.roll(grad_logits - high, EXPERTS, 1)
    grad_proj_ref[:, proj_width:] = (high + low).astype(jnp.bfloat16)
    grad_xn1 = dot_nt(grad_proj_ref[...], weight_ref[...])
    tok = tok_ref[...].astype(jnp.float32)
    scale = rms_scale(tok)
    unit = tok * scale
    gain_sum_ref[0:1, :] = jnp.sum(grad_xn1 * unit, axis=0, keepdims=True)
    grad_unit = grad_xn1 * gains_ref[0:1, :]
    grad_tok_ref[...] = (
        grad_hidden
        + scale * (grad_unit - unit * jnp.mean(grad_unit * unit, axis=-1, keepdims=True))
    ).astype(jnp.bfloat16)


def ring_order(peers):
    minor = peers // 4
    walk = []
    for col in range(minor):
        line = range(4) if col % 2 == 0 else range(3, -1, -1)
        walk += [row * minor + col for row in line]
    return walk


def ring_step(part, shift, peers):
    order = ring_order(peers)
    pairs = [(order[i], order[(i + shift) % peers]) for i in range(peers)]
    return lax.ppermute(part, "expert", pairs)


class RingGather:
    def __init__(self, part, peers, half):
        self.peers, self.half = peers, half
        self.from_left, self.from_right = [part], [part]
        self.far = None
        self.got = ()

    def step(self, *earlier):
        left, right = self.from_left[-1], self.from_right[-1]
        last = len(self.from_left) == self.peers // 2
        if last:
            left, right = left[: self.half], right[self.half :]
        left, right = self.sent = lax.optimization_barrier((left, right) + earlier)[:2]
        left, right = ring_step(left, 1, self.peers), ring_step(right, -1, self.peers)
        self.got = (left, right)
        if last:
            self.far = (left, right)
        else:
            self.from_left.append(left)
            self.from_right.append(right)
        return self

    def rows(self, k, first, count):
        if k < len(self.from_left):
            return self.from_left[k], first
        if k > self.peers // 2:
            return self.from_right[self.peers - k], first
        if first < self.half:
            return self.far[0], first
        return self.far[1], first - self.half

    def stack_rows(self, first, count):
        found = [self.rows(k, first, count) for k in range(self.peers)]
        return jnp.stack([array[at : at + count] for array, at in found])


class RingScatter:
    def __init__(self, part, far, peers):
        self.part, self.far, self.peers = part, far, peers
        self.at = peers // 2
        self.half = far[0].shape[0]

    def step(self, *earlier):
        peers, k, half = self.peers, self.at, self.half
        if k == peers // 2:
            left, right = lax.optimization_barrier(tuple(self.far) + earlier)[:2]
        else:
            left, right = self.part(k), self.part(peers - k)
            if earlier:
                self.left, self.right = lax.optimization_barrier(
                    (self.left, self.right) + earlier
                )[:2]
            if k == peers // 2 - 1:
                kept = left[half:].astype(jnp.bfloat16), right[:half].astype(jnp.bfloat16)
                left = jnp.concatenate([add_rows(left[:half], self.left), kept[0]], axis=0)
                right = jnp.concatenate([kept[1], add_rows(right[half:], self.right)], axis=0)
            else:
                left, right = add_rows(left, self.left), add_rows(right, self.right)
        left, right = self.sent = lax.optimization_barrier((left, right))
        self.left = ring_step(left, -1, peers)
        self.right = ring_step(right, 1, peers)
        self.got = (self.left, self.right)
        self.at = k - 1
        return self


def add_rows(left, right):
    return (left.astype(jnp.float32) + right.astype(jnp.float32)).astype(jnp.bfloat16)


def expert_kernel(sources, *refs):
    rows_refs = refs[:sources]
    grad_refs = refs[sources : 2 * sources]
    gate_refs = refs[2 * sources : 3 * sources]
    w_in_ref, w_out_ref = refs[3 * sources : 3 * sources + 2]
    (
        back_rows_ref,
        back_grads_ref,
        grad_gate_ref,
        picked_ref,
        grad_result_ref,
        activated_ref,
        grad_pre_ref,
    ) = refs[-7:]
    capacity, width = rows_refs[0].shape
    for k in range(sources):
        picked_ref[pl.ds(k * capacity, capacity), :] = rows_refs[k][...]
    pre_act = dot32(picked_ref[...], w_in_ref[...])
    gate_part = pre_act[:, :FF]
    up_part = pre_act[:, FF:]
    square = gate_part * gate_part
    bend = jnp.tanh(GELU_SCALE * gate_part * (1.0 + GELU_CUBE * square))
    lift = 0.5 * (1.0 + bend)
    gelu_val = gate_part * lift
    slope = lift + 0.5 * gate_part * (1.0 - bend * bend) * (
        GELU_SCALE * (1.0 + 3.0 * GELU_CUBE * square)
    )
    activated_ref[...] = (gelu_val * up_part).astype(jnp.bfloat16)
    result = dot32(activated_ref[...], w_out_ref[...])
    for k in range(sources):
        gates = gate_refs[k][...]
        span = slice(k * capacity, (k + 1) * capacity)
        grad_rows = grad_refs[k][...].astype(jnp.float32)
        grad_gate_ref[span, :] = jnp.sum(result[span] * grad_rows, axis=-1, keepdims=True)
        back_rows_ref[k] = (result[span] * gates).astype(jnp.bfloat16)
        grad_result_ref[span, :] = (grad_rows * gates).astype(jnp.bfloat16)
    grad_act = lax.dot_general(
        grad_result_ref[...],
        w_out_ref[...],
        (((1,), (1,)), ((), ())),
        preferred_element_type=jnp.float32,
    )
    grad_pre_ref[:, :FF] = (grad_act * up_part * slope).astype(jnp.bfloat16)
    grad_pre_ref[:, FF:] = (grad_act * gelu_val).astype(jnp.bfloat16)
    grad_in = lax.dot_general(
        grad_pre_ref[...],
        w_in_ref[...],
        (((1,), (1,)), ((), ())),
        preferred_element_type=jnp.float32,
    ).astype(jnp.bfloat16)
    for k in range(sources):
        back_grads_ref[k] = grad_in[k * capacity : (k + 1) * capacity]


def expert_pass(rows_list, grads_list, gate_slots, w_in, w_out, held_outs, position, first, count):
    sources = len(rows_list)
    local_experts, width, _ = w_in.shape
    slots = rows_list[0].shape[0]
    capacity = slots // local_experts
    held = sources * capacity
    block_spec = pl.BlockSpec((capacity, width), lambda e: (e + first, 0))
    back_spec = pl.BlockSpec((sources, capacity, width), lambda e: (0, e + first, 0))
    column_spec = pl.BlockSpec((None, held, 1), lambda e: (e + first, 0, 0))

    def kept_spec(columns):
        return pl.BlockSpec((None, held, columns), lambda e: (e + first, position[0], 0))

    def kept_shape(columns):
        return jax.ShapeDtypeStruct((local_experts, position[1] * held, columns), jnp.bfloat16)

    kept_widths = (width, width, FF, 2 * FF)
    first_held = 3 * sources + 2
    given = [(i, part) for i, part in enumerate(held_outs) if part is not None]
    return pl.pallas_call(
        functools.partial(expert_kernel, sources),
        grid=(count,),
        in_specs=[block_spec] * (2 * sources)
        + [pl.BlockSpec((capacity, 1), lambda e: (e + first, 0))] * sources
        + [
            pl.BlockSpec((None, width, 2 * FF), lambda e: (e + first, 0, 0)),
            pl.BlockSpec((None, FF, width), lambda e: (e + first, 0, 0)),
        ]
        + [pl.BlockSpec(memory_space=pl.ANY)] * len(given),
        out_specs=[back_spec, back_spec, column_spec] + [kept_spec(c) for c in kept_widths],
        out_shape=[
            jax.ShapeDtypeStruct((sources, slots, width), jnp.bfloat16),
            jax.ShapeDtypeStruct((sources, slots, width), jnp.bfloat16),
            jax.ShapeDtypeStruct((local_experts, held, 1), jnp.float32),
        ]
        + [kept_shape(c) for c in kept_widths],
        input_output_aliases={first_held + at: i for at, (i, _) in enumerate(given)},
        compiler_params=pltpu.CompilerParams(vmem_limit_bytes=60 * 1024 * 1024),
        cost_estimate=SMALL_COST,
        name="expert_pass",
    )(*rows_list, *grads_list, *gate_slots, w_in, w_out, *[part for _, part in given])


def block_call(kernel, operands, out_shape, name, scratch=(), prefetch=None):
    def spec(array, lead=(), rows=None):
        rest = array.shape[len(lead) :]
        at = lead + (0,) * len(rest)
        if rows is not None:
            count, block = rows if isinstance(rows, tuple) else (rows, 0)
            rest = (count,) + rest[1:]
            at = lead + (block,) + (0,) * (len(rest) - 1)
        return pl.BlockSpec((None,) * len(lead) + rest, lambda *_: at)

    scalars = [] if prefetch is None else [prefetch]
    return pl.pallas_call(
        kernel,
        grid_spec=pltpu.PrefetchScalarGridSpec(
            num_scalar_prefetch=len(scalars),
            grid=(1,),
            in_specs=[spec(*operand) for operand in operands],
            out_specs=[spec(shape) for shape in out_shape],
            scratch_shapes=list(scratch),
        ),
        out_shape=out_shape,
        compiler_params=pltpu.CompilerParams(vmem_limit_bytes=60 * 1024 * 1024),
        cost_estimate=SMALL_COST,
        name=name,
    )(*scalars, *[operand[0] for operand in operands])


def pick_kernel(shares, gated, first_ref, place_ref, *refs):
    at = 0
    outs = refs[sum(count for _, count in shares) + (len(shares) if gated else 0) :]
    for number, (k, count) in enumerate(shares):
        total, row = None, 0
        for block_ref in refs[at : at + count]:
            held = block_ref.shape[0]
            part = dot32(place_ref[k, :, row : row + held], block_ref[...])
            total = part if total is None else total + part
            row += held
        outs[number][...] = total.astype(jnp.bfloat16)
        at += count
        if gated:
            slot_gates(first_ref[0], place_ref[k], refs[at], outs[len(shares) + number])
            at += 1


def slot_gates(first_expert, place, pack_ref, out_ref):
    slots, rows = place.shape
    pack = pack_ref[...].astype(jnp.float32)
    halves = EXPERTS // EXTRA
    line = lax.broadcasted_iota(jnp.int32, (EXTRA, rows), 0)
    local_experts = slots * 4 // rows
    capacity = rows // 4
    for e in range(local_experts):
        gate = jnp.zeros((1, rows), jnp.float32)
        for half in range(halves):
            hit = line + half * EXTRA == first_expert + e
            for piece in range(PIECES):
                at = (piece * halves + half) * rows
                gate += jnp.sum(
                    jnp.where(hit, pack[:, at : at + rows], 0.0), axis=0, keepdims=True
                )
        span = slice(e * capacity, (e + 1) * capacity)
        out_ref[span, :] = jnp.sum(
            place[span].astype(jnp.float32) * gate, axis=-1, keepdims=True
        )


def pick_rows(first_expert, place, ring, distances, gated):
    _, slots, rows = place.shape
    half = rows // 2
    operands, shares = [], []
    for k in distances:
        spans = [(0, rows)]
        if k == ring.peers // 2 and ring.half < rows:
            spans = [(0, half), (half, half)]
        shares.append((k, len(spans)))
        for at, count in spans + ([(rows, EXTRA)] if gated else []):
            array, at = ring.rows(k, at, count)
            operands.append((array, (), (count, at // count)))
    width = operands[0][0].shape[-1]
    out_shape = [jax.ShapeDtypeStruct((slots, width), jnp.bfloat16) for _ in distances]
    if gated:
        out_shape += [jax.ShapeDtypeStruct((slots, 1), jnp.float32) for _ in distances]
    return block_call(
        functools.partial(pick_kernel, shares, gated),
        [(place,)] + operands,
        out_shape,
        "pick_rows",
        prefetch=first_expert,
    )


def spread_kernel(middle, spans, held, first_ref, place_ref, rows_ref, grads_ref, gate_ref, *refs):
    out_ref, *far_refs = refs[held:]
    place = place_ref[...]
    rows = place.shape[1]
    out_ref[:rows, :] = dot_tn(place, grads_ref[...]).astype(jnp.bfloat16)
    out_ref[rows + EXTRA :, :] = dot_tn(place, rows_ref[...]).astype(jnp.bfloat16)
    capacity = gate_ref.shape[1]
    expert = lax.broadcasted_iota(jnp.int32, (EXPERTS, rows), 0) - first_ref[0]
    gates = jnp.zeros((EXPERTS, rows), jnp.float32)
    for e in range(gate_ref.shape[0]):
        hit = place[e * capacity : (e + 1) * capacity].astype(jnp.float32)
        line = jnp.sum(hit * gate_ref[e], axis=0, keepdims=True)
        gates = jnp.where(expert == e, line, gates)
    pack_pieces(gates, out_ref, rows)

    @pl.when(pl.program_id(0) == middle)
    def _():
        for far_ref, (row, count) in zip(far_refs, spans):
            far_ref[...] = out_ref[row : row + count, :]


def spread_rows(first_expert, place, rows_back, grads_back, gate_slots, group, spans, held):
    sources, slots, rows = place.shape
    width = rows_back.shape[-1]
    local_experts = gate_slots.shape[0]
    base = group * GROUP
    by_source = pl.BlockSpec((None, slots, width), lambda k, f: (k, 0, 0))
    held = [] if held is None else [held]
    out_shape = [jax.ShapeDtypeStruct((sources, 2 * rows + EXTRA, width), jnp.bfloat16)]
    out_shape += [jax.ShapeDtypeStruct((count, width), jnp.bfloat16) for _, count in spans]
    out_specs = [pl.BlockSpec((None, 2 * rows + EXTRA, width), lambda k, f: (base + k, 0, 0))]
    out_specs += [pl.BlockSpec((count, width), lambda k, f: (0, 0)) for _, count in spans]
    return pl.pallas_call(
        functools.partial(spread_kernel, sources // 2 - base, spans, len(held)),
        grid_spec=pltpu.PrefetchScalarGridSpec(
            num_scalar_prefetch=1,
            grid=(GROUP,),
            in_specs=[
                pl.BlockSpec((None, slots, rows), lambda k, f: (base + k, 0, 0)),
                by_source,
                by_source,
                pl.BlockSpec((local_experts, slots // local_experts, 1), lambda k, f: (0, k, 0)),
            ]
            + [pl.BlockSpec(memory_space=pl.ANY)] * len(held),
            out_specs=out_specs,
        ),
        out_shape=out_shape,
        input_output_aliases={5 + i: i for i in range(len(held))},
        compiler_params=pltpu.CompilerParams(vmem_limit_bytes=60 * 1024 * 1024),
        cost_estimate=SMALL_COST,
        name="spread_rows",
    )(first_expert, place, rows_back, grads_back, gate_slots, *held)


def weight_grad_kernel(left_ref, right_ref, out_ref):
    out_ref[...] = dot_tn(left_ref[...], right_ref[...]).astype(jnp.bfloat16)


def weight_grads(left, right, first, count):
    _, held, height = left.shape
    columns = right.shape[-1]
    tile = min(height, 768)
    return pl.pallas_call(
        weight_grad_kernel,
        grid=(count, height // tile),
        in_specs=[
            pl.BlockSpec((None, held, tile), lambda e, i: (e + first, 0, i)),
            pl.BlockSpec((None, held, columns), lambda e, i: (e + first, 0, 0)),
        ],
        out_specs=pl.BlockSpec((None, tile, columns), lambda e, i: (e, i, 0)),
        out_shape=jax.ShapeDtypeStruct((count, height, columns), jnp.bfloat16),
        compiler_params=pltpu.CompilerParams(vmem_limit_bytes=60 * 1024 * 1024),
        cost_estimate=SMALL_COST,
        name="weight_grads",
    )(left, right)


def attention_forward(starts, tokens, seg_col, seg_row, routes, cos, sin, weights):
    count, rows, width = tokens.shape

    def by_micro(*shape):
        return pl.BlockSpec((None,) + shape, lambda m, s: (m,) + (0,) * len(shape))

    def shared(part):
        return pl.BlockSpec(part.shape, lambda m, s: (0, 0))

    kv_width = 2 * KEY_VALUE_HEADS * HEAD_SIZE
    shapes = [
        ((rows, width), jnp.bfloat16),
        ((rows, QUERY_HEADS * HEAD_SIZE), jnp.bfloat16),
        ((rows, kv_width), jnp.bfloat16),
        ((rows, QUERY_HEADS * HEAD_SIZE), jnp.bfloat16),
        ((rows, 128), jnp.float32),
        ((EXTRA, PIECES * EXPERTS // EXTRA * rows), jnp.bfloat16),
    ]
    return pl.pallas_call(
        attention_kernel,
        grid_spec=pltpu.PrefetchScalarGridSpec(
            num_scalar_prefetch=1,
            grid=(count,),
            in_specs=[
                by_micro(rows, width),
                by_micro(rows, 1),
                by_micro(1, rows),
                by_micro(rows, TOPK),
                shared(cos),
                shared(sin),
            ]
            + [shared(part) for part in weights],
            out_specs=[by_micro(*shape) for shape, _ in shapes]
            + [pl.BlockSpec((8, width), lambda m, s: (0, 0))],
        ),
        out_shape=[jax.ShapeDtypeStruct((count,) + shape, kind) for shape, kind in shapes]
        + [jax.ShapeDtypeStruct((8, width), jnp.float32)],
        compiler_params=pltpu.CompilerParams(vmem_limit_bytes=60 * 1024 * 1024),
        cost_estimate=SMALL_COST,
        name="attention_forward",
    )(starts, tokens, seg_col, seg_row, routes, cos, sin, *weights)


def join_kernel(starts_ref, *refs):
    for at, block_ref in enumerate(refs[:-1]):

        @pl.when(pl.program_id(0) == at)
        def _():
            refs[-1][...] = block_ref[...]


def join_blocks(starts, blocks):
    if len(blocks) == 1:
        return blocks[0]
    span, columns = blocks[0].shape
    return pl.pallas_call(
        join_kernel,
        grid_spec=pltpu.PrefetchScalarGridSpec(
            num_scalar_prefetch=1,
            grid=(len(blocks),),
            in_specs=[pl.BlockSpec((span, columns), lambda i, s: (0, 0)) for _ in blocks],
            out_specs=pl.BlockSpec((span, columns), lambda i, s: (s[i] // span, 0)),
        ),
        out_shape=jax.ShapeDtypeStruct((len(blocks) * span, columns), blocks[0].dtype),
        compiler_params=pltpu.CompilerParams(vmem_limit_bytes=60 * 1024 * 1024),
        cost_estimate=SMALL_COST,
        name="join_blocks",
    )(starts, *blocks)


def attention_grad_kernel(core_ref, xn1, mixed, *refs):
    count = xn1.shape[0]
    proj, attn, sums = [refs[i * count : (i + 1) * count] for i in range(3)]
    mine_ref, other_ref = refs[-2:]
    split = proj[0].shape[1]
    span = mine_ref.shape[0]
    grad = sum(dot_tn(xn1[m], proj[m][...]) for m in range(count))
    router = grad[:, split - 128 :]
    lane = lax.broadcasted_iota(jnp.int32, router.shape, 1)
    router = router + pltpu.roll(router, 128 - EXPERTS, 1)
    gain = sum(part[...] for part in sums)
    lines = [jnp.zeros((EXPERTS, gain.shape[1]), jnp.float32), gain]
    lines.append(jnp.zeros((128 - EXPERTS - gain.shape[0], gain.shape[1]), jnp.float32))
    router = jnp.where(lane < EXPERTS, router, jnp.concatenate(lines, axis=0).T)
    first = core_ref[0] == 0

    def put(columns, value):
        value = value.astype(jnp.bfloat16)
        low, high = value[:span], value[span:]
        mine_ref[:, columns] = jnp.where(first, low, high)
        other_ref[:, columns] = jnp.where(first, high, low)

    put(slice(0, split - 128), grad[:, : split - 128])
    put(slice(split - 128, split), router)
    put(slice(split, None), sum(dot_tn(mixed[m], attn[m][...]) for m in range(count)))


def attention_grads(core, xn1, mixed, proj, attn, gain_sums, parts):
    count, rows, width = xn1.shape
    span = width // parts
    lines = parts // 2
    columns = proj[0].shape[1] + attn[0].shape[1]
    by_line = pl.BlockSpec((count, rows, 2 * span), lambda i, c: (0, 0, i))

    def shared(part):
        return pl.BlockSpec(part.shape, lambda i, c: (0, 0))

    out_spec = pl.BlockSpec((None, span, columns), lambda i, c: (i, 0, 0))
    out_shape = jax.ShapeDtypeStruct((lines, span, columns), jnp.bfloat16)
    return pl.pallas_call(
        attention_grad_kernel,
        grid_spec=pltpu.PrefetchScalarGridSpec(
            num_scalar_prefetch=1,
            grid=(lines,),
            in_specs=[by_line, by_line]
            + [shared(p) for p in proj]
            + [shared(p) for p in attn]
            + [pl.BlockSpec((p.shape[0], 2 * span), lambda i, c: (0, i)) for p in gain_sums],
            out_specs=[out_spec, out_spec],
        ),
        out_shape=[out_shape, out_shape],
        compiler_params=pltpu.CompilerParams(vmem_limit_bytes=60 * 1024 * 1024),
        cost_estimate=SMALL_COST,
        name="attention_grads",
    )(core, xn1, mixed, *proj, *attn, *gain_sums)


def gather_blocks(part, dp_at, dp_count):
    span = part.shape[0]
    if span % 128 or dp_count != 4:
        whole = lax.all_gather(part, "dp", axis=0, tiled=True)
        return lambda *earlier: [whole], jnp.zeros((1,), jnp.int32)
    line = [(d, (d + 2) % 4) for d in range(4)]
    core = [(d, d ^ 1) for d in range(4)]
    across = lax.ppermute(part, "dp", line)
    beside = lax.ppermute(part, "dp", core)
    far = lax.rem(dp_at + 2, 4)
    owners = jnp.stack([dp_at, dp_at + 1 - 2 * lax.rem(dp_at, 2), far, far + 1 - 2 * lax.rem(far, 2)])

    def blocks(*earlier):
        moved = after(across, *earlier) if earlier else across
        return [part, beside, moved, lax.ppermute(moved, "dp", core)]

    return blocks, owners * span


def per_device(
    tokens,
    segments,
    routes,
    norm_one,
    norm_two,
    w_query,
    key_value_weight,
    w_out_attn,
    w_router,
    w_in,
    w_out,
    cotangent,
):
    micro_count, rows, width = tokens.shape
    micros = range(micro_count)
    peers = lax.axis_size("expert")
    dp_count = lax.axis_size("dp")
    local_experts = w_in.shape[0]
    experts = local_experts * peers
    capacity = rows // 4
    first_expert = lax.axis_index("expert") * local_experts
    q_width = w_query.shape[1]
    kv_width = key_value_weight.shape[1]
    proj_width = q_width + kv_width
    cosine_table, sine_values = rope_tables(rows, HEAD_SIZE)
    cos = jnp.concatenate([cosine_table, cosine_table], axis=1)
    sin = jnp.concatenate([-sine_values, sine_values], axis=1)
    order = ring_order(peers)
    spot = [order.index(dev) for dev in range(peers)]
    my_spot = jnp.array(spot, jnp.int32)[lax.axis_index("expert")]

    router_pad = jnp.zeros((w_router.shape[0], 126 - 2 * experts), jnp.bfloat16)
    first_weight = jnp.concatenate(
        [
            w_query,
            key_value_weight,
            w_router,
            w_router,
            norm_one[:, None],
            norm_two[:, None],
            router_pad,
        ],
        axis=1,
    )
    dp_at = lax.axis_index("dp").astype(jnp.int32)
    first_weights, starts = gather_blocks(first_weight, dp_at, dp_count)
    out_weights, _ = gather_blocks(w_out_attn, dp_at, dp_count)

    routes_rows = jnp.swapaxes(routes, 1, 2).reshape(-1, rows).astype(jnp.bfloat16)
    routes_rows = jnp.pad(
        routes_rows, ((0, EXTRA - routes_rows.shape[0]), (0, width - rows))
    )
    cot_rings = [
        RingGather(jnp.concatenate([cotangent[0], routes_rows], axis=0), peers, rows // 2),
        RingGather(cotangent[1], peers, rows // 2),
    ]
    steps = peers // 2
    for at in range(steps - 2):
        for ring in cot_rings:
            ring.step()
        if at == 0:
            first_weights = first_weights(*cot_rings[0].got, *cot_rings[1].got)
    first_at = first_expert.astype(jnp.int32).reshape(1)
    seg_col, seg_row = segments[:, :, None], segments[:, None, :]
    xn1, query, keyval, mixed, gates, gates_pack, gains = attention_forward(
        starts, tokens, seg_col, seg_row, routes, cos, sin, first_weights
    )
    for ring in cot_rings:
        ring.step(mixed)
    out_weights = out_weights(mixed)
    hidden, xn2 = [], []
    for m in micros:
        out = block_call(
            hidden_kernel,
            [(after(mixed, *xn2), (m,)), (tokens, (m,)), (gains,), (gates_pack, (m,))]
            + [(part,) for part in out_weights],
            [
                jax.ShapeDtypeStruct((rows, width), jnp.float32),
                jax.ShapeDtypeStruct((rows + EXTRA, width), jnp.bfloat16),
            ],
            "hidden_rows",
            prefetch=starts,
        )
        hidden.append(out[0])
        xn2.append(out[1])
    for ring in cot_rings:
        ring.step()
    got = cot_rings[0].got + cot_rings[1].got
    first_whole = join_blocks(starts, [after(first_weights[0], *got)] + first_weights[1:])
    out_whole = join_blocks(starts, [after(out_weights[0], first_whole)] + out_weights[1:])
    routes_all = cot_rings[0].stack_rows(rows, micro_count * TOPK)[:, :, :rows]
    routes_all = routes_all.reshape(peers, micro_count, TOPK, rows)
    places = [
        slot_hits(routes_all[:, m], first_expert, local_experts, capacity)
        .astype(jnp.bfloat16)
        .reshape(peers, -1, rows)
        for m in micros
    ]
    every = list(range(peers))
    late = [steps - 1, steps, steps + 1]
    early = [k for k in every if k not in late]
    row_rings = [RingGather(xn2[m], peers, rows // 2) for m in micros]
    row_rings[0].step()
    groups = peers // GROUP

    class Experts:
        kept = [None] * 4

        def __init__(self, m, calls):
            self.m = m
            self.calls = calls
            self.per_call = local_experts // calls
            self.outs = [[None] * 3 for _ in range(groups)]
            self.found = {}

        def pick_grads(self):
            place = places[self.m]
            self.grads = pick_rows(first_at, place, cot_rings[self.m], every, False)
            return self.grads[0]

        def pick(self, distances):
            out = pick_rows(first_at, places[self.m], row_rings[self.m], distances, True)
            self.found.update(zip(distances, zip(out, out[len(distances) :])))
            self.rows = [self.found[k][0] for k in every if k in self.found]
            self.gate_slots = [self.found[k][1] for k in every if k in self.found]
            return out[0]

        def call(self, number, *earlier):
            for g in range(groups):
                span = slice(g * GROUP, (g + 1) * GROUP)
                here = self.rows[span]
                here[0] = after(here[0], *earlier) if earlier else here[0]
                done = expert_pass(
                    here,
                    self.grads[span],
                    self.gate_slots[span],
                    w_in,
                    w_out,
                    self.outs[g] + Experts.kept,
                    (self.m * groups + g, micro_count * groups),
                    number * self.per_call,
                    self.per_call,
                )
                self.outs[g], Experts.kept = list(done[:3]), list(done[3:])
            return done[2]

        def spread(self, spans, *earlier):
            place = places[self.m]
            place = after(place, *earlier) if earlier else place
            self.sums = None
            for g in range(groups):
                out = spread_rows(first_at, place, *self.outs[g], g, spans, self.sums)
                self.sums = out[0]
                if g == groups // 2:
                    far = out[1:]
            return far

    calls = 2
    first, second = Experts(0, calls), Experts(1, calls)
    ring, ring_next = row_rings
    while len(ring.from_left) < steps - 1:
        ring.step(*places, out_whole)
    ring.step(first.pick_grads())
    ring.step(first.pick(early))
    places[0] = after(places[0], second.pick_grads())
    first.pick(late)
    ring_next.step(*ring.got)
    token = first.call(0)
    for number in range(1, calls):
        got = ring_next.got
        ring_next.step(token)
        token = first.call(number, *got)
    block = rows + EXTRA
    got = ring_next.got
    while len(ring_next.from_left) < steps:
        ring_next.step(token)
    far = first.spread([(0, block), (block, rows)], *got)
    got = ring_next.got
    while ring_next.far is None:
        ring_next.step()
    ring_first = RingScatter(lambda k: first.sums[k], far, peers)
    ring_first.step(*got)
    second.pick(early)
    second.pick(late)
    token = second.call(0)
    for number in range(1, calls):
        ring_first.step(token)
        token = second.call(number, *ring_first.sent)
    half = rows // 2
    spans = [(0, half), (half, block - half), (block, half), (block + half, half)]
    far = second.spread(spans)
    ring_grads = RingScatter(lambda k: second.sums[k, :block], far[:2], peers)
    ring_results = RingScatter(lambda k: second.sums[k, block:], far[2:], peers)
    ring_grads.step()
    got = ring_first.got
    while ring_first.at > 1:
        ring_first.step(second.sums)
    picked, grad_result, activated, grad_pre = Experts.kept
    place_at = jnp.stack([lax.rem(dp_at, 2), dp_at // 2])
    ring_grads.step()
    w_out_sum = weight_grads(
        after(activated, *ring_grads.sent, *ring_first.sent), grad_result, 0, local_experts
    )
    def backward(m, pieces, *earlier):
        own, left, right = pieces
        return block_call(
            backward_kernel,
            [
                (after(own, *earlier), (0,), block),
                (left, (), block),
                (right, (), block),
                (cotangent, (m,)),
                (hidden[m],),
                (tokens, (m,)),
                (query, (m,)),
                (keyval, (m,)),
                (seg_col, (m,)),
                (seg_row, (m,)),
                (gates, (m,)),
                (gains,),
                (cos,),
                (sin,),
                (first_whole,),
                (out_whole,),
            ],
            [
                jax.ShapeDtypeStruct((rows, width), jnp.bfloat16),
                jax.ShapeDtypeStruct((rows, proj_width + 128), jnp.bfloat16),
                jax.ShapeDtypeStruct((rows, width), jnp.bfloat16),
                jax.ShapeDtypeStruct((8, width), jnp.float32),
            ],
            "attention_backward",
            [pltpu.VMEM((rows, q_width), jnp.bfloat16)],
        )

    half = max(1, local_experts // 2)
    got = second_got = ring_grads.got
    ring_grads.step(w_out_sum)
    picked = after(picked, w_out_sum, *got, *ring_grads.sent)
    w_in_sum = weight_grads(picked, grad_pre, 0, half)
    while ring_grads.at > 1:
        ring_grads.step(w_in_sum)
    got = ring_first.got + ring_grads.got
    while ring_first.at > 0:
        ring_first.step(w_in_sum)

    def scatter(part, *earlier):
        return lax.psum_scatter(after(part, *earlier), "dp", scatter_dimension=1, tiled=True)

    grad_w_out = scatter(w_out_sum, *second_got)
    grad_w_in = [scatter(w_in_sum, *got)]
    picked = after(picked, w_in_sum, *got, *ring_first.sent)
    w_in_sum = weight_grads(picked, grad_pre, half, local_experts - half)
    grad_w_in.append(scatter(w_in_sum, *ring_first.got))
    ring_grads.step(w_in_sum)
    ring_results.step(w_in_sum)
    back_first = backward(
        0, (first.sums, ring_first.left, ring_first.right), *ring_grads.sent
    )
    ring_results.step(back_first[3])
    back_second = backward(
        1, (second.sums, ring_grads.left, ring_grads.right), back_first[3]
    )
    ring_results.step(back_second[3])
    grad_tokens, grad_proj, grad_attn, gain_sums = zip(back_first, back_second)
    mine, other = attention_grads(
        place_at, after(xn1, *ring_results.sent), mixed, grad_proj, grad_attn, gain_sums, dp_count
    )
    grads, grad_w_in, grad_w_out = reduce_packed(
        mine, other, my_spot, peers, dp_count, grad_w_in, grad_w_out, ring_results, (q_width, kv_width)
    )
    grad_query, grad_keyval, grad_small, grad_attn_out = grads
    wide = jnp.float32
    outputs = []
    for m, (own, ring, at) in enumerate(
        ((first.sums, ring_first, block), (second.sums, ring_results, 0))
    ):
        total = hidden[m] + own[0, block:].astype(wide)
        total = total + ring.left[at:].astype(wide) + ring.right[at:].astype(wide)
        outputs.append(total.astype(jnp.bfloat16))
    return (
        jnp.stack(outputs),
        jnp.stack(grad_tokens),
        grad_small[:, experts],
        grad_small[:, experts + 1],
        grad_query,
        grad_keyval,
        grad_attn_out,
        grad_small[:, :experts],
        grad_w_in,
        grad_w_out,
    )


def last_kernel(spot_ref, *refs):
    outs = refs[-4:]
    blocks = refs[:-4]
    peers = len(blocks) - 1
    piece = blocks[0].shape[0]
    for k, block_ref in enumerate(blocks):
        distance = k if k <= peers // 2 else k - 1
        spot = lax.rem(spot_ref[0] - distance + peers, peers)
        held = block_ref.shape[0]
        row = spot * piece + (held if k == peers // 2 + 1 else 0)
        at = 0
        for out_ref in outs:
            columns = out_ref.shape[1]
            out_ref[pl.ds(pl.multiple_of(row, 8), held), :] = block_ref[
                :, at : at + columns
            ].astype(jnp.float32)
            at += columns


def reduce_packed(mine, other, my_spot, peers, dp_count, grad_w_in, grad_w_out, ring_results, widths):
    lines, span, columns = mine.shape
    swap = [(d, d ^ 1) for d in range(dp_count)]
    while ring_results.at > 1:
        ring_results.step()
    total = add_rows(mine, lax.ppermute(other, "dp", swap))
    total = after(total, *ring_results.got)
    piece = span // peers
    total = total.reshape(lines, peers, piece, columns)

    def part(k):
        at = lax.rem(my_spot - k + peers, peers)
        return lax.dynamic_slice_in_dim(total, at, 1, axis=1).reshape(lines * piece, columns)

    half = lines * piece // 2
    farthest = part(peers // 2)
    ring = RingScatter(part, (farthest[:half], farthest[half:]), peers)
    ring.step()
    ring_results.step()
    ring.step(*ring_results.sent)
    while ring.at > 0:
        ring.step()
    own, left, right = [held.astype(jnp.float32) for held in (part(0), ring.left, ring.right)]
    mine = (own + left + right).astype(jnp.bfloat16).reshape(lines, piece, columns)
    mine = after(mine, *grad_w_in, grad_w_out, *ring_results.got)
    line = lax.axis_index("dp") // 2

    def for_line(at):
        return lax.dynamic_index_in_dim(mine, lax.rem(at, lines), 0, keepdims=False)

    share = for_line(line).astype(jnp.float32)
    for k in range(1, lines):
        pairs = [(d, (d + 2 * k) % dp_count) for d in range(dp_count)]
        share = share + lax.ppermute(for_line(line + k), "dp", pairs)
    gather = RingGather(share.astype(jnp.bfloat16), peers, piece // 2)
    gather.step()
    grad_w_out = grad_w_out.astype(jnp.float32)
    gather.step(grad_w_out)
    grad_w_in = jnp.concatenate([part.astype(jnp.float32) for part in grad_w_in], axis=0)
    gather.step(grad_w_in, *ring_results.got)
    while gather.far is None:
        gather.step()
    blocks = gather.from_left + list(gather.far) + gather.from_right[:0:-1]
    columns = (widths[0], widths[1], 128, columns - sum(widths) - 128)
    if piece % 16 == 0:
        grads = block_call(
            last_kernel,
            [(block,) for block in blocks],
            [jax.ShapeDtypeStruct((span, count), jnp.float32) for count in columns],
            "last_rows",
            prefetch=my_spot.astype(jnp.int32).reshape(1),
        )
    else:
        far = jnp.concatenate(gather.far, axis=0)
        by_distance = jnp.stack(gather.from_left + [far] + gather.from_right[:0:-1])
        distance = lax.rem(my_spot - jnp.arange(peers, dtype=jnp.int32) + peers, peers)
        by_spot = jnp.take(by_distance, distance, axis=0).reshape(span, -1).astype(jnp.float32)
        edges = [sum(columns[:i]) for i in range(5)]
        grads = [by_spot[:, edges[i] : edges[i + 1]] for i in range(4)]
    return grads, grad_w_in, grad_w_out


def solution(mesh):
    return jax.shard_map(
        per_device,
        mesh=mesh,
        in_specs=(
            P(None, ("dp", "expert"), None),
            P(None, ("dp", "expert")),
            P(None, ("dp", "expert"), None),
            P("dp"),
            P("dp"),
            P("dp", None),
            P("dp", None),
            P("dp", None),
            P("dp", None),
            P("expert", None, None),
            P("expert", None, None),
            P(None, ("dp", "expert"), None),
        ),
        out_specs=(
            P(None, ("dp", "expert"), None),
            P(None, ("dp", "expert"), None),
            P("dp"),
            P("dp"),
            P("dp", None),
            P("dp", None),
            P("dp", None),
            P("dp", None),
            P("expert", "dp", None),
            P("expert", "dp", None),
        ),
        check_vma=False,
    )
```

```python
import functools
import math

import jax
import jax.numpy as jnp
from jax import lax
from jax.experimental import pallas as pl
from jax.experimental.pallas import tpu as pltpu
from jax.sharding import PartitionSpec as P

QUERY_HEADS = 12
KEY_VALUE_HEADS = 2
HEAD_SIZE = 128
FF = 768
TOPK = 4
EXPERTS = 32
EXTRA = 16
PIECES = 3
GROUP = 8

eps_norm = 1e-06
rope_base = 1000000.0
mask_fill = -1e30
highest = lax.Precision.HIGHEST


def rms_scale(tensor):
    return lax.rsqrt(jnp.mean(tensor * tensor, axis=-1, keepdims=True) + eps_norm)


def rope_tables(sequence_length, head_width):
    positions = jnp.arange(sequence_length).astype(jnp.float32)
    frequency = rope_base ** (-(jnp.arange(head_width // 2).astype(jnp.float32) * 2.0) / head_width)
    angles = positions[:, None] * frequency[None, :]
    return (jnp.cos(angles), jnp.sin(angles))

SCORE_SCALE = 1.0 / math.sqrt(HEAD_SIZE)
GELU_SCALE = math.sqrt(2.0 / math.pi)
GELU_CUBE = 0.044715
SMALL_COST = pl.CostEstimate(flops=1_000_000, bytes_accessed=1_000_000, transcendentals=0)


def after(value, *earlier):
    return lax.optimization_barrier((value,) + earlier)[0]


def slot_hits(routes_all, first_expert, local_experts, capacity):
    rows = routes_all.shape[-1]
    names = first_expert + jnp.arange(local_experts, dtype=jnp.int32)
    named = routes_all[:, None].astype(jnp.int32) == names[None, :, None, None]
    member = jnp.any(named, axis=2)
    lower = (jnp.arange(rows)[:, None] < jnp.arange(rows)[None, :]).astype(jnp.bfloat16)
    rank = dot32(member.astype(jnp.bfloat16).reshape(-1, rows), lower).reshape(member.shape)
    slots = jnp.arange(capacity, dtype=jnp.float32)
    return member[:, :, None, :] & (rank[:, :, None, :] == slots[None, None, :, None])


def pack_pieces(values, out_ref, first_row):
    rows = values.shape[1]
    rest = values
    for piece in range(PIECES):
        part = rest.astype(jnp.bfloat16)
        rest = rest - part.astype(jnp.float32)
        for half in range(EXPERTS // EXTRA):
            at = (piece * (EXPERTS // EXTRA) + half) * rows
            out_ref[first_row : first_row + EXTRA, at : at + rows] = part[
                half * EXTRA : (half + 1) * EXTRA
            ]


def dot32(left, right):
    return jnp.dot(left, right, preferred_element_type=jnp.float32)


def dot_nt(left, right):
    return lax.dot_general(
        left, right, (((1,), (1,)), ((), ())), preferred_element_type=jnp.float32
    )


def dot_tn(left, right):
    return lax.dot_general(
        left, right, (((0,), (0,)), ((), ())), preferred_element_type=jnp.float32
    )


def mask_of(seg_col, seg_row):
    rows = seg_col.shape[0]
    query_at = lax.broadcasted_iota(jnp.int32, (rows, rows), 0)
    key_at = lax.broadcasted_iota(jnp.int32, (rows, rows), 1)
    return (seg_col == seg_row) & (query_at >= key_at)


def softmax_rows(query, key, allowed):
    scores = jnp.where(allowed, dot_nt(query, key) * SCORE_SCALE, mask_fill)
    weight = jnp.exp(scores - jnp.max(scores, axis=-1, keepdims=True))
    return weight / jnp.sum(weight, axis=-1, keepdims=True)


def from_blocks(starts_ref, rows_ref, blocks):
    total = None
    for at, block_ref in enumerate(blocks):
        span = block_ref.shape[0]
        columns = pl.ds(pl.multiple_of(starts_ref[at], 128), span)
        part = dot32(rows_ref[:, columns], block_ref[...])
        total = part if total is None else total + part
    return total


def attention_kernel(
    starts_ref,
    tok_ref,
    seg_col_ref,
    seg_row_ref,
    routes_ref,
    cos_ref,
    sin_ref,
    *refs,
):
    weight_refs = refs[:-7]
    xn1_ref, query_ref, keyval_ref, mixed_ref, gates_ref, gates_pack_ref, gains_ref = refs[-7:]

    @pl.when(pl.program_id(0) == 0)
    def _():
        for at, block_ref in enumerate(weight_refs):
            span, columns = block_ref.shape
            pad = block_ref[:, columns - 128 :].astype(jnp.float32).T
            place = pl.ds(pl.multiple_of(starts_ref[at], 128), span)
            gains_ref[:, place] = pad[2 * EXPERTS : 2 * EXPERTS + 8]

    tok = tok_ref[...].astype(jnp.float32)
    xn1_ref[...] = (tok * rms_scale(tok) * gains_ref[0:1, :]).astype(jnp.bfloat16)
    proj = from_blocks(starts_ref, xn1_ref, weight_refs)
    cos, sin = cos_ref[...], sin_ref[...]

    def rotate(part):
        return (part * cos + pltpu.roll(part, HEAD_SIZE // 2, 1) * sin).astype(jnp.bfloat16)

    q_width = QUERY_HEADS * HEAD_SIZE
    k_width = KEY_VALUE_HEADS * HEAD_SIZE
    for head in range(QUERY_HEADS):
        span = slice(head * HEAD_SIZE, (head + 1) * HEAD_SIZE)
        query_ref[:, span] = rotate(proj[:, span])
    for head in range(KEY_VALUE_HEADS):
        span = slice(head * HEAD_SIZE, (head + 1) * HEAD_SIZE)
        keyval_ref[:, span] = rotate(proj[:, q_width:][:, span])
    keyval_ref[:, k_width:] = proj[:, q_width + k_width : q_width + 2 * k_width].astype(
        jnp.bfloat16
    )
    logits = proj[:, q_width + 2 * k_width :]
    columns = lax.broadcasted_iota(jnp.int32, logits.shape, 1)
    named = [columns == routes_ref[:, j : j + 1] for j in range(TOPK)]
    chosen = [jnp.sum(jnp.where(hit, logits, 0.0), axis=-1, keepdims=True) for hit in named]
    top = functools.reduce(jnp.maximum, chosen)
    weight = [jnp.exp(part - top) for part in chosen]
    total = functools.reduce(jnp.add, weight)
    gates = jnp.full(logits.shape, -1.0, jnp.float32)
    for hit, part in zip(named, weight):
        gates = jnp.where(hit, part / total, gates)
    gates_ref[...] = gates
    pack_pieces(gates.T[:EXPERTS], gates_pack_ref, 0)
    allowed = mask_of(seg_col_ref[...], seg_row_ref[...])
    for head in range(QUERY_HEADS):
        span = slice(head * HEAD_SIZE, (head + 1) * HEAD_SIZE)
        group = head // (QUERY_HEADS // KEY_VALUE_HEADS)
        key = keyval_ref[:, group * HEAD_SIZE : (group + 1) * HEAD_SIZE]
        value = keyval_ref[:, k_width + group * HEAD_SIZE : k_width + (group + 1) * HEAD_SIZE]
        probs = softmax_rows(query_ref[:, span], key, allowed)
        mixed_ref[:, span] = dot32(probs.astype(jnp.bfloat16), value).astype(jnp.bfloat16)


def hidden_kernel(starts_ref, mixed_ref, tok_ref, gains_ref, pack_ref, *refs):
    weight_refs = refs[:-2]
    hidden_ref, xn2_ref = refs[-2:]
    rows = tok_ref.shape[0]
    hidden = tok_ref[...].astype(jnp.float32) + from_blocks(
        starts_ref, mixed_ref, weight_refs
    )
    hidden_ref[...] = hidden
    xn2_ref[:rows, :] = (hidden * rms_scale(hidden) * gains_ref[1:2, :]).astype(jnp.bfloat16)
    xn2_ref[rows:, :] = pack_ref[...]


def backward_kernel(
    own_ref,
    left_ref,
    right_ref,
    cot_ref,
    hidden_ref,
    tok_ref,
    query_ref,
    keyval_ref,
    seg_col_ref,
    seg_row_ref,
    gates_ref,
    gains_ref,
    cos_ref,
    sin_ref,
    *refs,
):
    weight_ref, out_weight_ref = refs[:2]
    grad_tok_ref, grad_proj_ref, grad_attn_ref, gain_sum_ref, mixed_grad_ref = refs[2:]
    width = tok_ref.shape[1]
    q_width = QUERY_HEADS * HEAD_SIZE
    k_width = KEY_VALUE_HEADS * HEAD_SIZE
    proj_width = q_width + 2 * k_width
    rows = tok_ref.shape[0]
    sums = [ref[...].astype(jnp.float32) for ref in (own_ref, left_ref, right_ref)]
    sums = sums[0] + sums[1] + sums[2]
    grad_xn2, pack = sums[:rows], sums[rows:]
    halves = EXPERTS // EXTRA
    lines = [
        sum(
            pack[:, (piece * halves + half) * rows : (piece * halves + half + 1) * rows]
            for piece in range(PIECES)
        )
        for half in range(halves)
    ]
    lines.append(jnp.zeros((128 - EXPERTS, rows), jnp.float32))
    grad_gates = jnp.concatenate(lines, axis=0).T
    hidden = hidden_ref[...]
    scale = rms_scale(hidden)
    unit = hidden * scale
    gain_sum_ref[...] = jnp.zeros(gain_sum_ref.shape, jnp.float32)
    gain_sum_ref[1:2, :] = jnp.sum(grad_xn2 * unit, axis=0, keepdims=True)
    grad_unit = grad_xn2 * gains_ref[1:2, :]
    grad_hidden = cot_ref[...].astype(jnp.float32) + scale * (
        grad_unit - unit * jnp.mean(grad_unit * unit, axis=-1, keepdims=True)
    )
    grad_attn_ref[...] = grad_hidden.astype(jnp.bfloat16)
    mixed_grad_ref[...] = dot_nt(grad_attn_ref[...], out_weight_ref[...]).astype(jnp.bfloat16)
    cos, sin = cos_ref[...], sin_ref[...]

    def unrotate(part):
        return (part * cos - pltpu.roll(part, HEAD_SIZE // 2, 1) * sin).astype(jnp.bfloat16)

    allowed = mask_of(seg_col_ref[...], seg_row_ref[...])
    per_group = QUERY_HEADS // KEY_VALUE_HEADS
    for group in range(KEY_VALUE_HEADS):
        key_span = slice(group * HEAD_SIZE, (group + 1) * HEAD_SIZE)
        value_span = slice(k_width + group * HEAD_SIZE, k_width + (group + 1) * HEAD_SIZE)
        key, value = keyval_ref[:, key_span], keyval_ref[:, value_span]
        grad_key = jnp.zeros(key.shape, jnp.float32)
        grad_value = jnp.zeros(key.shape, jnp.float32)
        for head in range(group * per_group, (group + 1) * per_group):
            span = slice(head * HEAD_SIZE, (head + 1) * HEAD_SIZE)
            query, grad_mixed = query_ref[:, span], mixed_grad_ref[:, span]
            probs = softmax_rows(query, key, allowed)
            grad_value += dot_tn(probs.astype(jnp.bfloat16), grad_mixed)
            grad_probs = dot_nt(grad_mixed, value)
            mean = jnp.sum(probs * grad_probs, axis=-1, keepdims=True)
            grad_scores = (probs * (grad_probs - mean)).astype(jnp.bfloat16)
            grad_proj_ref[:, span] = unrotate(dot32(grad_scores, key) * SCORE_SCALE)
            grad_key += dot_tn(grad_scores, query)
        grad_proj_ref[:, q_width + group * HEAD_SIZE : q_width + (group + 1) * HEAD_SIZE] = (
            unrotate(grad_key * SCORE_SCALE)
        )
        first = q_width + k_width + group * HEAD_SIZE
        grad_proj_ref[:, first : first + HEAD_SIZE] = grad_value.astype(jnp.bfloat16)
    gates = jnp.maximum(gates_ref[...], 0.0)
    grad_logits = gates * (grad_gates - jnp.sum(gates * grad_gates, axis=-1, keepdims=True))
    high = grad_logits.astype(jnp.bfloat16).astype(jnp.float32)
    low = pltpu.roll(grad_logits - high, EXPERTS, 1)
    grad_proj_ref[:, proj_width:] = (high + low).astype(jnp.bfloat16)
    grad_xn1 = dot_nt(grad_proj_ref[...], weight_ref[...])
    tok = tok_ref[...].astype(jnp.float32)
    scale = rms_scale(tok)
    unit = tok * scale
    gain_sum_ref[0:1, :] = jnp.sum(grad_xn1 * unit, axis=0, keepdims=True)
    grad_unit = grad_xn1 * gains_ref[0:1, :]
    grad_tok_ref[...] = (
        grad_hidden
        + scale * (grad_unit - unit * jnp.mean(grad_unit * unit, axis=-1, keepdims=True))
    ).astype(jnp.bfloat16)


def ring_order(peers):
    minor = peers // 4
    walk = []
    for col in range(minor):
        line = range(4) if col % 2 == 0 else range(3, -1, -1)
        walk += [row * minor + col for row in line]
    return walk


def ring_step(part, shift, peers):
    order = ring_order(peers)
    pairs = [(order[i], order[(i + shift) % peers]) for i in range(peers)]
    return lax.ppermute(part, "expert", pairs)


class RingGather:
    def __init__(self, part, peers, half):
        self.peers, self.half = peers, half
        self.from_left, self.from_right = [part], [part]
        self.far = None
        self.got = ()

    def step(self, *earlier):
        left, right = self.from_left[-1], self.from_right[-1]
        last = len(self.from_left) == self.peers // 2
        if last:
            left, right = left[: self.half], right[self.half :]
        left, right = self.sent = lax.optimization_barrier((left, right) + earlier)[:2]
        left, right = ring_step(left, 1, self.peers), ring_step(right, -1, self.peers)
        self.got = (left, right)
        if last:
            self.far = (left, right)
        else:
            self.from_left.append(left)
            self.from_right.append(right)
        return self

    def rows(self, k, first, count):
        if k < len(self.from_left):
            return self.from_left[k], first
        if k > self.peers // 2:
            return self.from_right[self.peers - k], first
        if first < self.half:
            return self.far[0], first
        return self.far[1], first - self.half

    def stack_rows(self, first, count):
        found = [self.rows(k, first, count) for k in range(self.peers)]
        return jnp.stack([array[at : at + count] for array, at in found])


class RingScatter:
    def __init__(self, part, far, peers):
        self.part, self.far, self.peers = part, far, peers
        self.at = peers // 2
        self.half = far[0].shape[0]

    def step(self, *earlier):
        peers, k, half = self.peers, self.at, self.half
        if k == peers // 2:
            left, right = lax.optimization_barrier(tuple(self.far) + earlier)[:2]
        else:
            left, right = self.part(k), self.part(peers - k)
            if earlier:
                self.left, self.right = lax.optimization_barrier(
                    (self.left, self.right) + earlier
                )[:2]
            if k == peers // 2 - 1:
                kept = left[half:].astype(jnp.bfloat16), right[:half].astype(jnp.bfloat16)
                left = jnp.concatenate([add_rows(left[:half], self.left), kept[0]], axis=0)
                right = jnp.concatenate([kept[1], add_rows(right[half:], self.right)], axis=0)
            else:
                left, right = add_rows(left, self.left), add_rows(right, self.right)
        left, right = self.sent = lax.optimization_barrier((left, right))
        self.left = ring_step(left, -1, peers)
        self.right = ring_step(right, 1, peers)
        self.got = (self.left, self.right)
        self.at = k - 1
        return self


def add_rows(left, right):
    return (left.astype(jnp.float32) + right.astype(jnp.float32)).astype(jnp.bfloat16)


def expert_kernel(sources, *refs):
    rows_refs = refs[:sources]
    grad_refs = refs[sources : 2 * sources]
    gate_refs = refs[2 * sources : 3 * sources]
    w_in_ref, w_out_ref = refs[3 * sources : 3 * sources + 2]
    (
        back_rows_ref,
        back_grads_ref,
        grad_gate_ref,
        picked_ref,
        grad_result_ref,
        activated_ref,
        grad_pre_ref,
    ) = refs[-7:]
    capacity, width = rows_refs[0].shape
    for k in range(sources):
        picked_ref[pl.ds(k * capacity, capacity), :] = rows_refs[k][...]
    pre_act = dot32(picked_ref[...], w_in_ref[...])
    gate_part = pre_act[:, :FF]
    up_part = pre_act[:, FF:]
    square = gate_part * gate_part
    bend = jnp.tanh(GELU_SCALE * gate_part * (1.0 + GELU_CUBE * square))
    lift = 0.5 * (1.0 + bend)
    gelu_val = gate_part * lift
    slope = lift + 0.5 * gate_part * (1.0 - bend * bend) * (
        GELU_SCALE * (1.0 + 3.0 * GELU_CUBE * square)
    )
    activated_ref[...] = (gelu_val * up_part).astype(jnp.bfloat16)
    result = dot32(activated_ref[...], w_out_ref[...])
    for k in range(sources):
        gates = gate_refs[k][...]
        span = slice(k * capacity, (k + 1) * capacity)
        grad_rows = grad_refs[k][...].astype(jnp.float32)
        grad_gate_ref[span, :] = jnp.sum(result[span] * grad_rows, axis=-1, keepdims=True)
        back_rows_ref[k] = (result[span] * gates).astype(jnp.bfloat16)
        grad_result_ref[span, :] = (grad_rows * gates).astype(jnp.bfloat16)
    grad_act = lax.dot_general(
        grad_result_ref[...],
        w_out_ref[...],
        (((1,), (1,)), ((), ())),
        preferred_element_type=jnp.float32,
    )
    grad_pre_ref[:, :FF] = (grad_act * up_part * slope).astype(jnp.bfloat16)
    grad_pre_ref[:, FF:] = (grad_act * gelu_val).astype(jnp.bfloat16)
    grad_in = lax.dot_general(
        grad_pre_ref[...],
        w_in_ref[...],
        (((1,), (1,)), ((), ())),
        preferred_element_type=jnp.float32,
    ).astype(jnp.bfloat16)
    for k in range(sources):
        back_grads_ref[k] = grad_in[k * capacity : (k + 1) * capacity]


def expert_pass(rows_list, grads_list, gate_slots, w_in, w_out, held_outs, position, first, count):
    sources = len(rows_list)
    local_experts, width, _ = w_in.shape
    slots = rows_list[0].shape[0]
    capacity = slots // local_experts
    held = sources * capacity
    block_spec = pl.BlockSpec((capacity, width), lambda e: (e + first, 0))
    back_spec = pl.BlockSpec((sources, capacity, width), lambda e: (0, e + first, 0))
    column_spec = pl.BlockSpec((None, held, 1), lambda e: (e + first, 0, 0))

    def kept_spec(columns):
        return pl.BlockSpec((None, held, columns), lambda e: (e + first, position[0], 0))

    def kept_shape(columns):
        return jax.ShapeDtypeStruct((local_experts, position[1] * held, columns), jnp.bfloat16)

    kept_widths = (width, width, FF, 2 * FF)
    first_held = 3 * sources + 2
    given = [(i, part) for i, part in enumerate(held_outs) if part is not None]
    return pl.pallas_call(
        functools.partial(expert_kernel, sources),
        grid=(count,),
        in_specs=[block_spec] * (2 * sources)
        + [pl.BlockSpec((capacity, 1), lambda e: (e + first, 0))] * sources
        + [
            pl.BlockSpec((None, width, 2 * FF), lambda e: (e + first, 0, 0)),
            pl.BlockSpec((None, FF, width), lambda e: (e + first, 0, 0)),
        ]
        + [pl.BlockSpec(memory_space=pl.ANY)] * len(given),
        out_specs=[back_spec, back_spec, column_spec] + [kept_spec(c) for c in kept_widths],
        out_shape=[
            jax.ShapeDtypeStruct((sources, slots, width), jnp.bfloat16),
            jax.ShapeDtypeStruct((sources, slots, width), jnp.bfloat16),
            jax.ShapeDtypeStruct((local_experts, held, 1), jnp.float32),
        ]
        + [kept_shape(c) for c in kept_widths],
        input_output_aliases={first_held + at: i for at, (i, _) in enumerate(given)},
        compiler_params=pltpu.CompilerParams(vmem_limit_bytes=60 * 1024 * 1024),
        cost_estimate=SMALL_COST,
        name="expert_pass",
    )(*rows_list, *grads_list, *gate_slots, w_in, w_out, *[part for _, part in given])


def block_call(kernel, operands, out_shape, name, scratch=(), prefetch=None):
    def spec(array, lead=(), rows=None):
        rest = array.shape[len(lead) :]
        at = lead + (0,) * len(rest)
        if rows is not None:
            count, block = rows if isinstance(rows, tuple) else (rows, 0)
            rest = (count,) + rest[1:]
            at = lead + (block,) + (0,) * (len(rest) - 1)
        return pl.BlockSpec((None,) * len(lead) + rest, lambda *_: at)

    scalars = [] if prefetch is None else [prefetch]
    return pl.pallas_call(
        kernel,
        grid_spec=pltpu.PrefetchScalarGridSpec(
            num_scalar_prefetch=len(scalars),
            grid=(1,),
            in_specs=[spec(*operand) for operand in operands],
            out_specs=[spec(shape) for shape in out_shape],
            scratch_shapes=list(scratch),
        ),
        out_shape=out_shape,
        compiler_params=pltpu.CompilerParams(vmem_limit_bytes=60 * 1024 * 1024),
        cost_estimate=SMALL_COST,
        name=name,
    )(*scalars, *[operand[0] for operand in operands])


def pick_kernel(shares, gated, first_ref, place_ref, *refs):
    at = 0
    outs = refs[sum(count for _, count in shares) + (len(shares) if gated else 0) :]
    for number, (k, count) in enumerate(shares):
        total, row = None, 0
        for block_ref in refs[at : at + count]:
            held = block_ref.shape[0]
            part = dot32(place_ref[k, :, row : row + held], block_ref[...])
            total = part if total is None else total + part
            row += held
        outs[number][...] = total.astype(jnp.bfloat16)
        at += count
        if gated:
            slot_gates(first_ref[0], place_ref[k], refs[at], outs[len(shares) + number])
            at += 1


def slot_gates(first_expert, place, pack_ref, out_ref):
    slots, rows = place.shape
    pack = pack_ref[...].astype(jnp.float32)
    halves = EXPERTS // EXTRA
    line = lax.broadcasted_iota(jnp.int32, (EXTRA, rows), 0)
    local_experts = slots * 4 // rows
    capacity = rows // 4
    for e in range(local_experts):
        gate = jnp.zeros((1, rows), jnp.float32)
        for half in range(halves):
            hit = line + half * EXTRA == first_expert + e
            for piece in range(PIECES):
                at = (piece * halves + half) * rows
                gate += jnp.sum(
                    jnp.where(hit, pack[:, at : at + rows], 0.0), axis=0, keepdims=True
                )
        span = slice(e * capacity, (e + 1) * capacity)
        out_ref[span, :] = jnp.sum(
            place[span].astype(jnp.float32) * gate, axis=-1, keepdims=True
        )


def pick_rows(first_expert, place, ring, distances, gated):
    _, slots, rows = place.shape
    half = rows // 2
    operands, shares = [], []
    for k in distances:
        spans = [(0, rows)]
        if k == ring.peers // 2 and ring.half < rows:
            spans = [(0, half), (half, half)]
        shares.append((k, len(spans)))
        for at, count in spans + ([(rows, EXTRA)] if gated else []):
            array, at = ring.rows(k, at, count)
            operands.append((array, (), (count, at // count)))
    width = operands[0][0].shape[-1]
    out_shape = [jax.ShapeDtypeStruct((slots, width), jnp.bfloat16) for _ in distances]
    if gated:
        out_shape += [jax.ShapeDtypeStruct((slots, 1), jnp.float32) for _ in distances]
    return block_call(
        functools.partial(pick_kernel, shares, gated),
        [(place,)] + operands,
        out_shape,
        "pick_rows",
        prefetch=first_expert,
    )


def spread_kernel(middle, spans, held, first_ref, place_ref, rows_ref, grads_ref, gate_ref, *refs):
    out_ref, *far_refs = refs[held:]
    place = place_ref[...]
    rows = place.shape[1]
    out_ref[:rows, :] = dot_tn(place, grads_ref[...]).astype(jnp.bfloat16)
    out_ref[rows + EXTRA :, :] = dot_tn(place, rows_ref[...]).astype(jnp.bfloat16)
    capacity = gate_ref.shape[1]
    expert = lax.broadcasted_iota(jnp.int32, (EXPERTS, rows), 0) - first_ref[0]
    gates = jnp.zeros((EXPERTS, rows), jnp.float32)
    for e in range(gate_ref.shape[0]):
        hit = place[e * capacity : (e + 1) * capacity].astype(jnp.float32)
        line = jnp.sum(hit * gate_ref[e], axis=0, keepdims=True)
        gates = jnp.where(expert == e, line, gates)
    pack_pieces(gates, out_ref, rows)

    @pl.when(pl.program_id(0) == middle)
    def _():
        for far_ref, (row, count) in zip(far_refs, spans):
            far_ref[...] = out_ref[row : row + count, :]


def spread_rows(first_expert, place, rows_back, grads_back, gate_slots, group, spans, held):
    sources, slots, rows = place.shape
    width = rows_back.shape[-1]
    local_experts = gate_slots.shape[0]
    base = group * GROUP
    by_source = pl.BlockSpec((None, slots, width), lambda k, f: (k, 0, 0))
    held = [] if held is None else [held]
    out_shape = [jax.ShapeDtypeStruct((sources, 2 * rows + EXTRA, width), jnp.bfloat16)]
    out_shape += [jax.ShapeDtypeStruct((count, width), jnp.bfloat16) for _, count in spans]
    out_specs = [pl.BlockSpec((None, 2 * rows + EXTRA, width), lambda k, f: (base + k, 0, 0))]
    out_specs += [pl.BlockSpec((count, width), lambda k, f: (0, 0)) for _, count in spans]
    return pl.pallas_call(
        functools.partial(spread_kernel, sources // 2 - base, spans, len(held)),
        grid_spec=pltpu.PrefetchScalarGridSpec(
            num_scalar_prefetch=1,
            grid=(GROUP,),
            in_specs=[
                pl.BlockSpec((None, slots, rows), lambda k, f: (base + k, 0, 0)),
                by_source,
                by_source,
                pl.BlockSpec((local_experts, slots // local_experts, 1), lambda k, f: (0, k, 0)),
            ]
            + [pl.BlockSpec(memory_space=pl.ANY)] * len(held),
            out_specs=out_specs,
        ),
        out_shape=out_shape,
        input_output_aliases={5 + i: i for i in range(len(held))},
        compiler_params=pltpu.CompilerParams(vmem_limit_bytes=60 * 1024 * 1024),
        cost_estimate=SMALL_COST,
        name="spread_rows",
    )(first_expert, place, rows_back, grads_back, gate_slots, *held)


def weight_grad_kernel(left_ref, right_ref, out_ref):
    out_ref[...] = dot_tn(left_ref[...], right_ref[...]).astype(jnp.bfloat16)


def weight_grads(left, right, first, count):
    _, held, height = left.shape
    columns = right.shape[-1]
    tile = min(height, 768)
    return pl.pallas_call(
        weight_grad_kernel,
        grid=(count, height // tile),
        in_specs=[
            pl.BlockSpec((None, held, tile), lambda e, i: (e + first, 0, i)),
            pl.BlockSpec((None, held, columns), lambda e, i: (e + first, 0, 0)),
        ],
        out_specs=pl.BlockSpec((None, tile, columns), lambda e, i: (e, i, 0)),
        out_shape=jax.ShapeDtypeStruct((count, height, columns), jnp.bfloat16),
        compiler_params=pltpu.CompilerParams(vmem_limit_bytes=60 * 1024 * 1024),
        cost_estimate=SMALL_COST,
        name="weight_grads",
    )(left, right)


def attention_forward(starts, tokens, seg_col, seg_row, routes, cos, sin, weights):
    count, rows, width = tokens.shape

    def by_micro(*shape):
        return pl.BlockSpec((None,) + shape, lambda m, s: (m,) + (0,) * len(shape))

    def shared(part):
        return pl.BlockSpec(part.shape, lambda m, s: (0, 0))

    kv_width = 2 * KEY_VALUE_HEADS * HEAD_SIZE
    shapes = [
        ((rows, width), jnp.bfloat16),
        ((rows, QUERY_HEADS * HEAD_SIZE), jnp.bfloat16),
        ((rows, kv_width), jnp.bfloat16),
        ((rows, QUERY_HEADS * HEAD_SIZE), jnp.bfloat16),
        ((rows, 128), jnp.float32),
        ((EXTRA, PIECES * EXPERTS // EXTRA * rows), jnp.bfloat16),
    ]
    return pl.pallas_call(
        attention_kernel,
        grid_spec=pltpu.PrefetchScalarGridSpec(
            num_scalar_prefetch=1,
            grid=(count,),
            in_specs=[
                by_micro(rows, width),
                by_micro(rows, 1),
                by_micro(1, rows),
                by_micro(rows, TOPK),
                shared(cos),
                shared(sin),
            ]
            + [shared(part) for part in weights],
            out_specs=[by_micro(*shape) for shape, _ in shapes]
            + [pl.BlockSpec((8, width), lambda m, s: (0, 0))],
        ),
        out_shape=[jax.ShapeDtypeStruct((count,) + shape, kind) for shape, kind in shapes]
        + [jax.ShapeDtypeStruct((8, width), jnp.float32)],
        compiler_params=pltpu.CompilerParams(vmem_limit_bytes=60 * 1024 * 1024),
        cost_estimate=SMALL_COST,
        name="attention_forward",
    )(starts, tokens, seg_col, seg_row, routes, cos, sin, *weights)


def join_kernel(starts_ref, *refs):
    for at, block_ref in enumerate(refs[:-1]):

        @pl.when(pl.program_id(0) == at)
        def _():
            refs[-1][...] = block_ref[...]


def join_blocks(starts, blocks):
    if len(blocks) == 1:
        return blocks[0]
    span, columns = blocks[0].shape
    return pl.pallas_call(
        join_kernel,
        grid_spec=pltpu.PrefetchScalarGridSpec(
            num_scalar_prefetch=1,
            grid=(len(blocks),),
            in_specs=[pl.BlockSpec((span, columns), lambda i, s: (0, 0)) for _ in blocks],
            out_specs=pl.BlockSpec((span, columns), lambda i, s: (s[i] // span, 0)),
        ),
        out_shape=jax.ShapeDtypeStruct((len(blocks) * span, columns), blocks[0].dtype),
        compiler_params=pltpu.CompilerParams(vmem_limit_bytes=60 * 1024 * 1024),
        cost_estimate=SMALL_COST,
        name="join_blocks",
    )(starts, *blocks)


def attention_grad_kernel(core_ref, xn1, mixed, *refs):
    count = xn1.shape[0]
    proj, attn, sums = [refs[i * count : (i + 1) * count] for i in range(3)]
    mine_ref, other_ref = refs[-2:]
    split = proj[0].shape[1]
    span = mine_ref.shape[0]
    grad = sum(dot_tn(xn1[m], proj[m][...]) for m in range(count))
    router = grad[:, split - 128 :]
    lane = lax.broadcasted_iota(jnp.int32, router.shape, 1)
    router = router + pltpu.roll(router, 128 - EXPERTS, 1)
    gain = sum(part[...] for part in sums)
    lines = [jnp.zeros((EXPERTS, gain.shape[1]), jnp.float32), gain]
    lines.append(jnp.zeros((128 - EXPERTS - gain.shape[0], gain.shape[1]), jnp.float32))
    router = jnp.where(lane < EXPERTS, router, jnp.concatenate(lines, axis=0).T)
    first = core_ref[0] == 0

    def put(columns, value):
        value = value.astype(jnp.bfloat16)
        low, high = value[:span], value[span:]
        mine_ref[:, columns] = jnp.where(first, low, high)
        other_ref[:, columns] = jnp.where(first, high, low)

    put(slice(0, split - 128), grad[:, : split - 128])
    put(slice(split - 128, split), router)
    put(slice(split, None), sum(dot_tn(mixed[m], attn[m][...]) for m in range(count)))


def attention_grads(core, xn1, mixed, proj, attn, gain_sums, parts):
    count, rows, width = xn1.shape
    span = width // parts
    lines = parts // 2
    columns = proj[0].shape[1] + attn[0].shape[1]
    by_line = pl.BlockSpec((count, rows, 2 * span), lambda i, c: (0, 0, i))

    def shared(part):
        return pl.BlockSpec(part.shape, lambda i, c: (0, 0))

    out_spec = pl.BlockSpec((None, span, columns), lambda i, c: (i, 0, 0))
    out_shape = jax.ShapeDtypeStruct((lines, span, columns), jnp.bfloat16)
    return pl.pallas_call(
        attention_grad_kernel,
        grid_spec=pltpu.PrefetchScalarGridSpec(
            num_scalar_prefetch=1,
            grid=(lines,),
            in_specs=[by_line, by_line]
            + [shared(p) for p in proj]
            + [shared(p) for p in attn]
            + [pl.BlockSpec((p.shape[0], 2 * span), lambda i, c: (0, i)) for p in gain_sums],
            out_specs=[out_spec, out_spec],
        ),
        out_shape=[out_shape, out_shape],
        compiler_params=pltpu.CompilerParams(vmem_limit_bytes=60 * 1024 * 1024),
        cost_estimate=SMALL_COST,
        name="attention_grads",
    )(core, xn1, mixed, *proj, *attn, *gain_sums)


def gather_blocks(part, dp_at, dp_count):
    span = part.shape[0]
    if span % 128 or dp_count != 4:
        whole = lax.all_gather(part, "dp", axis=0, tiled=True)
        return lambda *earlier: [whole], jnp.zeros((1,), jnp.int32)
    line = [(d, (d + 2) % 4) for d in range(4)]
    core = [(d, d ^ 1) for d in range(4)]
    across = lax.ppermute(part, "dp", line)
    beside = lax.ppermute(part, "dp", core)
    far = lax.rem(dp_at + 2, 4)
    owners = jnp.stack([dp_at, dp_at + 1 - 2 * lax.rem(dp_at, 2), far, far + 1 - 2 * lax.rem(far, 2)])

    def blocks(*earlier):
        moved = after(across, *earlier) if earlier else across
        return [part, beside, moved, lax.ppermute(moved, "dp", core)]

    return blocks, owners * span


def per_device(
    tokens,
    segments,
    routes,
    norm_one,
    norm_two,
    w_query,
    key_value_weight,
    w_out_attn,
    w_router,
    w_in,
    w_out,
    cotangent,
):
    micro_count, rows, width = tokens.shape
    micros = range(micro_count)
    peers = lax.axis_size("expert")
    dp_count = lax.axis_size("dp")
    local_experts = w_in.shape[0]
    experts = local_experts * peers
    capacity = rows // 4
    first_expert = lax.axis_index("expert") * local_experts
    q_width = w_query.shape[1]
    kv_width = key_value_weight.shape[1]
    proj_width = q_width + kv_width
    cosine_table, sine_values = rope_tables(rows, HEAD_SIZE)
    cos = jnp.concatenate([cosine_table, cosine_table], axis=1)
    sin = jnp.concatenate([-sine_values, sine_values], axis=1)
    order = ring_order(peers)
    spot = [order.index(dev) for dev in range(peers)]
    my_spot = jnp.array(spot, jnp.int32)[lax.axis_index("expert")]

    router_pad = jnp.zeros((w_router.shape[0], 126 - 2 * experts), jnp.bfloat16)
    first_weight = jnp.concatenate(
        [
            w_query,
            key_value_weight,
            w_router,
            w_router,
            norm_one[:, None],
            norm_two[:, None],
            router_pad,
        ],
        axis=1,
    )
    dp_at = lax.axis_index("dp").astype(jnp.int32)
    first_weights, starts = gather_blocks(first_weight, dp_at, dp_count)
    out_weights, _ = gather_blocks(w_out_attn, dp_at, dp_count)

    routes_rows = jnp.swapaxes(routes, 1, 2).reshape(-1, rows).astype(jnp.bfloat16)
    routes_rows = jnp.pad(
        routes_rows, ((0, EXTRA - routes_rows.shape[0]), (0, width - rows))
    )
    cot_rings = [
        RingGather(jnp.concatenate([cotangent[0], routes_rows], axis=0), peers, rows // 2),
        RingGather(cotangent[1], peers, rows // 2),
    ]
    steps = peers // 2
    for at in range(steps - 2):
        for ring in cot_rings:
            ring.step()
        if at == 0:
            first_weights = first_weights(*cot_rings[0].got, *cot_rings[1].got)
    first_at = first_expert.astype(jnp.int32).reshape(1)
    seg_col, seg_row = segments[:, :, None], segments[:, None, :]
    xn1, query, keyval, mixed, gates, gates_pack, gains = attention_forward(
        starts, tokens, seg_col, seg_row, routes, cos, sin, first_weights
    )
    cot_rings[0].step(mixed)
    out_weights = out_weights(mixed)
    hidden, xn2 = [], []
    for m in micros:
        out = block_call(
            hidden_kernel,
            [(after(mixed, *xn2), (m,)), (tokens, (m,)), (gains,), (gates_pack, (m,))]
            + [(part,) for part in out_weights],
            [
                jax.ShapeDtypeStruct((rows, width), jnp.float32),
                jax.ShapeDtypeStruct((rows + EXTRA, width), jnp.bfloat16),
            ],
            "hidden_rows",
            prefetch=starts,
        )
        hidden.append(out[0])
        xn2.append(out[1])
    cot_rings[1].step(xn2[0])
    for ring in cot_rings:
        ring.step()
    got = cot_rings[0].got + cot_rings[1].got
    first_whole = join_blocks(starts, [after(first_weights[0], *got)] + first_weights[1:])
    out_whole = join_blocks(starts, [after(out_weights[0], first_whole)] + out_weights[1:])
    routes_all = cot_rings[0].stack_rows(rows, micro_count * TOPK)[:, :, :rows]
    routes_all = routes_all.reshape(peers, micro_count, TOPK, rows)
    places = [
        slot_hits(routes_all[:, m], first_expert, local_experts, capacity)
        .astype(jnp.bfloat16)
        .reshape(peers, -1, rows)
        for m in micros
    ]
    every = list(range(peers))
    late = [steps - 1, steps, steps + 1]
    early = [k for k in every if k not in late]
    row_rings = [RingGather(xn2[m], peers, rows // 2) for m in micros]
    row_rings[0].step()
    groups = peers // GROUP

    class Experts:
        kept = [None] * 4

        def __init__(self, m, calls):
            self.m = m
            self.calls = calls
            self.per_call = local_experts // calls
            self.outs = [[None] * 3 for _ in range(groups)]
            self.found = {}

        def pick_grads(self):
            place = places[self.m]
            self.grads = pick_rows(first_at, place, cot_rings[self.m], every, False)
            return self.grads[0]

        def pick(self, distances):
            out = pick_rows(first_at, places[self.m], row_rings[self.m], distances, True)
            self.found.update(zip(distances, zip(out, out[len(distances) :])))
            self.rows = [self.found[k][0] for k in every if k in self.found]
            self.gate_slots = [self.found[k][1] for k in every if k in self.found]
            return out[0]

        def call(self, number, *earlier):
            for g in range(groups):
                span = slice(g * GROUP, (g + 1) * GROUP)
                here = self.rows[span]
                here[0] = after(here[0], *earlier) if earlier else here[0]
                done = expert_pass(
                    here,
                    self.grads[span],
                    self.gate_slots[span],
                    w_in,
                    w_out,
                    self.outs[g] + Experts.kept,
                    (self.m * groups + g, micro_count * groups),
                    number * self.per_call,
                    self.per_call,
                )
                self.outs[g], Experts.kept = list(done[:3]), list(done[3:])
            return done[2]

        def spread(self, spans, *earlier):
            place = places[self.m]
            place = after(place, *earlier) if earlier else place
            self.sums = None
            for g in range(groups):
                out = spread_rows(first_at, place, *self.outs[g], g, spans, self.sums)
                self.sums = out[0]
                if g == groups // 2:
                    far = out[1:]
            return far

    calls = 2
    first, second = Experts(0, calls), Experts(1, calls)
    ring, ring_next = row_rings
    while len(ring.from_left) < steps - 1:
        ring.step(*places, out_whole)
    ring.step(first.pick_grads())
    ring.step(first.pick(early), second.pick_grads())
    first.pick(late)
    ring_next.step(*ring.got)
    token = first.call(0)
    for number in range(1, calls):
        got = ring_next.got
        ring_next.step(token)
        token = first.call(number, *got)
    block = rows + EXTRA
    got = ring_next.got
    while len(ring_next.from_left) < steps:
        ring_next.step(token)
    far = first.spread([(0, block), (block, rows)], *got)
    got = ring_next.got
    while ring_next.far is None:
        ring_next.step()
    ring_first = RingScatter(lambda k: first.sums[k], far, peers)
    ring_first.step(*got)
    second.pick(early)
    second.pick(late)
    token = second.call(0)
    for number in range(1, calls):
        ring_first.step(token)
        token = second.call(number, *ring_first.sent)
    half = rows // 2
    spans = [(0, half), (half, block - half), (block, half), (block + half, half)]
    far = second.spread(spans)
    ring_grads = RingScatter(lambda k: second.sums[k, :block], far[:2], peers)
    ring_results = RingScatter(lambda k: second.sums[k, block:], far[2:], peers)
    ring_grads.step()
    got = ring_first.got
    while ring_first.at > 1:
        ring_first.step(second.sums)
    picked, grad_result, activated, grad_pre = Experts.kept
    place_at = jnp.stack([lax.rem(dp_at, 2), dp_at // 2])
    ring_grads.step()
    w_out_sum = weight_grads(
        after(activated, *ring_grads.sent, *ring_first.sent), grad_result, 0, local_experts
    )
    def backward(m, pieces, *earlier):
        own, left, right = pieces
        return block_call(
            backward_kernel,
            [
                (after(own, *earlier), (0,), block),
                (left, (), block),
                (right, (), block),
                (cotangent, (m,)),
                (hidden[m],),
                (tokens, (m,)),
                (query, (m,)),
                (keyval, (m,)),
                (seg_col, (m,)),
                (seg_row, (m,)),
                (gates, (m,)),
                (gains,),
                (cos,),
                (sin,),
                (first_whole,),
                (out_whole,),
            ],
            [
                jax.ShapeDtypeStruct((rows, width), jnp.bfloat16),
                jax.ShapeDtypeStruct((rows, proj_width + 128), jnp.bfloat16),
                jax.ShapeDtypeStruct((rows, width), jnp.bfloat16),
                jax.ShapeDtypeStruct((8, width), jnp.float32),
            ],
            "attention_backward",
            [pltpu.VMEM((rows, q_width), jnp.bfloat16)],
        )

    half = max(1, local_experts // 2)
    got = second_got = ring_grads.got
    ring_grads.step(w_out_sum)
    picked = after(picked, w_out_sum, *got, *ring_grads.sent)
    w_in_sum = weight_grads(picked, grad_pre, 0, half)
    while ring_grads.at > 1:
        ring_grads.step(w_in_sum)
    got = ring_first.got + ring_grads.got
    while ring_first.at > 0:
        ring_first.step(w_in_sum)

    def scatter(part, *earlier):
        return lax.psum_scatter(after(part, *earlier), "dp", scatter_dimension=1, tiled=True)

    grad_w_out = scatter(w_out_sum, *second_got)
    grad_w_in = [scatter(w_in_sum, *got)]
    picked = after(picked, w_in_sum, *got, *ring_first.sent)
    w_in_sum = weight_grads(picked, grad_pre, half, local_experts - half)
    grad_w_in.append(scatter(w_in_sum, *ring_first.got))
    ring_grads.step(w_in_sum)
    ring_results.step(w_in_sum)
    back_first = backward(
        0, (first.sums, ring_first.left, ring_first.right), *ring_grads.sent
    )
    ring_results.step(back_first[3])
    back_second = backward(
        1, (second.sums, ring_grads.left, ring_grads.right), back_first[3]
    )
    ring_results.step(back_second[3])
    grad_tokens, grad_proj, grad_attn, gain_sums = zip(back_first, back_second)
    mine, other = attention_grads(
        place_at, after(xn1, *ring_results.sent), mixed, grad_proj, grad_attn, gain_sums, dp_count
    )
    grads, grad_w_in, grad_w_out = reduce_packed(
        mine, other, my_spot, peers, dp_count, grad_w_in, grad_w_out, ring_results, (q_width, kv_width)
    )
    grad_query, grad_keyval, grad_small, grad_attn_out = grads
    wide = jnp.float32
    outputs = []
    for m, (own, ring, at) in enumerate(
        ((first.sums, ring_first, block), (second.sums, ring_results, 0))
    ):
        total = hidden[m] + own[0, block:].astype(wide)
        total = total + ring.left[at:].astype(wide) + ring.right[at:].astype(wide)
        outputs.append(total.astype(jnp.bfloat16))
    return (
        jnp.stack(outputs),
        jnp.stack(grad_tokens),
        grad_small[:, experts],
        grad_small[:, experts + 1],
        grad_query,
        grad_keyval,
        grad_attn_out,
        grad_small[:, :experts],
        grad_w_in,
        grad_w_out,
    )


def last_kernel(spot_ref, *refs):
    outs = refs[-4:]
    blocks = refs[:-4]
    peers = len(blocks) - 1
    piece = blocks[0].shape[0]
    for k, block_ref in enumerate(blocks):
        distance = k if k <= peers // 2 else k - 1
        spot = lax.rem(spot_ref[0] - distance + peers, peers)
        held = block_ref.shape[0]
        row = spot * piece + (held if k == peers // 2 + 1 else 0)
        at = 0
        for out_ref in outs:
            columns = out_ref.shape[1]
            out_ref[pl.ds(pl.multiple_of(row, 8), held), :] = block_ref[
                :, at : at + columns
            ].astype(jnp.float32)
            at += columns


def reduce_packed(mine, other, my_spot, peers, dp_count, grad_w_in, grad_w_out, ring_results, widths):
    lines, span, columns = mine.shape
    swap = [(d, d ^ 1) for d in range(dp_count)]
    other = after(other, *ring_results.got)
    ring_results.step()
    total = add_rows(mine, lax.ppermute(other, "dp", swap))
    total = after(total, *ring_results.sent)
    piece = span // peers
    total = total.reshape(lines, peers, piece, columns)

    def part(k):
        at = lax.rem(my_spot - k + peers, peers)
        return lax.dynamic_slice_in_dim(total, at, 1, axis=1).reshape(lines * piece, columns)

    half = lines * piece // 2
    farthest = part(peers // 2)
    ring = RingScatter(part, (farthest[:half], farthest[half:]), peers)
    ring.step()
    ring.step(*ring_results.got)
    while ring.at > 0:
        ring.step()
    own, left, right = [held.astype(jnp.float32) for held in (part(0), ring.left, ring.right)]
    mine = (own + left + right).astype(jnp.bfloat16).reshape(lines, piece, columns)
    mine = after(mine, *grad_w_in, grad_w_out, *ring_results.got)
    line = lax.axis_index("dp") // 2

    def for_line(at):
        return lax.dynamic_index_in_dim(mine, lax.rem(at, lines), 0, keepdims=False)

    share = for_line(line).astype(jnp.float32)
    for k in range(1, lines):
        pairs = [(d, (d + 2 * k) % dp_count) for d in range(dp_count)]
        share = share + lax.ppermute(for_line(line + k), "dp", pairs)
    gather = RingGather(share.astype(jnp.bfloat16), peers, piece // 2)
    gather.step()
    grad_w_out = grad_w_out.astype(jnp.float32)
    gather.step(grad_w_out)
    grad_w_in = jnp.concatenate([part.astype(jnp.float32) for part in grad_w_in], axis=0)
    gather.step(grad_w_in, *ring_results.got)
    while gather.far is None:
        gather.step()
    blocks = gather.from_left + list(gather.far) + gather.from_right[:0:-1]
    columns = (widths[0], widths[1], 128, columns - sum(widths) - 128)
    if piece % 16 == 0:
        grads = block_call(
            last_kernel,
            [(block,) for block in blocks],
            [jax.ShapeDtypeStruct((span, count), jnp.float32) for count in columns],
            "last_rows",
            prefetch=my_spot.astype(jnp.int32).reshape(1),
        )
    else:
        far = jnp.concatenate(gather.far, axis=0)
        by_distance = jnp.stack(gather.from_left + [far] + gather.from_right[:0:-1])
        distance = lax.rem(my_spot - jnp.arange(peers, dtype=jnp.int32) + peers, peers)
        by_spot = jnp.take(by_distance, distance, axis=0).reshape(span, -1).astype(jnp.float32)
        edges = [sum(columns[:i]) for i in range(5)]
        grads = [by_spot[:, edges[i] : edges[i + 1]] for i in range(4)]
    return grads, grad_w_in, grad_w_out


def solution(mesh):
    return jax.shard_map(
        per_device,
        mesh=mesh,
        in_specs=(
            P(None, ("dp", "expert"), None),
            P(None, ("dp", "expert")),
            P(None, ("dp", "expert"), None),
            P("dp"),
            P("dp"),
            P("dp", None),
            P("dp", None),
            P("dp", None),
            P("dp", None),
            P("expert", None, None),
            P("expert", None, None),
            P(None, ("dp", "expert"), None),
        ),
        out_specs=(
            P(None, ("dp", "expert"), None),
            P(None, ("dp", "expert"), None),
            P("dp"),
            P("dp"),
            P("dp", None),
            P("dp", None),
            P("dp", None),
            P("dp", None),
            P("expert", "dp", None),
            P("expert", "dp", None),
        ),
        check_vma=False,
    )
```

```python
import functools
import math

import jax
import jax.numpy as jnp
from jax import lax
from jax.experimental import pallas as pl
from jax.experimental.pallas import tpu as pltpu
from jax.sharding import PartitionSpec as P

QUERY_HEADS = 12
KEY_VALUE_HEADS = 2
HEAD_SIZE = 128
FF = 768
TOPK = 4
EXPERTS = 32
EXTRA = 16
PIECES = 3
GROUP = 8

eps_norm = 1e-06
rope_base = 1000000.0
mask_fill = -1e30
highest = lax.Precision.HIGHEST


def rms_scale(tensor):
    return lax.rsqrt(jnp.mean(tensor * tensor, axis=-1, keepdims=True) + eps_norm)


def rope_tables(sequence_length, head_width):
    positions = jnp.arange(sequence_length).astype(jnp.float32)
    frequency = rope_base ** (-(jnp.arange(head_width // 2).astype(jnp.float32) * 2.0) / head_width)
    angles = positions[:, None] * frequency[None, :]
    return (jnp.cos(angles), jnp.sin(angles))

SCORE_SCALE = 1.0 / math.sqrt(HEAD_SIZE)
GELU_SCALE = math.sqrt(2.0 / math.pi)
GELU_CUBE = 0.044715
SMALL_COST = pl.CostEstimate(flops=1_000_000, bytes_accessed=1_000_000, transcendentals=0)


def after(value, *earlier):
    return lax.optimization_barrier((value,) + earlier)[0]


def slot_hits(routes_all, first_expert, local_experts, capacity):
    rows = routes_all.shape[-1]
    names = first_expert + jnp.arange(local_experts, dtype=jnp.int32)
    named = routes_all[:, None].astype(jnp.int32) == names[None, :, None, None]
    member = jnp.any(named, axis=2)
    lower = (jnp.arange(rows)[:, None] < jnp.arange(rows)[None, :]).astype(jnp.bfloat16)
    rank = dot32(member.astype(jnp.bfloat16).reshape(-1, rows), lower).reshape(member.shape)
    slots = jnp.arange(capacity, dtype=jnp.float32)
    return member[:, :, None, :] & (rank[:, :, None, :] == slots[None, None, :, None])


def pack_pieces(values, out_ref, first_row):
    rows = values.shape[1]
    rest = values
    for piece in range(PIECES):
        part = rest.astype(jnp.bfloat16)
        rest = rest - part.astype(jnp.float32)
        for half in range(EXPERTS // EXTRA):
            at = (piece * (EXPERTS // EXTRA) + half) * rows
            out_ref[first_row : first_row + EXTRA, at : at + rows] = part[
                half * EXTRA : (half + 1) * EXTRA
            ]


def dot32(left, right):
    return jnp.dot(left, right, preferred_element_type=jnp.float32)


def dot_nt(left, right):
    return lax.dot_general(
        left, right, (((1,), (1,)), ((), ())), preferred_element_type=jnp.float32
    )


def dot_tn(left, right):
    return lax.dot_general(
        left, right, (((0,), (0,)), ((), ())), preferred_element_type=jnp.float32
    )


def mask_of(seg_col, seg_row):
    rows = seg_col.shape[0]
    query_at = lax.broadcasted_iota(jnp.int32, (rows, rows), 0)
    key_at = lax.broadcasted_iota(jnp.int32, (rows, rows), 1)
    return (seg_col == seg_row) & (query_at >= key_at)


def softmax_rows(query, key, allowed):
    scores = jnp.where(allowed, dot_nt(query, key) * SCORE_SCALE, mask_fill)
    weight = jnp.exp(scores - jnp.max(scores, axis=-1, keepdims=True))
    return weight / jnp.sum(weight, axis=-1, keepdims=True)


def from_blocks(starts_ref, rows_ref, blocks):
    total = None
    for at, block_ref in enumerate(blocks):
        span = block_ref.shape[0]
        columns = pl.ds(pl.multiple_of(starts_ref[at], 128), span)
        part = dot32(rows_ref[:, columns], block_ref[...])
        total = part if total is None else total + part
    return total


def attention_kernel(
    starts_ref,
    tok_ref,
    seg_col_ref,
    seg_row_ref,
    routes_ref,
    cos_ref,
    sin_ref,
    *refs,
):
    weight_refs = refs[:-7]
    xn1_ref, query_ref, keyval_ref, mixed_ref, gates_ref, gates_pack_ref, gains_ref = refs[-7:]

    @pl.when(pl.program_id(0) == 0)
    def _():
        for at, block_ref in enumerate(weight_refs):
            span, columns = block_ref.shape
            pad = block_ref[:, columns - 128 :].astype(jnp.float32).T
            place = pl.ds(pl.multiple_of(starts_ref[at], 128), span)
            gains_ref[:, place] = pad[2 * EXPERTS : 2 * EXPERTS + 8]

    tok = tok_ref[...].astype(jnp.float32)
    xn1_ref[...] = (tok * rms_scale(tok) * gains_ref[0:1, :]).astype(jnp.bfloat16)
    proj = from_blocks(starts_ref, xn1_ref, weight_refs)
    cos, sin = cos_ref[...], sin_ref[...]

    def rotate(part):
        return (part * cos + pltpu.roll(part, HEAD_SIZE // 2, 1) * sin).astype(jnp.bfloat16)

    q_width = QUERY_HEADS * HEAD_SIZE
    k_width = KEY_VALUE_HEADS * HEAD_SIZE
    for head in range(QUERY_HEADS):
        span = slice(head * HEAD_SIZE, (head + 1) * HEAD_SIZE)
        query_ref[:, span] = rotate(proj[:, span])
    for head in range(KEY_VALUE_HEADS):
        span = slice(head * HEAD_SIZE, (head + 1) * HEAD_SIZE)
        keyval_ref[:, span] = rotate(proj[:, q_width:][:, span])
    keyval_ref[:, k_width:] = proj[:, q_width + k_width : q_width + 2 * k_width].astype(
        jnp.bfloat16
    )
    logits = proj[:, q_width + 2 * k_width :]
    columns = lax.broadcasted_iota(jnp.int32, logits.shape, 1)
    named = [columns == routes_ref[:, j : j + 1] for j in range(TOPK)]
    chosen = [jnp.sum(jnp.where(hit, logits, 0.0), axis=-1, keepdims=True) for hit in named]
    top = functools.reduce(jnp.maximum, chosen)
    weight = [jnp.exp(part - top) for part in chosen]
    total = functools.reduce(jnp.add, weight)
    gates = jnp.full(logits.shape, -1.0, jnp.float32)
    for hit, part in zip(named, weight):
        gates = jnp.where(hit, part / total, gates)
    gates_ref[...] = gates
    pack_pieces(gates.T[:EXPERTS], gates_pack_ref, 0)
    allowed = mask_of(seg_col_ref[...], seg_row_ref[...])
    for head in range(QUERY_HEADS):
        span = slice(head * HEAD_SIZE, (head + 1) * HEAD_SIZE)
        group = head // (QUERY_HEADS // KEY_VALUE_HEADS)
        key = keyval_ref[:, group * HEAD_SIZE : (group + 1) * HEAD_SIZE]
        value = keyval_ref[:, k_width + group * HEAD_SIZE : k_width + (group + 1) * HEAD_SIZE]
        probs = softmax_rows(query_ref[:, span], key, allowed)
        mixed_ref[:, span] = dot32(probs.astype(jnp.bfloat16), value).astype(jnp.bfloat16)


def hidden_kernel(starts_ref, mixed_ref, tok_ref, gains_ref, pack_ref, *refs):
    weight_refs = refs[:-2]
    hidden_ref, xn2_ref = refs[-2:]
    rows = tok_ref.shape[0]
    hidden = tok_ref[...].astype(jnp.float32) + from_blocks(
        starts_ref, mixed_ref, weight_refs
    )
    hidden_ref[...] = hidden
    xn2_ref[:rows, :] = (hidden * rms_scale(hidden) * gains_ref[1:2, :]).astype(jnp.bfloat16)
    xn2_ref[rows:, :] = pack_ref[...]


def backward_kernel(
    own_ref,
    left_ref,
    right_ref,
    cot_ref,
    hidden_ref,
    tok_ref,
    query_ref,
    keyval_ref,
    seg_col_ref,
    seg_row_ref,
    gates_ref,
    gains_ref,
    cos_ref,
    sin_ref,
    *refs,
):
    weight_ref, out_weight_ref = refs[:2]
    grad_tok_ref, grad_proj_ref, grad_attn_ref, gain_sum_ref, mixed_grad_ref = refs[2:]
    width = tok_ref.shape[1]
    q_width = QUERY_HEADS * HEAD_SIZE
    k_width = KEY_VALUE_HEADS * HEAD_SIZE
    proj_width = q_width + 2 * k_width
    rows = tok_ref.shape[0]
    sums = [ref[...].astype(jnp.float32) for ref in (own_ref, left_ref, right_ref)]
    sums = sums[0] + sums[1] + sums[2]
    grad_xn2, pack = sums[:rows], sums[rows:]
    halves = EXPERTS // EXTRA
    lines = [
        sum(
            pack[:, (piece * halves + half) * rows : (piece * halves + half + 1) * rows]
            for piece in range(PIECES)
        )
        for half in range(halves)
    ]
    lines.append(jnp.zeros((128 - EXPERTS, rows), jnp.float32))
    grad_gates = jnp.concatenate(lines, axis=0).T
    hidden = hidden_ref[...]
    scale = rms_scale(hidden)
    unit = hidden * scale
    gain_sum_ref[...] = jnp.zeros(gain_sum_ref.shape, jnp.float32)
    gain_sum_ref[1:2, :] = jnp.sum(grad_xn2 * unit, axis=0, keepdims=True)
    grad_unit = grad_xn2 * gains_ref[1:2, :]
    grad_hidden = cot_ref[...].astype(jnp.float32) + scale * (
        grad_unit - unit * jnp.mean(grad_unit * unit, axis=-1, keepdims=True)
    )
    grad_attn_ref[...] = grad_hidden.astype(jnp.bfloat16)
    mixed_grad_ref[...] = dot_nt(grad_attn_ref[...], out_weight_ref[...]).astype(jnp.bfloat16)
    cos, sin = cos_ref[...], sin_ref[...]

    def unrotate(part):
        return (part * cos - pltpu.roll(part, HEAD_SIZE // 2, 1) * sin).astype(jnp.bfloat16)

    allowed = mask_of(seg_col_ref[...], seg_row_ref[...])
    per_group = QUERY_HEADS // KEY_VALUE_HEADS
    for group in range(KEY_VALUE_HEADS):
        key_span = slice(group * HEAD_SIZE, (group + 1) * HEAD_SIZE)
        value_span = slice(k_width + group * HEAD_SIZE, k_width + (group + 1) * HEAD_SIZE)
        key, value = keyval_ref[:, key_span], keyval_ref[:, value_span]
        grad_key = jnp.zeros(key.shape, jnp.float32)
        grad_value = jnp.zeros(key.shape, jnp.float32)
        for head in range(group * per_group, (group + 1) * per_group):
            span = slice(head * HEAD_SIZE, (head + 1) * HEAD_SIZE)
            query, grad_mixed = query_ref[:, span], mixed_grad_ref[:, span]
            probs = softmax_rows(query, key, allowed)
            grad_value += dot_tn(probs.astype(jnp.bfloat16), grad_mixed)
            grad_probs = dot_nt(grad_mixed, value)
            mean = jnp.sum(probs * grad_probs, axis=-1, keepdims=True)
            grad_scores = (probs * (grad_probs - mean)).astype(jnp.bfloat16)
            grad_proj_ref[:, span] = unrotate(dot32(grad_scores, key) * SCORE_SCALE)
            grad_key += dot_tn(grad_scores, query)
        grad_proj_ref[:, q_width + group * HEAD_SIZE : q_width + (group + 1) * HEAD_SIZE] = (
            unrotate(grad_key * SCORE_SCALE)
        )
        first = q_width + k_width + group * HEAD_SIZE
        grad_proj_ref[:, first : first + HEAD_SIZE] = grad_value.astype(jnp.bfloat16)
    gates = jnp.maximum(gates_ref[...], 0.0)
    grad_logits = gates * (grad_gates - jnp.sum(gates * grad_gates, axis=-1, keepdims=True))
    high = grad_logits.astype(jnp.bfloat16).astype(jnp.float32)
    low = pltpu.roll(grad_logits - high, EXPERTS, 1)
    grad_proj_ref[:, proj_width:] = (high + low).astype(jnp.bfloat16)
    grad_xn1 = dot_nt(grad_proj_ref[...], weight_ref[...])
    tok = tok_ref[...].astype(jnp.float32)
    scale = rms_scale(tok)
    unit = tok * scale
    gain_sum_ref[0:1, :] = jnp.sum(grad_xn1 * unit, axis=0, keepdims=True)
    grad_unit = grad_xn1 * gains_ref[0:1, :]
    grad_tok_ref[...] = (
        grad_hidden
        + scale * (grad_unit - unit * jnp.mean(grad_unit * unit, axis=-1, keepdims=True))
    ).astype(jnp.bfloat16)


def ring_order(peers):
    minor = peers // 4
    walk = []
    for col in range(minor):
        line = range(4) if col % 2 == 0 else range(3, -1, -1)
        walk += [row * minor + col for row in line]
    return walk


def ring_step(part, shift, peers):
    order = ring_order(peers)
    pairs = [(order[i], order[(i + shift) % peers]) for i in range(peers)]
    return lax.ppermute(part, "expert", pairs)


class RingGather:
    def __init__(self, part, peers, half):
        self.peers, self.half = peers, half
        self.from_left, self.from_right = [part], [part]
        self.far = None
        self.got = ()

    def step(self, *earlier):
        left, right = self.from_left[-1], self.from_right[-1]
        last = len(self.from_left) == self.peers // 2
        if last:
            left, right = left[: self.half], right[self.half :]
        left, right = self.sent = lax.optimization_barrier((left, right) + earlier)[:2]
        left, right = ring_step(left, 1, self.peers), ring_step(right, -1, self.peers)
        self.got = (left, right)
        if last:
            self.far = (left, right)
        else:
            self.from_left.append(left)
            self.from_right.append(right)
        return self

    def rows(self, k, first, count):
        if k < len(self.from_left):
            return self.from_left[k], first
        if k > self.peers // 2:
            return self.from_right[self.peers - k], first
        if first < self.half:
            return self.far[0], first
        return self.far[1], first - self.half

    def stack_rows(self, first, count):
        found = [self.rows(k, first, count) for k in range(self.peers)]
        return jnp.stack([array[at : at + count] for array, at in found])


class RingScatter:
    def __init__(self, part, far, peers):
        self.part, self.far, self.peers = part, far, peers
        self.at = peers // 2
        self.half = far[0].shape[0]

    def step(self, *earlier):
        peers, k, half = self.peers, self.at, self.half
        if k == peers // 2:
            left, right = lax.optimization_barrier(tuple(self.far) + earlier)[:2]
        else:
            left, right = self.part(k), self.part(peers - k)
            if earlier:
                self.left, self.right = lax.optimization_barrier(
                    (self.left, self.right) + earlier
                )[:2]
            if k == peers // 2 - 1:
                kept = left[half:].astype(jnp.bfloat16), right[:half].astype(jnp.bfloat16)
                left = jnp.concatenate([add_rows(left[:half], self.left), kept[0]], axis=0)
                right = jnp.concatenate([kept[1], add_rows(right[half:], self.right)], axis=0)
            else:
                left, right = add_rows(left, self.left), add_rows(right, self.right)
        left, right = self.sent = lax.optimization_barrier((left, right))
        self.left = ring_step(left, -1, peers)
        self.right = ring_step(right, 1, peers)
        self.got = (self.left, self.right)
        self.at = k - 1
        return self


def add_rows(left, right):
    return (left.astype(jnp.float32) + right.astype(jnp.float32)).astype(jnp.bfloat16)


def expert_kernel(sources, *refs):
    rows_refs = refs[:sources]
    grad_refs = refs[sources : 2 * sources]
    gate_refs = refs[2 * sources : 3 * sources]
    w_in_ref, w_out_ref = refs[3 * sources : 3 * sources + 2]
    (
        back_rows_ref,
        back_grads_ref,
        grad_gate_ref,
        picked_ref,
        grad_result_ref,
        activated_ref,
        grad_pre_ref,
    ) = refs[-7:]
    capacity, width = rows_refs[0].shape
    for k in range(sources):
        picked_ref[pl.ds(k * capacity, capacity), :] = rows_refs[k][...]
    pre_act = dot32(picked_ref[...], w_in_ref[...])
    gate_part = pre_act[:, :FF]
    up_part = pre_act[:, FF:]
    square = gate_part * gate_part
    bend = jnp.tanh(GELU_SCALE * gate_part * (1.0 + GELU_CUBE * square))
    lift = 0.5 * (1.0 + bend)
    gelu_val = gate_part * lift
    slope = lift + 0.5 * gate_part * (1.0 - bend * bend) * (
        GELU_SCALE * (1.0 + 3.0 * GELU_CUBE * square)
    )
    activated_ref[...] = (gelu_val * up_part).astype(jnp.bfloat16)
    result = dot32(activated_ref[...], w_out_ref[...])
    for k in range(sources):
        gates = gate_refs[k][...]
        span = slice(k * capacity, (k + 1) * capacity)
        grad_rows = grad_refs[k][...].astype(jnp.float32)
        grad_gate_ref[span, :] = jnp.sum(result[span] * grad_rows, axis=-1, keepdims=True)
        back_rows_ref[k] = (result[span] * gates).astype(jnp.bfloat16)
        grad_result_ref[span, :] = (grad_rows * gates).astype(jnp.bfloat16)
    grad_act = lax.dot_general(
        grad_result_ref[...],
        w_out_ref[...],
        (((1,), (1,)), ((), ())),
        preferred_element_type=jnp.float32,
    )
    grad_pre_ref[:, :FF] = (grad_act * up_part * slope).astype(jnp.bfloat16)
    grad_pre_ref[:, FF:] = (grad_act * gelu_val).astype(jnp.bfloat16)
    grad_in = lax.dot_general(
        grad_pre_ref[...],
        w_in_ref[...],
        (((1,), (1,)), ((), ())),
        preferred_element_type=jnp.float32,
    ).astype(jnp.bfloat16)
    for k in range(sources):
        back_grads_ref[k] = grad_in[k * capacity : (k + 1) * capacity]


def expert_pass(rows_list, grads_list, gate_slots, w_in, w_out, held_outs, position, first, count):
    sources = len(rows_list)
    local_experts, width, _ = w_in.shape
    slots = rows_list[0].shape[0]
    capacity = slots // local_experts
    held = sources * capacity
    block_spec = pl.BlockSpec((capacity, width), lambda e: (e + first, 0))
    back_spec = pl.BlockSpec((sources, capacity, width), lambda e: (0, e + first, 0))
    column_spec = pl.BlockSpec((None, held, 1), lambda e: (e + first, 0, 0))

    def kept_spec(columns):
        return pl.BlockSpec((None, held, columns), lambda e: (e + first, position[0], 0))

    def kept_shape(columns):
        return jax.ShapeDtypeStruct((local_experts, position[1] * held, columns), jnp.bfloat16)

    kept_widths = (width, width, FF, 2 * FF)
    first_held = 3 * sources + 2
    given = [(i, part) for i, part in enumerate(held_outs) if part is not None]
    return pl.pallas_call(
        functools.partial(expert_kernel, sources),
        grid=(count,),
        in_specs=[block_spec] * (2 * sources)
        + [pl.BlockSpec((capacity, 1), lambda e: (e + first, 0))] * sources
        + [
            pl.BlockSpec((None, width, 2 * FF), lambda e: (e + first, 0, 0)),
            pl.BlockSpec((None, FF, width), lambda e: (e + first, 0, 0)),
        ]
        + [pl.BlockSpec(memory_space=pl.ANY)] * len(given),
        out_specs=[back_spec, back_spec, column_spec] + [kept_spec(c) for c in kept_widths],
        out_shape=[
            jax.ShapeDtypeStruct((sources, slots, width), jnp.bfloat16),
            jax.ShapeDtypeStruct((sources, slots, width), jnp.bfloat16),
            jax.ShapeDtypeStruct((local_experts, held, 1), jnp.float32),
        ]
        + [kept_shape(c) for c in kept_widths],
        input_output_aliases={first_held + at: i for at, (i, _) in enumerate(given)},
        compiler_params=pltpu.CompilerParams(vmem_limit_bytes=60 * 1024 * 1024),
        cost_estimate=SMALL_COST,
        name="expert_pass",
    )(*rows_list, *grads_list, *gate_slots, w_in, w_out, *[part for _, part in given])


def block_call(kernel, operands, out_shape, name, scratch=(), prefetch=None):
    def spec(array, lead=(), rows=None):
        rest = array.shape[len(lead) :]
        at = lead + (0,) * len(rest)
        if rows is not None:
            count, block = rows if isinstance(rows, tuple) else (rows, 0)
            rest = (count,) + rest[1:]
            at = lead + (block,) + (0,) * (len(rest) - 1)
        return pl.BlockSpec((None,) * len(lead) + rest, lambda *_: at)

    scalars = [] if prefetch is None else [prefetch]
    return pl.pallas_call(
        kernel,
        grid_spec=pltpu.PrefetchScalarGridSpec(
            num_scalar_prefetch=len(scalars),
            grid=(1,),
            in_specs=[spec(*operand) for operand in operands],
            out_specs=[spec(shape) for shape in out_shape],
            scratch_shapes=list(scratch),
        ),
        out_shape=out_shape,
        compiler_params=pltpu.CompilerParams(vmem_limit_bytes=60 * 1024 * 1024),
        cost_estimate=SMALL_COST,
        name=name,
    )(*scalars, *[operand[0] for operand in operands])


def pick_kernel(shares, gated, first_ref, place_ref, *refs):
    at = 0
    outs = refs[sum(count for _, count in shares) + (len(shares) if gated else 0) :]
    for number, (k, count) in enumerate(shares):
        total, row = None, 0
        for block_ref in refs[at : at + count]:
            held = block_ref.shape[0]
            part = dot32(place_ref[k, :, row : row + held], block_ref[...])
            total = part if total is None else total + part
            row += held
        outs[number][...] = total.astype(jnp.bfloat16)
        at += count
        if gated:
            slot_gates(first_ref[0], place_ref[k], refs[at], outs[len(shares) + number])
            at += 1


def slot_gates(first_expert, place, pack_ref, out_ref):
    slots, rows = place.shape
    pack = pack_ref[...].astype(jnp.float32)
    halves = EXPERTS // EXTRA
    line = lax.broadcasted_iota(jnp.int32, (EXTRA, rows), 0)
    local_experts = slots * 4 // rows
    capacity = rows // 4
    for e in range(local_experts):
        gate = jnp.zeros((1, rows), jnp.float32)
        for half in range(halves):
            hit = line + half * EXTRA == first_expert + e
            for piece in range(PIECES):
                at = (piece * halves + half) * rows
                gate += jnp.sum(
                    jnp.where(hit, pack[:, at : at + rows], 0.0), axis=0, keepdims=True
                )
        span = slice(e * capacity, (e + 1) * capacity)
        out_ref[span, :] = jnp.sum(
            place[span].astype(jnp.float32) * gate, axis=-1, keepdims=True
        )


def pick_rows(first_expert, place, ring, distances, gated):
    _, slots, rows = place.shape
    half = rows // 2
    operands, shares = [], []
    for k in distances:
        spans = [(0, rows)]
        if k == ring.peers // 2 and ring.half < rows:
            spans = [(0, half), (half, half)]
        shares.append((k, len(spans)))
        for at, count in spans + ([(rows, EXTRA)] if gated else []):
            array, at = ring.rows(k, at, count)
            operands.append((array, (), (count, at // count)))
    width = operands[0][0].shape[-1]
    out_shape = [jax.ShapeDtypeStruct((slots, width), jnp.bfloat16) for _ in distances]
    if gated:
        out_shape += [jax.ShapeDtypeStruct((slots, 1), jnp.float32) for _ in distances]
    return block_call(
        functools.partial(pick_kernel, shares, gated),
        [(place,)] + operands,
        out_shape,
        "pick_rows",
        prefetch=first_expert,
    )


def spread_kernel(middle, spans, held, first_ref, place_ref, rows_ref, grads_ref, gate_ref, *refs):
    out_ref, *far_refs = refs[held:]
    place = place_ref[...]
    rows = place.shape[1]
    out_ref[:rows, :] = dot_tn(place, grads_ref[...]).astype(jnp.bfloat16)
    out_ref[rows + EXTRA :, :] = dot_tn(place, rows_ref[...]).astype(jnp.bfloat16)
    capacity = gate_ref.shape[1]
    expert = lax.broadcasted_iota(jnp.int32, (EXPERTS, rows), 0) - first_ref[0]
    gates = jnp.zeros((EXPERTS, rows), jnp.float32)
    for e in range(gate_ref.shape[0]):
        hit = place[e * capacity : (e + 1) * capacity].astype(jnp.float32)
        line = jnp.sum(hit * gate_ref[e], axis=0, keepdims=True)
        gates = jnp.where(expert == e, line, gates)
    pack_pieces(gates, out_ref, rows)

    @pl.when(pl.program_id(0) == middle)
    def _():
        for far_ref, (row, count) in zip(far_refs, spans):
            far_ref[...] = out_ref[row : row + count, :]


def spread_rows(first_expert, place, rows_back, grads_back, gate_slots, group, spans, held):
    sources, slots, rows = place.shape
    width = rows_back.shape[-1]
    local_experts = gate_slots.shape[0]
    base = group * GROUP
    by_source = pl.BlockSpec((None, slots, width), lambda k, f: (k, 0, 0))
    held = [] if held is None else [held]
    out_shape = [jax.ShapeDtypeStruct((sources, 2 * rows + EXTRA, width), jnp.bfloat16)]
    out_shape += [jax.ShapeDtypeStruct((count, width), jnp.bfloat16) for _, count in spans]
    out_specs = [pl.BlockSpec((None, 2 * rows + EXTRA, width), lambda k, f: (base + k, 0, 0))]
    out_specs += [pl.BlockSpec((count, width), lambda k, f: (0, 0)) for _, count in spans]
    return pl.pallas_call(
        functools.partial(spread_kernel, sources // 2 - base, spans, len(held)),
        grid_spec=pltpu.PrefetchScalarGridSpec(
            num_scalar_prefetch=1,
            grid=(GROUP,),
            in_specs=[
                pl.BlockSpec((None, slots, rows), lambda k, f: (base + k, 0, 0)),
                by_source,
                by_source,
                pl.BlockSpec((local_experts, slots // local_experts, 1), lambda k, f: (0, k, 0)),
            ]
            + [pl.BlockSpec(memory_space=pl.ANY)] * len(held),
            out_specs=out_specs,
        ),
        out_shape=out_shape,
        input_output_aliases={5 + i: i for i in range(len(held))},
        compiler_params=pltpu.CompilerParams(vmem_limit_bytes=60 * 1024 * 1024),
        cost_estimate=SMALL_COST,
        name="spread_rows",
    )(first_expert, place, rows_back, grads_back, gate_slots, *held)


def weight_grad_kernel(left_ref, right_ref, out_ref):
    out_ref[...] = dot_tn(left_ref[...], right_ref[...]).astype(jnp.bfloat16)


def weight_grads(left, right, first, count):
    _, held, height = left.shape
    columns = right.shape[-1]
    tile = min(height, 768)
    return pl.pallas_call(
        weight_grad_kernel,
        grid=(count, height // tile),
        in_specs=[
            pl.BlockSpec((None, held, tile), lambda e, i: (e + first, 0, i)),
            pl.BlockSpec((None, held, columns), lambda e, i: (e + first, 0, 0)),
        ],
        out_specs=pl.BlockSpec((None, tile, columns), lambda e, i: (e, i, 0)),
        out_shape=jax.ShapeDtypeStruct((count, height, columns), jnp.bfloat16),
        compiler_params=pltpu.CompilerParams(vmem_limit_bytes=60 * 1024 * 1024),
        cost_estimate=SMALL_COST,
        name="weight_grads",
    )(left, right)


def attention_forward(starts, tokens, seg_col, seg_row, routes, cos, sin, weights):
    count, rows, width = tokens.shape

    def by_micro(*shape):
        return pl.BlockSpec((None,) + shape, lambda m, s: (m,) + (0,) * len(shape))

    def shared(part):
        return pl.BlockSpec(part.shape, lambda m, s: (0, 0))

    kv_width = 2 * KEY_VALUE_HEADS * HEAD_SIZE
    shapes = [
        ((rows, width), jnp.bfloat16),
        ((rows, QUERY_HEADS * HEAD_SIZE), jnp.bfloat16),
        ((rows, kv_width), jnp.bfloat16),
        ((rows, QUERY_HEADS * HEAD_SIZE), jnp.bfloat16),
        ((rows, 128), jnp.float32),
        ((EXTRA, PIECES * EXPERTS // EXTRA * rows), jnp.bfloat16),
    ]
    return pl.pallas_call(
        attention_kernel,
        grid_spec=pltpu.PrefetchScalarGridSpec(
            num_scalar_prefetch=1,
            grid=(count,),
            in_specs=[
                by_micro(rows, width),
                by_micro(rows, 1),
                by_micro(1, rows),
                by_micro(rows, TOPK),
                shared(cos),
                shared(sin),
            ]
            + [shared(part) for part in weights],
            out_specs=[by_micro(*shape) for shape, _ in shapes]
            + [pl.BlockSpec((8, width), lambda m, s: (0, 0))],
        ),
        out_shape=[jax.ShapeDtypeStruct((count,) + shape, kind) for shape, kind in shapes]
        + [jax.ShapeDtypeStruct((8, width), jnp.float32)],
        compiler_params=pltpu.CompilerParams(vmem_limit_bytes=60 * 1024 * 1024),
        cost_estimate=SMALL_COST,
        name="attention_forward",
    )(starts, tokens, seg_col, seg_row, routes, cos, sin, *weights)


def join_kernel(starts_ref, *refs):
    for at, block_ref in enumerate(refs[:-1]):

        @pl.when(pl.program_id(0) == at)
        def _():
            refs[-1][...] = block_ref[...]


def join_blocks(starts, blocks):
    if len(blocks) == 1:
        return blocks[0]
    span, columns = blocks[0].shape
    return pl.pallas_call(
        join_kernel,
        grid_spec=pltpu.PrefetchScalarGridSpec(
            num_scalar_prefetch=1,
            grid=(len(blocks),),
            in_specs=[pl.BlockSpec((span, columns), lambda i, s: (0, 0)) for _ in blocks],
            out_specs=pl.BlockSpec((span, columns), lambda i, s: (s[i] // span, 0)),
        ),
        out_shape=jax.ShapeDtypeStruct((len(blocks) * span, columns), blocks[0].dtype),
        compiler_params=pltpu.CompilerParams(vmem_limit_bytes=60 * 1024 * 1024),
        cost_estimate=SMALL_COST,
        name="join_blocks",
    )(starts, *blocks)


def attention_grad_kernel(core_ref, xn1, mixed, *refs):
    count = xn1.shape[0]
    proj, attn, sums = [refs[i * count : (i + 1) * count] for i in range(3)]
    mine_ref, other_ref = refs[-2:]
    split = proj[0].shape[1]
    span = mine_ref.shape[0]
    grad = sum(dot_tn(xn1[m], proj[m][...]) for m in range(count))
    router = grad[:, split - 128 :]
    lane = lax.broadcasted_iota(jnp.int32, router.shape, 1)
    router = router + pltpu.roll(router, 128 - EXPERTS, 1)
    gain = sum(part[...] for part in sums)
    lines = [jnp.zeros((EXPERTS, gain.shape[1]), jnp.float32), gain]
    lines.append(jnp.zeros((128 - EXPERTS - gain.shape[0], gain.shape[1]), jnp.float32))
    router = jnp.where(lane < EXPERTS, router, jnp.concatenate(lines, axis=0).T)
    first = core_ref[0] == 0

    def put(columns, value):
        value = value.astype(jnp.bfloat16)
        low, high = value[:span], value[span:]
        mine_ref[:, columns] = jnp.where(first, low, high)
        other_ref[:, columns] = jnp.where(first, high, low)

    put(slice(0, split - 128), grad[:, : split - 128])
    put(slice(split - 128, split), router)
    put(slice(split, None), sum(dot_tn(mixed[m], attn[m][...]) for m in range(count)))


def attention_grads(core, xn1, mixed, proj, attn, gain_sums, parts):
    count, rows, width = xn1.shape
    span = width // parts
    lines = parts // 2
    columns = proj[0].shape[1] + attn[0].shape[1]
    by_line = pl.BlockSpec((count, rows, 2 * span), lambda i, c: (0, 0, i))

    def shared(part):
        return pl.BlockSpec(part.shape, lambda i, c: (0, 0))

    out_spec = pl.BlockSpec((None, span, columns), lambda i, c: (i, 0, 0))
    out_shape = jax.ShapeDtypeStruct((lines, span, columns), jnp.bfloat16)
    return pl.pallas_call(
        attention_grad_kernel,
        grid_spec=pltpu.PrefetchScalarGridSpec(
            num_scalar_prefetch=1,
            grid=(lines,),
            in_specs=[by_line, by_line]
            + [shared(p) for p in proj]
            + [shared(p) for p in attn]
            + [pl.BlockSpec((p.shape[0], 2 * span), lambda i, c: (0, i)) for p in gain_sums],
            out_specs=[out_spec, out_spec],
        ),
        out_shape=[out_shape, out_shape],
        compiler_params=pltpu.CompilerParams(vmem_limit_bytes=60 * 1024 * 1024),
        cost_estimate=SMALL_COST,
        name="attention_grads",
    )(core, xn1, mixed, *proj, *attn, *gain_sums)


def gather_blocks(part, dp_at, dp_count):
    span = part.shape[0]
    if span % 128 or dp_count != 4:
        whole = lax.all_gather(part, "dp", axis=0, tiled=True)
        return lambda *earlier: [whole], jnp.zeros((1,), jnp.int32)
    line = [(d, (d + 2) % 4) for d in range(4)]
    core = [(d, d ^ 1) for d in range(4)]
    across = lax.ppermute(part, "dp", line)
    beside = lax.ppermute(part, "dp", core)
    far = lax.rem(dp_at + 2, 4)
    owners = jnp.stack([dp_at, dp_at + 1 - 2 * lax.rem(dp_at, 2), far, far + 1 - 2 * lax.rem(far, 2)])

    def blocks(*earlier):
        moved = after(across, *earlier) if earlier else across
        return [part, beside, moved, lax.ppermute(moved, "dp", core)]

    return blocks, owners * span


def per_device(
    tokens,
    segments,
    routes,
    norm_one,
    norm_two,
    w_query,
    key_value_weight,
    w_out_attn,
    w_router,
    w_in,
    w_out,
    cotangent,
):
    micro_count, rows, width = tokens.shape
    micros = range(micro_count)
    peers = lax.axis_size("expert")
    dp_count = lax.axis_size("dp")
    local_experts = w_in.shape[0]
    experts = local_experts * peers
    capacity = rows // 4
    first_expert = lax.axis_index("expert") * local_experts
    q_width = w_query.shape[1]
    kv_width = key_value_weight.shape[1]
    proj_width = q_width + kv_width
    cosine_table, sine_values = rope_tables(rows, HEAD_SIZE)
    cos = jnp.concatenate([cosine_table, cosine_table], axis=1)
    sin = jnp.concatenate([-sine_values, sine_values], axis=1)
    order = ring_order(peers)
    spot = [order.index(dev) for dev in range(peers)]
    my_spot = jnp.array(spot, jnp.int32)[lax.axis_index("expert")]

    router_pad = jnp.zeros((w_router.shape[0], 126 - 2 * experts), jnp.bfloat16)
    first_weight = jnp.concatenate(
        [
            w_query,
            key_value_weight,
            w_router,
            w_router,
            norm_one[:, None],
            norm_two[:, None],
            router_pad,
        ],
        axis=1,
    )
    dp_at = lax.axis_index("dp").astype(jnp.int32)
    first_weights, starts = gather_blocks(first_weight, dp_at, dp_count)
    out_weights, _ = gather_blocks(w_out_attn, dp_at, dp_count)

    routes_rows = jnp.swapaxes(routes, 1, 2).reshape(-1, rows).astype(jnp.bfloat16)
    routes_rows = jnp.pad(
        routes_rows, ((0, EXTRA - routes_rows.shape[0]), (0, width - rows))
    )
    cot_rings = [
        RingGather(jnp.concatenate([cotangent[0], routes_rows], axis=0), peers, rows // 2),
        RingGather(cotangent[1], peers, rows // 2),
    ]
    steps = peers // 2
    for at in range(steps - 2):
        for ring in cot_rings:
            ring.step()
        if at == 0:
            first_weights = first_weights(*cot_rings[0].got, *cot_rings[1].got)
    first_at = first_expert.astype(jnp.int32).reshape(1)
    seg_col, seg_row = segments[:, :, None], segments[:, None, :]
    xn1, query, keyval, mixed, gates, gates_pack, gains = attention_forward(
        starts, tokens, seg_col, seg_row, routes, cos, sin, first_weights
    )
    for ring in cot_rings:
        ring.step(mixed)
    out_weights = out_weights(mixed)
    hidden, xn2 = [], []
    for m in micros:
        out = block_call(
            hidden_kernel,
            [(after(mixed, *xn2), (m,)), (tokens, (m,)), (gains,), (gates_pack, (m,))]
            + [(part,) for part in out_weights],
            [
                jax.ShapeDtypeStruct((rows, width), jnp.float32),
                jax.ShapeDtypeStruct((rows + EXTRA, width), jnp.bfloat16),
            ],
            "hidden_rows",
            prefetch=starts,
        )
        hidden.append(out[0])
        xn2.append(out[1])
    for ring in cot_rings:
        ring.step()
    got = cot_rings[0].got + cot_rings[1].got
    first_whole = join_blocks(starts, [after(first_weights[0], *got)] + first_weights[1:])
    out_whole = join_blocks(starts, [after(out_weights[0], first_whole)] + out_weights[1:])
    routes_all = cot_rings[0].stack_rows(rows, micro_count * TOPK)[:, :, :rows]
    routes_all = routes_all.reshape(peers, micro_count, TOPK, rows)
    places = [
        slot_hits(routes_all[:, m], first_expert, local_experts, capacity)
        .astype(jnp.bfloat16)
        .reshape(peers, -1, rows)
        for m in micros
    ]
    every = list(range(peers))
    late = [steps - 1, steps, steps + 1]
    early = [k for k in every if k not in late]
    row_rings = [RingGather(xn2[m], peers, rows // 2) for m in micros]
    row_rings[0].step()
    groups = peers // GROUP

    class Experts:
        kept = [None] * 4

        def __init__(self, m, calls):
            self.m = m
            self.calls = calls
            self.per_call = local_experts // calls
            self.outs = [[None] * 3 for _ in range(groups)]
            self.found = {}

        def pick_grads(self):
            place = places[self.m]
            self.grads = pick_rows(first_at, place, cot_rings[self.m], every, False)
            return self.grads[0]

        def pick(self, distances):
            out = pick_rows(first_at, places[self.m], row_rings[self.m], distances, True)
            self.found.update(zip(distances, zip(out, out[len(distances) :])))
            self.rows = [self.found[k][0] for k in every if k in self.found]
            self.gate_slots = [self.found[k][1] for k in every if k in self.found]
            return out[0]

        def call(self, number, *earlier):
            for g in range(groups):
                span = slice(g * GROUP, (g + 1) * GROUP)
                here = self.rows[span]
                here[0] = after(here[0], *earlier) if earlier else here[0]
                done = expert_pass(
                    here,
                    self.grads[span],
                    self.gate_slots[span],
                    w_in,
                    w_out,
                    self.outs[g] + Experts.kept,
                    (self.m * groups + g, micro_count * groups),
                    number * self.per_call,
                    self.per_call,
                )
                self.outs[g], Experts.kept = list(done[:3]), list(done[3:])
            return done[2]

        def spread(self, spans, *earlier):
            place = places[self.m]
            place = after(place, *earlier) if earlier else place
            self.sums = None
            for g in range(groups):
                out = spread_rows(first_at, place, *self.outs[g], g, spans, self.sums)
                self.sums = out[0]
                if g == groups // 2:
                    far = out[1:]
            return far

    calls = 2
    first, second = Experts(0, calls), Experts(1, calls)
    ring, ring_next = row_rings
    while len(ring.from_left) < steps - 1:
        ring.step(*places, out_whole)
    ring.step(first.pick_grads())
    ring.step(first.pick(early), second.pick_grads())
    first.pick(late)
    ring_next.step(*ring.got)
    token = first.call(0)
    for number in range(1, calls):
        got = ring_next.got
        ring_next.step(token)
        token = first.call(number, *got)
    block = rows + EXTRA
    got = ring_next.got
    while len(ring_next.from_left) < steps:
        ring_next.step(token)
    far = first.spread([(0, block), (block, rows)], *got)
    got = ring_next.got
    while ring_next.far is None:
        ring_next.step()
    ring_first = RingScatter(lambda k: first.sums[k], far, peers)
    ring_first.step(*got)
    second.pick(early)
    second.pick(late)
    token = second.call(0)
    for number in range(1, calls):
        ring_first.step(token)
        token = second.call(number, *ring_first.sent)
    half = rows // 2
    spans = [(0, half), (half, block - half), (block, half), (block + half, half)]
    far = second.spread(spans)
    ring_grads = RingScatter(lambda k: second.sums[k, :block], far[:2], peers)
    ring_results = RingScatter(lambda k: second.sums[k, block:], far[2:], peers)
    ring_grads.step()
    got = ring_first.got
    while ring_first.at > 1:
        ring_first.step(second.sums)
    picked, grad_result, activated, grad_pre = Experts.kept
    place_at = jnp.stack([lax.rem(dp_at, 2), dp_at // 2])
    ring_grads.step()
    w_out_sum = weight_grads(
        after(activated, *ring_grads.sent, *ring_first.sent), grad_result, 0, local_experts
    )
    def backward(m, pieces, *earlier):
        own, left, right = pieces
        return block_call(
            backward_kernel,
            [
                (after(own, *earlier), (0,), block),
                (left, (), block),
                (right, (), block),
                (cotangent, (m,)),
                (hidden[m],),
                (tokens, (m,)),
                (query, (m,)),
                (keyval, (m,)),
                (seg_col, (m,)),
                (seg_row, (m,)),
                (gates, (m,)),
                (gains,),
                (cos,),
                (sin,),
                (first_whole,),
                (out_whole,),
            ],
            [
                jax.ShapeDtypeStruct((rows, width), jnp.bfloat16),
                jax.ShapeDtypeStruct((rows, proj_width + 128), jnp.bfloat16),
                jax.ShapeDtypeStruct((rows, width), jnp.bfloat16),
                jax.ShapeDtypeStruct((8, width), jnp.float32),
            ],
            "attention_backward",
            [pltpu.VMEM((rows, q_width), jnp.bfloat16)],
        )

    half = max(1, local_experts // 2)
    got = second_got = ring_grads.got
    ring_grads.step(w_out_sum)
    picked = after(picked, w_out_sum, *got, *ring_grads.sent)
    w_in_sum = weight_grads(picked, grad_pre, 0, half)
    while ring_grads.at > 1:
        ring_grads.step(w_in_sum)
    got = ring_first.got + ring_grads.got
    while ring_first.at > 0:
        ring_first.step(w_in_sum)

    def scatter(part, *earlier):
        return lax.psum_scatter(after(part, *earlier), "dp", scatter_dimension=1, tiled=True)

    grad_w_out = scatter(w_out_sum, *second_got)
    grad_w_in = [scatter(w_in_sum, *got)]
    picked = after(picked, w_in_sum, *got, *ring_first.sent)
    w_in_sum = weight_grads(picked, grad_pre, half, local_experts - half)
    grad_w_in.append(scatter(w_in_sum, *ring_first.got))
    ring_grads.step(w_in_sum)
    ring_results.step(w_in_sum)
    back_first = backward(
        0, (first.sums, ring_first.left, ring_first.right), *ring_grads.sent
    )
    ring_results.step(back_first[3])
    back_second = backward(
        1, (second.sums, ring_grads.left, ring_grads.right), back_first[3]
    )
    ring_results.step(back_second[3])
    grad_tokens, grad_proj, grad_attn, gain_sums = zip(back_first, back_second)
    mine, other = attention_grads(
        place_at, after(xn1, *ring_results.sent), mixed, grad_proj, grad_attn, gain_sums, dp_count
    )
    grads, grad_w_in, grad_w_out = reduce_packed(
        mine, other, my_spot, peers, dp_count, grad_w_in, grad_w_out, ring_results, (q_width, kv_width)
    )
    grad_query, grad_keyval, grad_small, grad_attn_out = grads
    wide = jnp.float32
    outputs = []
    for m, (own, ring, at) in enumerate(
        ((first.sums, ring_first, block), (second.sums, ring_results, 0))
    ):
        total = hidden[m] + own[0, block:].astype(wide)
        total = total + ring.left[at:].astype(wide) + ring.right[at:].astype(wide)
        outputs.append(total.astype(jnp.bfloat16))
    return (
        jnp.stack(outputs),
        jnp.stack(grad_tokens),
        grad_small[:, experts],
        grad_small[:, experts + 1],
        grad_query,
        grad_keyval,
        grad_attn_out,
        grad_small[:, :experts],
        grad_w_in,
        grad_w_out,
    )


def last_kernel(spot_ref, *refs):
    outs = refs[-4:]
    blocks = refs[:-4]
    peers = len(blocks) - 1
    piece = blocks[0].shape[0]
    for k, block_ref in enumerate(blocks):
        distance = k if k <= peers // 2 else k - 1
        spot = lax.rem(spot_ref[0] - distance + peers, peers)
        held = block_ref.shape[0]
        row = spot * piece + (held if k == peers // 2 + 1 else 0)
        at = 0
        for out_ref in outs:
            columns = out_ref.shape[1]
            out_ref[pl.ds(pl.multiple_of(row, 8), held), :] = block_ref[
                :, at : at + columns
            ].astype(jnp.float32)
            at += columns


def reduce_packed(mine, other, my_spot, peers, dp_count, grad_w_in, grad_w_out, ring_results, widths):
    lines, span, columns = mine.shape
    swap = [(d, d ^ 1) for d in range(dp_count)]
    other = after(other, *ring_results.got)
    ring_results.step()
    total = add_rows(mine, lax.ppermute(other, "dp", swap))
    total = after(total, *ring_results.sent)
    piece = span // peers
    total = total.reshape(lines, peers, piece, columns)

    def part(k):
        at = lax.rem(my_spot - k + peers, peers)
        return lax.dynamic_slice_in_dim(total, at, 1, axis=1).reshape(lines * piece, columns)

    half = lines * piece // 2
    farthest = part(peers // 2)
    ring = RingScatter(part, (farthest[:half], farthest[half:]), peers)
    ring.step()
    ring.step(*ring_results.got)
    while ring.at > 0:
        ring.step()
    own, left, right = [held.astype(jnp.float32) for held in (part(0), ring.left, ring.right)]
    mine = (own + left + right).astype(jnp.bfloat16).reshape(lines, piece, columns)
    mine = after(mine, *grad_w_in, grad_w_out, *ring_results.got)
    line = lax.axis_index("dp") // 2

    def for_line(at):
        return lax.dynamic_index_in_dim(mine, lax.rem(at, lines), 0, keepdims=False)

    share = for_line(line).astype(jnp.float32)
    for k in range(1, lines):
        pairs = [(d, (d + 2 * k) % dp_count) for d in range(dp_count)]
        share = share + lax.ppermute(for_line(line + k), "dp", pairs)
    gather = RingGather(share.astype(jnp.bfloat16), peers, piece // 2)
    gather.step()
    grad_w_out = grad_w_out.astype(jnp.float32)
    gather.step(grad_w_out)
    grad_w_in = jnp.concatenate([part.astype(jnp.float32) for part in grad_w_in], axis=0)
    gather.step(grad_w_in, *ring_results.got)
    while gather.far is None:
        gather.step()
    blocks = gather.from_left + list(gather.far) + gather.from_right[:0:-1]
    columns = (widths[0], widths[1], 128, columns - sum(widths) - 128)
    if piece % 16 == 0:
        grads = block_call(
            last_kernel,
            [(block,) for block in blocks],
            [jax.ShapeDtypeStruct((span, count), jnp.float32) for count in columns],
            "last_rows",
            prefetch=my_spot.astype(jnp.int32).reshape(1),
        )
    else:
        far = jnp.concatenate(gather.far, axis=0)
        by_distance = jnp.stack(gather.from_left + [far] + gather.from_right[:0:-1])
        distance = lax.rem(my_spot - jnp.arange(peers, dtype=jnp.int32) + peers, peers)
        by_spot = jnp.take(by_distance, distance, axis=0).reshape(span, -1).astype(jnp.float32)
        edges = [sum(columns[:i]) for i in range(5)]
        grads = [by_spot[:, edges[i] : edges[i + 1]] for i in range(4)]
    return grads, grad_w_in, grad_w_out


def solution(mesh):
    return jax.shard_map(
        per_device,
        mesh=mesh,
        in_specs=(
            P(None, ("dp", "expert"), None),
            P(None, ("dp", "expert")),
            P(None, ("dp", "expert"), None),
            P("dp"),
            P("dp"),
            P("dp", None),
            P("dp", None),
            P("dp", None),
            P("dp", None),
            P("expert", None, None),
            P("expert", None, None),
            P(None, ("dp", "expert"), None),
        ),
        out_specs=(
            P(None, ("dp", "expert"), None),
            P(None, ("dp", "expert"), None),
            P("dp"),
            P("dp"),
            P("dp", None),
            P("dp", None),
            P("dp", None),
            P("dp", None),
            P("expert", "dp", None),
            P("expert", "dp", None),
        ),
        check_vma=False,
    )
```

```python
import functools
import math

import jax
import jax.numpy as jnp
from jax import lax
from jax.experimental import pallas as pl
from jax.experimental.pallas import tpu as pltpu
from jax.sharding import PartitionSpec as P

QUERY_HEADS = 12
KEY_VALUE_HEADS = 2
HEAD_SIZE = 128
FF = 768
TOPK = 4
EXPERTS = 32
EXTRA = 16
PIECES = 3
GROUP = 8

eps_norm = 1e-06
rope_base = 1000000.0
mask_fill = -1e30
highest = lax.Precision.HIGHEST


def rms_scale(tensor):
    return lax.rsqrt(jnp.mean(tensor * tensor, axis=-1, keepdims=True) + eps_norm)


def rope_tables(sequence_length, head_width):
    positions = jnp.arange(sequence_length).astype(jnp.float32)
    frequency = rope_base ** (-(jnp.arange(head_width // 2).astype(jnp.float32) * 2.0) / head_width)
    angles = positions[:, None] * frequency[None, :]
    return (jnp.cos(angles), jnp.sin(angles))

SCORE_SCALE = 1.0 / math.sqrt(HEAD_SIZE)
GELU_SCALE = math.sqrt(2.0 / math.pi)
GELU_CUBE = 0.044715
SMALL_COST = pl.CostEstimate(flops=1_000_000, bytes_accessed=1_000_000, transcendentals=0)


def after(value, *earlier):
    return lax.optimization_barrier((value,) + earlier)[0]


def slot_hits(routes_all, first_expert, local_experts, capacity):
    rows = routes_all.shape[-1]
    names = first_expert + jnp.arange(local_experts, dtype=jnp.int32)
    named = routes_all[:, None].astype(jnp.int32) == names[None, :, None, None]
    member = jnp.any(named, axis=2)
    lower = (jnp.arange(rows)[:, None] < jnp.arange(rows)[None, :]).astype(jnp.bfloat16)
    rank = dot32(member.astype(jnp.bfloat16).reshape(-1, rows), lower).reshape(member.shape)
    slots = jnp.arange(capacity, dtype=jnp.float32)
    return member[:, :, None, :] & (rank[:, :, None, :] == slots[None, None, :, None])


def pack_pieces(values, out_ref, first_row):
    rows = values.shape[1]
    rest = values
    for piece in range(PIECES):
        part = rest.astype(jnp.bfloat16)
        rest = rest - part.astype(jnp.float32)
        for half in range(EXPERTS // EXTRA):
            at = (piece * (EXPERTS // EXTRA) + half) * rows
            out_ref[first_row : first_row + EXTRA, at : at + rows] = part[
                half * EXTRA : (half + 1) * EXTRA
            ]


def dot32(left, right):
    return jnp.dot(left, right, preferred_element_type=jnp.float32)


def dot_nt(left, right):
    return lax.dot_general(
        left, right, (((1,), (1,)), ((), ())), preferred_element_type=jnp.float32
    )


def dot_tn(left, right):
    return lax.dot_general(
        left, right, (((0,), (0,)), ((), ())), preferred_element_type=jnp.float32
    )


def mask_of(seg_col, seg_row):
    rows = seg_col.shape[0]
    query_at = lax.broadcasted_iota(jnp.int32, (rows, rows), 0)
    key_at = lax.broadcasted_iota(jnp.int32, (rows, rows), 1)
    return (seg_col == seg_row) & (query_at >= key_at)


def softmax_rows(query, key, allowed):
    scores = jnp.where(allowed, dot_nt(query, key) * SCORE_SCALE, mask_fill)
    weight = jnp.exp(scores - jnp.max(scores, axis=-1, keepdims=True))
    return weight / jnp.sum(weight, axis=-1, keepdims=True)


def from_blocks(starts_ref, rows_ref, blocks):
    total = None
    for at, block_ref in enumerate(blocks):
        span = block_ref.shape[0]
        columns = pl.ds(pl.multiple_of(starts_ref[at], 128), span)
        part = dot32(rows_ref[:, columns], block_ref[...])
        total = part if total is None else total + part
    return total


def attention_kernel(
    starts_ref,
    tok_ref,
    seg_col_ref,
    seg_row_ref,
    routes_ref,
    cos_ref,
    sin_ref,
    *refs,
):
    weight_refs = refs[:-7]
    xn1_ref, query_ref, keyval_ref, mixed_ref, gates_ref, gates_pack_ref, gains_ref = refs[-7:]

    @pl.when(pl.program_id(0) == 0)
    def _():
        for at, block_ref in enumerate(weight_refs):
            span, columns = block_ref.shape
            pad = block_ref[:, columns - 128 :].astype(jnp.float32).T
            place = pl.ds(pl.multiple_of(starts_ref[at], 128), span)
            gains_ref[:, place] = pad[2 * EXPERTS : 2 * EXPERTS + 8]

    tok = tok_ref[...].astype(jnp.float32)
    xn1_ref[...] = (tok * rms_scale(tok) * gains_ref[0:1, :]).astype(jnp.bfloat16)
    proj = from_blocks(starts_ref, xn1_ref, weight_refs)
    cos, sin = cos_ref[...], sin_ref[...]

    def rotate(part):
        return (part * cos + pltpu.roll(part, HEAD_SIZE // 2, 1) * sin).astype(jnp.bfloat16)

    q_width = QUERY_HEADS * HEAD_SIZE
    k_width = KEY_VALUE_HEADS * HEAD_SIZE
    for head in range(QUERY_HEADS):
        span = slice(head * HEAD_SIZE, (head + 1) * HEAD_SIZE)
        query_ref[:, span] = rotate(proj[:, span])
    for head in range(KEY_VALUE_HEADS):
        span = slice(head * HEAD_SIZE, (head + 1) * HEAD_SIZE)
        keyval_ref[:, span] = rotate(proj[:, q_width:][:, span])
    keyval_ref[:, k_width:] = proj[:, q_width + k_width : q_width + 2 * k_width].astype(
        jnp.bfloat16
    )
    logits = proj[:, q_width + 2 * k_width :]
    columns = lax.broadcasted_iota(jnp.int32, logits.shape, 1)
    named = [columns == routes_ref[:, j : j + 1] for j in range(TOPK)]
    chosen = [jnp.sum(jnp.where(hit, logits, 0.0), axis=-1, keepdims=True) for hit in named]
    top = functools.reduce(jnp.maximum, chosen)
    weight = [jnp.exp(part - top) for part in chosen]
    total = functools.reduce(jnp.add, weight)
    gates = jnp.full(logits.shape, -1.0, jnp.float32)
    for hit, part in zip(named, weight):
        gates = jnp.where(hit, part / total, gates)
    gates_ref[...] = gates
    pack_pieces(gates.T[:EXPERTS], gates_pack_ref, 0)
    allowed = mask_of(seg_col_ref[...], seg_row_ref[...])
    for head in range(QUERY_HEADS):
        span = slice(head * HEAD_SIZE, (head + 1) * HEAD_SIZE)
        group = head // (QUERY_HEADS // KEY_VALUE_HEADS)
        key = keyval_ref[:, group * HEAD_SIZE : (group + 1) * HEAD_SIZE]
        value = keyval_ref[:, k_width + group * HEAD_SIZE : k_width + (group + 1) * HEAD_SIZE]
        probs = softmax_rows(query_ref[:, span], key, allowed)
        mixed_ref[:, span] = dot32(probs.astype(jnp.bfloat16), value).astype(jnp.bfloat16)


def hidden_kernel(starts_ref, mixed_ref, tok_ref, gains_ref, pack_ref, *refs):
    weight_refs = refs[:-2]
    hidden_ref, xn2_ref = refs[-2:]
    rows = tok_ref.shape[0]
    hidden = tok_ref[...].astype(jnp.float32) + from_blocks(
        starts_ref, mixed_ref, weight_refs
    )
    hidden_ref[...] = hidden
    xn2_ref[:rows, :] = (hidden * rms_scale(hidden) * gains_ref[1:2, :]).astype(jnp.bfloat16)
    xn2_ref[rows:, :] = pack_ref[...]


def backward_kernel(
    own_ref,
    left_ref,
    right_ref,
    cot_ref,
    hidden_ref,
    tok_ref,
    query_ref,
    keyval_ref,
    seg_col_ref,
    seg_row_ref,
    gates_ref,
    gains_ref,
    cos_ref,
    sin_ref,
    *refs,
):
    weight_ref, out_weight_ref = refs[:2]
    grad_tok_ref, grad_proj_ref, grad_attn_ref, gain_sum_ref, mixed_grad_ref = refs[2:]
    width = tok_ref.shape[1]
    q_width = QUERY_HEADS * HEAD_SIZE
    k_width = KEY_VALUE_HEADS * HEAD_SIZE
    proj_width = q_width + 2 * k_width
    rows = tok_ref.shape[0]
    sums = [ref[...].astype(jnp.float32) for ref in (own_ref, left_ref, right_ref)]
    sums = sums[0] + sums[1] + sums[2]
    grad_xn2, pack = sums[:rows], sums[rows:]
    halves = EXPERTS // EXTRA
    lines = [
        sum(
            pack[:, (piece * halves + half) * rows : (piece * halves + half + 1) * rows]
            for piece in range(PIECES)
        )
        for half in range(halves)
    ]
    lines.append(jnp.zeros((128 - EXPERTS, rows), jnp.float32))
    grad_gates = jnp.concatenate(lines, axis=0).T
    hidden = hidden_ref[...]
    scale = rms_scale(hidden)
    unit = hidden * scale
    gain_sum_ref[...] = jnp.zeros(gain_sum_ref.shape, jnp.float32)
    gain_sum_ref[1:2, :] = jnp.sum(grad_xn2 * unit, axis=0, keepdims=True)
    grad_unit = grad_xn2 * gains_ref[1:2, :]
    grad_hidden = cot_ref[...].astype(jnp.float32) + scale * (
        grad_unit - unit * jnp.mean(grad_unit * unit, axis=-1, keepdims=True)
    )
    grad_attn_ref[...] = grad_hidden.astype(jnp.bfloat16)
    mixed_grad_ref[...] = dot_nt(grad_attn_ref[...], out_weight_ref[...]).astype(jnp.bfloat16)
    cos, sin = cos_ref[...], sin_ref[...]

    def unrotate(part):
        return (part * cos - pltpu.roll(part, HEAD_SIZE // 2, 1) * sin).astype(jnp.bfloat16)

    allowed = mask_of(seg_col_ref[...], seg_row_ref[...])
    per_group = QUERY_HEADS // KEY_VALUE_HEADS
    for group in range(KEY_VALUE_HEADS):
        key_span = slice(group * HEAD_SIZE, (group + 1) * HEAD_SIZE)
        value_span = slice(k_width + group * HEAD_SIZE, k_width + (group + 1) * HEAD_SIZE)
        key, value = keyval_ref[:, key_span], keyval_ref[:, value_span]
        grad_key = jnp.zeros(key.shape, jnp.float32)
        grad_value = jnp.zeros(key.shape, jnp.float32)
        for head in range(group * per_group, (group + 1) * per_group):
            span = slice(head * HEAD_SIZE, (head + 1) * HEAD_SIZE)
            query, grad_mixed = query_ref[:, span], mixed_grad_ref[:, span]
            probs = softmax_rows(query, key, allowed)
            grad_value += dot_tn(probs.astype(jnp.bfloat16), grad_mixed)
            grad_probs = dot_nt(grad_mixed, value)
            mean = jnp.sum(probs * grad_probs, axis=-1, keepdims=True)
            grad_scores = (probs * (grad_probs - mean)).astype(jnp.bfloat16)
            grad_proj_ref[:, span] = unrotate(dot32(grad_scores, key) * SCORE_SCALE)
            grad_key += dot_tn(grad_scores, query)
        grad_proj_ref[:, q_width + group * HEAD_SIZE : q_width + (group + 1) * HEAD_SIZE] = (
            unrotate(grad_key * SCORE_SCALE)
        )
        first = q_width + k_width + group * HEAD_SIZE
        grad_proj_ref[:, first : first + HEAD_SIZE] = grad_value.astype(jnp.bfloat16)
    gates = jnp.maximum(gates_ref[...], 0.0)
    grad_logits = gates * (grad_gates - jnp.sum(gates * grad_gates, axis=-1, keepdims=True))
    high = grad_logits.astype(jnp.bfloat16).astype(jnp.float32)
    low = pltpu.roll(grad_logits - high, EXPERTS, 1)
    grad_proj_ref[:, proj_width:] = (high + low).astype(jnp.bfloat16)
    grad_xn1 = dot_nt(grad_proj_ref[...], weight_ref[...])
    tok = tok_ref[...].astype(jnp.float32)
    scale = rms_scale(tok)
    unit = tok * scale
    gain_sum_ref[0:1, :] = jnp.sum(grad_xn1 * unit, axis=0, keepdims=True)
    grad_unit = grad_xn1 * gains_ref[0:1, :]
    grad_tok_ref[...] = (
        grad_hidden
        + scale * (grad_unit - unit * jnp.mean(grad_unit * unit, axis=-1, keepdims=True))
    ).astype(jnp.bfloat16)


def ring_order(peers):
    minor = peers // 4
    walk = []
    for col in range(minor):
        line = range(4) if col % 2 == 0 else range(3, -1, -1)
        walk += [row * minor + col for row in line]
    return walk


def ring_step(part, shift, peers):
    order = ring_order(peers)
    pairs = [(order[i], order[(i + shift) % peers]) for i in range(peers)]
    return lax.ppermute(part, "expert", pairs)


class RingGather:
    def __init__(self, part, peers, half):
        self.peers, self.half = peers, half
        self.from_left, self.from_right = [part], [part]
        self.far = None
        self.got = ()

    def step(self, *earlier):
        left, right = self.from_left[-1], self.from_right[-1]
        last = len(self.from_left) == self.peers // 2
        if last:
            left, right = left[: self.half], right[self.half :]
        left, right = self.sent = lax.optimization_barrier((left, right) + earlier)[:2]
        left, right = ring_step(left, 1, self.peers), ring_step(right, -1, self.peers)
        self.got = (left, right)
        if last:
            self.far = (left, right)
        else:
            self.from_left.append(left)
            self.from_right.append(right)
        return self

    def rows(self, k, first, count):
        if k < len(self.from_left):
            return self.from_left[k], first
        if k > self.peers // 2:
            return self.from_right[self.peers - k], first
        if first < self.half:
            return self.far[0], first
        return self.far[1], first - self.half

    def stack_rows(self, first, count):
        found = [self.rows(k, first, count) for k in range(self.peers)]
        return jnp.stack([array[at : at + count] for array, at in found])


class RingScatter:
    def __init__(self, part, far, peers):
        self.part, self.far, self.peers = part, far, peers
        self.at = peers // 2
        self.half = far[0].shape[0]

    def step(self, *earlier):
        peers, k, half = self.peers, self.at, self.half
        if k == peers // 2:
            left, right = lax.optimization_barrier(tuple(self.far) + earlier)[:2]
        else:
            left, right = self.part(k), self.part(peers - k)
            if earlier:
                self.left, self.right = lax.optimization_barrier(
                    (self.left, self.right) + earlier
                )[:2]
            if k == peers // 2 - 1:
                kept = left[half:].astype(jnp.bfloat16), right[:half].astype(jnp.bfloat16)
                left = jnp.concatenate([add_rows(left[:half], self.left), kept[0]], axis=0)
                right = jnp.concatenate([kept[1], add_rows(right[half:], self.right)], axis=0)
            else:
                left, right = add_rows(left, self.left), add_rows(right, self.right)
        left, right = self.sent = lax.optimization_barrier((left, right))
        self.left = ring_step(left, -1, peers)
        self.right = ring_step(right, 1, peers)
        self.got = (self.left, self.right)
        self.at = k - 1
        return self


def add_rows(left, right):
    return (left.astype(jnp.float32) + right.astype(jnp.float32)).astype(jnp.bfloat16)


def expert_kernel(sources, *refs):
    rows_refs = refs[:sources]
    grad_refs = refs[sources : 2 * sources]
    gate_refs = refs[2 * sources : 3 * sources]
    w_in_ref, w_out_ref = refs[3 * sources : 3 * sources + 2]
    (
        back_rows_ref,
        back_grads_ref,
        grad_gate_ref,
        picked_ref,
        grad_result_ref,
        activated_ref,
        grad_pre_ref,
    ) = refs[-7:]
    capacity, width = rows_refs[0].shape
    for k in range(sources):
        picked_ref[pl.ds(k * capacity, capacity), :] = rows_refs[k][...]
    pre_act = dot32(picked_ref[...], w_in_ref[...])
    gate_part = pre_act[:, :FF]
    up_part = pre_act[:, FF:]
    square = gate_part * gate_part
    bend = jnp.tanh(GELU_SCALE * gate_part * (1.0 + GELU_CUBE * square))
    lift = 0.5 * (1.0 + bend)
    gelu_val = gate_part * lift
    slope = lift + 0.5 * gate_part * (1.0 - bend * bend) * (
        GELU_SCALE * (1.0 + 3.0 * GELU_CUBE * square)
    )
    activated_ref[...] = (gelu_val * up_part).astype(jnp.bfloat16)
    result = dot32(activated_ref[...], w_out_ref[...])
    for k in range(sources):
        gates = gate_refs[k][...]
        span = slice(k * capacity, (k + 1) * capacity)
        grad_rows = grad_refs[k][...].astype(jnp.float32)
        grad_gate_ref[span, :] = jnp.sum(result[span] * grad_rows, axis=-1, keepdims=True)
        back_rows_ref[k] = (result[span] * gates).astype(jnp.bfloat16)
        grad_result_ref[span, :] = (grad_rows * gates).astype(jnp.bfloat16)
    grad_act = lax.dot_general(
        grad_result_ref[...],
        w_out_ref[...],
        (((1,), (1,)), ((), ())),
        preferred_element_type=jnp.float32,
    )
    grad_pre_ref[:, :FF] = (grad_act * up_part * slope).astype(jnp.bfloat16)
    grad_pre_ref[:, FF:] = (grad_act * gelu_val).astype(jnp.bfloat16)
    grad_in = lax.dot_general(
        grad_pre_ref[...],
        w_in_ref[...],
        (((1,), (1,)), ((), ())),
        preferred_element_type=jnp.float32,
    ).astype(jnp.bfloat16)
    for k in range(sources):
        back_grads_ref[k] = grad_in[k * capacity : (k + 1) * capacity]


def expert_pass(rows_list, grads_list, gate_slots, w_in, w_out, held_outs, position, first, count):
    sources = len(rows_list)
    local_experts, width, _ = w_in.shape
    slots = rows_list[0].shape[0]
    capacity = slots // local_experts
    held = sources * capacity
    block_spec = pl.BlockSpec((capacity, width), lambda e: (e + first, 0))
    back_spec = pl.BlockSpec((sources, capacity, width), lambda e: (0, e + first, 0))
    column_spec = pl.BlockSpec((None, held, 1), lambda e: (e + first, 0, 0))

    def kept_spec(columns):
        return pl.BlockSpec((None, held, columns), lambda e: (e + first, position[0], 0))

    def kept_shape(columns):
        return jax.ShapeDtypeStruct((local_experts, position[1] * held, columns), jnp.bfloat16)

    kept_widths = (width, width, FF, 2 * FF)
    first_held = 3 * sources + 2
    given = [(i, part) for i, part in enumerate(held_outs) if part is not None]
    return pl.pallas_call(
        functools.partial(expert_kernel, sources),
        grid=(count,),
        in_specs=[block_spec] * (2 * sources)
        + [pl.BlockSpec((capacity, 1), lambda e: (e + first, 0))] * sources
        + [
            pl.BlockSpec((None, width, 2 * FF), lambda e: (e + first, 0, 0)),
            pl.BlockSpec((None, FF, width), lambda e: (e + first, 0, 0)),
        ]
        + [pl.BlockSpec(memory_space=pl.ANY)] * len(given),
        out_specs=[back_spec, back_spec, column_spec] + [kept_spec(c) for c in kept_widths],
        out_shape=[
            jax.ShapeDtypeStruct((sources, slots, width), jnp.bfloat16),
            jax.ShapeDtypeStruct((sources, slots, width), jnp.bfloat16),
            jax.ShapeDtypeStruct((local_experts, held, 1), jnp.float32),
        ]
        + [kept_shape(c) for c in kept_widths],
        input_output_aliases={first_held + at: i for at, (i, _) in enumerate(given)},
        compiler_params=pltpu.CompilerParams(vmem_limit_bytes=60 * 1024 * 1024),
        cost_estimate=SMALL_COST,
        name="expert_pass",
    )(*rows_list, *grads_list, *gate_slots, w_in, w_out, *[part for _, part in given])


def block_call(kernel, operands, out_shape, name, scratch=(), prefetch=None):
    def spec(array, lead=(), rows=None):
        rest = array.shape[len(lead) :]
        at = lead + (0,) * len(rest)
        if rows is not None:
            count, block = rows if isinstance(rows, tuple) else (rows, 0)
            rest = (count,) + rest[1:]
            at = lead + (block,) + (0,) * (len(rest) - 1)
        return pl.BlockSpec((None,) * len(lead) + rest, lambda *_: at)

    scalars = [] if prefetch is None else [prefetch]
    return pl.pallas_call(
        kernel,
        grid_spec=pltpu.PrefetchScalarGridSpec(
            num_scalar_prefetch=len(scalars),
            grid=(1,),
            in_specs=[spec(*operand) for operand in operands],
            out_specs=[spec(shape) for shape in out_shape],
            scratch_shapes=list(scratch),
        ),
        out_shape=out_shape,
        compiler_params=pltpu.CompilerParams(vmem_limit_bytes=60 * 1024 * 1024),
        cost_estimate=SMALL_COST,
        name=name,
    )(*scalars, *[operand[0] for operand in operands])


def pick_kernel(shares, gated, first_ref, place_ref, *refs):
    at = 0
    outs = refs[sum(count for _, count in shares) + (len(shares) if gated else 0) :]
    for number, (k, count) in enumerate(shares):
        total, row = None, 0
        for block_ref in refs[at : at + count]:
            held = block_ref.shape[0]
            part = dot32(place_ref[k, :, row : row + held], block_ref[...])
            total = part if total is None else total + part
            row += held
        outs[number][...] = total.astype(jnp.bfloat16)
        at += count
        if gated:
            slot_gates(first_ref[0], place_ref[k], refs[at], outs[len(shares) + number])
            at += 1


def slot_gates(first_expert, place, pack_ref, out_ref):
    slots, rows = place.shape
    pack = pack_ref[...].astype(jnp.float32)
    halves = EXPERTS // EXTRA
    line = lax.broadcasted_iota(jnp.int32, (EXTRA, rows), 0)
    local_experts = slots * 4 // rows
    capacity = rows // 4
    for e in range(local_experts):
        gate = jnp.zeros((1, rows), jnp.float32)
        for half in range(halves):
            hit = line + half * EXTRA == first_expert + e
            for piece in range(PIECES):
                at = (piece * halves + half) * rows
                gate += jnp.sum(
                    jnp.where(hit, pack[:, at : at + rows], 0.0), axis=0, keepdims=True
                )
        span = slice(e * capacity, (e + 1) * capacity)
        out_ref[span, :] = jnp.sum(
            place[span].astype(jnp.float32) * gate, axis=-1, keepdims=True
        )


def pick_rows(first_expert, place, ring, distances, gated):
    _, slots, rows = place.shape
    half = rows // 2
    operands, shares = [], []
    for k in distances:
        spans = [(0, rows)]
        if k == ring.peers // 2 and ring.half < rows:
            spans = [(0, half), (half, half)]
        shares.append((k, len(spans)))
        for at, count in spans + ([(rows, EXTRA)] if gated else []):
            array, at = ring.rows(k, at, count)
            operands.append((array, (), (count, at // count)))
    width = operands[0][0].shape[-1]
    out_shape = [jax.ShapeDtypeStruct((slots, width), jnp.bfloat16) for _ in distances]
    if gated:
        out_shape += [jax.ShapeDtypeStruct((slots, 1), jnp.float32) for _ in distances]
    return block_call(
        functools.partial(pick_kernel, shares, gated),
        [(place,)] + operands,
        out_shape,
        "pick_rows",
        prefetch=first_expert,
    )


def spread_kernel(middle, spans, held, first_ref, place_ref, rows_ref, grads_ref, gate_ref, *refs):
    out_ref, *far_refs = refs[held:]
    place = place_ref[...]
    rows = place.shape[1]
    out_ref[:rows, :] = dot_tn(place, grads_ref[...]).astype(jnp.bfloat16)
    out_ref[rows + EXTRA :, :] = dot_tn(place, rows_ref[...]).astype(jnp.bfloat16)
    capacity = gate_ref.shape[1]
    expert = lax.broadcasted_iota(jnp.int32, (EXPERTS, rows), 0) - first_ref[0]
    gates = jnp.zeros((EXPERTS, rows), jnp.float32)
    for e in range(gate_ref.shape[0]):
        hit = place[e * capacity : (e + 1) * capacity].astype(jnp.float32)
        line = jnp.sum(hit * gate_ref[e], axis=0, keepdims=True)
        gates = jnp.where(expert == e, line, gates)
    pack_pieces(gates, out_ref, rows)

    @pl.when(pl.program_id(0) == middle)
    def _():
        for far_ref, (row, count) in zip(far_refs, spans):
            far_ref[...] = out_ref[row : row + count, :]


def spread_rows(first_expert, place, rows_back, grads_back, gate_slots, group, spans, held):
    sources, slots, rows = place.shape
    width = rows_back.shape[-1]
    local_experts = gate_slots.shape[0]
    base = group * GROUP
    by_source = pl.BlockSpec((None, slots, width), lambda k, f: (k, 0, 0))
    held = [] if held is None else [held]
    out_shape = [jax.ShapeDtypeStruct((sources, 2 * rows + EXTRA, width), jnp.bfloat16)]
    out_shape += [jax.ShapeDtypeStruct((count, width), jnp.bfloat16) for _, count in spans]
    out_specs = [pl.BlockSpec((None, 2 * rows + EXTRA, width), lambda k, f: (base + k, 0, 0))]
    out_specs += [pl.BlockSpec((count, width), lambda k, f: (0, 0)) for _, count in spans]
    return pl.pallas_call(
        functools.partial(spread_kernel, sources // 2 - base, spans, len(held)),
        grid_spec=pltpu.PrefetchScalarGridSpec(
            num_scalar_prefetch=1,
            grid=(GROUP,),
            in_specs=[
                pl.BlockSpec((None, slots, rows), lambda k, f: (base + k, 0, 0)),
                by_source,
                by_source,
                pl.BlockSpec((local_experts, slots // local_experts, 1), lambda k, f: (0, k, 0)),
            ]
            + [pl.BlockSpec(memory_space=pl.ANY)] * len(held),
            out_specs=out_specs,
        ),
        out_shape=out_shape,
        input_output_aliases={5 + i: i for i in range(len(held))},
        compiler_params=pltpu.CompilerParams(vmem_limit_bytes=60 * 1024 * 1024),
        cost_estimate=SMALL_COST,
        name="spread_rows",
    )(first_expert, place, rows_back, grads_back, gate_slots, *held)


def weight_grad_kernel(left_ref, right_ref, out_ref):
    out_ref[...] = dot_tn(left_ref[...], right_ref[...]).astype(jnp.bfloat16)


def weight_grads(left, right, first, count):
    _, held, height = left.shape
    columns = right.shape[-1]
    tile = min(height, 768)
    return pl.pallas_call(
        weight_grad_kernel,
        grid=(count, height // tile),
        in_specs=[
            pl.BlockSpec((None, held, tile), lambda e, i: (e + first, 0, i)),
            pl.BlockSpec((None, held, columns), lambda e, i: (e + first, 0, 0)),
        ],
        out_specs=pl.BlockSpec((None, tile, columns), lambda e, i: (e, i, 0)),
        out_shape=jax.ShapeDtypeStruct((count, height, columns), jnp.bfloat16),
        compiler_params=pltpu.CompilerParams(vmem_limit_bytes=60 * 1024 * 1024),
        cost_estimate=SMALL_COST,
        name="weight_grads",
    )(left, right)


def attention_forward(starts, tokens, seg_col, seg_row, routes, cos, sin, weights):
    count, rows, width = tokens.shape

    def by_micro(*shape):
        return pl.BlockSpec((None,) + shape, lambda m, s: (m,) + (0,) * len(shape))

    def shared(part):
        return pl.BlockSpec(part.shape, lambda m, s: (0, 0))

    kv_width = 2 * KEY_VALUE_HEADS * HEAD_SIZE
    shapes = [
        ((rows, width), jnp.bfloat16),
        ((rows, QUERY_HEADS * HEAD_SIZE), jnp.bfloat16),
        ((rows, kv_width), jnp.bfloat16),
        ((rows, QUERY_HEADS * HEAD_SIZE), jnp.bfloat16),
        ((rows, 128), jnp.float32),
        ((EXTRA, PIECES * EXPERTS // EXTRA * rows), jnp.bfloat16),
    ]
    return pl.pallas_call(
        attention_kernel,
        grid_spec=pltpu.PrefetchScalarGridSpec(
            num_scalar_prefetch=1,
            grid=(count,),
            in_specs=[
                by_micro(rows, width),
                by_micro(rows, 1),
                by_micro(1, rows),
                by_micro(rows, TOPK),
                shared(cos),
                shared(sin),
            ]
            + [shared(part) for part in weights],
            out_specs=[by_micro(*shape) for shape, _ in shapes]
            + [pl.BlockSpec((8, width), lambda m, s: (0, 0))],
        ),
        out_shape=[jax.ShapeDtypeStruct((count,) + shape, kind) for shape, kind in shapes]
        + [jax.ShapeDtypeStruct((8, width), jnp.float32)],
        compiler_params=pltpu.CompilerParams(vmem_limit_bytes=60 * 1024 * 1024),
        cost_estimate=SMALL_COST,
        name="attention_forward",
    )(starts, tokens, seg_col, seg_row, routes, cos, sin, *weights)


def join_kernel(starts_ref, *refs):
    for at, block_ref in enumerate(refs[:-1]):

        @pl.when(pl.program_id(0) == at)
        def _():
            refs[-1][...] = block_ref[...]


def join_blocks(starts, blocks):
    if len(blocks) == 1:
        return blocks[0]
    span, columns = blocks[0].shape
    return pl.pallas_call(
        join_kernel,
        grid_spec=pltpu.PrefetchScalarGridSpec(
            num_scalar_prefetch=1,
            grid=(len(blocks),),
            in_specs=[pl.BlockSpec((span, columns), lambda i, s: (0, 0)) for _ in blocks],
            out_specs=pl.BlockSpec((span, columns), lambda i, s: (s[i] // span, 0)),
        ),
        out_shape=jax.ShapeDtypeStruct((len(blocks) * span, columns), blocks[0].dtype),
        compiler_params=pltpu.CompilerParams(vmem_limit_bytes=60 * 1024 * 1024),
        cost_estimate=SMALL_COST,
        name="join_blocks",
    )(starts, *blocks)


def attention_grad_kernel(core_ref, xn1, mixed, *refs):
    count = xn1.shape[0]
    proj, attn, sums = [refs[i * count : (i + 1) * count] for i in range(3)]
    mine_ref, other_ref = refs[-2:]
    split = proj[0].shape[1]
    span = mine_ref.shape[0]
    grad = sum(dot_tn(xn1[m], proj[m][...]) for m in range(count))
    router = grad[:, split - 128 :]
    lane = lax.broadcasted_iota(jnp.int32, router.shape, 1)
    router = router + pltpu.roll(router, 128 - EXPERTS, 1)
    gain = sum(part[...] for part in sums)
    lines = [jnp.zeros((EXPERTS, gain.shape[1]), jnp.float32), gain]
    lines.append(jnp.zeros((128 - EXPERTS - gain.shape[0], gain.shape[1]), jnp.float32))
    router = jnp.where(lane < EXPERTS, router, jnp.concatenate(lines, axis=0).T)
    first = core_ref[0] == 0

    def put(columns, value):
        value = value.astype(jnp.bfloat16)
        low, high = value[:span], value[span:]
        mine_ref[:, columns] = jnp.where(first, low, high)
        other_ref[:, columns] = jnp.where(first, high, low)

    put(slice(0, split - 128), grad[:, : split - 128])
    put(slice(split - 128, split), router)
    put(slice(split, None), sum(dot_tn(mixed[m], attn[m][...]) for m in range(count)))


def attention_grads(core, xn1, mixed, proj, attn, gain_sums, parts):
    count, rows, width = xn1.shape
    span = width // parts
    lines = parts // 2
    columns = proj[0].shape[1] + attn[0].shape[1]
    by_line = pl.BlockSpec((count, rows, 2 * span), lambda i, c: (0, 0, i))

    def shared(part):
        return pl.BlockSpec(part.shape, lambda i, c: (0, 0))

    out_spec = pl.BlockSpec((None, span, columns), lambda i, c: (i, 0, 0))
    out_shape = jax.ShapeDtypeStruct((lines, span, columns), jnp.bfloat16)
    return pl.pallas_call(
        attention_grad_kernel,
        grid_spec=pltpu.PrefetchScalarGridSpec(
            num_scalar_prefetch=1,
            grid=(lines,),
            in_specs=[by_line, by_line]
            + [shared(p) for p in proj]
            + [shared(p) for p in attn]
            + [pl.BlockSpec((p.shape[0], 2 * span), lambda i, c: (0, i)) for p in gain_sums],
            out_specs=[out_spec, out_spec],
        ),
        out_shape=[out_shape, out_shape],
        compiler_params=pltpu.CompilerParams(vmem_limit_bytes=60 * 1024 * 1024),
        cost_estimate=SMALL_COST,
        name="attention_grads",
    )(core, xn1, mixed, *proj, *attn, *gain_sums)


def gather_blocks(part, dp_at, dp_count):
    span = part.shape[0]
    if span % 128 or dp_count != 4:
        whole = lax.all_gather(part, "dp", axis=0, tiled=True)
        return lambda *earlier: [whole], jnp.zeros((1,), jnp.int32)
    line = [(d, (d + 2) % 4) for d in range(4)]
    core = [(d, d ^ 1) for d in range(4)]
    across = lax.ppermute(part, "dp", line)
    beside = lax.ppermute(part, "dp", core)
    far = lax.rem(dp_at + 2, 4)
    owners = jnp.stack([dp_at, dp_at + 1 - 2 * lax.rem(dp_at, 2), far, far + 1 - 2 * lax.rem(far, 2)])

    def blocks(*earlier):
        moved = after(across, *earlier) if earlier else across
        return [part, beside, moved, lax.ppermute(moved, "dp", core)]

    return blocks, owners * span


def per_device(
    tokens,
    segments,
    routes,
    norm_one,
    norm_two,
    w_query,
    key_value_weight,
    w_out_attn,
    w_router,
    w_in,
    w_out,
    cotangent,
):
    micro_count, rows, width = tokens.shape
    micros = range(micro_count)
    peers = lax.axis_size("expert")
    dp_count = lax.axis_size("dp")
    local_experts = w_in.shape[0]
    experts = local_experts * peers
    capacity = rows // 4
    first_expert = lax.axis_index("expert") * local_experts
    q_width = w_query.shape[1]
    kv_width = key_value_weight.shape[1]
    proj_width = q_width + kv_width
    cosine_table, sine_values = rope_tables(rows, HEAD_SIZE)
    cos = jnp.concatenate([cosine_table, cosine_table], axis=1)
    sin = jnp.concatenate([-sine_values, sine_values], axis=1)
    order = ring_order(peers)
    spot = [order.index(dev) for dev in range(peers)]
    my_spot = jnp.array(spot, jnp.int32)[lax.axis_index("expert")]

    router_pad = jnp.zeros((w_router.shape[0], 126 - 2 * experts), jnp.bfloat16)
    first_weight = jnp.concatenate(
        [
            w_query,
            key_value_weight,
            w_router,
            w_router,
            norm_one[:, None],
            norm_two[:, None],
            router_pad,
        ],
        axis=1,
    )
    dp_at = lax.axis_index("dp").astype(jnp.int32)
    first_weights, starts = gather_blocks(first_weight, dp_at, dp_count)
    out_weights, _ = gather_blocks(w_out_attn, dp_at, dp_count)

    routes_rows = jnp.swapaxes(routes, 1, 2).reshape(-1, rows).astype(jnp.bfloat16)
    routes_rows = jnp.pad(
        routes_rows, ((0, EXTRA - routes_rows.shape[0]), (0, width - rows))
    )
    cot_rings = [
        RingGather(jnp.concatenate([cotangent[0], routes_rows], axis=0), peers, rows // 2),
        RingGather(cotangent[1], peers, rows // 2),
    ]
    steps = peers // 2
    for at in range(steps - 2):
        for ring in cot_rings:
            ring.step()
        if at == 0:
            first_weights = first_weights(*cot_rings[0].got, *cot_rings[1].got)
    first_at = first_expert.astype(jnp.int32).reshape(1)
    seg_col, seg_row = segments[:, :, None], segments[:, None, :]
    xn1, query, keyval, mixed, gates, gates_pack, gains = attention_forward(
        starts, tokens, seg_col, seg_row, routes, cos, sin, first_weights
    )
    for ring in cot_rings:
        ring.step(mixed)
    out_weights = out_weights(mixed)
    hidden, xn2 = [], []
    for m in micros:
        out = block_call(
            hidden_kernel,
            [(after(mixed, *xn2), (m,)), (tokens, (m,)), (gains,), (gates_pack, (m,))]
            + [(part,) for part in out_weights],
            [
                jax.ShapeDtypeStruct((rows, width), jnp.float32),
                jax.ShapeDtypeStruct((rows + EXTRA, width), jnp.bfloat16),
            ],
            "hidden_rows",
            prefetch=starts,
        )
        hidden.append(out[0])
        xn2.append(out[1])
    for ring in cot_rings:
        ring.step()
    got = cot_rings[0].got + cot_rings[1].got
    first_whole = join_blocks(starts, [after(first_weights[0], *got)] + first_weights[1:])
    routes_all = cot_rings[0].stack_rows(rows, micro_count * TOPK)[:, :, :rows]
    routes_all = routes_all.reshape(peers, micro_count, TOPK, rows)
    places = [
        slot_hits(routes_all[:, m], first_expert, local_experts, capacity)
        .astype(jnp.bfloat16)
        .reshape(peers, -1, rows)
        for m in micros
    ]
    every = list(range(peers))
    late = [steps - 1, steps, steps + 1]
    early = [k for k in every if k not in late]
    row_rings = [RingGather(xn2[m], peers, rows // 2) for m in micros]
    row_rings[0].step()
    groups = peers // GROUP

    class Experts:
        kept = [None] * 4

        def __init__(self, m, calls):
            self.m = m
            self.calls = calls
            self.per_call = local_experts // calls
            self.outs = [[None] * 3 for _ in range(groups)]
            self.found = {}

        def pick_grads(self):
            place = places[self.m]
            self.grads = pick_rows(first_at, place, cot_rings[self.m], every, False)
            return self.grads[0]

        def pick(self, distances):
            out = pick_rows(first_at, places[self.m], row_rings[self.m], distances, True)
            self.found.update(zip(distances, zip(out, out[len(distances) :])))
            self.rows = [self.found[k][0] for k in every if k in self.found]
            self.gate_slots = [self.found[k][1] for k in every if k in self.found]
            return out[0]

        def call(self, number, *earlier):
            for g in range(groups):
                span = slice(g * GROUP, (g + 1) * GROUP)
                here = self.rows[span]
                here[0] = after(here[0], *earlier) if earlier else here[0]
                done = expert_pass(
                    here,
                    self.grads[span],
                    self.gate_slots[span],
                    w_in,
                    w_out,
                    self.outs[g] + Experts.kept,
                    (self.m * groups + g, micro_count * groups),
                    number * self.per_call,
                    self.per_call,
                )
                self.outs[g], Experts.kept = list(done[:3]), list(done[3:])
            return done[2]

        def spread(self, spans, *earlier):
            place = places[self.m]
            place = after(place, *earlier) if earlier else place
            self.sums = None
            for g in range(groups):
                out = spread_rows(first_at, place, *self.outs[g], g, spans, self.sums)
                self.sums = out[0]
                if g == groups // 2:
                    far = out[1:]
            return far

    calls = 2
    first, second = Experts(0, calls), Experts(1, calls)
    ring, ring_next = row_rings
    while len(ring.from_left) < steps - 1:
        ring.step(*places)
    ring.step(first.pick_grads(), first_whole)
    ring.step(first.pick(early), second.pick_grads())
    first.pick(late)
    ring_next.step(*ring.got)
    token = first.call(0)
    for number in range(1, calls):
        got = ring_next.got
        ring_next.step(token)
        token = first.call(number, *got)
    block = rows + EXTRA
    got = ring_next.got
    while len(ring_next.from_left) < steps:
        ring_next.step(token)
    far = first.spread([(0, block), (block, rows)], *got)
    got = ring_next.got
    while ring_next.far is None:
        ring_next.step()
    ring_first = RingScatter(lambda k: first.sums[k], far, peers)
    ring_first.step(*got)
    second.pick(early)
    out_whole = join_blocks(starts, [after(out_weights[0], first.sums)] + out_weights[1:])
    places[1] = after(places[1], out_whole)
    second.pick(late)
    token = second.call(0)
    for number in range(1, calls):
        ring_first.step(token)
        token = second.call(number, *ring_first.sent)
    half = rows // 2
    spans = [(0, half), (half, block - half), (block, half), (block + half, half)]
    far = second.spread(spans)
    ring_grads = RingScatter(lambda k: second.sums[k, :block], far[:2], peers)
    ring_results = RingScatter(lambda k: second.sums[k, block:], far[2:], peers)
    ring_grads.step()
    got = ring_first.got
    while ring_first.at > 1:
        ring_first.step(second.sums)
    picked, grad_result, activated, grad_pre = Experts.kept
    place_at = jnp.stack([lax.rem(dp_at, 2), dp_at // 2])
    ring_grads.step()
    w_out_sum = weight_grads(
        after(activated, *ring_grads.sent, *ring_first.sent), grad_result, 0, local_experts
    )
    def backward(m, pieces, *earlier):
        own, left, right = pieces
        return block_call(
            backward_kernel,
            [
                (after(own, *earlier), (0,), block),
                (left, (), block),
                (right, (), block),
                (cotangent, (m,)),
                (hidden[m],),
                (tokens, (m,)),
                (query, (m,)),
                (keyval, (m,)),
                (seg_col, (m,)),
                (seg_row, (m,)),
                (gates, (m,)),
                (gains,),
                (cos,),
                (sin,),
                (first_whole,),
                (out_whole,),
            ],
            [
                jax.ShapeDtypeStruct((rows, width), jnp.bfloat16),
                jax.ShapeDtypeStruct((rows, proj_width + 128), jnp.bfloat16),
                jax.ShapeDtypeStruct((rows, width), jnp.bfloat16),
                jax.ShapeDtypeStruct((8, width), jnp.float32),
            ],
            "attention_backward",
            [pltpu.VMEM((rows, q_width), jnp.bfloat16)],
        )

    half = max(1, local_experts // 2)
    got = second_got = ring_grads.got
    ring_grads.step(w_out_sum)
    picked = after(picked, w_out_sum, *got, *ring_grads.sent)
    w_in_sum = weight_grads(picked, grad_pre, 0, half)
    while ring_grads.at > 1:
        ring_grads.step(w_in_sum)
    got = ring_first.got + ring_grads.got
    while ring_first.at > 0:
        ring_first.step(w_in_sum)

    def scatter(part, *earlier):
        return lax.psum_scatter(after(part, *earlier), "dp", scatter_dimension=1, tiled=True)

    grad_w_out = scatter(w_out_sum, *second_got)
    grad_w_in = [scatter(w_in_sum, *got)]
    picked = after(picked, w_in_sum, *got, *ring_first.sent)
    w_in_sum = weight_grads(picked, grad_pre, half, local_experts - half)
    grad_w_in.append(scatter(w_in_sum, *ring_first.got))
    ring_grads.step(w_in_sum)
    ring_results.step(w_in_sum)
    back_first = backward(
        0, (first.sums, ring_first.left, ring_first.right), *ring_grads.sent
    )
    ring_results.step(back_first[3])
    back_second = backward(
        1, (second.sums, ring_grads.left, ring_grads.right), back_first[3]
    )
    ring_results.step(back_second[3])
    grad_tokens, grad_proj, grad_attn, gain_sums = zip(back_first, back_second)
    mine, other = attention_grads(
        place_at, after(xn1, *ring_results.sent), mixed, grad_proj, grad_attn, gain_sums, dp_count
    )
    grads, grad_w_in, grad_w_out = reduce_packed(
        mine, other, my_spot, peers, dp_count, grad_w_in, grad_w_out, ring_results, (q_width, kv_width)
    )
    grad_query, grad_keyval, grad_small, grad_attn_out = grads
    wide = jnp.float32
    outputs = []
    for m, (own, ring, at) in enumerate(
        ((first.sums, ring_first, block), (second.sums, ring_results, 0))
    ):
        total = hidden[m] + own[0, block:].astype(wide)
        total = total + ring.left[at:].astype(wide) + ring.right[at:].astype(wide)
        outputs.append(total.astype(jnp.bfloat16))
    return (
        jnp.stack(outputs),
        jnp.stack(grad_tokens),
        grad_small[:, experts],
        grad_small[:, experts + 1],
        grad_query,
        grad_keyval,
        grad_attn_out,
        grad_small[:, :experts],
        grad_w_in,
        grad_w_out,
    )


def last_kernel(spot_ref, *refs):
    outs = refs[-4:]
    blocks = refs[:-4]
    peers = len(blocks) - 1
    piece = blocks[0].shape[0]
    for k, block_ref in enumerate(blocks):
        distance = k if k <= peers // 2 else k - 1
        spot = lax.rem(spot_ref[0] - distance + peers, peers)
        held = block_ref.shape[0]
        row = spot * piece + (held if k == peers // 2 + 1 else 0)
        at = 0
        for out_ref in outs:
            columns = out_ref.shape[1]
            out_ref[pl.ds(pl.multiple_of(row, 8), held), :] = block_ref[
                :, at : at + columns
            ].astype(jnp.float32)
            at += columns


def reduce_packed(mine, other, my_spot, peers, dp_count, grad_w_in, grad_w_out, ring_results, widths):
    lines, span, columns = mine.shape
    swap = [(d, d ^ 1) for d in range(dp_count)]
    other = after(other, *ring_results.got)
    ring_results.step()
    total = add_rows(mine, lax.ppermute(other, "dp", swap))
    total = after(total, *ring_results.sent)
    piece = span // peers
    total = total.reshape(lines, peers, piece, columns)

    def part(k):
        at = lax.rem(my_spot - k + peers, peers)
        return lax.dynamic_slice_in_dim(total, at, 1, axis=1).reshape(lines * piece, columns)

    half = lines * piece // 2
    farthest = part(peers // 2)
    ring = RingScatter(part, (farthest[:half], farthest[half:]), peers)
    ring.step()
    ring.step(*ring_results.got)
    while ring.at > 0:
        ring.step()
    own, left, right = [held.astype(jnp.float32) for held in (part(0), ring.left, ring.right)]
    mine = (own + left + right).astype(jnp.bfloat16).reshape(lines, piece, columns)
    mine = after(mine, *grad_w_in, grad_w_out, *ring_results.got)
    line = lax.axis_index("dp") // 2

    def for_line(at):
        return lax.dynamic_index_in_dim(mine, lax.rem(at, lines), 0, keepdims=False)

    share = for_line(line).astype(jnp.float32)
    for k in range(1, lines):
        pairs = [(d, (d + 2 * k) % dp_count) for d in range(dp_count)]
        share = share + lax.ppermute(for_line(line + k), "dp", pairs)
    gather = RingGather(share.astype(jnp.bfloat16), peers, piece // 2)
    gather.step()
    grad_w_out = grad_w_out.astype(jnp.float32)
    gather.step(grad_w_out)
    grad_w_in = jnp.concatenate([part.astype(jnp.float32) for part in grad_w_in], axis=0)
    gather.step(grad_w_in, *ring_results.got)
    while gather.far is None:
        gather.step()
    blocks = gather.from_left + list(gather.far) + gather.from_right[:0:-1]
    columns = (widths[0], widths[1], 128, columns - sum(widths) - 128)
    if piece % 16 == 0:
        grads = block_call(
            last_kernel,
            [(block,) for block in blocks],
            [jax.ShapeDtypeStruct((span, count), jnp.float32) for count in columns],
            "last_rows",
            prefetch=my_spot.astype(jnp.int32).reshape(1),
        )
    else:
        far = jnp.concatenate(gather.far, axis=0)
        by_distance = jnp.stack(gather.from_left + [far] + gather.from_right[:0:-1])
        distance = lax.rem(my_spot - jnp.arange(peers, dtype=jnp.int32) + peers, peers)
        by_spot = jnp.take(by_distance, distance, axis=0).reshape(span, -1).astype(jnp.float32)
        edges = [sum(columns[:i]) for i in range(5)]
        grads = [by_spot[:, edges[i] : edges[i + 1]] for i in range(4)]
    return grads, grad_w_in, grad_w_out


def solution(mesh):
    return jax.shard_map(
        per_device,
        mesh=mesh,
        in_specs=(
            P(None, ("dp", "expert"), None),
            P(None, ("dp", "expert")),
            P(None, ("dp", "expert"), None),
            P("dp"),
            P("dp"),
            P("dp", None),
            P("dp", None),
            P("dp", None),
            P("dp", None),
            P("expert", None, None),
            P("expert", None, None),
            P(None, ("dp", "expert"), None),
        ),
        out_specs=(
            P(None, ("dp", "expert"), None),
            P(None, ("dp", "expert"), None),
            P("dp"),
            P("dp"),
            P("dp", None),
            P("dp", None),
            P("dp", None),
            P("dp", None),
            P("expert", "dp", None),
            P("expert", "dp", None),
        ),
        check_vma=False,
    )
```
